32 devices in a mesh: seq: 8 (over y, x, core), head: 4 (over z).
Axes of the slice: x: 2, y: 2, z: 4, core: 2. Of those that a mesh axis runs over, the one named last changes fastest.
Arguments:
- teacher_queries: bfloat16 [2048, 8192], P('seq', 'head'), may hold values from -16 to 16, as said below
- student_queries: bfloat16 [2048, 4096], P('seq', 'head'), may hold values from -16 to 16, as said below
- token_counts: int32 [8], replicated, may hold values from 1 to 256, 1536 in all
Outputs:
- student_grad: float32 [2048, 4096], P('seq', 'head')
- loss: float32 [], replicated
The draws below stay inside these ranges and needn't reach their ends.
Inputs may be any that keep to these rules, and one draw needn't show every extreme that they name: `teacher_queries`: query entries are real values of order one; the entries of a row may share a scale. `student_queries`: query entries are real values of order one; the entries of a row may share a scale. `token_counts`: the counts sum to 1536; the largest equals 256.
All inputs are finite; a program needn't handle non-finite values.
Results may differ from the reference program's by a relative error of at most 0.0035.
Values may be sent and summed in bfloat16 or wider, within the bound.
No kernel may reach another device: no remote copies, remote signals or barrier semaphores. Data moves between devices by JAX's collectives and lax.ppermute only.
A program may use at most 64 MiB of HBM per device.

```python
import math
import jax
import jax.numpy as jnp
import numpy as np
from jax import lax

DT = 8192
DS = 4096
H_REL = 128
TOK_DEV = 256
SEQ_LEN = 2048
LIVE = 1536
N_SEQ = 8


def draw_teacher_queries(key, part):
    values = jax.random.normal(key, (SEQ_LEN, DT), jnp.float32)
    return jnp.clip(values, -16.0, 16.0).astype(jnp.bfloat16)


def draw_student_queries(key, part):
    values = jax.random.normal(key, (SEQ_LEN, DS), jnp.float32)
    return jnp.clip(values, -16.0, 16.0).astype(jnp.bfloat16)


def length_profile(count, total, most, skew):
    loads = [(1 << 20) // math.isqrt(standing ** skew) + 1 for standing in range(2, count + 1)]
    surplus, given = total - most - (count - 1), [1] * (count - 1)
    while surplus > 0:
        candidates = [i for i in range(count - 1) if given[i] < most]
        mass, budget = sum([loads[i] for i in candidates]), surplus
        for i in candidates:
            addition = min(most - given[i], max(1, budget * loads[i] // mass), surplus)
            given[i] = given[i] + addition
            surplus = surplus - addition
    return np.array([most] + given)


def uneven(key, count, total, bound, slope):
    if count == 2:
        one = jax.random.randint(key, (), max(1, total - bound), min(bound, total - 1) + 1)
        return jnp.stack([one, total - one])
    tallies = jnp.asarray(length_profile(count, total, bound, slope), jnp.int32)
    twos = (count - 1) // 2
    giver, receiver = tallies[1:1 + 2 * twos:2], tallies[2:2 + 2 * twos:2]
    slack = jnp.minimum(giver - 1, bound - receiver)
    moved = jax.random.randint(jax.random.fold_in(key, 1), (twos,), 0, 1 << 20) % (slack + 1)
    tallies = tallies.at[1:1 + 2 * twos:2].set(giver - moved).at[2:2 + 2 * twos:2].set(receiver + moved)
    return tallies[jax.random.permutation(jax.random.fold_in(key, 2), count)]


def setup_inputs(seed: int = 0) -> dict:
    keys = jax.random.split(jax.random.key(seed), 4)
    return {
        "teacher_queries": draw_teacher_queries(jax.random.fold_in(keys[3], 71), 0),
        "student_queries": draw_student_queries(jax.random.fold_in(keys[3], 71), 0),
        "token_counts": uneven(keys[2], N_SEQ, LIVE, TOK_DEV, 2).astype(jnp.int32),
    }


NEGATIVE = -1.0e30


def reference(teacher_queries, student_queries, token_counts):
    seq_rows = SEQ_LEN
    teacher_dim = DT // H_REL
    student_dim = DS // H_REL
    teacher_scale = teacher_dim ** -0.5
    student_scale = student_dim ** -0.5
    positions = jnp.arange(seq_rows, dtype=jnp.int32)
    owner_table = (positions // TOK_DEV)[:, None] == jnp.arange(N_SEQ, dtype=jnp.int32)[None, :]
    real_count = jnp.sum(jnp.where(owner_table, token_counts[None, :], 0), axis=1).astype(jnp.int32)
    is_real = (positions % TOK_DEV) < real_count
    allowed = (positions[None, :] <= positions[:, None]) & (is_real[None, :] | (positions[None, :] == positions[:, None]))
    teacher_heads = teacher_queries.reshape(seq_rows, H_REL, teacher_dim).transpose(1, 0, 2)
    student_heads = student_queries.reshape(seq_rows, H_REL, student_dim).transpose(1, 0, 2)

    def log_probs(logits):
        top_value = jnp.max(jnp.where(allowed, logits, NEGATIVE), axis=1)
        total_sum = jnp.sum(jnp.where(allowed, jnp.exp(logits - top_value[:, None]), 0.0), axis=1)
        return top_value + jnp.log(total_sum)

    def per_head(pair):
        teacher_part = pair[0].astype(jnp.float32)
        student_part = pair[1].astype(jnp.float32)
        teacher_logits = jnp.dot(teacher_part, teacher_part.T, precision=lax.Precision.HIGHEST) * teacher_scale
        student_logits = jnp.dot(student_part, student_part.T, precision=lax.Precision.HIGHEST) * student_scale
        teacher_lse = log_probs(teacher_logits)
        student_lse = log_probs(student_logits)
        teacher_prob = jnp.where(allowed, jnp.exp(teacher_logits - teacher_lse[:, None]), 0.0)
        student_prob = jnp.where(allowed, jnp.exp(student_logits - student_lse[:, None]), 0.0)
        row_kl = jnp.sum(teacher_prob * (teacher_logits - student_logits), axis=1) - teacher_lse + student_lse
        kl_sum = jnp.sum(jnp.where(is_real, row_kl, 0.0))
        weights = jnp.where(is_real[:, None], student_prob - teacher_prob, 0.0).astype(jnp.bfloat16)
        weights = lax.optimization_barrier(weights).astype(jnp.float32)
        gradient = jnp.dot(weights, student_part, precision=lax.Precision.HIGHEST)
        gradient = gradient + jnp.dot(weights.T, student_part, precision=lax.Precision.HIGHEST)
        return kl_sum, gradient * student_scale

    kl_sums, gradients = lax.map(per_head, (teacher_heads, student_heads))
    loss = jnp.sum(kl_sums) / (H_REL * jnp.sum(token_counts).astype(jnp.float32))
    student_grad = gradients.transpose(1, 0, 2).reshape(seq_rows, DS)
    return student_grad, loss
```

```python
import functools
import math

import jax
import jax.numpy as jnp
from jax import lax
from jax.experimental import pallas as pl
from jax.experimental.pallas import tpu as pltpu
from jax.sharding import PartitionSpec as P

DT = 8192
DS = 4096
H_REL = 128
TEACHER_DIM = DT // H_REL
STUDENT_DIM = DS // H_REL

NEGATIVE = -1e30
LOG2E = math.log2(math.e)
PAD = 8


def split_high_low(values):
    high = values.astype(jnp.bfloat16)
    low = (values - high.astype(jnp.float32)).astype(jnp.bfloat16)
    return high, low


def relation_kernel(
    blocks,
    heads,
    tiles,
    counts_ref,
    teacher_ref,
    student_ref,
    grad_ref,
    kl_ref,
    teacher_pack,
    student_pack,
    teacher_key,
    student_key,
    teacher_row,
    student_row,
    student_col,
    teacher_prob,
    student_prob,
    grad_cols,
    grad_rows,
):
    rows = teacher_ref.shape[0] // blocks
    live = tiles * rows

    offsets = []
    start = 0
    for b in range(blocks):
        offsets.append(start)
        start = start + counts_ref[b]

    window = rows + PAD
    position = lax.broadcasted_iota(jnp.int32, (window, rows), 0)
    token = lax.broadcasted_iota(jnp.int32, (window, rows), 1)
    teacher_pack[pl.ds(0, PAD), :] = jnp.zeros((PAD, teacher_pack.shape[1]), jnp.float32)
    student_pack[pl.ds(0, PAD), :] = jnp.zeros((PAD, student_pack.shape[1]), jnp.float32)
    bases, shifts = [], []
    for b in range(blocks):
        here = pl.ds(b * rows, rows)
        base = pl.multiple_of(offsets[b] // PAD * PAD, PAD) if b else 0
        shift = offsets[b] - base
        bases.append(base)
        shifts.append(shift)
        place = ((position == token + shift) & (token < counts_ref[b])).astype(jnp.bfloat16)
        for source, pack in ((teacher_ref, teacher_pack), (student_ref, student_pack)):
            moved = jnp.dot(place, source[here, :], preferred_element_type=jnp.float32)
            pack[pl.ds(base, PAD), :] = pack[pl.ds(base, PAD), :] + moved[:PAD]
            pack[pl.ds(base + PAD, rows), :] = moved[PAD:]

    for h in range(heads):
        for i in range(tiles):
            here = pl.ds(i * rows, rows)
            teacher = teacher_pack[here, h * TEACHER_DIM : (h + 1) * TEACHER_DIM]
            student = student_pack[here, h * STUDENT_DIM : (h + 1) * STUDENT_DIM]
            tb = teacher.astype(jnp.bfloat16)
            sb = student.astype(jnp.bfloat16)
            teacher_key[h, here, :] = jnp.concatenate([tb, tb], axis=1)
            student_key[h, here, :] = jnp.concatenate([sb, sb], axis=1)
            teacher_t = teacher.T
            student_t = student.T
            high, low = split_high_low(teacher_t * (LOG2E * TEACHER_DIM**-0.5))
            teacher_row[h, i] = jnp.concatenate([high, low], axis=0)
            high, low = split_high_low(student_t * (LOG2E * STUDENT_DIM**-0.5))
            student_row[h, i] = jnp.concatenate([high, low], axis=0)
            student_col[h, i] = student_t.astype(jnp.bfloat16)

    diag_allowed = lax.broadcasted_iota(jnp.int32, (rows, rows), 0) <= lax.broadcasted_iota(
        jnp.int32, (rows, rows), 1
    )

    def head_step(h, kl_total):
        for i in range(tiles):
            stats = []
            for j in range(i + 1):
                keys = pl.ds(j * rows, rows)
                teacher = jnp.dot(
                    teacher_key[h, keys, :], teacher_row[h, i], preferred_element_type=jnp.float32
                )
                student = jnp.dot(
                    student_key[h, keys, :], student_row[h, i], preferred_element_type=jnp.float32
                )
                if i == j:
                    teacher = jnp.where(diag_allowed, teacher, NEGATIVE)
                    student = jnp.where(diag_allowed, student, NEGATIVE)
                teacher_top = jnp.max(teacher, axis=0, keepdims=True)
                student_top = jnp.max(student, axis=0, keepdims=True)
                teacher_exp = jnp.exp2(teacher - teacher_top)
                student_exp = jnp.exp2(student - student_top)
                teacher_prob[j] = teacher_exp
                student_prob[j] = student_exp
                stats.append(
                    (
                        teacher_top,
                        student_top,
                        jnp.sum(teacher_exp, axis=0, keepdims=True),
                        jnp.sum(student_exp, axis=0, keepdims=True),
                        jnp.sum(teacher_exp * (teacher - student), axis=0, keepdims=True),
                    )
                )
            teacher_max = functools.reduce(jnp.maximum, [s[0] for s in stats])
            student_max = functools.reduce(jnp.maximum, [s[1] for s in stats])
            teacher_fix = [jnp.exp2(s[0] - teacher_max) for s in stats]
            student_fix = [jnp.exp2(s[1] - student_max) for s in stats]
            teacher_sum = sum(f * s[2] for f, s in zip(teacher_fix, stats))
            student_sum = sum(f * s[3] for f, s in zip(student_fix, stats))
            cross_sum = sum(f * s[4] for f, s in zip(teacher_fix, stats))
            divergence = (
                cross_sum / teacher_sum
                - teacher_max
                - jnp.log2(teacher_sum)
                + student_max
                + jnp.log2(student_sum)
            )
            kl_total = kl_total + divergence
            teacher_inv = 1.0 / teacher_sum
            student_inv = 1.0 / student_sum
            row_grad = jnp.zeros((STUDENT_DIM, rows), jnp.float32)
            for j in range(i + 1):
                weights = (
                    student_prob[j] * (student_fix[j] * student_inv)
                    - teacher_prob[j] * (teacher_fix[j] * teacher_inv)
                ).astype(jnp.bfloat16)
                row_grad = row_grad + jnp.dot(
                    student_col[h, j], weights, preferred_element_type=jnp.float32
                )
                key_grad = lax.dot_general(
                    student_col[h, i],
                    weights,
                    (((1,), (1,)), ((), ())),
                    preferred_element_type=jnp.float32,
                )
                if j < i:
                    grad_cols[h, j] = grad_cols[h, j] + key_grad
                else:
                    grad_cols[h, i] = row_grad + key_grad
        return kl_total

    kl_total = lax.fori_loop(0, heads, head_step, jnp.zeros((1, rows), jnp.float32))
    kl_ref[...] = kl_total * math.log(2.0)

    for i in range(tiles):
        columns = grad_cols[:, i].reshape(heads * STUDENT_DIM, rows)
        grad_rows[pl.ds(i * rows, rows), :] = columns.T * (STUDENT_DIM**-0.5)
    grad_rows[pl.ds(live, window), :] = jnp.zeros((window, heads * STUDENT_DIM), jnp.float32)
    position = lax.broadcasted_iota(jnp.int32, (rows, window), 1)
    token = lax.broadcasted_iota(jnp.int32, (rows, window), 0)
    for b in range(blocks):
        place = ((position == token + shifts[b]) & (token < counts_ref[b])).astype(jnp.bfloat16)
        block = grad_rows[pl.ds(bases[b], window), :].astype(jnp.bfloat16)
        grad_ref[pl.ds(b * rows, rows), :] = jnp.dot(
            place, block, preferred_element_type=jnp.float32
        ).astype(grad_ref.dtype)


def relation(teacher, student, token_counts):
    blocks = token_counts.shape[0]
    tokens = teacher.shape[0]
    rows = tokens // blocks
    tiles = tokens * 3 // 4 // rows
    heads = teacher.shape[1] // TEACHER_DIM
    live = tiles * rows
    f32, bf16 = jnp.float32, jnp.bfloat16
    vmem = pl.BlockSpec(memory_space=pltpu.VMEM)
    return pl.pallas_call(
        functools.partial(relation_kernel, blocks, heads, tiles),
        in_specs=[pl.BlockSpec(memory_space=pltpu.SMEM), vmem, vmem],
        out_specs=[vmem, vmem],
        out_shape=[
            jax.ShapeDtypeStruct((tokens, heads * STUDENT_DIM), bf16),
            jax.ShapeDtypeStruct((1, rows), f32),
        ],
        scratch_shapes=[
            pltpu.VMEM((live + rows + PAD, heads * TEACHER_DIM), f32),
            pltpu.VMEM((live + rows + PAD, heads * STUDENT_DIM), f32),
            pltpu.VMEM((heads, live, 2 * TEACHER_DIM), bf16),
            pltpu.VMEM((heads, live, 2 * STUDENT_DIM), bf16),
            pltpu.VMEM((heads, tiles, 2 * TEACHER_DIM, rows), bf16),
            pltpu.VMEM((heads, tiles, 2 * STUDENT_DIM, rows), bf16),
            pltpu.VMEM((heads, tiles, STUDENT_DIM, rows), bf16),
            pltpu.VMEM((tiles, rows, rows), f32),
            pltpu.VMEM((tiles, rows, rows), f32),
            pltpu.VMEM((heads, tiles, STUDENT_DIM, rows), f32),
            pltpu.VMEM((live + rows + PAD, heads * STUDENT_DIM), f32),
        ],
        compiler_params=pltpu.CompilerParams(vmem_limit_bytes=48 * 1024 * 1024),
        name="relation",
    )(token_counts, teacher, student)


def local(teacher_queries, student_queries, token_counts):
    teacher = lax.all_to_all(teacher_queries, "seq", 1, 0, tiled=True)
    student = lax.all_to_all(student_queries, "seq", 1, 0, tiled=True)
    grad, kl = relation(teacher, student, token_counts)
    loss = lax.psum(jnp.sum(kl), ("seq", "head")) / (
        H_REL * jnp.sum(token_counts).astype(jnp.float32)
    )
    student_grad = lax.all_to_all(grad, "seq", 0, 1, tiled=True).astype(jnp.float32)
    return (student_grad, loss)


def solution(mesh):
    return jax.shard_map(
        local,
        mesh=mesh,
        in_specs=(P("seq", "head"), P("seq", "head"), P()),
        out_specs=(P("seq", "head"), P()),
        check_vma=False,
    )
```

```python
import functools
import math

import jax
import jax.numpy as jnp
from jax import lax
from jax.experimental import pallas as pl
from jax.experimental.pallas import tpu as pltpu
from jax.sharding import PartitionSpec as P

DT = 8192
DS = 4096
H_REL = 128
TEACHER_DIM = DT // H_REL
STUDENT_DIM = DS // H_REL

NEGATIVE = -1e30
LOG2E = math.log2(math.e)
PAD = 8
LANES = 128


def split_high_low(values):
    high = values.astype(jnp.bfloat16)
    low = (values - high.astype(jnp.float32)).astype(jnp.bfloat16)
    return high, low


def at_columns(index, count, width, act):
    if width % LANES == 0:
        act(pl.ds(pl.multiple_of(index * width, LANES), width))
    else:
        for part in range(count):
            pl.when(index == part)(functools.partial(act, pl.ds(part * width, width)))


def pack_kernel(blocks, me_ref, teacher_ref, student_ref, *sends):
    teacher_width = teacher_ref.shape[1] // blocks
    student_width = student_ref.shape[1] // blocks
    for k in range(blocks):
        to = jnp.bitwise_xor(me_ref[0], k)

        def put_teacher(columns, send=sends[k]):
            send[:, :teacher_width] = teacher_ref[:, columns]

        def put_student(columns, send=sends[k]):
            send[:, teacher_width:] = student_ref[:, columns]

        at_columns(to, blocks, teacher_width, put_teacher)
        at_columns(to, blocks, student_width, put_student)


def unpack_kernel(blocks, live, me_ref, kl_ref, *refs):
    grad_ref, loss_ref = refs[blocks:]
    for k in range(blocks):

        def put(columns, source=refs[k]):
            grad_ref[:, columns] = source[...].astype(jnp.float32)

        at_columns(jnp.bitwise_xor(me_ref[0], k), blocks, refs[k].shape[1], put)
    total = jnp.sum(kl_ref[...], axis=0, keepdims=True)
    loss_ref[...] = total * (1.0 / (H_REL * live))


def relation_kernel(blocks, heads, tiles, me_ref, counts_ref, *refs):
    sources = refs[:blocks]
    grads = refs[blocks : 2 * blocks]
    (
        kl_ref,
        pack,
        teacher_key,
        student_key,
        teacher_row,
        student_row,
        student_col,
        teacher_prob,
        student_prob,
        grad_cols,
        grad_rows,
    ) = refs[2 * blocks :]
    rows = sources[0].shape[0]
    live = tiles * rows
    window = rows + PAD
    student_at = heads * TEACHER_DIM

    position = lax.broadcasted_iota(jnp.int32, (window, rows), 0)
    token = lax.broadcasted_iota(jnp.int32, (window, rows), 1)
    pack[...] = jnp.zeros(pack.shape, jnp.float32)
    places = []
    for k in range(blocks):
        owner = jnp.bitwise_xor(me_ref[0], k)
        start = sum(jnp.where(b < owner, counts_ref[b], 0) for b in range(blocks))
        base = pl.multiple_of(start // PAD * PAD, PAD)
        places.append((base, start - base, counts_ref[owner]))
    for source, (base, shift, count) in zip(sources, places):
        place = ((position == token + shift) & (token < count)).astype(jnp.bfloat16)
        moved = jnp.dot(place, source[...], preferred_element_type=jnp.float32)
        pack[pl.ds(base, window), :] = pack[pl.ds(base, window), :] + moved

    for h in range(heads):
        for i in range(tiles):
            here = pl.ds(i * rows, rows)
            teacher = pack[here, h * TEACHER_DIM : (h + 1) * TEACHER_DIM]
            student = pack[here, student_at + h * STUDENT_DIM : student_at + (h + 1) * STUDENT_DIM]
            tb = teacher.astype(jnp.bfloat16)
            sb = student.astype(jnp.bfloat16)
            teacher_key[h, here, :] = jnp.concatenate([tb, tb], axis=1)
            student_key[h, here, :] = jnp.concatenate([sb, sb], axis=1)
            teacher_t = teacher.T
            student_t = student.T
            high, low = split_high_low(teacher_t * (LOG2E * TEACHER_DIM**-0.5))
            teacher_row[h, i] = jnp.concatenate([high, low], axis=0)
            high, low = split_high_low(student_t * (LOG2E * STUDENT_DIM**-0.5))
            student_row[h, i] = jnp.concatenate([high, low], axis=0)
            student_col[h, i] = student_t.astype(jnp.bfloat16)

    diag_allowed = lax.broadcasted_iota(jnp.int32, (rows, rows), 0) <= lax.broadcasted_iota(
        jnp.int32, (rows, rows), 1
    )

    def head_step(h, kl_total):
        for i in range(tiles):
            stats = []
            for j in range(i + 1):
                keys = pl.ds(j * rows, rows)
                teacher = jnp.dot(
                    teacher_key[h, keys, :], teacher_row[h, i], preferred_element_type=jnp.float32
                )
                student = jnp.dot(
                    student_key[h, keys, :], student_row[h, i], preferred_element_type=jnp.float32
                )
                if i == j:
                    teacher = jnp.where(diag_allowed, teacher, NEGATIVE)
                    student = jnp.where(diag_allowed, student, NEGATIVE)
                teacher_top = jnp.max(teacher, axis=0, keepdims=True)
                student_top = jnp.max(student, axis=0, keepdims=True)
                teacher_exp = jnp.exp2(teacher - teacher_top)
                student_exp = jnp.exp2(student - student_top)
                teacher_prob[j] = teacher_exp
                student_prob[j] = student_exp
                stats.append(
                    (
                        teacher_top,
                        student_top,
                        jnp.sum(teacher_exp, axis=0, keepdims=True),
                        jnp.sum(student_exp, axis=0, keepdims=True),
                        jnp.sum(teacher_exp * (teacher - student), axis=0, keepdims=True),
                    )
                )
            teacher_max = functools.reduce(jnp.maximum, [s[0] for s in stats])
            student_max = functools.reduce(jnp.maximum, [s[1] for s in stats])
            teacher_fix = [jnp.exp2(s[0] - teacher_max) for s in stats]
            student_fix = [jnp.exp2(s[1] - student_max) for s in stats]
            teacher_sum = sum(f * s[2] for f, s in zip(teacher_fix, stats))
            student_sum = sum(f * s[3] for f, s in zip(student_fix, stats))
            cross_sum = sum(f * s[4] for f, s in zip(teacher_fix, stats))
            divergence = (
                cross_sum / teacher_sum
                - teacher_max
                - jnp.log2(teacher_sum)
                + student_max
                + jnp.log2(student_sum)
            )
            kl_total = kl_total + divergence
            teacher_inv = 1.0 / teacher_sum
            student_inv = 1.0 / student_sum
            row_grad = jnp.zeros((STUDENT_DIM, rows), jnp.float32)
            for j in range(i + 1):
                weights = (
                    student_prob[j] * (student_fix[j] * student_inv)
                    - teacher_prob[j] * (teacher_fix[j] * teacher_inv)
                ).astype(jnp.bfloat16)
                row_grad = row_grad + jnp.dot(
                    student_col[h, j], weights, preferred_element_type=jnp.float32
                )
                key_grad = lax.dot_general(
                    student_col[h, i],
                    weights,
                    (((1,), (1,)), ((), ())),
                    preferred_element_type=jnp.float32,
                )
                if j < i:
                    grad_cols[h, j] = grad_cols[h, j] + key_grad
                else:
                    grad_cols[h, i] = row_grad + key_grad
        return kl_total

    kl_total = lax.fori_loop(0, heads, head_step, jnp.zeros((1, rows), jnp.float32))
    kl_ref[...] = jnp.broadcast_to(
        jnp.sum(kl_total, axis=1, keepdims=True) * math.log(2.0), kl_ref.shape
    )

    for i in range(tiles):
        columns = grad_cols[:, i].reshape(heads * STUDENT_DIM, rows)
        grad_rows[pl.ds(i * rows, rows), :] = columns.T * (STUDENT_DIM**-0.5)
    grad_rows[pl.ds(live, window), :] = jnp.zeros((window, heads * STUDENT_DIM), jnp.float32)
    position = lax.broadcasted_iota(jnp.int32, (rows, window), 1)
    token = lax.broadcasted_iota(jnp.int32, (rows, window), 0)
    for grad, (base, shift, count) in zip(grads, places):
        place = ((position == token + shift) & (token < count)).astype(jnp.bfloat16)
        block = grad_rows[pl.ds(base, window), :].astype(jnp.bfloat16)
        grad[...] = jnp.dot(place, block, preferred_element_type=jnp.float32).astype(grad.dtype)


def local(teacher_queries, student_queries, token_counts):
    f32, bf16 = jnp.float32, jnp.bfloat16
    blocks = lax.axis_size("seq")
    devices = blocks * lax.axis_size("head")
    rows = teacher_queries.shape[0]
    heads = teacher_queries.shape[1] // TEACHER_DIM // blocks
    tiles = blocks * 3 // 4
    live = tiles * rows
    width = heads * (TEACHER_DIM + STUDENT_DIM)
    vmem = pl.BlockSpec(memory_space=pltpu.VMEM)
    smem = pl.BlockSpec(memory_space=pltpu.SMEM)
    params = pltpu.CompilerParams(vmem_limit_bytes=48 * 1024 * 1024)
    me = lax.axis_index("seq").reshape(1)

    def exchange(sends):
        return [
            send if k == 0 else lax.ppermute(send, "seq", [(i, i ^ k) for i in range(blocks)])
            for k, send in enumerate(sends)
        ]

    sends = pl.pallas_call(
        functools.partial(pack_kernel, blocks),
        in_specs=[smem, vmem, vmem],
        out_specs=[vmem] * blocks,
        out_shape=[jax.ShapeDtypeStruct((rows, width), bf16)] * blocks,
        compiler_params=params,
        name="pack",
    )(me, teacher_queries, student_queries)
    sources = exchange(sends)
    *grads, kl = pl.pallas_call(
        functools.partial(relation_kernel, blocks, heads, tiles),
        in_specs=[smem, smem] + [vmem] * blocks,
        out_specs=[vmem] * (blocks + 1),
        out_shape=[jax.ShapeDtypeStruct((rows, heads * STUDENT_DIM), bf16)] * blocks
        + [jax.ShapeDtypeStruct((devices, 128), f32)],
        scratch_shapes=[
            pltpu.VMEM((live + rows + PAD, width), f32),
            pltpu.VMEM((heads, live, 2 * TEACHER_DIM), bf16),
            pltpu.VMEM((heads, live, 2 * STUDENT_DIM), bf16),
            pltpu.VMEM((heads, tiles, 2 * TEACHER_DIM, rows), bf16),
            pltpu.VMEM((heads, tiles, 2 * STUDENT_DIM, rows), bf16),
            pltpu.VMEM((heads, tiles, STUDENT_DIM, rows), bf16),
            pltpu.VMEM((tiles, rows, rows), f32),
            pltpu.VMEM((tiles, rows, rows), f32),
            pltpu.VMEM((heads, tiles, STUDENT_DIM, rows), f32),
            pltpu.VMEM((live + rows + PAD, heads * STUDENT_DIM), f32),
        ],
        compiler_params=params,
        name="relation",
    )(me, token_counts, *sources)
    kl = lax.all_to_all(kl, ("seq", "head"), 0, 0, tiled=True)
    grads = exchange(grads)
    grad, loss = pl.pallas_call(
        functools.partial(unpack_kernel, blocks, live),
        in_specs=[smem] + [vmem] * (blocks + 1),
        out_specs=[vmem, vmem],
        out_shape=[
            jax.ShapeDtypeStruct((rows, student_queries.shape[1]), f32),
            jax.ShapeDtypeStruct((1, 128), f32),
        ],
        compiler_params=params,
        name="unpack",
    )(me, kl, *grads)
    return (grad, loss[0, 0])


def solution(mesh):
    return jax.shard_map(
        local,
        mesh=mesh,
        in_specs=(P("seq", "head"), P("seq", "head"), P()),
        out_specs=(P("seq", "head"), P()),
        check_vma=False,
    )
```

```python
import functools
import math

import jax
import jax.numpy as jnp
from jax import lax
from jax.experimental import pallas as pl
from jax.experimental.pallas import tpu as pltpu
from jax.sharding import PartitionSpec as P

DT = 8192
DS = 4096
H_REL = 128
TEACHER_DIM = DT // H_REL
STUDENT_DIM = DS // H_REL

NEGATIVE = -1e30
LOG2E = math.log2(math.e)
TEACHER_SCALE = LOG2E * TEACHER_DIM**-0.5
STUDENT_SCALE = LOG2E * STUDENT_DIM**-0.5
PAD = 8
LANES = 128
TAIL = 16
DEPTH = 256
SAFE_NORM = 320.0


def split_high_low(values):
    high = values.astype(jnp.bfloat16)
    low = (values - high.astype(jnp.float32)).astype(jnp.bfloat16)
    return high, low


def split_three(values):
    high = values.astype(jnp.bfloat16)
    rest = values - high.astype(jnp.float32)
    return (high,) + split_high_low(rest)


def at_columns(index, count, width, act):
    if width % LANES == 0:
        act(pl.ds(pl.multiple_of(index * width, LANES), width))
    else:
        for part in range(count):
            pl.when(index == part)(functools.partial(act, pl.ds(part * width, width)))


def pack_kernel(blocks, me_ref, teacher_ref, student_ref, *sends):
    teacher_width = teacher_ref.shape[1] // blocks
    student_width = student_ref.shape[1] // blocks
    for k in range(blocks):
        to = jnp.bitwise_xor(me_ref[0], k)

        def put_teacher(columns, send=sends[k]):
            send[:, :teacher_width] = teacher_ref[:, columns]

        def put_student(columns, send=sends[k]):
            send[:, teacher_width:] = student_ref[:, columns]

        at_columns(to, blocks, teacher_width, put_teacher)
        at_columns(to, blocks, student_width, put_student)


def pair_sum(parts):
    while len(parts) > 1:
        parts = [a + b for a, b in zip(parts[::2], parts[1::2])]
    return parts[0]


def sum_kernel(*refs):
    total = pair_sum([ref[...].astype(jnp.float32) for ref in refs[:-1]])
    refs[-1][...] = jnp.sum(total, axis=0, keepdims=True)


def unpack_kernel(blocks, me_ref, *refs):
    grad_ref = refs[blocks]
    for k in range(blocks):

        def put(columns, source=refs[k]):
            grad_ref[:, columns] = source[: grad_ref.shape[0], :].astype(jnp.float32)

        at_columns(jnp.bitwise_xor(me_ref[0], k), blocks, refs[k].shape[1], put)


def fold(values):
    rows, columns = values.shape
    return jnp.sum(values.reshape(rows // 8, 8, columns), axis=0)


def relation_kernel(blocks, heads, tiles, me_ref, counts_ref, *refs):
    sources = refs[:blocks]
    grads = refs[blocks : 2 * blocks]
    (
        pack,
        key_op,
        row_op,
        student_col,
        teacher_prob,
        student_prob,
        grad_cols,
        grad_rows,
        kl_sum,
    ) = refs[2 * blocks :]
    f32, bf16 = jnp.float32, jnp.bfloat16
    rows = sources[0].shape[0]
    live = tiles * rows
    window = rows + PAD
    student_at = heads * TEACHER_DIM
    filled = 2 * TEACHER_DIM + 2 * STUDENT_DIM

    position = lax.broadcasted_iota(jnp.int32, (window, rows), 0)
    token = lax.broadcasted_iota(jnp.int32, (window, rows), 1)
    pack[...] = jnp.zeros(pack.shape, f32)
    places = []
    for k in range(blocks):
        owner = jnp.bitwise_xor(me_ref[0], k)
        start = sum(jnp.where(b < owner, counts_ref[b], 0) for b in range(blocks))
        base = pl.multiple_of(start // PAD * PAD, PAD)
        places.append((base, start - base, counts_ref[owner]))
    for source, (base, shift, count) in zip(sources, places):
        place = ((position == token + shift) & (token < count)).astype(bf16)
        moved = jnp.dot(place, source[...], preferred_element_type=f32)
        pack[pl.ds(base, window), :] = pack[pl.ds(base, window), :] + moved

    ones = jnp.ones((rows, DEPTH - filled), bf16)
    spare = lax.broadcasted_iota(jnp.int32, (DEPTH - filled, rows), 0)
    teacher_gap = jnp.zeros((2 * STUDENT_DIM, rows), bf16)
    student_gap = jnp.zeros((2 * TEACHER_DIM, rows), bf16)
    norms = []

    def shift_rows(norm):
        parts = [part.astype(f32) for part in split_three(-norm)]
        out = jnp.where(spare == 0, parts[0], 0.0)
        out = jnp.where(spare == 1, parts[1], out)
        return jnp.where(spare == 2, parts[2], out).astype(bf16)

    for i in range(tiles):
        here = pl.ds(i * rows, rows)
        tile = pack[here, :]
        tile_t = tile.T
        tile_b = tile.astype(bf16)
        for h in range(heads):
            tb = tile_b[:, h * TEACHER_DIM : (h + 1) * TEACHER_DIM]
            at = student_at + h * STUDENT_DIM
            sb = tile_b[:, at : at + STUDENT_DIM]
            key_op[h, here, :] = jnp.concatenate([tb, tb, sb, sb, ones], axis=1)
            teacher_t = tile_t[h * TEACHER_DIM : (h + 1) * TEACHER_DIM, :]
            student_t = tile_t[at : at + STUDENT_DIM, :]
            student_col[h, i] = student_t.astype(bf16)
            teacher_norm = TEACHER_SCALE * jnp.sum(teacher_t * teacher_t, axis=0, keepdims=True)
            student_norm = STUDENT_SCALE * jnp.sum(student_t * student_t, axis=0, keepdims=True)
            norms += [teacher_norm, student_norm]
            high, low = split_high_low(teacher_t * TEACHER_SCALE)
            teacher_op = [high, low, teacher_gap, shift_rows(teacher_norm)]
            row_op[h, i, :, :rows] = jnp.concatenate(teacher_op, axis=0)
            high, low = split_high_low(student_t * STUDENT_SCALE)
            student_op = [student_gap, high, low, shift_rows(student_norm)]
            row_op[h, i, :, rows:] = jnp.concatenate(student_op, axis=0)

    safe = jnp.max(functools.reduce(jnp.maximum, norms)) <= SAFE_NORM
    key_pos = lax.broadcasted_iota(jnp.int32, (rows, rows), 0)
    row_pos = lax.broadcasted_iota(jnp.int32, (rows, rows), 1)

    def logits(h, i, j):
        keys = pl.ds(pl.multiple_of(j * rows, rows), rows)
        both = jnp.dot(key_op[h, keys, :], row_op[h, i], preferred_element_type=f32)
        return both[:, :rows], both[:, rows:]

    def row_term(h, j, weights):
        return jnp.dot(student_col[h, j], weights, preferred_element_type=f32)

    def key_term(h, i, weights):
        return lax.dot_general(
            student_col[h, i], weights, (((1,), (1,)), ((), ())), preferred_element_type=f32
        )

    @pl.when(safe)
    def shifted_by_own_logit():
        def head_step(h, kl_total):
            for i in range(tiles):
                teacher_sum = student_sum = cross_sum = jnp.zeros((8, rows), f32)
                for j in range(i + 1):
                    teacher, student = logits(h, i, j)
                    if i == j:
                        teacher = jnp.where(key_pos <= row_pos, teacher, NEGATIVE)
                        student = jnp.where(key_pos <= row_pos, student, NEGATIVE)
                    teacher_exp = jnp.exp2(teacher)
                    student_exp = jnp.exp2(student)
                    teacher_prob[j] = teacher_exp
                    student_prob[j] = student_exp
                    teacher_sum = teacher_sum + fold(teacher_exp)
                    student_sum = student_sum + fold(student_exp)
                    cross_sum = cross_sum + fold(teacher_exp * (teacher - student))
                teacher_sum = jnp.sum(teacher_sum, axis=0, keepdims=True)
                student_sum = jnp.sum(student_sum, axis=0, keepdims=True)
                cross_sum = jnp.sum(cross_sum, axis=0, keepdims=True)
                teacher_inv = 1.0 / teacher_sum
                student_inv = 1.0 / student_sum
                kl_total = kl_total + (
                    cross_sum * teacher_inv - jnp.log2(teacher_sum) + jnp.log2(student_sum)
                )
                row_grad = jnp.zeros((STUDENT_DIM, rows), f32)
                for j in range(i + 1):
                    weights = (
                        student_prob[j] * student_inv - teacher_prob[j] * teacher_inv
                    ).astype(bf16)
                    row_grad = row_grad + row_term(h, j, weights)
                    key_grad = key_term(h, i, weights)
                    if j < i:
                        grad_cols[h, j] = grad_cols[h, j] + key_grad
                    else:
                        grad_cols[h, i] = row_grad + key_grad
            return kl_total

        kl_sum[...] = lax.fori_loop(0, heads, head_step, jnp.zeros((1, rows), f32))

    @pl.when(jnp.logical_not(safe))
    def shifted_by_maximum():
        kl_sum[...] = jnp.zeros((1, rows), f32)
        grad_cols[...] = jnp.zeros(grad_cols.shape, f32)

        def masked(h, i, j):
            allowed = key_pos + j * rows <= row_pos + i * rows
            teacher, student = logits(h, i, j)
            return jnp.where(allowed, teacher, NEGATIVE), jnp.where(allowed, student, NEGATIVE)

        def row_step(step, _):
            h, i = step // tiles, step % tiles

            def advance(j, state):
                teacher_max, teacher_sum, cross_sum, student_max, student_sum = state
                teacher, student = masked(h, i, j)
                teacher_top = jnp.maximum(teacher_max, jnp.max(teacher, axis=0, keepdims=True))
                student_top = jnp.maximum(student_max, jnp.max(student, axis=0, keepdims=True))
                teacher_exp = jnp.exp2(teacher - teacher_top)
                student_exp = jnp.exp2(student - student_top)
                shrink = jnp.exp2(teacher_max - teacher_top)
                cross = jnp.sum(teacher_exp * (teacher - student), axis=0, keepdims=True)
                return (
                    teacher_top,
                    teacher_sum * shrink + jnp.sum(teacher_exp, axis=0, keepdims=True),
                    cross_sum * shrink + cross,
                    student_top,
                    student_sum * jnp.exp2(student_max - student_top)
                    + jnp.sum(student_exp, axis=0, keepdims=True),
                )

            lowest = jnp.full((1, rows), NEGATIVE, f32)
            zeros = jnp.zeros((1, rows), f32)
            teacher_max, teacher_sum, cross_sum, student_max, student_sum = lax.fori_loop(
                0, i + 1, advance, (lowest, zeros, zeros, lowest, zeros)
            )
            teacher_lse = teacher_max + jnp.log2(teacher_sum)
            student_lse = student_max + jnp.log2(student_sum)
            kl_sum[...] = kl_sum[...] + (cross_sum / teacher_sum - teacher_lse + student_lse)

            def spread(j, row_grad):
                teacher, student = masked(h, i, j)
                weights = jnp.exp2(student - student_lse) - jnp.exp2(teacher - teacher_lse)
                weights = weights.astype(bf16)
                grad_cols[h, j] = grad_cols[h, j] + key_term(h, i, weights)
                return row_grad + row_term(h, j, weights)

            row_grad = lax.fori_loop(0, i + 1, spread, jnp.zeros((STUDENT_DIM, rows), f32))
            grad_cols[h, i] = grad_cols[h, i] + row_grad
            return 0

        lax.fori_loop(0, heads * tiles, row_step, 0)

    for i in range(tiles):
        columns = grad_cols[:, i].reshape(heads * STUDENT_DIM, rows)
        grad_rows[pl.ds(i * rows, rows), :] = columns.T * (STUDENT_DIM**-0.5)
    grad_rows[pl.ds(live, window), :] = jnp.zeros((window, heads * STUDENT_DIM), f32)
    divergence = jnp.sum(kl_sum[...], axis=1, keepdims=True) * math.log(2.0)
    parts = [part.astype(f32) for part in split_three(divergence)]
    line = lax.broadcasted_iota(jnp.int32, (TAIL, heads * STUDENT_DIM), 0)
    tail = jnp.where(line == 0, parts[0], 0.0)
    tail = jnp.where(line == 1, parts[1], tail)
    tail = jnp.where(line == 2, parts[2], tail).astype(bf16)
    position = lax.broadcasted_iota(jnp.int32, (rows, window), 1)
    token = lax.broadcasted_iota(jnp.int32, (rows, window), 0)
    for grad, (base, shift, count) in zip(grads, places):
        place = ((position == token + shift) & (token < count)).astype(bf16)
        block = grad_rows[pl.ds(base, window), :].astype(bf16)
        grad[:rows, :] = jnp.dot(place, block, preferred_element_type=f32).astype(bf16)
        grad[rows:, :] = tail


def local(teacher_queries, student_queries, token_counts):
    f32, bf16 = jnp.float32, jnp.bfloat16
    blocks = lax.axis_size("seq")
    rows = teacher_queries.shape[0]
    heads = teacher_queries.shape[1] // TEACHER_DIM // blocks
    tiles = blocks * 3 // 4
    live = tiles * rows
    width = heads * (TEACHER_DIM + STUDENT_DIM)
    vmem = pl.BlockSpec(memory_space=pltpu.VMEM)
    smem = pl.BlockSpec(memory_space=pltpu.SMEM)
    params = pltpu.CompilerParams(vmem_limit_bytes=48 * 1024 * 1024)
    me = lax.axis_index("seq").reshape(1)

    far_first = sorted(range(1, blocks), key=lambda k: -(k >> 1).bit_count())

    def exchange(sends):
        out = list(sends)
        for k in far_first:
            out[k] = lax.ppermute(sends[k], "seq", [(i, i ^ k) for i in range(blocks)])
        return out

    sends = pl.pallas_call(
        functools.partial(pack_kernel, blocks),
        in_specs=[smem, vmem, vmem],
        out_specs=[vmem] * blocks,
        out_shape=[jax.ShapeDtypeStruct((rows, width), bf16)] * blocks,
        compiler_params=params,
        name="pack",
    )(me, teacher_queries, student_queries)
    sources = exchange(sends)
    grads = pl.pallas_call(
        functools.partial(relation_kernel, blocks, heads, tiles),
        in_specs=[smem, smem] + [vmem] * blocks,
        out_specs=[vmem] * blocks,
        out_shape=[jax.ShapeDtypeStruct((rows + TAIL, heads * STUDENT_DIM), bf16)] * blocks,
        scratch_shapes=[
            pltpu.VMEM((live + rows + PAD, width), f32),
            pltpu.VMEM((heads, live, DEPTH), bf16),
            pltpu.VMEM((heads, tiles, DEPTH, 2 * rows), bf16),
            pltpu.VMEM((heads, tiles, STUDENT_DIM, rows), bf16),
            pltpu.VMEM((tiles, rows, rows), f32),
            pltpu.VMEM((tiles, rows, rows), f32),
            pltpu.VMEM((heads, tiles, STUDENT_DIM, rows), f32),
            pltpu.VMEM((live + rows + PAD, heads * STUDENT_DIM), f32),
            pltpu.VMEM((1, rows), f32),
        ],
        compiler_params=params,
        name="relation",
    )(me, token_counts, *sources)
    grads = exchange(grads)
    kl = pl.pallas_call(
        sum_kernel,
        grid=(1,),
        in_specs=[pl.BlockSpec((TAIL, heads * STUDENT_DIM), lambda _: (rows // TAIL, 0))] * blocks,
        out_specs=pl.BlockSpec((1, heads * STUDENT_DIM), lambda _: (0, 0)),
        out_shape=jax.ShapeDtypeStruct((1, heads * STUDENT_DIM), f32),
        name="sum_kl",
    )(*grads)
    groups = lax.axis_size("head")
    total = pair_sum(
        [kl]
        + [
            lax.ppermute(kl, "head", [(i, i ^ k) for i in range(groups)])
            for k in range(1, groups)
        ]
    )
    grad = pl.pallas_call(
        functools.partial(unpack_kernel, blocks),
        in_specs=[smem] + [vmem] * blocks,
        out_specs=vmem,
        out_shape=jax.ShapeDtypeStruct((rows, student_queries.shape[1]), f32),
        compiler_params=params,
        name="unpack",
    )(me, *grads)
    return (grad, total[0, 0] / (H_REL * jnp.sum(token_counts).astype(f32)))


def solution(mesh):
    return jax.shard_map(
        local,
        mesh=mesh,
        in_specs=(P("seq", "head"), P("seq", "head"), P()),
        out_specs=(P("seq", "head"), P()),
        check_vma=False,
    )
```

```python
import functools
import math

import jax
import jax.numpy as jnp
from jax import lax
from jax.experimental import pallas as pl
from jax.experimental.pallas import tpu as pltpu
from jax.sharding import PartitionSpec as P

DT = 8192
DS = 4096
H_REL = 128
TEACHER_DIM = DT // H_REL
STUDENT_DIM = DS // H_REL

NEGATIVE = -1e30
LOG2E = math.log2(math.e)
TEACHER_SCALE = LOG2E * TEACHER_DIM**-0.5
STUDENT_SCALE = LOG2E * STUDENT_DIM**-0.5
PAD = 8
LANES = 128
TAIL = 16
DEPTH = 256
SAFE_NORM = 320.0


def split_high_low(values):
    high = values.astype(jnp.bfloat16)
    low = (values - high.astype(jnp.float32)).astype(jnp.bfloat16)
    return high, low


def split_three(values):
    high = values.astype(jnp.bfloat16)
    rest = values - high.astype(jnp.float32)
    return (high,) + split_high_low(rest)


def at_columns(index, count, width, act):
    if width % LANES == 0:
        act(pl.ds(pl.multiple_of(index * width, LANES), width))
    else:
        for part in range(count):
            pl.when(index == part)(functools.partial(act, pl.ds(part * width, width)))


def pack_folded_kernel(blocks, chunks, me_ref, teacher_ref, student_ref, *refs):
    sends, student, sems = refs[: 2 * chunks], refs[2 * chunks], refs[2 * chunks + 1]
    rows = teacher_ref.shape[0]
    half = rows // 2
    copies = [pltpu.make_async_copy(student_ref, student, sems.at[2 * chunks * blocks // 2])]
    for chunk in range(chunks):
        for core in range(2):
            for k in range(blocks // 2):
                to = jnp.bitwise_xor(me_ref[0], 2 * k + core)
                at = pl.multiple_of((to * chunks + chunk) * LANES, LANES)
                copies.append(
                    pltpu.make_async_copy(
                        teacher_ref.at[:, pl.ds(at, LANES)],
                        sends[2 * chunk + core].at[k, pl.ds(0, rows)],
                        sems.at[(2 * chunk + core) * (blocks // 2) + k],
                    )
                )
    for copy in copies:
        copy.start()
    copies[0].wait()
    for core in range(2):
        for k in range(blocks // 2):
            to = jnp.bitwise_xor(me_ref[0], 2 * k + core)
            lanes = pl.ds(pl.multiple_of(to * LANES, LANES), LANES)
            top, bottom = student[:half, lanes], student[half:, lanes]
            for chunk in range(chunks):
                part = slice(chunk * (LANES // 2), (chunk + 1) * (LANES // 2))
                sends[2 * chunk + core][k, rows:, :] = jnp.concatenate(
                    [top[:, part], bottom[:, part]], axis=1
                )
    for copy in copies[1:]:
        copy.wait()


def pack_plain_kernel(blocks, me_ref, teacher_ref, student_ref, *sends):
    teacher_width = teacher_ref.shape[1] // blocks
    student_width = student_ref.shape[1] // blocks
    for core in range(2):
        for k in range(blocks // 2):
            to = jnp.bitwise_xor(me_ref[0], 2 * k + core)

            def put_teacher(columns, send=sends[core], k=k):
                send[k, :, :teacher_width] = teacher_ref[:, columns]

            def put_student(columns, send=sends[core], k=k):
                send[k, :, teacher_width:] = student_ref[:, columns]

            at_columns(to, blocks, teacher_width, put_teacher)
            at_columns(to, blocks, student_width, put_student)


def merge_kernel(kept_ref, swapped_ref, *sends):
    for k, send in enumerate(sends):
        send[0] = kept_ref[k + 1]
        send[1] = swapped_ref[k + 1]


def pair_sum(parts):
    while len(parts) > 1:
        parts = [a + b for a, b in zip(parts[::2], parts[1::2])]
    return parts[0]


def arrived(refs):
    return [refs[0].at[0], refs[1].at[0]] + [ref.at[core] for ref in refs[2:] for core in range(2)]


def sum_kernel(counts_ref, *refs):
    blocks = arrived(refs[:-1])
    total = pair_sum([block[block.shape[0] - TAIL :, :].astype(jnp.float32) for block in blocks])
    tokens = sum(counts_ref[b] for b in range(len(blocks)))
    refs[-1][...] = jnp.sum(total, axis=0, keepdims=True) / (H_REL * tokens).astype(jnp.float32)


def unpack_kernel(me_ref, *refs):
    grad_ref = refs[-1]
    blocks = arrived(refs[:-1])
    for k, block in enumerate(blocks):

        def put(columns, block=block):
            grad_ref[:, columns] = block[: grad_ref.shape[0], :].astype(jnp.float32)

        at_columns(jnp.bitwise_xor(me_ref[0], k), len(blocks), block.shape[1], put)


def fold(values):
    rows, columns = values.shape
    return jnp.sum(values.reshape(rows // 8, 8, columns), axis=0)


def relation_kernel(folded, heads, tiles, n_in, n_done, last, me_ref, counts_ref, *refs):
    sources = arrived(refs[:n_in])
    done = refs[n_in : n_in + 2 * n_done]
    out_a, out_b, pack, key_op, row_op, student_col, teacher_prob, student_prob = refs[
        n_in + 2 * n_done : n_in + 2 * n_done + 8
    ]
    if last:
        grad_cols, kl_sum, grad_rows = refs[n_in + 2 * n_done + 8 :]
    else:
        grad_cols, kl_sum = out_a, out_b
    f32, bf16 = jnp.float32, jnp.bfloat16
    blocks = len(sources)
    rows = teacher_prob.shape[1]
    half = rows // 2
    live = tiles * rows
    window = rows + PAD
    student_at = heads * TEACHER_DIM
    student_width = heads * STUDENT_DIM
    filled = 2 * TEACHER_DIM + 2 * STUDENT_DIM

    position = lax.broadcasted_iota(jnp.int32, (window, rows), 0)
    token = lax.broadcasted_iota(jnp.int32, (window, rows), 1)
    pack[...] = jnp.zeros(pack.shape, f32)
    places = []
    for k in range(blocks):
        owner = jnp.bitwise_xor(me_ref[0], k)
        start = sum(jnp.where(b < owner, counts_ref[b], 0) for b in range(blocks))
        base = pl.multiple_of(start // PAD * PAD, PAD)
        places.append((base, start - base, counts_ref[owner]))
    for source, (base, shift, count) in zip(sources, places):
        place = ((position == token + shift) & (token < count)).astype(bf16)
        here = pl.ds(base, window)
        if folded:
            moved = jnp.dot(place, source[:rows, :], preferred_element_type=f32)
            pack[here, :student_at] = pack[here, :student_at] + moved
            student = source[rows:, :]
            moved = jnp.dot(
                place[:, :half], student[:, :student_width], preferred_element_type=f32
            ) + jnp.dot(place[:, half:], student[:, student_width:], preferred_element_type=f32)
            pack[here, student_at:] = pack[here, student_at:] + moved
        else:
            moved = jnp.dot(place, source[...], preferred_element_type=f32)
            pack[here, :] = pack[here, :] + moved

    ones = jnp.ones((rows, DEPTH - filled), bf16)
    spare = lax.broadcasted_iota(jnp.int32, (DEPTH - filled, rows), 0)
    teacher_gap = jnp.zeros((2 * STUDENT_DIM, rows), bf16)
    student_gap = jnp.zeros((2 * TEACHER_DIM, rows), bf16)
    norms = []

    def shift_rows(norm):
        parts = [part.astype(f32) for part in split_three(-norm)]
        out = jnp.where(spare == 0, parts[0], 0.0)
        out = jnp.where(spare == 1, parts[1], out)
        return jnp.where(spare == 2, parts[2], out).astype(bf16)

    for i in range(tiles):
        here = pl.ds(i * rows, rows)
        tile = pack[here, :]
        tile_t = tile.T
        tile_b = tile.astype(bf16)
        for h in range(heads):
            tb = tile_b[:, h * TEACHER_DIM : (h + 1) * TEACHER_DIM]
            at = student_at + h * STUDENT_DIM
            sb = tile_b[:, at : at + STUDENT_DIM]
            key_op[h, here, :] = jnp.concatenate([tb, tb, sb, sb, ones], axis=1)
            teacher_t = tile_t[h * TEACHER_DIM : (h + 1) * TEACHER_DIM, :]
            student_t = tile_t[at : at + STUDENT_DIM, :]
            student_col[h, i] = student_t.astype(bf16)
            teacher_norm = TEACHER_SCALE * jnp.sum(teacher_t * teacher_t, axis=0, keepdims=True)
            student_norm = STUDENT_SCALE * jnp.sum(student_t * student_t, axis=0, keepdims=True)
            norms += [teacher_norm, student_norm]
            high, low = split_high_low(teacher_t * TEACHER_SCALE)
            teacher_op = [high, low, teacher_gap, shift_rows(teacher_norm)]
            row_op[h, i, :, :rows] = jnp.concatenate(teacher_op, axis=0)
            high, low = split_high_low(student_t * STUDENT_SCALE)
            student_op = [student_gap, high, low, shift_rows(student_norm)]
            row_op[h, i, :, rows:] = jnp.concatenate(student_op, axis=0)

    safe = jnp.max(functools.reduce(jnp.maximum, norms)) <= SAFE_NORM
    key_pos = lax.broadcasted_iota(jnp.int32, (rows, rows), 0)
    row_pos = lax.broadcasted_iota(jnp.int32, (rows, rows), 1)

    def logits(h, i, j):
        keys = pl.ds(pl.multiple_of(j * rows, rows), rows)
        both = jnp.dot(key_op[h, keys, :], row_op[h, i], preferred_element_type=f32)
        return both[:, :rows], both[:, rows:]

    def row_term(h, j, weights):
        return jnp.dot(student_col[h, j], weights, preferred_element_type=f32)

    def key_term(h, i, weights):
        return lax.dot_general(
            student_col[h, i], weights, (((1,), (1,)), ((), ())), preferred_element_type=f32
        )

    @pl.when(safe)
    def shifted_by_own_logit():
        def head_step(h, kl_total):
            for i in range(tiles):
                teacher_sum = student_sum = cross_sum = jnp.zeros((8, rows), f32)
                for j in range(i + 1):
                    teacher, student = logits(h, i, j)
                    if i == j:
                        teacher = jnp.where(key_pos <= row_pos, teacher, NEGATIVE)
                        student = jnp.where(key_pos <= row_pos, student, NEGATIVE)
                    teacher_exp = jnp.exp2(teacher)
                    student_exp = jnp.exp2(student)
                    teacher_prob[j] = teacher_exp
                    student_prob[j] = student_exp
                    teacher_sum = teacher_sum + fold(teacher_exp)
                    student_sum = student_sum + fold(student_exp)
                    cross_sum = cross_sum + fold(teacher_exp * (teacher - student))
                teacher_sum = jnp.sum(teacher_sum, axis=0, keepdims=True)
                student_sum = jnp.sum(student_sum, axis=0, keepdims=True)
                cross_sum = jnp.sum(cross_sum, axis=0, keepdims=True)
                teacher_inv = 1.0 / teacher_sum
                student_inv = 1.0 / student_sum
                kl_total = kl_total + (
                    cross_sum * teacher_inv - jnp.log2(teacher_sum) + jnp.log2(student_sum)
                )
                row_grad = jnp.zeros((STUDENT_DIM, rows), f32)
                for j in range(i + 1):
                    weights = (
                        student_prob[j] * student_inv - teacher_prob[j] * teacher_inv
                    ).astype(bf16)
                    row_grad = row_grad + row_term(h, j, weights)
                    key_grad = key_term(h, i, weights)
                    if j < i:
                        grad_cols[h, j] = grad_cols[h, j] + key_grad
                    else:
                        grad_cols[h, i] = row_grad + key_grad
            return kl_total

        kl_sum[...] = lax.fori_loop(0, heads, head_step, jnp.zeros((1, rows), f32))

    @pl.when(jnp.logical_not(safe))
    def shifted_by_maximum():
        kl_sum[...] = jnp.zeros((1, rows), f32)
        grad_cols[...] = jnp.zeros(grad_cols.shape, f32)

        def masked(h, i, j):
            allowed = key_pos + j * rows <= row_pos + i * rows
            teacher, student = logits(h, i, j)
            return jnp.where(allowed, teacher, NEGATIVE), jnp.where(allowed, student, NEGATIVE)

        def row_step(step, _):
            h, i = step // tiles, step % tiles

            def advance(j, state):
                teacher_max, teacher_sum, cross_sum, student_max, student_sum = state
                teacher, student = masked(h, i, j)
                teacher_top = jnp.maximum(teacher_max, jnp.max(teacher, axis=0, keepdims=True))
                student_top = jnp.maximum(student_max, jnp.max(student, axis=0, keepdims=True))
                teacher_exp = jnp.exp2(teacher - teacher_top)
                student_exp = jnp.exp2(student - student_top)
                shrink = jnp.exp2(teacher_max - teacher_top)
                cross = jnp.sum(teacher_exp * (teacher - student), axis=0, keepdims=True)
                return (
                    teacher_top,
                    teacher_sum * shrink + jnp.sum(teacher_exp, axis=0, keepdims=True),
                    cross_sum * shrink + cross,
                    student_top,
                    student_sum * jnp.exp2(student_max - student_top)
                    + jnp.sum(student_exp, axis=0, keepdims=True),
                )

            lowest = jnp.full((1, rows), NEGATIVE, f32)
            zeros = jnp.zeros((1, rows), f32)
            teacher_max, teacher_sum, cross_sum, student_max, student_sum = lax.fori_loop(
                0, i + 1, advance, (lowest, zeros, zeros, lowest, zeros)
            )
            teacher_lse = teacher_max + jnp.log2(teacher_sum)
            student_lse = student_max + jnp.log2(student_sum)
            kl_sum[...] = kl_sum[...] + (cross_sum / teacher_sum - teacher_lse + student_lse)

            def spread(j, row_grad):
                teacher, student = masked(h, i, j)
                weights = jnp.exp2(student - student_lse) - jnp.exp2(teacher - teacher_lse)
                weights = weights.astype(bf16)
                grad_cols[h, j] = grad_cols[h, j] + key_term(h, i, weights)
                return row_grad + row_term(h, j, weights)

            row_grad = lax.fori_loop(0, i + 1, spread, jnp.zeros((STUDENT_DIM, rows), f32))
            grad_cols[h, i] = grad_cols[h, i] + row_grad
            return 0

        lax.fori_loop(0, heads * tiles, row_step, 0)

    if not last:
        return

    parts = [ref for ref in done[::2]] + [grad_cols]
    total_width = len(parts) * student_width
    for i in range(tiles):
        columns = jnp.concatenate([p[:, i].reshape(student_width, rows) for p in parts], axis=0)
        grad_rows[pl.ds(i * rows, rows), :] = columns.T * (STUDENT_DIM**-0.5)
    grad_rows[pl.ds(live, window), :] = jnp.zeros((window, total_width), f32)
    kl_total = sum([ref[...] for ref in done[1::2]] + [kl_sum[...]])
    divergence = jnp.sum(kl_total, axis=1, keepdims=True) * math.log(2.0)
    thirds = [part.astype(f32) for part in split_three(divergence)]
    line = lax.broadcasted_iota(jnp.int32, (TAIL, total_width), 0)
    tail = jnp.where(line == 0, thirds[0], 0.0)
    tail = jnp.where(line == 1, thirds[1], tail)
    tail = jnp.where(line == 2, thirds[2], tail).astype(bf16)
    position = lax.broadcasted_iota(jnp.int32, (rows, window), 1)
    token = lax.broadcasted_iota(jnp.int32, (rows, window), 0)
    for k, (base, shift, count) in enumerate(places):
        out = out_b if k % 2 else out_a
        place = ((position == token + shift) & (token < count)).astype(bf16)
        block = grad_rows[pl.ds(base, window), :].astype(bf16)
        out[k // 2, :rows, :] = jnp.dot(place, block, preferred_element_type=f32).astype(bf16)
        out[k // 2, rows:, :] = tail


def local(teacher_queries, student_queries, token_counts):
    f32, bf16 = jnp.float32, jnp.bfloat16
    blocks = lax.axis_size("seq")
    chips = blocks // 2
    groups = lax.axis_size("head")
    rows = teacher_queries.shape[0]
    heads = teacher_queries.shape[1] // TEACHER_DIM // blocks
    tiles = blocks * 3 // 4
    live = tiles * rows
    folded = heads * STUDENT_DIM == LANES
    chunks = 2 if folded else 1
    chunk_heads = heads // chunks
    teacher_width = chunk_heads * TEACHER_DIM
    student_width = chunk_heads * STUDENT_DIM
    if folded:
        send_shape = (chips, rows + rows // 2, LANES)
    else:
        send_shape = (chips, rows, teacher_width + student_width)
    vmem = pl.BlockSpec(memory_space=pltpu.VMEM)
    smem = pl.BlockSpec(memory_space=pltpu.SMEM)
    params = pltpu.CompilerParams(vmem_limit_bytes=40 * 1024 * 1024)
    me = lax.axis_index("seq").reshape(1)
    far_first = sorted(range(1, chips), key=lambda k: -k.bit_count())

    def exchange(kept, swapped):
        swapped = lax.ppermute(swapped, "seq", [(i, i ^ 1) for i in range(blocks)])
        shape = (2,) + kept.shape[1:]
        sends = pl.pallas_call(
            merge_kernel,
            in_specs=[vmem] * 2,
            out_specs=[vmem] * (chips - 1),
            out_shape=[jax.ShapeDtypeStruct(shape, bf16)] * (chips - 1),
            compiler_params=params,
            name="merge",
        )(kept, swapped)
        out = [None] * (chips - 1)
        for k in far_first:
            pairs = [(i, i ^ (2 * k)) for i in range(blocks)]
            out[k - 1] = lax.ppermute(sends[k - 1], "seq", pairs)
        return [kept, swapped] + out

    packed = jax.ShapeDtypeStruct(send_shape, bf16)
    if folded:
        anywhere = pl.BlockSpec(memory_space=pl.ANY)
        sends = pl.pallas_call(
            functools.partial(pack_folded_kernel, blocks, chunks),
            in_specs=[smem, anywhere, anywhere],
            out_specs=[vmem] * (2 * chunks),
            out_shape=[packed] * (2 * chunks),
            scratch_shapes=[
                pltpu.VMEM(student_queries.shape, bf16),
                pltpu.SemaphoreType.DMA((chunks * blocks + 1,)),
            ],
            compiler_params=params,
            name="pack",
        )(me, teacher_queries, student_queries)
    else:
        sends = pl.pallas_call(
            functools.partial(pack_plain_kernel, blocks),
            in_specs=[smem, vmem, vmem],
            out_specs=[vmem] * 2,
            out_shape=[packed] * 2,
            compiler_params=params,
            name="pack",
        )(me, teacher_queries, student_queries)
    incoming = [exchange(*sends[2 * c : 2 * c + 2]) for c in range(chunks)]

    result = jax.ShapeDtypeStruct((chunk_heads, tiles, STUDENT_DIM, rows), f32)
    message = jax.ShapeDtypeStruct((chips, rows + TAIL, heads * STUDENT_DIM), bf16)
    kl_shape = jax.ShapeDtypeStruct((1, rows), f32)
    pairs = chunk_heads * tiles * (tiles + 1) // 2 * rows * rows
    done = []
    for c in range(chunks):
        last = c == chunks - 1
        scratch = [
            pltpu.VMEM((live + rows + PAD, teacher_width + student_width), f32),
            pltpu.VMEM((chunk_heads, live, DEPTH), bf16),
            pltpu.VMEM((chunk_heads, tiles, DEPTH, 2 * rows), bf16),
            pltpu.VMEM((chunk_heads, tiles, STUDENT_DIM, rows), bf16),
            pltpu.VMEM((tiles, rows, rows), f32),
            pltpu.VMEM((tiles, rows, rows), f32),
        ]
        if last:
            scratch += [
                pltpu.VMEM(result.shape, f32),
                pltpu.VMEM(kl_shape.shape, f32),
                pltpu.VMEM((live + rows + PAD, heads * STUDENT_DIM), f32),
            ]
        inputs = [me, token_counts, *incoming[c], *done]
        done += pl.pallas_call(
            functools.partial(
                relation_kernel, folded, chunk_heads, tiles, len(incoming[c]), c, last
            ),
            in_specs=[smem, smem] + [vmem] * (len(inputs) - 2),
            out_specs=[vmem] * 2,
            out_shape=[message, message] if last else [result, kl_shape],
            scratch_shapes=scratch,
            compiler_params=params,
            cost_estimate=pl.CostEstimate(
                flops=4 * pairs * DEPTH, bytes_accessed=8 * pairs, transcendentals=2 * pairs
            ),
            name="relation",
        )(*inputs)
    returned = exchange(*done[-2:])
    kl = pl.pallas_call(
        sum_kernel,
        in_specs=[smem] + [vmem] * len(returned),
        out_specs=vmem,
        out_shape=jax.ShapeDtypeStruct((1, heads * STUDENT_DIM), f32),
        compiler_params=params,
        name="sum_kl",
    )(token_counts, *returned)
    loss = pair_sum(
        [kl]
        + [
            lax.ppermute(kl, "head", [(i, i ^ k) for i in range(groups)])
            for k in range(1, groups)
        ]
    )
    grad = pl.pallas_call(
        unpack_kernel,
        in_specs=[smem] + [vmem] * len(returned),
        out_specs=vmem,
        out_shape=jax.ShapeDtypeStruct((rows, student_queries.shape[1]), f32),
        compiler_params=params,
        name="unpack",
    )(me, *returned)
    return (grad, loss[0, 0])


def solution(mesh):
    return jax.shard_map(
        local,
        mesh=mesh,
        in_specs=(P("seq", "head"), P("seq", "head"), P()),
        out_specs=(P("seq", "head"), P()),
        check_vma=False,
    )
```

```python
import functools
import math

import jax
import jax.numpy as jnp
from jax import lax
from jax.experimental import pallas as pl
from jax.experimental.pallas import tpu as pltpu
from jax.sharding import PartitionSpec as P

DT = 8192
DS = 4096
H_REL = 128
TEACHER_DIM = DT // H_REL
STUDENT_DIM = DS // H_REL

NEGATIVE = -1e30
LOG2E = math.log2(math.e)
TEACHER_SCALE = LOG2E * TEACHER_DIM**-0.5
STUDENT_SCALE = LOG2E * STUDENT_DIM**-0.5
PAD = 8
LANES = 128
TAIL = 16
DEPTH = 256
SAFE_NORM = 320.0


def split_high_low(values):
    high = values.astype(jnp.bfloat16)
    low = (values - high.astype(jnp.float32)).astype(jnp.bfloat16)
    return high, low


def split_three(values):
    high = values.astype(jnp.bfloat16)
    rest = values - high.astype(jnp.float32)
    return (high,) + split_high_low(rest)


def at_columns(index, count, width, act):
    if width % LANES == 0:
        act(pl.ds(pl.multiple_of(index * width, LANES), width))
    else:
        for part in range(count):
            pl.when(index == part)(functools.partial(act, pl.ds(part * width, width)))


def pack_folded_kernel(blocks, chunks, me_ref, teacher_ref, student_ref, *refs):
    sends, student, sems = refs[: 2 * chunks], refs[2 * chunks], refs[2 * chunks + 1]
    rows = teacher_ref.shape[0]
    half = rows // 2
    copies = [pltpu.make_async_copy(student_ref, student, sems.at[2 * chunks * blocks // 2])]
    for chunk in range(chunks):
        for core in range(2):
            for k in range(blocks // 2):
                to = jnp.bitwise_xor(me_ref[0], 2 * k + core)
                at = pl.multiple_of((to * chunks + chunk) * LANES, LANES)
                copies.append(
                    pltpu.make_async_copy(
                        teacher_ref.at[:, pl.ds(at, LANES)],
                        sends[2 * chunk + core].at[k, pl.ds(0, rows)],
                        sems.at[(2 * chunk + core) * (blocks // 2) + k],
                    )
                )
    for copy in copies:
        copy.start()
    copies[0].wait()
    for core in range(2):
        for k in range(blocks // 2):
            to = jnp.bitwise_xor(me_ref[0], 2 * k + core)
            lanes = pl.ds(pl.multiple_of(to * LANES, LANES), LANES)
            top, bottom = student[:half, lanes], student[half:, lanes]
            for chunk in range(chunks):
                part = slice(chunk * (LANES // 2), (chunk + 1) * (LANES // 2))
                sends[2 * chunk + core][k, rows:, :] = jnp.concatenate(
                    [top[:, part], bottom[:, part]], axis=1
                )
    for copy in copies[1:]:
        copy.wait()


def pack_plain_kernel(blocks, me_ref, teacher_ref, student_ref, *sends):
    teacher_width = teacher_ref.shape[1] // blocks
    student_width = student_ref.shape[1] // blocks
    for core in range(2):
        for k in range(blocks // 2):
            to = jnp.bitwise_xor(me_ref[0], 2 * k + core)

            def put_teacher(columns, send=sends[core], k=k):
                send[k, :, :teacher_width] = teacher_ref[:, columns]

            def put_student(columns, send=sends[core], k=k):
                send[k, :, teacher_width:] = student_ref[:, columns]

            at_columns(to, blocks, teacher_width, put_teacher)
            at_columns(to, blocks, student_width, put_student)


def pair_sum(parts):
    while len(parts) > 1:
        parts = [a + b for a, b in zip(parts[::2], parts[1::2])]
    return parts[0]


def merge_kernel(chips, kept_ref, swapped_ref, *refs):
    for k, send in enumerate(refs[: chips - 1]):
        send[0] = kept_ref[k + 1, : send.shape[1], :]
        send[1] = swapped_ref[k + 1, : send.shape[1], :]
    if len(refs) == chips:
        own, other = [
            jnp.sum(ref[0, ref.shape[1] - TAIL :, :].astype(jnp.float32), axis=0, keepdims=True)
            for ref in (kept_ref, swapped_ref)
        ]
        refs[-1][...] = own + other


def arrived(refs):
    return [refs[0].at[0], refs[1].at[0]] + [ref.at[core] for ref in refs[2:] for core in range(2)]


def unpack_kernel(me_ref, *refs):
    grad_ref = refs[-1]
    blocks = arrived(refs[:-1])
    for k, block in enumerate(blocks):

        def put(columns, block=block):
            grad_ref[:, columns] = block[: grad_ref.shape[0], :].astype(jnp.float32)

        at_columns(jnp.bitwise_xor(me_ref[0], k), len(blocks), block.shape[1], put)


def fold(values):
    rows, columns = values.shape
    return jnp.sum(values.reshape(rows // 8, 8, columns), axis=0)


def relation_kernel(folded, heads, tiles, n_in, n_done, last, me_ref, counts_ref, *refs):
    sources = arrived(refs[:n_in])
    done = refs[n_in : n_in + 3 * n_done]
    rest = list(refs[n_in + 3 * n_done :])
    out, rest = (rest[:2], rest[2:]) if last else (rest[:3], rest[3:])
    pack, key_op, row_op, student_col, student_pad, teacher_prob, student_prob, weights_ref = rest[:8]
    if last:
        row_grad, key_grad, kl_sum, grad_rows = rest[8:]
    else:
        row_grad, key_grad, kl_sum = out
    f32, bf16 = jnp.float32, jnp.bfloat16
    blocks = len(sources)
    rows = teacher_prob.shape[2]
    half = rows // 2
    live = tiles * rows
    window = rows + PAD
    student_at = heads * TEACHER_DIM
    student_width = heads * STUDENT_DIM
    filled = 2 * TEACHER_DIM + 2 * STUDENT_DIM

    position = lax.broadcasted_iota(jnp.int32, (window, rows), 0)
    token = lax.broadcasted_iota(jnp.int32, (window, rows), 1)
    pack[...] = jnp.zeros(pack.shape, f32)
    places = []
    for k in range(blocks):
        owner = jnp.bitwise_xor(me_ref[0], k)
        start = sum(jnp.where(b < owner, counts_ref[b], 0) for b in range(blocks))
        base = pl.multiple_of(start // PAD * PAD, PAD)
        places.append((base, start - base, counts_ref[owner]))
    for source, (base, shift, count) in zip(sources, places):
        place = ((position == token + shift) & (token < count)).astype(bf16)
        here = pl.ds(base, window)
        if folded:
            moved = jnp.dot(place, source[:rows, :], preferred_element_type=f32)
            pack[here, :student_at] = pack[here, :student_at] + moved
            student = source[rows:, :]
            moved = jnp.dot(
                place[:, :half], student[:, :student_width], preferred_element_type=f32
            ) + jnp.dot(place[:, half:], student[:, student_width:], preferred_element_type=f32)
            pack[here, student_at:] = pack[here, student_at:] + moved
        else:
            moved = jnp.dot(place, source[...], preferred_element_type=f32)
            pack[here, :] = pack[here, :] + moved

    ones = jnp.ones((rows, DEPTH - filled), bf16)
    spare = lax.broadcasted_iota(jnp.int32, (DEPTH - filled, rows), 0)
    teacher_gap = jnp.zeros((2 * STUDENT_DIM, rows), bf16)
    student_gap = jnp.zeros((2 * TEACHER_DIM, rows), bf16)
    lane_head = lax.broadcasted_iota(jnp.int32, (rows, student_width), 1) // STUDENT_DIM
    norms = []

    def shift_rows(norm):
        parts = [part.astype(f32) for part in split_three(-norm)]
        out = jnp.where(spare == 0, parts[0], 0.0)
        out = jnp.where(spare == 1, parts[1], out)
        return jnp.where(spare == 2, parts[2], out).astype(bf16)

    for i in range(tiles):
        here = pl.ds(i * rows, rows)
        tile = pack[here, :]
        tile_t = tile.T
        tile_b = tile.astype(bf16)
        tile_s = tile[:, student_at:]
        for h in range(heads):
            tb = tile_b[:, h * TEACHER_DIM : (h + 1) * TEACHER_DIM]
            at = student_at + h * STUDENT_DIM
            sb = tile_b[:, at : at + STUDENT_DIM]
            key_op[h, here, :] = jnp.concatenate([tb, tb, sb, sb, ones], axis=1)
            teacher_t = tile_t[h * TEACHER_DIM : (h + 1) * TEACHER_DIM, :]
            student_t = tile_t[at : at + STUDENT_DIM, :]
            student_col[h, :, here] = student_t.astype(bf16)
            student_pad[h, here, :] = jnp.where(lane_head == h, tile_s, 0.0).astype(bf16)
            teacher_norm = TEACHER_SCALE * jnp.sum(teacher_t * teacher_t, axis=0, keepdims=True)
            student_norm = STUDENT_SCALE * jnp.sum(student_t * student_t, axis=0, keepdims=True)
            norms += [teacher_norm, student_norm]
            high, low = split_high_low(teacher_t * TEACHER_SCALE)
            teacher_op = [high, low, teacher_gap, shift_rows(teacher_norm)]
            row_op[h, i, :, :rows] = jnp.concatenate(teacher_op, axis=0)
            high, low = split_high_low(student_t * STUDENT_SCALE)
            student_op = [student_gap, high, low, shift_rows(student_norm)]
            row_op[h, i, :, rows:] = jnp.concatenate(student_op, axis=0)

    safe = jnp.max(functools.reduce(jnp.maximum, norms)) <= SAFE_NORM
    key_pos = lax.broadcasted_iota(jnp.int32, (rows, rows), 0)
    row_pos = lax.broadcasted_iota(jnp.int32, (rows, rows), 1)

    def logits(h, i, j):
        keys = pl.ds(pl.multiple_of(j * rows, rows), rows)
        both = jnp.dot(key_op[h, keys, :], row_op[h, i], preferred_element_type=f32)
        return both[:, :rows], both[:, rows:]

    @pl.when(safe)
    def shifted_by_own_logit():
        key_grad[...] = jnp.zeros(key_grad.shape, f32)

        def exponentials(h, i, j, sums):
            teacher, student = logits(h, i, j)
            if i == j:
                teacher = jnp.where(key_pos <= row_pos, teacher, NEGATIVE)
                student = jnp.where(key_pos <= row_pos, student, NEGATIVE)
            teacher_exp = jnp.exp2(teacher)
            student_exp = jnp.exp2(student)
            teacher_prob[i % 2, j] = teacher_exp
            student_prob[i % 2, j] = student_exp
            new = (fold(teacher_exp), fold(student_exp), fold(teacher_exp * (teacher - student)))
            return new if sums is None else tuple(a + b for a, b in zip(sums, new))

        def weights(i, j, teacher_inv, student_inv):
            value = student_prob[i % 2, j] * student_inv - teacher_prob[i % 2, j] * teacher_inv
            weights_ref[j * rows : (j + 1) * rows, i * rows : (i + 1) * rows] = value.astype(bf16)

        def head_step(h, kl_total):
            inverse = None
            for i in range(tiles + 1):
                sums = None
                for j in range(i + 1):
                    if i < tiles:
                        sums = exponentials(h, i, j, sums)
                    if j < i:
                        weights(i - 1, j, *inverse)
                if i:
                    upto = i * rows
                    row_grad[h, :, upto - rows : upto] = jnp.dot(
                        student_col[h, :, :upto],
                        weights_ref[:upto, upto - rows : upto],
                        preferred_element_type=f32,
                    )
                if i < tiles:
                    teacher_sum, student_sum, cross_sum = [
                        jnp.sum(part, axis=0, keepdims=True) for part in sums
                    ]
                    inverse = (1.0 / teacher_sum, 1.0 / student_sum)
                    kl_total = kl_total + (
                        cross_sum * inverse[0] - jnp.log2(teacher_sum) + jnp.log2(student_sum)
                    )
            for j in range(tiles):
                here = slice(j * rows, (j + 1) * rows)
                key_grad[here, :] = key_grad[here, :] + jnp.dot(
                    weights_ref[here, j * rows :],
                    student_pad[h, j * rows :, :],
                    preferred_element_type=f32,
                )
            return kl_total

        kl_sum[...] = lax.fori_loop(0, heads, head_step, jnp.zeros((1, rows), f32))

    @pl.when(jnp.logical_not(safe))
    def shifted_by_maximum():
        kl_sum[...] = jnp.zeros((1, rows), f32)
        key_grad[...] = jnp.zeros(key_grad.shape, f32)

        def masked(h, i, j):
            allowed = key_pos + j * rows <= row_pos + i * rows
            teacher, student = logits(h, i, j)
            return jnp.where(allowed, teacher, NEGATIVE), jnp.where(allowed, student, NEGATIVE)

        def row_step(step, _):
            h, i = step // tiles, step % tiles
            here = pl.ds(pl.multiple_of(i * rows, rows), rows)

            def advance(j, state):
                teacher_max, teacher_sum, cross_sum, student_max, student_sum = state
                teacher, student = masked(h, i, j)
                teacher_top = jnp.maximum(teacher_max, jnp.max(teacher, axis=0, keepdims=True))
                student_top = jnp.maximum(student_max, jnp.max(student, axis=0, keepdims=True))
                teacher_exp = jnp.exp2(teacher - teacher_top)
                student_exp = jnp.exp2(student - student_top)
                shrink = jnp.exp2(teacher_max - teacher_top)
                cross = jnp.sum(teacher_exp * (teacher - student), axis=0, keepdims=True)
                return (
                    teacher_top,
                    teacher_sum * shrink + jnp.sum(teacher_exp, axis=0, keepdims=True),
                    cross_sum * shrink + cross,
                    student_top,
                    student_sum * jnp.exp2(student_max - student_top)
                    + jnp.sum(student_exp, axis=0, keepdims=True),
                )

            lowest = jnp.full((1, rows), NEGATIVE, f32)
            zeros = jnp.zeros((1, rows), f32)
            teacher_max, teacher_sum, cross_sum, student_max, student_sum = lax.fori_loop(
                0, i + 1, advance, (lowest, zeros, zeros, lowest, zeros)
            )
            teacher_lse = teacher_max + jnp.log2(teacher_sum)
            student_lse = student_max + jnp.log2(student_sum)
            kl_sum[...] = kl_sum[...] + (cross_sum / teacher_sum - teacher_lse + student_lse)

            def spread(j, total):
                teacher, student = masked(h, i, j)
                value = jnp.exp2(student - student_lse) - jnp.exp2(teacher - teacher_lse)
                value = value.astype(bf16)
                keys = pl.ds(pl.multiple_of(j * rows, rows), rows)
                key_grad[keys, :] = key_grad[keys, :] + jnp.dot(
                    value, student_pad[h, here, :], preferred_element_type=f32
                )
                return total + jnp.dot(
                    student_col[h, :, keys], value, preferred_element_type=f32
                )

            row_grad[h, :, here] = lax.fori_loop(
                0, i + 1, spread, jnp.zeros((STUDENT_DIM, rows), f32)
            )
            return 0

        lax.fori_loop(0, heads * tiles, row_step, 0)

    if not last:
        return

    row_parts = [*done[::3], row_grad]
    key_parts = [*done[1::3], key_grad]
    total_width = len(row_parts) * student_width
    for i in range(tiles):
        here = slice(i * rows, (i + 1) * rows)
        columns = jnp.concatenate(
            [part[h, :, here] for part in row_parts for h in range(heads)], axis=0
        )
        lanes = jnp.concatenate([part[here, :] for part in key_parts], axis=1)
        grad_rows[here, :] = (columns.T + lanes) * (STUDENT_DIM**-0.5)
    grad_rows[pl.ds(live, window), :] = jnp.zeros((window, total_width), f32)
    kl_total = sum([ref[...] for ref in done[2::3]] + [kl_sum[...]])
    divergence = jnp.sum(kl_total, axis=1, keepdims=True) * math.log(2.0)
    thirds = [part.astype(f32) for part in split_three(divergence)]
    line = lax.broadcasted_iota(jnp.int32, (TAIL, total_width), 0)
    tail = jnp.where(line == 0, thirds[0], 0.0)
    tail = jnp.where(line == 1, thirds[1], tail)
    tail = jnp.where(line == 2, thirds[2], tail).astype(bf16)
    position = lax.broadcasted_iota(jnp.int32, (rows, window), 1)
    token = lax.broadcasted_iota(jnp.int32, (rows, window), 0)
    for k, (base, shift, count) in enumerate(places):
        place = ((position == token + shift) & (token < count)).astype(bf16)
        block = grad_rows[pl.ds(base, window), :].astype(bf16)
        out[k % 2][k // 2, :rows, :] = jnp.dot(place, block, preferred_element_type=f32).astype(bf16)
        out[k % 2][k // 2, rows:, :] = tail


def local(teacher_queries, student_queries, token_counts):
    f32, bf16 = jnp.float32, jnp.bfloat16
    blocks = lax.axis_size("seq")
    chips = blocks // 2
    groups = lax.axis_size("head")
    rows = teacher_queries.shape[0]
    heads = teacher_queries.shape[1] // TEACHER_DIM // blocks
    tiles = blocks * 3 // 4
    live = tiles * rows
    folded = heads * STUDENT_DIM == LANES
    chunks = 2 if folded else 1
    chunk_heads = heads // chunks
    teacher_width = chunk_heads * TEACHER_DIM
    student_width = chunk_heads * STUDENT_DIM
    if folded:
        send_shape = (chips, rows + rows // 2, LANES)
    else:
        send_shape = (chips, rows, teacher_width + student_width)
    vmem = pl.BlockSpec(memory_space=pltpu.VMEM)
    smem = pl.BlockSpec(memory_space=pltpu.SMEM)
    params = pltpu.CompilerParams(vmem_limit_bytes=40 * 1024 * 1024)
    me = lax.axis_index("seq").reshape(1)
    far_first = sorted(range(1, chips), key=lambda k: -k.bit_count())

    def exchange(kept, swapped, tail=0):
        swapped = lax.ppermute(swapped, "seq", [(i, i ^ 1) for i in range(blocks)])
        shape = (2, kept.shape[1] - tail, kept.shape[2])
        out_shape = [jax.ShapeDtypeStruct(shape, bf16)] * (chips - 1)
        if tail:
            out_shape.append(jax.ShapeDtypeStruct((1, kept.shape[2]), f32))
        sends = pl.pallas_call(
            functools.partial(merge_kernel, chips),
            in_specs=[vmem] * 2,
            out_specs=[vmem] * len(out_shape),
            out_shape=out_shape,
            compiler_params=params,
            name="merge",
        )(kept, swapped)
        out = [None] * (chips - 1)
        for k in far_first:
            pairs = [(i, i ^ (2 * k)) for i in range(blocks)]
            out[k - 1] = lax.ppermute(sends[k - 1], "seq", pairs)
        return [kept, swapped] + out, sends[chips - 1 :]

    def tree_sum(value, axis, size, stride):
        return pair_sum(
            [value]
            + [
                lax.ppermute(value, axis, [(i, i ^ (k * stride)) for i in range(size)])
                for k in range(1, size // stride)
            ]
        )

    packed = jax.ShapeDtypeStruct(send_shape, bf16)
    if folded:
        anywhere = pl.BlockSpec(memory_space=pltpu.HBM)
        sends = pl.pallas_call(
            functools.partial(pack_folded_kernel, blocks, chunks),
            in_specs=[smem, anywhere, anywhere],
            out_specs=[vmem] * (2 * chunks),
            out_shape=[packed] * (2 * chunks),
            scratch_shapes=[
                pltpu.VMEM(student_queries.shape, bf16),
                pltpu.SemaphoreType.DMA((chunks * blocks + 1,)),
            ],
            compiler_params=params,
            name="pack",
        )(me, teacher_queries, student_queries)
    else:
        sends = pl.pallas_call(
            functools.partial(pack_plain_kernel, blocks),
            in_specs=[smem, vmem, vmem],
            out_specs=[vmem] * 2,
            out_shape=[packed] * 2,
            compiler_params=params,
            name="pack",
        )(me, teacher_queries, student_queries)
    incoming = [exchange(*sends[2 * c : 2 * c + 2])[0] for c in range(chunks)]

    result = [
        jax.ShapeDtypeStruct((chunk_heads, STUDENT_DIM, live), f32),
        jax.ShapeDtypeStruct((live, student_width), f32),
        jax.ShapeDtypeStruct((1, rows), f32),
    ]
    message = jax.ShapeDtypeStruct((chips, rows + TAIL, heads * STUDENT_DIM), bf16)
    pairs = chunk_heads * tiles * (tiles + 1) // 2 * rows * rows
    done = []
    for c in range(chunks):
        last = c == chunks - 1
        scratch = [
            pltpu.VMEM((live + rows + PAD, teacher_width + student_width), f32),
            pltpu.VMEM((chunk_heads, live, DEPTH), bf16),
            pltpu.VMEM((chunk_heads, tiles, DEPTH, 2 * rows), bf16),
            pltpu.VMEM((chunk_heads, STUDENT_DIM, live), bf16),
            pltpu.VMEM((chunk_heads, live, student_width), bf16),
            pltpu.VMEM((2, tiles, rows, rows), f32),
            pltpu.VMEM((2, tiles, rows, rows), f32),
            pltpu.VMEM((live, live), bf16),
        ]
        if last:
            scratch += [pltpu.VMEM(part.shape, f32) for part in result]
            scratch.append(pltpu.VMEM((live + rows + PAD, heads * STUDENT_DIM), f32))
        inputs = [me, token_counts, *incoming[c], *done]
        done += pl.pallas_call(
            functools.partial(
                relation_kernel, folded, chunk_heads, tiles, len(incoming[c]), c, last
            ),
            in_specs=[smem, smem] + [vmem] * (len(inputs) - 2),
            out_specs=[vmem] * (2 if last else 3),
            out_shape=[message, message] if last else result,
            scratch_shapes=scratch,
            compiler_params=params,
            cost_estimate=pl.CostEstimate(
                flops=4 * pairs * DEPTH, bytes_accessed=8 * pairs, transcendentals=2 * pairs
            ),
            name="relation",
        )(*inputs)
    returned, (kl,) = exchange(*done[-2:], tail=TAIL)
    kl = tree_sum(kl, "head", groups, 1)
    kl = tree_sum(kl, "seq", blocks, 2)
    loss = kl[0, 0] / (H_REL * jnp.sum(token_counts)).astype(f32)
    grad = pl.pallas_call(
        unpack_kernel,
        in_specs=[smem] + [vmem] * len(returned),
        out_specs=vmem,
        out_shape=jax.ShapeDtypeStruct((rows, student_queries.shape[1]), f32),
        compiler_params=params,
        name="unpack",
    )(me, *returned)
    return (grad, loss)


def solution(mesh):
    return jax.shard_map(
        local,
        mesh=mesh,
        in_specs=(P("seq", "head"), P("seq", "head"), P()),
        out_specs=(P("seq", "head"), P()),
        check_vma=False,
    )
```

```python
import functools
import math

import jax
import jax.numpy as jnp
from jax import lax
from jax.experimental import pallas as pl
from jax.experimental.pallas import tpu as pltpu
from jax.sharding import PartitionSpec as P

DT = 8192
DS = 4096
H_REL = 128
TEACHER_DIM = DT // H_REL
STUDENT_DIM = DS // H_REL

NEGATIVE = -1e30
LOG2E = math.log2(math.e)
TEACHER_SCALE = LOG2E * TEACHER_DIM**-0.5
STUDENT_SCALE = LOG2E * STUDENT_DIM**-0.5
PAD = 8
LANES = 128
TAIL = 16
DEPTH = 256
SAFE_NORM = 320.0


def split_high_low(values):
    high = values.astype(jnp.bfloat16)
    low = (values - high.astype(jnp.float32)).astype(jnp.bfloat16)
    return high, low


def split_three(values):
    high = values.astype(jnp.bfloat16)
    rest = values - high.astype(jnp.float32)
    return (high,) + split_high_low(rest)


def at_columns(index, count, width, act):
    if width % LANES == 0:
        act(pl.ds(pl.multiple_of(index * width, LANES), width))
    else:
        for part in range(count):
            pl.when(index == part)(functools.partial(act, pl.ds(part * width, width)))


def pack_folded_kernel(blocks, chunks, me_ref, teacher_ref, student_ref, *refs):
    sends, student, sems = refs[: 2 * chunks], refs[2 * chunks], refs[2 * chunks + 1]
    rows = teacher_ref.shape[0]
    half = rows // 2
    copies = [pltpu.make_async_copy(student_ref, student, sems.at[2 * chunks * blocks // 2])]
    for chunk in range(chunks):
        for core in range(2):
            for k in range(blocks // 2):
                to = jnp.bitwise_xor(me_ref[0], 2 * k + core)
                at = pl.multiple_of((to * chunks + chunk) * LANES, LANES)
                copies.append(
                    pltpu.make_async_copy(
                        teacher_ref.at[:, pl.ds(at, LANES)],
                        sends[2 * chunk + core].at[k, pl.ds(0, rows)],
                        sems.at[(2 * chunk + core) * (blocks // 2) + k],
                    )
                )
    for copy in copies:
        copy.start()
    copies[0].wait()
    for core in range(2):
        for k in range(blocks // 2):
            to = jnp.bitwise_xor(me_ref[0], 2 * k + core)
            lanes = pl.ds(pl.multiple_of(to * LANES, LANES), LANES)
            top, bottom = student[:half, lanes], student[half:, lanes]
            for chunk in range(chunks):
                part = slice(chunk * (LANES // 2), (chunk + 1) * (LANES // 2))
                sends[2 * chunk + core][k, rows:, :] = jnp.concatenate(
                    [top[:, part], bottom[:, part]], axis=1
                )
    for copy in copies[1:]:
        copy.wait()


def pack_plain_kernel(blocks, me_ref, teacher_ref, student_ref, *sends):
    teacher_width = teacher_ref.shape[1] // blocks
    student_width = student_ref.shape[1] // blocks
    for core in range(2):
        for k in range(blocks // 2):
            to = jnp.bitwise_xor(me_ref[0], 2 * k + core)

            def put_teacher(columns, send=sends[core], k=k):
                send[k, :, :teacher_width] = teacher_ref[:, columns]

            def put_student(columns, send=sends[core], k=k):
                send[k, :, teacher_width:] = student_ref[:, columns]

            at_columns(to, blocks, teacher_width, put_teacher)
            at_columns(to, blocks, student_width, put_student)


def pair_sum(parts):
    while len(parts) > 1:
        parts = [a + b for a, b in zip(parts[::2], parts[1::2])]
    return parts[0]


def tail_rows(value, width):
    thirds = [part.astype(jnp.float32) for part in split_three(value)]
    line = lax.broadcasted_iota(jnp.int32, (TAIL, width), 0)
    tail = jnp.where(line == 0, thirds[0], 0.0)
    tail = jnp.where(line == 1, thirds[1], tail)
    return jnp.where(line == 2, thirds[2], tail).astype(jnp.bfloat16)


def merge_kernel(chips, kept_ref, swapped_ref, *refs):
    kls, sends = refs[: 1 - chips], refs[1 - chips :]
    rows = kept_ref.shape[1]
    tail = tail_rows(pair_sum([kl[...] for kl in kls]), kept_ref.shape[2]) if kls else None
    for k, send in enumerate(sends):
        send[0, :rows, :] = kept_ref[k + 1]
        send[1, :rows, :] = swapped_ref[k + 1]
        if kls:
            send[0, rows:, :] = tail
            send[1, rows:, :] = tail


def arrived(refs):
    return [refs[0].at[0], refs[1].at[0]] + [ref.at[core] for ref in refs[2:] for core in range(2)]


def sum_kernel(groups, counts_ref, *refs):
    out_ref = refs[-1]
    own = pair_sum([ref[...] for ref in refs[:groups]])
    tails = [ref[0, ref.shape[1] - TAIL :, :].astype(jnp.float32) for ref in refs[groups:-1]]
    total = pair_sum(
        [jnp.broadcast_to(own, out_ref.shape)] + [jnp.sum(t, axis=0, keepdims=True) for t in tails]
    )
    tokens = sum(counts_ref[b] for b in range(counts_ref.shape[0]))
    out_ref[...] = total / (H_REL * tokens).astype(jnp.float32)


def unpack_kernel(me_ref, *refs):
    grad_ref = refs[-1]
    blocks = arrived(refs[:-1])
    for k, block in enumerate(blocks):

        def put(columns, block=block):
            grad_ref[:, columns] = block[: grad_ref.shape[0], :].astype(jnp.float32)

        at_columns(jnp.bitwise_xor(me_ref[0], k), len(blocks), block.shape[1], put)


def fold(values):
    rows, columns = values.shape
    return jnp.sum(values.reshape(rows // 8, 8, columns), axis=0)


def relation_kernel(folded, heads, tiles, n_in, n_done, last, me_ref, counts_ref, *refs):
    sources = arrived(refs[:n_in])
    done = refs[n_in : n_in + 3 * n_done]
    rest = list(refs[n_in + 3 * n_done :])
    out, rest = rest[:3], rest[3:]
    pack, key_op, row_op, student_col, student_pad, teacher_prob, student_prob, weights_ref = rest[:8]
    if last:
        row_grad, key_grad, kl_sum, grad_rows = rest[8:]
    else:
        row_grad, key_grad, kl_sum = out
    f32, bf16 = jnp.float32, jnp.bfloat16
    blocks = len(sources)
    rows = teacher_prob.shape[2]
    half = rows // 2
    live = tiles * rows
    window = rows + PAD
    student_at = heads * TEACHER_DIM
    student_width = heads * STUDENT_DIM
    filled = 2 * TEACHER_DIM + 2 * STUDENT_DIM

    position = lax.broadcasted_iota(jnp.int32, (window, rows), 0)
    token = lax.broadcasted_iota(jnp.int32, (window, rows), 1)
    pack[...] = jnp.zeros(pack.shape, f32)
    places = []
    for k in range(blocks):
        owner = jnp.bitwise_xor(me_ref[0], k)
        start = sum(jnp.where(b < owner, counts_ref[b], 0) for b in range(blocks))
        base = pl.multiple_of(start // PAD * PAD, PAD)
        places.append((base, start - base, counts_ref[owner]))
    for source, (base, shift, count) in zip(sources, places):
        place = ((position == token + shift) & (token < count)).astype(bf16)
        here = pl.ds(base, window)
        if folded:
            moved = jnp.dot(place, source[:rows, :], preferred_element_type=f32)
            pack[here, :student_at] = pack[here, :student_at] + moved
            student = source[rows:, :]
            moved = jnp.dot(
                place[:, :half], student[:, :student_width], preferred_element_type=f32
            ) + jnp.dot(place[:, half:], student[:, student_width:], preferred_element_type=f32)
            pack[here, student_at:] = pack[here, student_at:] + moved
        else:
            moved = jnp.dot(place, source[...], preferred_element_type=f32)
            pack[here, :] = pack[here, :] + moved

    ones = jnp.ones((rows, DEPTH - filled), bf16)
    spare = lax.broadcasted_iota(jnp.int32, (DEPTH - filled, rows), 0)
    teacher_gap = jnp.zeros((2 * STUDENT_DIM, rows), bf16)
    student_gap = jnp.zeros((2 * TEACHER_DIM, rows), bf16)
    lane_head = lax.broadcasted_iota(jnp.int32, (rows, student_width), 1) // STUDENT_DIM
    norms = []

    def shift_rows(norm):
        parts = [part.astype(f32) for part in split_three(-norm)]
        out = jnp.where(spare == 0, parts[0], 0.0)
        out = jnp.where(spare == 1, parts[1], out)
        return jnp.where(spare == 2, parts[2], out).astype(bf16)

    for i in range(tiles):
        here = pl.ds(i * rows, rows)
        tile = pack[here, :]
        tile_t = tile.T
        tile_b = tile.astype(bf16)
        tile_s = tile[:, student_at:]
        for h in range(heads):
            tb = tile_b[:, h * TEACHER_DIM : (h + 1) * TEACHER_DIM]
            at = student_at + h * STUDENT_DIM
            sb = tile_b[:, at : at + STUDENT_DIM]
            key_op[h, here, :] = jnp.concatenate([tb, tb, sb, sb, ones], axis=1)
            teacher_t = tile_t[h * TEACHER_DIM : (h + 1) * TEACHER_DIM, :]
            student_t = tile_t[at : at + STUDENT_DIM, :]
            student_col[h, :, here] = student_t.astype(bf16)
            student_pad[h, here, :] = jnp.where(lane_head == h, tile_s, 0.0).astype(bf16)
            teacher_norm = TEACHER_SCALE * jnp.sum(teacher_t * teacher_t, axis=0, keepdims=True)
            student_norm = STUDENT_SCALE * jnp.sum(student_t * student_t, axis=0, keepdims=True)
            norms += [teacher_norm, student_norm]
            high, low = split_high_low(teacher_t * TEACHER_SCALE)
            teacher_op = [high, low, teacher_gap, shift_rows(teacher_norm)]
            row_op[h, i, :, :rows] = jnp.concatenate(teacher_op, axis=0)
            high, low = split_high_low(student_t * STUDENT_SCALE)
            student_op = [student_gap, high, low, shift_rows(student_norm)]
            row_op[h, i, :, rows:] = jnp.concatenate(student_op, axis=0)

    safe = jnp.max(functools.reduce(jnp.maximum, norms)) <= SAFE_NORM
    key_pos = lax.broadcasted_iota(jnp.int32, (rows, rows), 0)
    row_pos = lax.broadcasted_iota(jnp.int32, (rows, rows), 1)

    def logits(h, i, j):
        keys = pl.ds(pl.multiple_of(j * rows, rows), rows)
        both = jnp.dot(key_op[h, keys, :], row_op[h, i], preferred_element_type=f32)
        return both[:, :rows], both[:, rows:]

    @pl.when(safe)
    def shifted_by_own_logit():
        key_grad[...] = jnp.zeros(key_grad.shape, f32)

        def exponentials(h, i, model, prob):
            upto = (i + 1) * rows
            op = row_op[h, i, :, model * rows : (model + 1) * rows]
            values = jnp.dot(key_op[h, :upto, :], op, preferred_element_type=f32)
            diagonal = jnp.where(key_pos <= row_pos, values[i * rows :], NEGATIVE)
            total = cross = jnp.zeros((8, rows), f32)
            for j in range(i + 1):
                value = diagonal if j == i else values[j * rows : (j + 1) * rows]
                exp = jnp.exp2(value)
                prob[i % 2, j] = exp
                total = total + fold(exp)
                weight = teacher_prob[i % 2, j] if model else exp
                cross = cross + fold(weight * value)
            return [jnp.sum(part, axis=0, keepdims=True) for part in (total, cross)]

        def weights(i, j, teacher_inv, student_inv):
            value = student_prob[i % 2, j] * student_inv - teacher_prob[i % 2, j] * teacher_inv
            weights_ref[j * rows : (j + 1) * rows, i * rows : (i + 1) * rows] = value.astype(bf16)

        def head_step(h, kl_total):
            inverse = None
            for i in range(tiles + 1):
                if i < tiles:
                    teacher_sum, teacher_cross = exponentials(h, i, 0, teacher_prob)
                    student_sum, student_cross = exponentials(h, i, 1, student_prob)
                if i:
                    upto = i * rows
                    for j in range(i):
                        weights(i - 1, j, *inverse)
                    row_grad[h, :, upto - rows : upto] = jnp.dot(
                        student_col[h, :, :upto],
                        weights_ref[:upto, upto - rows : upto],
                        preferred_element_type=f32,
                    )
                if i < tiles:
                    inverse = (1.0 / teacher_sum, 1.0 / student_sum)
                    kl_total = kl_total + (
                        (teacher_cross - student_cross) * inverse[0]
                        - jnp.log2(teacher_sum)
                        + jnp.log2(student_sum)
                    )
            for j in range(tiles):
                here = slice(j * rows, (j + 1) * rows)
                key_grad[here, :] = key_grad[here, :] + jnp.dot(
                    weights_ref[here, j * rows :],
                    student_pad[h, j * rows :, :],
                    preferred_element_type=f32,
                )
            return kl_total

        kl_sum[...] = lax.fori_loop(0, heads, head_step, jnp.zeros((1, rows), f32))

    @pl.when(jnp.logical_not(safe))
    def shifted_by_maximum():
        kl_sum[...] = jnp.zeros((1, rows), f32)
        key_grad[...] = jnp.zeros(key_grad.shape, f32)

        def masked(h, i, j):
            allowed = key_pos + j * rows <= row_pos + i * rows
            teacher, student = logits(h, i, j)
            return jnp.where(allowed, teacher, NEGATIVE), jnp.where(allowed, student, NEGATIVE)

        def row_step(step, _):
            h, i = step // tiles, step % tiles
            here = pl.ds(pl.multiple_of(i * rows, rows), rows)

            def advance(j, state):
                teacher_max, teacher_sum, cross_sum, student_max, student_sum = state
                teacher, student = masked(h, i, j)
                teacher_top = jnp.maximum(teacher_max, jnp.max(teacher, axis=0, keepdims=True))
                student_top = jnp.maximum(student_max, jnp.max(student, axis=0, keepdims=True))
                teacher_exp = jnp.exp2(teacher - teacher_top)
                student_exp = jnp.exp2(student - student_top)
                shrink = jnp.exp2(teacher_max - teacher_top)
                cross = jnp.sum(teacher_exp * (teacher - student), axis=0, keepdims=True)
                return (
                    teacher_top,
                    teacher_sum * shrink + jnp.sum(teacher_exp, axis=0, keepdims=True),
                    cross_sum * shrink + cross,
                    student_top,
                    student_sum * jnp.exp2(student_max - student_top)
                    + jnp.sum(student_exp, axis=0, keepdims=True),
                )

            lowest = jnp.full((1, rows), NEGATIVE, f32)
            zeros = jnp.zeros((1, rows), f32)
            teacher_max, teacher_sum, cross_sum, student_max, student_sum = lax.fori_loop(
                0, i + 1, advance, (lowest, zeros, zeros, lowest, zeros)
            )
            teacher_lse = teacher_max + jnp.log2(teacher_sum)
            student_lse = student_max + jnp.log2(student_sum)
            kl_sum[...] = kl_sum[...] + (cross_sum / teacher_sum - teacher_lse + student_lse)

            def spread(j, total):
                teacher, student = masked(h, i, j)
                value = jnp.exp2(student - student_lse) - jnp.exp2(teacher - teacher_lse)
                value = value.astype(bf16)
                keys = pl.ds(pl.multiple_of(j * rows, rows), rows)
                key_grad[keys, :] = key_grad[keys, :] + jnp.dot(
                    value, student_pad[h, here, :], preferred_element_type=f32
                )
                return total + jnp.dot(
                    student_col[h, :, keys], value, preferred_element_type=f32
                )

            row_grad[h, :, here] = lax.fori_loop(
                0, i + 1, spread, jnp.zeros((STUDENT_DIM, rows), f32)
            )
            return 0

        lax.fori_loop(0, heads * tiles, row_step, 0)

    if not last:
        return

    row_parts = [*done[::3], row_grad]
    key_parts = [*done[1::3], key_grad]
    total_width = len(row_parts) * student_width
    for i in range(tiles):
        here = slice(i * rows, (i + 1) * rows)
        columns = jnp.concatenate(
            [part[h, :, here] for part in row_parts for h in range(heads)], axis=0
        )
        lanes = jnp.concatenate([part[here, :] for part in key_parts], axis=1)
        grad_rows[here, :] = (columns.T + lanes) * (STUDENT_DIM**-0.5)
    grad_rows[pl.ds(live, window), :] = jnp.zeros((window, total_width), f32)
    kl_total = sum([ref[...] for ref in done[2::3]] + [kl_sum[...]])
    out[2][...] = jnp.broadcast_to(
        jnp.sum(kl_total, axis=1, keepdims=True) * math.log(2.0), out[2].shape
    )
    position = lax.broadcasted_iota(jnp.int32, (rows, window), 1)
    token = lax.broadcasted_iota(jnp.int32, (rows, window), 0)
    for k, (base, shift, count) in enumerate(places):
        place = ((position == token + shift) & (token < count)).astype(bf16)
        block = grad_rows[pl.ds(base, window), :].astype(bf16)
        out[k % 2][k // 2] = jnp.dot(place, block, preferred_element_type=f32).astype(bf16)


def local(teacher_queries, student_queries, token_counts):
    f32, bf16 = jnp.float32, jnp.bfloat16
    blocks = lax.axis_size("seq")
    chips = blocks // 2
    groups = lax.axis_size("head")
    rows = teacher_queries.shape[0]
    heads = teacher_queries.shape[1] // TEACHER_DIM // blocks
    tiles = blocks * 3 // 4
    live = tiles * rows
    folded = heads * STUDENT_DIM == LANES
    chunks = 2 if folded else 1
    chunk_heads = heads // chunks
    teacher_width = chunk_heads * TEACHER_DIM
    student_width = chunk_heads * STUDENT_DIM
    if folded:
        send_shape = (chips, rows + rows // 2, LANES)
    else:
        send_shape = (chips, rows, teacher_width + student_width)
    vmem = pl.BlockSpec(memory_space=pltpu.VMEM)
    smem = pl.BlockSpec(memory_space=pltpu.SMEM)
    params = pltpu.CompilerParams(vmem_limit_bytes=40 * 1024 * 1024)
    me = lax.axis_index("seq").reshape(1)
    far_first = sorted(range(1, chips), key=lambda k: -k.bit_count())

    def exchange(kept, swapped, kls=()):
        swapped = lax.ppermute(swapped, "seq", [(i, i ^ 1) for i in range(blocks)])
        shape = (2, kept.shape[1] + (TAIL if kls else 0), kept.shape[2])
        sends = pl.pallas_call(
            functools.partial(merge_kernel, chips),
            in_specs=[vmem] * (2 + len(kls)),
            out_specs=[vmem] * (chips - 1),
            out_shape=[jax.ShapeDtypeStruct(shape, bf16)] * (chips - 1),
            compiler_params=params,
            name="merge",
        )(kept, swapped, *kls)
        out = [None] * (chips - 1)
        for k in far_first:
            pairs = [(i, i ^ (2 * k)) for i in range(blocks)]
            out[k - 1] = lax.ppermute(sends[k - 1], "seq", pairs)
        return [kept, swapped] + out

    packed = jax.ShapeDtypeStruct(send_shape, bf16)
    if folded:
        anywhere = pl.BlockSpec(memory_space=pltpu.HBM)
        sends = pl.pallas_call(
            functools.partial(pack_folded_kernel, blocks, chunks),
            in_specs=[smem, anywhere, anywhere],
            out_specs=[vmem] * (2 * chunks),
            out_shape=[packed] * (2 * chunks),
            scratch_shapes=[
                pltpu.VMEM(student_queries.shape, bf16),
                pltpu.SemaphoreType.DMA((chunks * blocks + 1,)),
            ],
            compiler_params=pltpu.CompilerParams(vmem_limit_bytes=52 * 1024 * 1024),
            name="pack",
        )(me, teacher_queries, student_queries)
    else:
        sends = pl.pallas_call(
            functools.partial(pack_plain_kernel, blocks),
            in_specs=[smem, vmem, vmem],
            out_specs=[vmem] * 2,
            out_shape=[packed] * 2,
            compiler_params=params,
            name="pack",
        )(me, teacher_queries, student_queries)
    incoming = [exchange(*sends[2 * c : 2 * c + 2]) for c in range(chunks)]

    result = [
        jax.ShapeDtypeStruct((chunk_heads, STUDENT_DIM, live), f32),
        jax.ShapeDtypeStruct((live, student_width), f32),
        jax.ShapeDtypeStruct((1, rows), f32),
    ]
    message = jax.ShapeDtypeStruct((chips, rows, heads * STUDENT_DIM), bf16)
    divergence = jax.ShapeDtypeStruct((1, heads * STUDENT_DIM), f32)
    pairs = chunk_heads * tiles * (tiles + 1) // 2 * rows * rows
    done = []
    for c in range(chunks):
        last = c == chunks - 1
        scratch = [
            pltpu.VMEM((live + rows + PAD, teacher_width + student_width), f32),
            pltpu.VMEM((chunk_heads, live, DEPTH), bf16),
            pltpu.VMEM((chunk_heads, tiles, DEPTH, 2 * rows), bf16),
            pltpu.VMEM((chunk_heads, STUDENT_DIM, live), bf16),
            pltpu.VMEM((chunk_heads, live, student_width), bf16),
            pltpu.VMEM((2, tiles, rows, rows), f32),
            pltpu.VMEM((2, tiles, rows, rows), f32),
            pltpu.VMEM((live, live), bf16),
        ]
        if last:
            scratch += [pltpu.VMEM(part.shape, f32) for part in result]
            scratch.append(pltpu.VMEM((live + rows + PAD, heads * STUDENT_DIM), f32))
        inputs = [me, token_counts, *incoming[c], *done]
        done += pl.pallas_call(
            functools.partial(
                relation_kernel, folded, chunk_heads, tiles, len(incoming[c]), c, last
            ),
            in_specs=[smem, smem] + [vmem] * (len(inputs) - 2),
            out_specs=[vmem] * 3,
            out_shape=[message, message, divergence] if last else result,
            scratch_shapes=scratch,
            compiler_params=params,
            cost_estimate=pl.CostEstimate(
                flops=4 * pairs * DEPTH, bytes_accessed=8 * pairs, transcendentals=2 * pairs
            ),
            name="relation",
        )(*inputs)
    kept, swapped, kl = done[-3:]
    kls = [kl] + [
        lax.ppermute(kl, "head", [(i, i ^ k) for i in range(groups)]) for k in range(1, groups)
    ]
    returned = exchange(kept, swapped, kls)
    half_loss = pl.pallas_call(
        functools.partial(sum_kernel, groups),
        in_specs=[smem] + [vmem] * (groups + chips - 1),
        out_specs=vmem,
        out_shape=divergence,
        compiler_params=params,
        name="sum_kl",
    )(token_counts, *kls, *returned[2:])
    loss = half_loss + lax.ppermute(half_loss, "seq", [(i, i ^ 1) for i in range(blocks)])
    grad = pl.pallas_call(
        unpack_kernel,
        in_specs=[smem] + [vmem] * len(returned),
        out_specs=vmem,
        out_shape=jax.ShapeDtypeStruct((rows, student_queries.shape[1]), f32),
        compiler_params=params,
        name="unpack",
    )(me, *returned)
    return (grad, loss[0, 0])


def solution(mesh):
    return jax.shard_map(
        local,
        mesh=mesh,
        in_specs=(P("seq", "head"), P("seq", "head"), P()),
        out_specs=(P("seq", "head"), P()),
        check_vma=False,
    )
```

```python
import functools
import math

import jax
import jax.numpy as jnp
from jax import lax
from jax.experimental import pallas as pl
from jax.experimental.pallas import tpu as pltpu
from jax.sharding import PartitionSpec as P

DT = 8192
DS = 4096
H_REL = 128
TEACHER_DIM = DT // H_REL
STUDENT_DIM = DS // H_REL

NEGATIVE = -1e30
LOG2E = math.log2(math.e)
TEACHER_SCALE = LOG2E * TEACHER_DIM**-0.5
STUDENT_SCALE = LOG2E * STUDENT_DIM**-0.5
PAD = 8
LANES = 128
TAIL = 16
SHIFT = 16
SAFE_NORM = 320.0


def split_high_low(values):
    high = values.astype(jnp.bfloat16)
    low = (values - high.astype(jnp.float32)).astype(jnp.bfloat16)
    return high, low


def split_three(values):
    high = values.astype(jnp.bfloat16)
    rest = values - high.astype(jnp.float32)
    return (high,) + split_high_low(rest)


def at_columns(index, count, width, act):
    if width % LANES == 0:
        act(pl.ds(pl.multiple_of(index * width, LANES), width))
    else:
        for part in range(count):
            pl.when(index == part)(functools.partial(act, pl.ds(part * width, width)))


def pack_folded_kernel(blocks, chunks, me_ref, teacher_ref, student_ref, *refs):
    sends, student, sems = refs[: 2 * chunks], refs[2 * chunks], refs[2 * chunks + 1]
    rows = teacher_ref.shape[0]
    half = rows // 2
    copies = [pltpu.make_async_copy(student_ref, student, sems.at[2 * chunks * blocks // 2])]
    for chunk in range(chunks):
        for core in range(2):
            for k in range(blocks // 2):
                to = jnp.bitwise_xor(me_ref[0], 2 * k + core)
                at = pl.multiple_of((to * chunks + chunk) * LANES, LANES)
                copies.append(
                    pltpu.make_async_copy(
                        teacher_ref.at[:, pl.ds(at, LANES)],
                        sends[2 * chunk + core].at[k, pl.ds(0, rows)],
                        sems.at[(2 * chunk + core) * (blocks // 2) + k],
                    )
                )
    for copy in copies:
        copy.start()
    copies[0].wait()
    for core in range(2):
        for k in range(blocks // 2):
            to = jnp.bitwise_xor(me_ref[0], 2 * k + core)
            lanes = pl.ds(pl.multiple_of(to * LANES, LANES), LANES)
            top, bottom = student[:half, lanes], student[half:, lanes]
            for chunk in range(chunks):
                part = slice(chunk * (LANES // 2), (chunk + 1) * (LANES // 2))
                sends[2 * chunk + core][k, rows:, :] = jnp.concatenate(
                    [top[:, part], bottom[:, part]], axis=1
                )
    for copy in copies[1:]:
        copy.wait()


def pack_plain_kernel(blocks, me_ref, teacher_ref, student_ref, *sends):
    teacher_width = teacher_ref.shape[1] // blocks
    student_width = student_ref.shape[1] // blocks
    for core in range(2):
        for k in range(blocks // 2):
            to = jnp.bitwise_xor(me_ref[0], 2 * k + core)

            def put_teacher(columns, send=sends[core], k=k):
                send[k, :, :teacher_width] = teacher_ref[:, columns]

            def put_student(columns, send=sends[core], k=k):
                send[k, :, teacher_width:] = student_ref[:, columns]

            at_columns(to, blocks, teacher_width, put_teacher)
            at_columns(to, blocks, student_width, put_student)


def pair_sum(parts):
    while len(parts) > 1:
        parts = [a + b for a, b in zip(parts[::2], parts[1::2])]
    return parts[0]


def tail_rows(value, width):
    thirds = [part.astype(jnp.float32) for part in split_three(value)]
    line = lax.broadcasted_iota(jnp.int32, (TAIL, width), 0)
    tail = jnp.where(line == 0, thirds[0], 0.0)
    tail = jnp.where(line == 1, thirds[1], tail)
    return jnp.where(line == 2, thirds[2], tail).astype(jnp.bfloat16)


def merge_kernel(order, kept_ref, swapped_ref, *sends):
    for k, send in zip(order, sends):
        send[0] = kept_ref[k]
        send[1] = swapped_ref[k]


def arrived(order, refs):
    blocks = [refs[0].at[0], refs[1].at[0]]
    for k in range(1, len(order) + 1):
        blocks += [refs[2 + order.index(k)].at[core] for core in range(2)]
    return blocks


def unpack_kernel(order, me_ref, counts_ref, *refs):
    grad_ref, loss_ref = refs[-2:]
    rows = grad_ref.shape[0]
    blocks = arrived(order, refs[:-2])
    for k, block in enumerate(blocks):

        def put(columns, block=block):
            grad_ref[:, columns] = block[:rows, :].astype(jnp.float32)

        at_columns(jnp.bitwise_xor(me_ref[0], k), len(blocks), block.shape[1], put)
    total = pair_sum([block[rows:, :].astype(jnp.float32) for block in blocks])
    tokens = sum(counts_ref[b] for b in range(len(blocks)))
    total = jnp.sum(total, axis=0, keepdims=True) / (H_REL * tokens).astype(jnp.float32)
    loss_ref[...] = jnp.broadcast_to(total[:, :1], loss_ref.shape)


def packed_start(me, counts_ref, blocks, k):
    owner = jnp.bitwise_xor(me, k)
    start = sum(jnp.where(b < owner, counts_ref[b], 0) for b in range(blocks))
    base = pl.multiple_of(start // PAD * PAD, PAD)
    return base, start - base, counts_ref[owner]


def place_kernel(me_ref, counts_ref, place_ref, place_t_ref):
    blocks, window, rows = place_ref.shape
    position = lax.broadcasted_iota(jnp.int32, (window, rows), 0)
    token = lax.broadcasted_iota(jnp.int32, (window, rows), 1)
    position_t = lax.broadcasted_iota(jnp.int32, (rows, window), 1)
    token_t = lax.broadcasted_iota(jnp.int32, (rows, window), 0)
    for k in range(blocks):
        _, shift, count = packed_start(me_ref[0], counts_ref, blocks, k)
        place = (position == token + shift) & (token < count)
        place_ref[k] = place.astype(jnp.bfloat16)
        place = (position_t == token_t + shift) & (token_t < count)
        place_t_ref[k] = place.astype(jnp.bfloat16)


def fold(values):
    rows, columns = values.shape
    return jnp.sum(values.reshape(rows // 8, 8, columns), axis=0)


def key_kernel(rows, weights_ref, student_pad, key_grad):
    heads, live, _ = weights_ref.shape
    for at in range(0, live, rows):
        parts = [
            jnp.dot(
                weights_ref[h, at : at + rows, at:],
                student_pad[h, at:, :],
                preferred_element_type=jnp.float32,
            )
            for h in range(heads)
        ]
        key_grad[at : at + rows, :] = sum(parts)


def relation_kernel(folded, heads, tiles, order, n_in, last, me_ref, counts_ref, place_ref, *refs):
    sources = arrived(order, refs[:n_in])
    rest = list(refs[n_in:])
    if last:
        kl_before, row_grad, weights_ref, student_pad, kl_out, *rest = rest
    else:
        kl_before = None
        row_grad, key_grad, kl_out, weights_ref, student_pad, *rest = rest
    (
        pack,
        teacher_key,
        student_key,
        teacher_row,
        student_row,
        student_col,
        teacher_prob,
        student_prob,
        kl_sum,
    ) = rest
    f32, bf16 = jnp.float32, jnp.bfloat16
    blocks = len(sources)
    rows = teacher_prob.shape[2]
    half = rows // 2
    live = tiles * rows
    window = rows + PAD
    student_at = heads * TEACHER_DIM
    student_width = heads * STUDENT_DIM

    pack[...] = jnp.zeros(pack.shape, f32)
    for k, source in enumerate(sources):
        base, _, _ = packed_start(me_ref[0], counts_ref, blocks, k)
        here = pl.ds(base, window)
        place = place_ref[k]
        if folded:
            moved = jnp.dot(place, source[:rows, :], preferred_element_type=f32)
            pack[here, :student_at] = pack[here, :student_at] + moved
            student = source[rows:, :]
            moved = jnp.dot(
                place[:, :half], student[:, :student_width], preferred_element_type=f32
            ) + jnp.dot(place[:, half:], student[:, student_width:], preferred_element_type=f32)
            pack[here, student_at:] = pack[here, student_at:] + moved
        else:
            moved = jnp.dot(place, source[...], preferred_element_type=f32)
            pack[here, :] = pack[here, :] + moved

    ones = jnp.ones((rows, SHIFT), bf16)
    spare = lax.broadcasted_iota(jnp.int32, (SHIFT, rows), 0)
    lane_head = lax.broadcasted_iota(jnp.int32, (rows, student_width), 1) // STUDENT_DIM
    norms = []

    def shift_rows(norm):
        parts = [part.astype(f32) for part in split_three(-norm)]
        out = jnp.where(spare == 0, parts[0], 0.0)
        out = jnp.where(spare == 1, parts[1], out)
        return jnp.where(spare == 2, parts[2], out).astype(bf16)

    for i in range(tiles):
        here = pl.ds(i * rows, rows)
        tile = pack[here, :]
        tile_t = tile.T
        tile_b = tile.astype(bf16)
        tile_s = tile[:, student_at:]
        for h in range(heads):
            tb = tile_b[:, h * TEACHER_DIM : (h + 1) * TEACHER_DIM]
            at = student_at + h * STUDENT_DIM
            sb = tile_b[:, at : at + STUDENT_DIM]
            teacher_key[h, here, :] = jnp.concatenate([tb, tb, ones], axis=1)
            student_key[h, here, :] = jnp.concatenate([sb, sb, ones], axis=1)
            teacher_t = tile_t[h * TEACHER_DIM : (h + 1) * TEACHER_DIM, :]
            student_t = tile_t[at : at + STUDENT_DIM, :]
            student_col[h, :, here] = student_t.astype(bf16)
            student_pad[h, here, :] = jnp.where(lane_head == h, tile_s, 0.0).astype(bf16)
            teacher_norm = TEACHER_SCALE * jnp.sum(teacher_t * teacher_t, axis=0, keepdims=True)
            student_norm = STUDENT_SCALE * jnp.sum(student_t * student_t, axis=0, keepdims=True)
            norms += [teacher_norm, student_norm]
            high, low = split_high_low(teacher_t * TEACHER_SCALE)
            teacher_row[h, i] = jnp.concatenate([high, low, shift_rows(teacher_norm)], axis=0)
            high, low = split_high_low(student_t * STUDENT_SCALE)
            student_row[h, i] = jnp.concatenate([high, low, shift_rows(student_norm)], axis=0)

    safe = jnp.max(functools.reduce(jnp.maximum, norms)) <= SAFE_NORM
    key_pos = lax.broadcasted_iota(jnp.int32, (rows, rows), 0)
    row_pos = lax.broadcasted_iota(jnp.int32, (rows, rows), 1)

    @pl.when(safe)
    def shifted_by_own_logit():
        def exponentials(h, i, model, prob):
            upto = (i + 1) * rows
            key, row = (student_key, student_row) if model else (teacher_key, teacher_row)
            values = jnp.dot(key[h, :upto, :], row[h, i], preferred_element_type=f32)
            diagonal = jnp.where(key_pos <= row_pos, values[i * rows :], NEGATIVE)
            total = cross = jnp.zeros((8, rows), f32)
            for j in range(i + 1):
                value = diagonal if j == i else values[j * rows : (j + 1) * rows]
                exp = jnp.exp2(value)
                prob[i % 2, j] = exp
                total = total + fold(exp)
                weight = teacher_prob[i % 2, j] if model else exp
                cross = cross + fold(weight * value)
            return [jnp.sum(part, axis=0, keepdims=True) for part in (total, cross)]

        def weights(h, i, j, teacher_inv, student_inv):
            value = student_prob[i % 2, j] * student_inv - teacher_prob[i % 2, j] * teacher_inv
            here = (h, slice(j * rows, (j + 1) * rows), slice(i * rows, (i + 1) * rows))
            weights_ref[here] = value.astype(bf16)

        def head_step(h, kl_total):
            inverse = None
            for i in range(tiles + 1):
                if i < tiles:
                    teacher_sum, teacher_cross = exponentials(h, i, 0, teacher_prob)
                    student_sum, student_cross = exponentials(h, i, 1, student_prob)
                if i:
                    upto = i * rows
                    for j in range(i):
                        weights(h, i - 1, j, *inverse)
                    row_grad[h, :, upto - rows : upto] = jnp.dot(
                        student_col[h, :, :upto],
                        weights_ref[h, :upto, upto - rows : upto],
                        preferred_element_type=f32,
                    )
                if i < tiles:
                    inverse = (1.0 / teacher_sum, 1.0 / student_sum)
                    kl_total = kl_total + (
                        (teacher_cross - student_cross) * inverse[0]
                        - jnp.log2(teacher_sum)
                        + jnp.log2(student_sum)
                    )
            return kl_total

        kl_sum[...] = lax.fori_loop(0, heads, head_step, jnp.zeros((1, rows), f32))

    @pl.when(jnp.logical_not(safe))
    def shifted_by_maximum():
        kl_sum[...] = jnp.zeros((1, rows), f32)

        def masked(h, i, j):
            allowed = key_pos + j * rows <= row_pos + i * rows
            keys = pl.ds(pl.multiple_of(j * rows, rows), rows)
            return [
                jnp.where(
                    allowed,
                    jnp.dot(key[h, keys, :], row[h, i], preferred_element_type=f32),
                    NEGATIVE,
                )
                for key, row in ((teacher_key, teacher_row), (student_key, student_row))
            ]

        def row_step(step, _):
            h, i = step // tiles, step % tiles
            here = pl.ds(pl.multiple_of(i * rows, rows), rows)

            def advance(j, state):
                teacher_max, teacher_sum, cross_sum, student_max, student_sum = state
                teacher, student = masked(h, i, j)
                teacher_top = jnp.maximum(teacher_max, jnp.max(teacher, axis=0, keepdims=True))
                student_top = jnp.maximum(student_max, jnp.max(student, axis=0, keepdims=True))
                teacher_exp = jnp.exp2(teacher - teacher_top)
                student_exp = jnp.exp2(student - student_top)
                shrink = jnp.exp2(teacher_max - teacher_top)
                cross = jnp.sum(teacher_exp * (teacher - student), axis=0, keepdims=True)
                return (
                    teacher_top,
                    teacher_sum * shrink + jnp.sum(teacher_exp, axis=0, keepdims=True),
                    cross_sum * shrink + cross,
                    student_top,
                    student_sum * jnp.exp2(student_max - student_top)
                    + jnp.sum(student_exp, axis=0, keepdims=True),
                )

            lowest = jnp.full((1, rows), NEGATIVE, f32)
            zeros = jnp.zeros((1, rows), f32)
            teacher_max, teacher_sum, cross_sum, student_max, student_sum = lax.fori_loop(
                0, i + 1, advance, (lowest, zeros, zeros, lowest, zeros)
            )
            teacher_lse = teacher_max + jnp.log2(teacher_sum)
            student_lse = student_max + jnp.log2(student_sum)
            kl_sum[...] = kl_sum[...] + (cross_sum / teacher_sum - teacher_lse + student_lse)

            def spread(j, total):
                teacher, student = masked(h, i, j)
                value = jnp.exp2(student - student_lse) - jnp.exp2(teacher - teacher_lse)
                value = value.astype(bf16)
                keys = pl.ds(pl.multiple_of(j * rows, rows), rows)
                weights_ref[h, keys, here] = value
                return total + jnp.dot(
                    student_col[h, :, keys], value, preferred_element_type=f32
                )

            row_grad[h, :, here] = lax.fori_loop(
                0, i + 1, spread, jnp.zeros((STUDENT_DIM, rows), f32)
            )
            return 0

        lax.fori_loop(0, heads * tiles, row_step, 0)

    kl_total = jnp.sum(kl_sum[...], axis=1, keepdims=True) * math.log(2.0)
    if last:
        kl_out[...] = kl_total + (kl_before[...] if kl_before is not None else 0.0)
        return
    kl_out[...] = jnp.broadcast_to(kl_total, kl_out.shape)

    key_kernel(rows, weights_ref, student_pad, key_grad)


def finish_kernel(heads, tiles, groups, chunks, me_ref, counts_ref, place_t_ref, *refs):
    kls, rest = refs[:groups], list(refs[groups:])
    row_parts, key_parts = rest[:chunks], rest[chunks : 2 * chunks]
    kept_ref, swapped_ref, grad_rows = rest[2 * chunks :]
    f32, bf16 = jnp.float32, jnp.bfloat16
    blocks, rows, window = place_t_ref.shape
    live = tiles * rows
    total_width = grad_rows.shape[1]

    for i in range(tiles):
        here = slice(i * rows, (i + 1) * rows)
        columns = jnp.concatenate(
            [part[h, :, here] for part in row_parts for h in range(heads)], axis=0
        )
        lanes = jnp.concatenate([part[here, :] for part in key_parts], axis=1)
        grad_rows[here, :] = (columns.T + lanes) * (STUDENT_DIM**-0.5)
    grad_rows[live:, :] = jnp.zeros((grad_rows.shape[0] - live, total_width), f32)
    tail = tail_rows(pair_sum([kl[:, :total_width] for kl in kls]), total_width)
    for k in range(blocks):
        base, _, _ = packed_start(me_ref[0], counts_ref, blocks, k)
        block = grad_rows[pl.ds(base, window), :].astype(bf16)
        out = swapped_ref if k % 2 else kept_ref
        value = jnp.dot(place_t_ref[k], block, preferred_element_type=f32)
        out[k // 2, :rows, :] = value.astype(bf16)
        out[k // 2, rows:, :] = tail


def local(teacher_queries, student_queries, token_counts):
    f32, bf16 = jnp.float32, jnp.bfloat16
    blocks = lax.axis_size("seq")
    chips = blocks // 2
    groups = lax.axis_size("head")
    rows = teacher_queries.shape[0]
    heads = teacher_queries.shape[1] // TEACHER_DIM // blocks
    tiles = blocks * 3 // 4
    live = tiles * rows
    folded = heads * STUDENT_DIM == LANES
    chunks = 2 if folded else 1
    chunk_heads = heads // chunks
    teacher_width = chunk_heads * TEACHER_DIM
    student_width = chunk_heads * STUDENT_DIM
    if folded:
        send_shape = (chips, rows + rows // 2, LANES)
    else:
        send_shape = (chips, rows, teacher_width + student_width)
    vmem = pl.BlockSpec(memory_space=pltpu.VMEM)
    smem = pl.BlockSpec(memory_space=pltpu.SMEM)
    params = pltpu.CompilerParams(vmem_limit_bytes=40 * 1024 * 1024)
    me = lax.axis_index("seq").reshape(1)
    order = sorted(range(1, chips), key=lambda k: -k.bit_count())

    def call(kernel, name, out_shape, *inputs, n_smem=0, **kwargs):
        out_specs = [vmem] * len(out_shape)
        in_specs = [smem] * n_smem + [vmem] * (len(inputs) - n_smem)
        kwargs = {"compiler_params": params, "in_specs": in_specs, **kwargs}
        return pl.pallas_call(kernel, out_specs=out_specs, out_shape=out_shape, name=name, **kwargs)(
            *inputs
        )

    def exchange(kept, swapped):
        swapped = lax.ppermute(swapped, "seq", [(i, i ^ 1) for i in range(blocks)])
        message = jax.ShapeDtypeStruct((2,) + kept.shape[1:], bf16)
        sends = call(
            functools.partial(merge_kernel, order),
            "merge",
            [message] * (chips - 1),
            kept,
            swapped,
        )
        return [kept, swapped] + [
            lax.ppermute(send, "seq", [(i, i ^ (2 * k)) for i in range(blocks)])
            for k, send in zip(order, sends)
        ]

    packed = jax.ShapeDtypeStruct(send_shape, bf16)
    if folded:
        anywhere = pl.BlockSpec(memory_space=pltpu.HBM)
        sends = pl.pallas_call(
            functools.partial(pack_folded_kernel, blocks, chunks),
            in_specs=[smem, anywhere, anywhere],
            out_specs=[vmem] * (2 * chunks),
            out_shape=[packed] * (2 * chunks),
            scratch_shapes=[
                pltpu.VMEM(student_queries.shape, bf16),
                pltpu.SemaphoreType.DMA((chunks * blocks + 1,)),
            ],
            compiler_params=pltpu.CompilerParams(vmem_limit_bytes=52 * 1024 * 1024),
            name="pack",
        )(me, teacher_queries, student_queries)
    else:
        sends = pl.pallas_call(
            functools.partial(pack_plain_kernel, blocks),
            in_specs=[smem, vmem, vmem],
            out_specs=[vmem] * 2,
            out_shape=[packed] * 2,
            compiler_params=params,
            name="pack",
        )(me, teacher_queries, student_queries)
    incoming = [exchange(*sends[2 * c : 2 * c + 2]) for c in range(chunks)]

    window = rows + PAD
    place, place_t = call(
        place_kernel,
        "place",
        [
            jax.ShapeDtypeStruct((blocks, window, rows), bf16),
            jax.ShapeDtypeStruct((blocks, rows, window), bf16),
        ],
        me,
        token_counts,
        n_smem=2,
    )
    row_grad = jax.ShapeDtypeStruct((chunk_heads, STUDENT_DIM, live), f32)
    key_grad = jax.ShapeDtypeStruct((live, student_width), f32)
    weights = jax.ShapeDtypeStruct((chunk_heads, live, live), bf16)
    student_pad = jax.ShapeDtypeStruct((chunk_heads, live, student_width), bf16)
    divergence = jax.ShapeDtypeStruct((1, LANES), f32)
    message = jax.ShapeDtypeStruct((chips, rows + TAIL, heads * STUDENT_DIM), bf16)
    pairs = chunk_heads * tiles * (tiles + 1) // 2 * rows * rows
    row_parts, key_parts, kl = [], [], []
    for c in range(chunks):
        last = c == chunks - 1
        if last:
            outs, held = [row_grad, weights, student_pad, divergence], []
        else:
            outs, held = [row_grad, key_grad, divergence], [weights, student_pad]
        scratch = [pltpu.VMEM(part.shape, part.dtype) for part in held] + [
            pltpu.VMEM((live + window, teacher_width + student_width), f32),
            pltpu.VMEM((chunk_heads, live, 2 * TEACHER_DIM + SHIFT), bf16),
            pltpu.VMEM((chunk_heads, live, 2 * STUDENT_DIM + SHIFT), bf16),
            pltpu.VMEM((chunk_heads, tiles, 2 * TEACHER_DIM + SHIFT, rows), bf16),
            pltpu.VMEM((chunk_heads, tiles, 2 * STUDENT_DIM + SHIFT, rows), bf16),
            pltpu.VMEM((chunk_heads, STUDENT_DIM, live), bf16),
            pltpu.VMEM((2, tiles, rows, rows), f32),
            pltpu.VMEM((2, tiles, rows, rows), f32),
            pltpu.VMEM((1, rows), f32),
        ]
        n_in = len(incoming[c])
        if last and not kl:
            kl = [jnp.zeros((1, LANES), f32)]
        made = call(
            functools.partial(relation_kernel, folded, chunk_heads, tiles, order, n_in, last),
            "relation",
            outs,
            me,
            token_counts,
            place,
            *incoming[c],
            *(kl if last else []),
            n_smem=2,
            scratch_shapes=scratch,
            cost_estimate=pl.CostEstimate(
                flops=4 * pairs * LANES, bytes_accessed=8 * pairs, transcendentals=2 * pairs
            ),
        )
        row_parts.append(made[0])
        kl = [made[-1]]
        if not last:
            key_parts.append(made[1])
    key_parts += call(
        functools.partial(key_kernel, rows),
        "keys",
        [key_grad],
        made[1],
        made[2],
        cost_estimate=pl.CostEstimate(
            flops=2 * pairs * LANES, bytes_accessed=2 * pairs, transcendentals=0
        ),
    )
    kls = kl + [
        lax.ppermute(kl[0], "head", [(i, i ^ k) for i in range(groups)]) for k in range(1, groups)
    ]
    kept, swapped = call(
        functools.partial(finish_kernel, chunk_heads, tiles, groups, chunks),
        "finish",
        [message, message],
        me,
        token_counts,
        place_t,
        *kls,
        *row_parts,
        *key_parts,
        n_smem=2,
        scratch_shapes=[pltpu.VMEM((live + window, heads * STUDENT_DIM), f32)],
    )
    returned = exchange(kept, swapped)
    grad, loss = call(
        functools.partial(unpack_kernel, order),
        "unpack",
        [jax.ShapeDtypeStruct((rows, student_queries.shape[1]), f32), divergence],
        me,
        token_counts,
        *returned,
        n_smem=2,
    )
    return (grad, loss[0, 0])


def solution(mesh):
    return jax.shard_map(
        local,
        mesh=mesh,
        in_specs=(P("seq", "head"), P("seq", "head"), P()),
        out_specs=(P("seq", "head"), P()),
        check_vma=False,
    )
```

```python
import functools
import math

import jax
import jax.numpy as jnp
from jax import lax
from jax.experimental import pallas as pl
from jax.experimental.pallas import tpu as pltpu
from jax.sharding import PartitionSpec as P

DT = 8192
DS = 4096
H_REL = 128
TEACHER_DIM = DT // H_REL
STUDENT_DIM = DS // H_REL

NEGATIVE = -1e30
LOG2E = math.log2(math.e)
TEACHER_SCALE = LOG2E * TEACHER_DIM**-0.5
STUDENT_SCALE = LOG2E * STUDENT_DIM**-0.5
PAD = 8
LANES = 128
TAIL = 16
SHIFT = 16
SAFE_NORM = 320.0


def split_high_low(values):
    high = values.astype(jnp.bfloat16)
    low = (values - high.astype(jnp.float32)).astype(jnp.bfloat16)
    return high, low


def split_three(values):
    high = values.astype(jnp.bfloat16)
    rest = values - high.astype(jnp.float32)
    return (high,) + split_high_low(rest)


def at_columns(index, count, width, act):
    if width % LANES == 0:
        act(pl.ds(pl.multiple_of(index * width, LANES), width))
    else:
        for part in range(count):
            pl.when(index == part)(functools.partial(act, pl.ds(part * width, width)))


def pack_folded_kernel(blocks, chunks, me_ref, teacher_ref, student_ref, *refs):
    sends, student, sems = refs[: 2 * chunks], refs[2 * chunks], refs[2 * chunks + 1]
    rows = teacher_ref.shape[0]
    half = rows // 2
    copies = [pltpu.make_async_copy(student_ref, student, sems.at[2 * chunks * blocks // 2])]
    for chunk in range(chunks):
        for core in range(2):
            for k in range(blocks // 2):
                to = jnp.bitwise_xor(me_ref[0], 2 * k + core)
                at = pl.multiple_of((to * chunks + chunk) * LANES, LANES)
                copies.append(
                    pltpu.make_async_copy(
                        teacher_ref.at[:, pl.ds(at, LANES)],
                        sends[2 * chunk + core].at[k, pl.ds(0, rows)],
                        sems.at[(2 * chunk + core) * (blocks // 2) + k],
                    )
                )
    for copy in copies:
        copy.start()
    copies[0].wait()
    for core in range(2):
        for k in range(blocks // 2):
            to = jnp.bitwise_xor(me_ref[0], 2 * k + core)
            lanes = pl.ds(pl.multiple_of(to * LANES, LANES), LANES)
            top, bottom = student[:half, lanes], student[half:, lanes]
            for chunk in range(chunks):
                part = slice(chunk * (LANES // 2), (chunk + 1) * (LANES // 2))
                sends[2 * chunk + core][k, rows:, :] = jnp.concatenate(
                    [top[:, part], bottom[:, part]], axis=1
                )
    for copy in copies[1:]:
        copy.wait()


def pack_plain_kernel(blocks, me_ref, teacher_ref, student_ref, *sends):
    teacher_width = teacher_ref.shape[1] // blocks
    student_width = student_ref.shape[1] // blocks
    for core in range(2):
        for k in range(blocks // 2):
            to = jnp.bitwise_xor(me_ref[0], 2 * k + core)

            def put_teacher(columns, send=sends[core], k=k):
                send[k, :, :teacher_width] = teacher_ref[:, columns]

            def put_student(columns, send=sends[core], k=k):
                send[k, :, teacher_width:] = student_ref[:, columns]

            at_columns(to, blocks, teacher_width, put_teacher)
            at_columns(to, blocks, student_width, put_student)


def pair_sum(parts):
    while len(parts) > 1:
        parts = [a + b for a, b in zip(parts[::2], parts[1::2])]
    return parts[0]


def tail_rows(value, width):
    thirds = [part.astype(jnp.float32) for part in split_three(value)]
    line = lax.broadcasted_iota(jnp.int32, (TAIL, width), 0)
    tail = jnp.where(line == 0, thirds[0], 0.0)
    tail = jnp.where(line == 1, thirds[1], tail)
    return jnp.where(line == 2, thirds[2], tail).astype(jnp.bfloat16)


def merge_kernel(order, kept_ref, swapped_ref, *sends):
    for k, send in zip(order, sends):
        send[0] = kept_ref[k]
        send[1] = swapped_ref[k]


def arrived(order, refs):
    blocks = [refs[0].at[0], refs[1].at[0]]
    for k in range(1, len(order) + 1):
        blocks += [refs[2 + order.index(k)].at[core] for core in range(2)]
    return blocks


def unpack_kernel(order, me_ref, *refs):
    grad_ref, loss_ref = refs[-2:]
    rows = grad_ref.shape[0]
    blocks = arrived(order, refs[:-2])
    for k, block in enumerate(blocks):

        def put(columns, block=block):
            grad_ref[:, columns] = block[:rows, :].astype(jnp.float32)

        at_columns(jnp.bitwise_xor(me_ref[0], k), len(blocks), block.shape[1], put)
    total = pair_sum([block[rows:, :].astype(jnp.float32) for block in blocks])
    loss_ref[...] = jnp.sum(total, axis=0, keepdims=True)


def packed_start(me, counts_ref, blocks, k):
    owner = jnp.bitwise_xor(me, k)
    start = sum(jnp.where(b < owner, counts_ref[b], 0) for b in range(blocks))
    base = pl.multiple_of(start // PAD * PAD, PAD)
    return base, start - base, counts_ref[owner]


def place_kernel(me_ref, counts_ref, place_ref, place_t_ref):
    blocks, window, rows = place_ref.shape
    position = lax.broadcasted_iota(jnp.int32, (window, rows), 0)
    token = lax.broadcasted_iota(jnp.int32, (window, rows), 1)
    position_t = lax.broadcasted_iota(jnp.int32, (rows, window), 1)
    token_t = lax.broadcasted_iota(jnp.int32, (rows, window), 0)
    for k in range(blocks):
        _, shift, count = packed_start(me_ref[0], counts_ref, blocks, k)
        place = (position == token + shift) & (token < count)
        place_ref[k] = place.astype(jnp.bfloat16)
        place = (position_t == token_t + shift) & (token_t < count)
        place_t_ref[k] = place.astype(jnp.bfloat16)


def fold(values):
    rows, columns = values.shape
    return jnp.sum(values.reshape(rows // 8, 8, columns), axis=0)


def key_kernel(rows, weights_ref, student_pad, key_grad):
    heads, live, _ = weights_ref.shape
    for at in range(0, live, rows):
        parts = [
            jnp.dot(
                weights_ref[h, at : at + rows, at:],
                student_pad[h, at:, :],
                preferred_element_type=jnp.float32,
            )
            for h in range(heads)
        ]
        key_grad[at : at + rows, :] = sum(parts)


def relation_kernel(folded, heads, tiles, order, n_in, last, me_ref, counts_ref, place_ref, *refs):
    sources = arrived(order, refs[:n_in])
    rest = list(refs[n_in:])
    if last:
        kl_before, row_grad, weights_ref, student_pad, kl_out, *rest = rest
    else:
        kl_before = None
        row_grad, key_grad, kl_out, weights_ref, student_pad, *rest = rest
    (
        pack,
        teacher_key,
        student_key,
        teacher_row,
        student_row,
        student_col,
        teacher_prob,
        student_prob,
        kl_sum,
    ) = rest
    f32, bf16 = jnp.float32, jnp.bfloat16
    blocks = len(sources)
    rows = teacher_prob.shape[3]
    half = rows // 2
    live = tiles * rows
    window = rows + PAD
    student_at = heads * TEACHER_DIM
    student_width = heads * STUDENT_DIM

    pack[...] = jnp.zeros(pack.shape, f32)
    for k, source in enumerate(sources):
        base, _, _ = packed_start(me_ref[0], counts_ref, blocks, k)
        here = pl.ds(base, window)
        place = place_ref[k]
        if folded:
            moved = jnp.dot(place, source[:rows, :], preferred_element_type=f32)
            pack[here, :student_at] = pack[here, :student_at] + moved
            student = source[rows:, :]
            moved = jnp.dot(
                place[:, :half], student[:, :student_width], preferred_element_type=f32
            ) + jnp.dot(place[:, half:], student[:, student_width:], preferred_element_type=f32)
            pack[here, student_at:] = pack[here, student_at:] + moved
        else:
            moved = jnp.dot(place, source[...], preferred_element_type=f32)
            pack[here, :] = pack[here, :] + moved

    teacher_depth, student_depth = teacher_key.shape[2], student_key.shape[2]
    teacher_ones = jnp.ones((rows, teacher_depth - 2 * TEACHER_DIM), bf16)
    student_ones = jnp.ones((rows, student_depth - 2 * STUDENT_DIM), bf16)
    teacher_gap = jnp.zeros((teacher_depth - 2 * TEACHER_DIM - SHIFT, rows), bf16)
    student_gap = jnp.zeros((student_depth - 2 * STUDENT_DIM - SHIFT, rows), bf16)
    spare = lax.broadcasted_iota(jnp.int32, (SHIFT, rows), 0)
    lane_head = lax.broadcasted_iota(jnp.int32, (rows, student_width), 1) // STUDENT_DIM
    norms = []

    def shift_rows(norm):
        parts = [part.astype(f32) for part in split_three(-norm)]
        out = jnp.where(spare == 0, parts[0], 0.0)
        out = jnp.where(spare == 1, parts[1], out)
        return jnp.where(spare == 2, parts[2], out).astype(bf16)

    for i in range(tiles):
        here = pl.ds(i * rows, rows)
        tile = pack[here, :]
        tile_t = tile.T
        tile_b = tile.astype(bf16)
        tile_s = tile[:, student_at:]
        for h in range(heads):
            tb = tile_b[:, h * TEACHER_DIM : (h + 1) * TEACHER_DIM]
            at = student_at + h * STUDENT_DIM
            sb = tile_b[:, at : at + STUDENT_DIM]
            teacher_key[h, here, :] = jnp.concatenate([tb, tb, teacher_ones], axis=1)
            student_key[h, here, :] = jnp.concatenate([sb, sb, student_ones], axis=1)
            teacher_t = tile_t[h * TEACHER_DIM : (h + 1) * TEACHER_DIM, :]
            student_t = tile_t[at : at + STUDENT_DIM, :]
            student_col[h, :, here] = student_t.astype(bf16)
            student_pad[h, here, :] = jnp.where(lane_head == h, tile_s, 0.0).astype(bf16)
            teacher_norm = TEACHER_SCALE * jnp.sum(teacher_t * teacher_t, axis=0, keepdims=True)
            student_norm = STUDENT_SCALE * jnp.sum(student_t * student_t, axis=0, keepdims=True)
            norms += [teacher_norm, student_norm]
            high, low = split_high_low(teacher_t * TEACHER_SCALE)
            shift = shift_rows(teacher_norm)
            teacher_row[h, i] = jnp.concatenate([high, low, shift, teacher_gap], axis=0)
            high, low = split_high_low(student_t * STUDENT_SCALE)
            shift = shift_rows(student_norm)
            student_row[h, i] = jnp.concatenate([high, low, shift, student_gap], axis=0)

    safe = jnp.max(functools.reduce(jnp.maximum, norms)) <= SAFE_NORM
    key_pos = lax.broadcasted_iota(jnp.int32, (rows, rows), 0)
    row_pos = lax.broadcasted_iota(jnp.int32, (rows, rows), 1)

    @pl.when(safe)
    def shifted_by_own_logit():
        def exponentials(h, i, model, prob):
            upto = (i + 1) * rows
            key, row = (student_key, student_row) if model else (teacher_key, teacher_row)
            values = jnp.dot(key[h, :upto, :], row[h, i], preferred_element_type=f32)
            diagonal = jnp.where(key_pos <= row_pos, values[i * rows :], NEGATIVE)
            total = cross = jnp.zeros((8, rows), f32)
            for j in range(i + 1):
                value = diagonal if j == i else values[j * rows : (j + 1) * rows]
                exp = jnp.exp2(value)
                prob[h, i % 2, j] = exp
                total = total + fold(exp)
                weight = teacher_prob[h, i % 2, j] if model else exp
                cross = cross + fold(weight * value)
            return [jnp.sum(part, axis=0, keepdims=True) for part in (total, cross)]

        def weights(h, i, j, teacher_inv, student_inv):
            value = (
                student_prob[h, i % 2, j] * student_inv - teacher_prob[h, i % 2, j] * teacher_inv
            )
            here = (h, slice(j * rows, (j + 1) * rows), slice(i * rows, (i + 1) * rows))
            weights_ref[here] = value.astype(bf16)

        kl_total = jnp.zeros((1, rows), f32)
        inverse = [None] * heads
        for i in range(tiles + 1):
            for h in range(heads):
                if i < tiles:
                    teacher_sum, teacher_cross = exponentials(h, i, 0, teacher_prob)
                    student_sum, student_cross = exponentials(h, i, 1, student_prob)
                if i:
                    upto = i * rows
                    for j in range(i):
                        weights(h, i - 1, j, *inverse[h])
                    row_grad[h, :, upto - rows : upto] = jnp.dot(
                        student_col[h, :, :upto],
                        weights_ref[h, :upto, upto - rows : upto],
                        preferred_element_type=f32,
                    )
                if i < tiles:
                    inverse[h] = (1.0 / teacher_sum, 1.0 / student_sum)
                    kl_total = kl_total + (
                        (teacher_cross - student_cross) * inverse[h][0]
                        - jnp.log2(teacher_sum)
                        + jnp.log2(student_sum)
                    )
        kl_sum[...] = kl_total

    @pl.when(jnp.logical_not(safe))
    def shifted_by_maximum():
        kl_sum[...] = jnp.zeros((1, rows), f32)

        def masked(h, i, j):
            allowed = key_pos + j * rows <= row_pos + i * rows
            keys = pl.ds(pl.multiple_of(j * rows, rows), rows)
            return [
                jnp.where(
                    allowed,
                    jnp.dot(key[h, keys, :], row[h, i], preferred_element_type=f32),
                    NEGATIVE,
                )
                for key, row in ((teacher_key, teacher_row), (student_key, student_row))
            ]

        def row_step(step, _):
            h, i = step // tiles, step % tiles
            here = pl.ds(pl.multiple_of(i * rows, rows), rows)

            def advance(j, state):
                teacher_max, teacher_sum, cross_sum, student_max, student_sum = state
                teacher, student = masked(h, i, j)
                teacher_top = jnp.maximum(teacher_max, jnp.max(teacher, axis=0, keepdims=True))
                student_top = jnp.maximum(student_max, jnp.max(student, axis=0, keepdims=True))
                teacher_exp = jnp.exp2(teacher - teacher_top)
                student_exp = jnp.exp2(student - student_top)
                shrink = jnp.exp2(teacher_max - teacher_top)
                cross = jnp.sum(teacher_exp * (teacher - student), axis=0, keepdims=True)
                return (
                    teacher_top,
                    teacher_sum * shrink + jnp.sum(teacher_exp, axis=0, keepdims=True),
                    cross_sum * shrink + cross,
                    student_top,
                    student_sum * jnp.exp2(student_max - student_top)
                    + jnp.sum(student_exp, axis=0, keepdims=True),
                )

            lowest = jnp.full((1, rows), NEGATIVE, f32)
            zeros = jnp.zeros((1, rows), f32)
            teacher_max, teacher_sum, cross_sum, student_max, student_sum = lax.fori_loop(
                0, i + 1, advance, (lowest, zeros, zeros, lowest, zeros)
            )
            teacher_lse = teacher_max + jnp.log2(teacher_sum)
            student_lse = student_max + jnp.log2(student_sum)
            kl_sum[...] = kl_sum[...] + (cross_sum / teacher_sum - teacher_lse + student_lse)

            def spread(j, total):
                teacher, student = masked(h, i, j)
                value = jnp.exp2(student - student_lse) - jnp.exp2(teacher - teacher_lse)
                value = value.astype(bf16)
                keys = pl.ds(pl.multiple_of(j * rows, rows), rows)
                weights_ref[h, keys, here] = value
                return total + jnp.dot(
                    student_col[h, :, keys], value, preferred_element_type=f32
                )

            row_grad[h, :, here] = lax.fori_loop(
                0, i + 1, spread, jnp.zeros((STUDENT_DIM, rows), f32)
            )
            return 0

        lax.fori_loop(0, heads * tiles, row_step, 0)

    tokens = sum(counts_ref[b] for b in range(blocks))
    share = jnp.full((1, rows), math.log(2.0), f32) / (H_REL * tokens).astype(f32)
    kl_total = jnp.sum(kl_sum[...] * share, axis=1, keepdims=True)
    if last:
        kl_out[...] = kl_total + (kl_before[...] if kl_before is not None else 0.0)
        return
    kl_out[...] = jnp.broadcast_to(kl_total, kl_out.shape)

    key_kernel(rows, weights_ref, student_pad, key_grad)


def finish_kernel(heads, tiles, groups, chunks, me_ref, counts_ref, place_t_ref, *refs):
    kls, rest = refs[:groups], list(refs[groups:])
    row_parts, key_parts = rest[:chunks], rest[chunks : 2 * chunks]
    kept_ref, swapped_ref, grad_rows = rest[2 * chunks :]
    f32, bf16 = jnp.float32, jnp.bfloat16
    blocks, rows, window = place_t_ref.shape
    live = tiles * rows
    total_width = grad_rows.shape[1]

    for i in range(tiles):
        here = slice(i * rows, (i + 1) * rows)
        columns = jnp.concatenate(
            [part[h, :, here] for part in row_parts for h in range(heads)], axis=0
        )
        lanes = jnp.concatenate([part[here, :] for part in key_parts], axis=1)
        grad_rows[here, :] = (columns.T + lanes) * (STUDENT_DIM**-0.5)
    grad_rows[live:, :] = jnp.zeros((grad_rows.shape[0] - live, total_width), f32)
    tail = tail_rows(pair_sum([kl[:, :total_width] for kl in kls]), total_width)
    for k in range(blocks):
        base, _, _ = packed_start(me_ref[0], counts_ref, blocks, k)
        block = grad_rows[pl.ds(base, window), :].astype(bf16)
        out = swapped_ref if k % 2 else kept_ref
        value = jnp.dot(place_t_ref[k], block, preferred_element_type=f32)
        out[k // 2, :rows, :] = value.astype(bf16)
        out[k // 2, rows:, :] = tail


def local(teacher_queries, student_queries, token_counts):
    f32, bf16 = jnp.float32, jnp.bfloat16
    blocks = lax.axis_size("seq")
    chips = blocks // 2
    groups = lax.axis_size("head")
    rows = teacher_queries.shape[0]
    heads = teacher_queries.shape[1] // TEACHER_DIM // blocks
    tiles = blocks * 3 // 4
    live = tiles * rows
    folded = heads * STUDENT_DIM == LANES
    chunks = 2 if folded else 1
    chunk_heads = heads // chunks
    teacher_width = chunk_heads * TEACHER_DIM
    student_width = chunk_heads * STUDENT_DIM
    if folded:
        send_shape = (chips, rows + rows // 2, LANES)
    else:
        send_shape = (chips, rows, teacher_width + student_width)
    vmem = pl.BlockSpec(memory_space=pltpu.VMEM)
    smem = pl.BlockSpec(memory_space=pltpu.SMEM)
    params = pltpu.CompilerParams(vmem_limit_bytes=40 * 1024 * 1024)
    me = lax.axis_index("seq").reshape(1)
    order = list(range(1, chips))

    def call(kernel, name, out_shape, *inputs, n_smem=0, **kwargs):
        out_specs = [vmem] * len(out_shape)
        in_specs = [smem] * n_smem + [vmem] * (len(inputs) - n_smem)
        kwargs = {"compiler_params": params, "in_specs": in_specs, **kwargs}
        return pl.pallas_call(kernel, out_specs=out_specs, out_shape=out_shape, name=name, **kwargs)(
            *inputs
        )

    def exchange(kept, swapped):
        swapped = lax.ppermute(swapped, "seq", [(i, i ^ 1) for i in range(blocks)])
        message = jax.ShapeDtypeStruct((2,) + kept.shape[1:], bf16)
        sends = call(
            functools.partial(merge_kernel, order),
            "merge",
            [message] * (chips - 1),
            kept,
            swapped,
        )
        return [kept, swapped] + [
            lax.ppermute(send, "seq", [(i, i ^ (2 * k)) for i in range(blocks)])
            for k, send in zip(order, sends)
        ]

    packed = jax.ShapeDtypeStruct(send_shape, bf16)
    if folded:
        anywhere = pl.BlockSpec(memory_space=pltpu.HBM)
        sends = pl.pallas_call(
            functools.partial(pack_folded_kernel, blocks, chunks),
            in_specs=[smem, anywhere, anywhere],
            out_specs=[vmem] * (2 * chunks),
            out_shape=[packed] * (2 * chunks),
            scratch_shapes=[
                pltpu.VMEM(student_queries.shape, bf16),
                pltpu.SemaphoreType.DMA((chunks * blocks + 1,)),
            ],
            compiler_params=pltpu.CompilerParams(vmem_limit_bytes=52 * 1024 * 1024),
            name="pack",
        )(me, teacher_queries, student_queries)
    else:
        sends = pl.pallas_call(
            functools.partial(pack_plain_kernel, blocks),
            in_specs=[smem, vmem, vmem],
            out_specs=[vmem] * 2,
            out_shape=[packed] * 2,
            compiler_params=params,
            name="pack",
        )(me, teacher_queries, student_queries)
    incoming = [exchange(*sends[2 * c : 2 * c + 2]) for c in range(chunks)]

    window = rows + PAD
    place, place_t = call(
        place_kernel,
        "place",
        [
            jax.ShapeDtypeStruct((blocks, window, rows), bf16),
            jax.ShapeDtypeStruct((blocks, rows, window), bf16),
        ],
        me,
        token_counts,
        n_smem=2,
    )
    row_grad = jax.ShapeDtypeStruct((chunk_heads, STUDENT_DIM, live), f32)
    key_grad = jax.ShapeDtypeStruct((live, student_width), f32)
    weights = jax.ShapeDtypeStruct((chunk_heads, live, live), bf16)
    student_pad = jax.ShapeDtypeStruct((chunk_heads, live, student_width), bf16)
    divergence = jax.ShapeDtypeStruct((1, LANES), f32)
    message = jax.ShapeDtypeStruct((chips, rows + TAIL, heads * STUDENT_DIM), bf16)
    pairs = chunk_heads * tiles * (tiles + 1) // 2 * rows * rows
    row_parts, key_parts, kl = [], [], []
    for c in range(chunks):
        last = c == chunks - 1
        if last:
            outs, held = [row_grad, weights, student_pad, divergence], []
        else:
            outs, held = [row_grad, key_grad, divergence], [weights, student_pad]
        scratch = [pltpu.VMEM(part.shape, part.dtype) for part in held] + [
            pltpu.VMEM((live + window, teacher_width + student_width), f32),
            pltpu.VMEM((chunk_heads, live, 2 * LANES), bf16),
            pltpu.VMEM((chunk_heads, live, LANES), bf16),
            pltpu.VMEM((chunk_heads, tiles, 2 * LANES, rows), bf16),
            pltpu.VMEM((chunk_heads, tiles, LANES, rows), bf16),
            pltpu.VMEM((chunk_heads, STUDENT_DIM, live), bf16),
            pltpu.VMEM((chunk_heads, 2, tiles, rows, rows), f32),
            pltpu.VMEM((chunk_heads, 2, tiles, rows, rows), f32),
            pltpu.VMEM((1, rows), f32),
        ]
        n_in = len(incoming[c])
        if last and not kl:
            kl = [jnp.zeros((1, LANES), f32)]
        made = call(
            functools.partial(relation_kernel, folded, chunk_heads, tiles, order, n_in, last),
            "relation",
            outs,
            me,
            token_counts,
            place,
            *incoming[c],
            *(kl if last else []),
            n_smem=2,
            scratch_shapes=scratch,
            cost_estimate=pl.CostEstimate(
                flops=4 * pairs * LANES, bytes_accessed=8 * pairs, transcendentals=2 * pairs
            ),
        )
        row_parts.append(made[0])
        kl = [made[-1]]
        if not last:
            key_parts.append(made[1])
    key_parts += call(
        functools.partial(key_kernel, rows),
        "keys",
        [key_grad],
        made[1],
        made[2],
        cost_estimate=pl.CostEstimate(
            flops=2 * pairs * LANES, bytes_accessed=2 * pairs, transcendentals=0
        ),
    )
    kls = kl + [
        lax.ppermute(kl[0], "head", [(i, i ^ k) for i in range(groups)]) for k in range(1, groups)
    ]
    kept, swapped = call(
        functools.partial(finish_kernel, chunk_heads, tiles, groups, chunks),
        "finish",
        [message, message],
        me,
        token_counts,
        place_t,
        *kls,
        *row_parts,
        *key_parts,
        n_smem=2,
        scratch_shapes=[pltpu.VMEM((live + window, heads * STUDENT_DIM), f32)],
    )
    returned = exchange(kept, swapped)
    grad, loss = call(
        functools.partial(unpack_kernel, order),
        "unpack",
        [
            jax.ShapeDtypeStruct((rows, student_queries.shape[1]), f32),
            jax.ShapeDtypeStruct((1, heads * STUDENT_DIM), f32),
        ],
        me,
        *returned,
        n_smem=1,
    )
    return (grad, loss[0, 0])


def solution(mesh):
    return jax.shard_map(
        local,
        mesh=mesh,
        in_specs=(P("seq", "head"), P("seq", "head"), P()),
        out_specs=(P("seq", "head"), P()),
        check_vma=False,
    )
```

```python
import functools
import math

import jax
import jax.numpy as jnp
from jax import lax
from jax.experimental import pallas as pl
from jax.experimental.pallas import tpu as pltpu
from jax.sharding import PartitionSpec as P

DT = 8192
DS = 4096
H_REL = 128
TEACHER_DIM = DT // H_REL
STUDENT_DIM = DS // H_REL

NEGATIVE = -1e30
LOG2E = math.log2(math.e)
TEACHER_SCALE = LOG2E * TEACHER_DIM**-0.5
STUDENT_SCALE = LOG2E * STUDENT_DIM**-0.5
PAD = 8
LANES = 128
TAIL = 16
SHIFT = 16
SAFE_NORM = 320.0


def split_high_low(values):
    high = values.astype(jnp.bfloat16)
    low = (values - high.astype(jnp.float32)).astype(jnp.bfloat16)
    return high, low


def split_three(values):
    high = values.astype(jnp.bfloat16)
    rest = values - high.astype(jnp.float32)
    return (high,) + split_high_low(rest)


def at_columns(index, count, width, act):
    if width % LANES == 0:
        act(pl.ds(pl.multiple_of(index * width, LANES), width))
    else:
        for part in range(count):
            pl.when(index == part)(functools.partial(act, pl.ds(part * width, width)))


def pack_kernel(blocks, chunks, me_ref, teacher_ref, student_ref, *refs):
    sends, sem = refs[: 2 * (chunks + 1)], refs[2 * (chunks + 1)]
    copies = []
    for part in range(chunks + 1):
        source = teacher_ref if part else student_ref
        width = sends[2 * part].shape[2]
        for k in range(blocks):
            to = jnp.bitwise_xor(me_ref[0], k)
            index = to * chunks + part - 1 if part else to
            at = pl.multiple_of(index * width, width)
            copies.append(
                pltpu.make_async_copy(
                    source.at[:, pl.ds(at, width)],
                    sends[2 * part + k % 2].at[k // 2],
                    sem.at[part * blocks + k],
                )
            )
    for copy in copies:
        copy.start()
    for copy in copies:
        copy.wait()


def pack_narrow_kernel(blocks, me_ref, teacher_ref, student_ref, *sends):
    for part, source in enumerate((student_ref, teacher_ref)):
        width = sends[2 * part].shape[2]
        for k in range(blocks):

            def put(columns, send=sends[2 * part + k % 2], k=k, source=source):
                send[k // 2] = source[:, columns]

            at_columns(jnp.bitwise_xor(me_ref[0], k), blocks, width, put)


def pair_sum(parts):
    while len(parts) > 1:
        parts = [a + b for a, b in zip(parts[::2], parts[1::2])]
    return parts[0]


def tail_rows(value, width):
    thirds = [part.astype(jnp.float32) for part in split_three(value)]
    line = lax.broadcasted_iota(jnp.int32, (TAIL, width), 0)
    tail = jnp.where(line == 0, thirds[0], 0.0)
    tail = jnp.where(line == 1, thirds[1], tail)
    return jnp.where(line == 2, thirds[2], tail).astype(jnp.bfloat16)


def merge_kernel(kept_ref, swapped_ref, *sends):
    for k, send in enumerate(sends, 1):
        send[0] = kept_ref[k]
        send[1] = swapped_ref[k]


def arrived(refs):
    return [refs[0].at[0], refs[1].at[0]] + [ref.at[core] for ref in refs[2:] for core in range(2)]


def unpack_kernel(me_ref, *refs):
    grad_ref, loss_ref = refs[-2:]
    rows = grad_ref.shape[0]
    blocks = arrived(refs[:-2])
    for k, block in enumerate(blocks):

        def put(columns, block=block):
            grad_ref[:, columns] = block[:rows, :].astype(jnp.float32)

        at_columns(jnp.bitwise_xor(me_ref[0], k), len(blocks), block.shape[1], put)
    total = pair_sum([block[rows:, :].astype(jnp.float32) for block in blocks])
    loss_ref[...] = jnp.sum(total, axis=0, keepdims=True)


def packed_start(me, counts_ref, blocks, k):
    owner = jnp.bitwise_xor(me, k)
    start = sum(jnp.where(b < owner, counts_ref[b], 0) for b in range(blocks))
    base = pl.multiple_of(start // PAD * PAD, PAD)
    return base, start - base, counts_ref[owner]


def place_kernel(me_ref, counts_ref, place_ref, place_t_ref):
    blocks, window, rows = place_ref.shape
    position = lax.broadcasted_iota(jnp.int32, (window, rows), 0)
    token = lax.broadcasted_iota(jnp.int32, (window, rows), 1)
    position_t = lax.broadcasted_iota(jnp.int32, (rows, window), 1)
    token_t = lax.broadcasted_iota(jnp.int32, (rows, window), 0)
    for k in range(blocks):
        _, shift, count = packed_start(me_ref[0], counts_ref, blocks, k)
        place = (position == token + shift) & (token < count)
        place_ref[k] = place.astype(jnp.bfloat16)
        place = (position_t == token_t + shift) & (token_t < count)
        place_t_ref[k] = place.astype(jnp.bfloat16)


def fold(values):
    rows, columns = values.shape
    return jnp.sum(values.reshape(rows // 8, 8, columns), axis=0)


def lay_out(sources, me, counts_ref, place_ref, pack):
    _, window, _ = place_ref.shape
    pack[...] = jnp.zeros(pack.shape, jnp.float32)
    for k, source in enumerate(sources):
        base, _, _ = packed_start(me, counts_ref, len(sources), k)
        here = pl.ds(base, window)
        moved = jnp.dot(place_ref[k], source[...], preferred_element_type=jnp.float32)
        pack[here, :] = pack[here, :] + moved


def operands(pack, key_op, row_op, heads, width, scale, norms, also=None):
    f32, bf16 = jnp.float32, jnp.bfloat16
    _, tiles, depth, rows = row_op.shape
    ones = jnp.ones((rows, depth - 2 * width), bf16)
    gap = jnp.zeros((depth - 2 * width - SHIFT, rows), bf16)
    spare = lax.broadcasted_iota(jnp.int32, (SHIFT, rows), 0)
    for i in range(tiles):
        here = slice(i * rows, (i + 1) * rows)
        tile = pack[here, :]
        tile_t = tile.T
        tile_b = tile.astype(bf16)
        for h in range(heads):
            part = tile_b[:, h * width : (h + 1) * width]
            key_op[h, here, :] = jnp.concatenate([part, part, ones], axis=1)
            part_t = tile_t[h * width : (h + 1) * width, :]
            norm = scale * jnp.sum(part_t * part_t, axis=0, keepdims=True)
            norms.append(norm)
            thirds = [third.astype(f32) for third in split_three(-norm)]
            shift = jnp.where(spare == 0, thirds[0], 0.0)
            shift = jnp.where(spare == 1, thirds[1], shift)
            shift = jnp.where(spare == 2, thirds[2], shift).astype(bf16)
            high, low = split_high_low(part_t * scale)
            row_op[h, i] = jnp.concatenate([high, low, shift, gap], axis=0)
            if also is not None:
                also(h, here, tile, part_t)


def is_safe(norms):
    return jnp.max(functools.reduce(jnp.maximum, norms)) <= SAFE_NORM


def diagonal_mask(rows):
    key_pos = lax.broadcasted_iota(jnp.int32, (rows, rows), 0)
    return key_pos <= lax.broadcasted_iota(jnp.int32, (rows, rows), 1)


def row_logits(key_op, row_op, h, i, allowed):
    rows = row_op.shape[3]
    for j in range(i + 1):
        keys = key_op[h, j * rows : (j + 1) * rows, :]
        value = jnp.dot(keys, row_op[h, i], preferred_element_type=jnp.float32)
        yield jnp.where(allowed, value, NEGATIVE) if j == i else value


def tile_logits(key_op, row_op, h, i, j, allowed):
    rows = row_op.shape[3]
    keys = pl.ds(pl.multiple_of(j * rows, rows), rows)
    value = jnp.dot(key_op[h, keys, :], row_op[h, i], preferred_element_type=jnp.float32)
    return jnp.where(jnp.logical_or(allowed, j < i), value, NEGATIVE)


def total(values):
    return jnp.sum(values, axis=0, keepdims=True)


def student_kernel(heads, tiles, n_in, me_ref, counts_ref, place_ref, *refs):
    sources = arrived(refs[:n_in])
    logits_ref, lse_ref, student_col, student_pad, pack, key_op, row_op = refs[n_in:]
    f32, bf16 = jnp.float32, jnp.bfloat16
    rows = row_op.shape[3]
    lay_out(sources, me_ref[0], counts_ref, place_ref, pack)
    lane_head = lax.broadcasted_iota(jnp.int32, (rows, heads * STUDENT_DIM), 1) // STUDENT_DIM

    def also(h, here, tile, part_t):
        student_col[h, :, here] = part_t.astype(bf16)
        student_pad[h, here, :] = jnp.where(lane_head == h, tile, 0.0).astype(bf16)

    norms = []
    operands(pack, key_op, row_op, heads, STUDENT_DIM, STUDENT_SCALE, norms, also)
    safe = is_safe(norms)
    allowed = diagonal_mask(rows)

    @pl.when(safe)
    def shifted_by_own_logit():
        def head_step(h, _):
            for i in range(tiles):
                exp_sum = jnp.zeros((8, rows), f32)
                for j, value in enumerate(row_logits(key_op, row_op, h, i, allowed)):
                    logits_ref[h, i * (i + 1) // 2 + j] = value
                    exp_sum = exp_sum + fold(jnp.exp2(value))
                lse_ref[h, i] = jnp.log2(total(exp_sum))
            return 0

        lax.fori_loop(0, heads, head_step, 0)

    @pl.when(jnp.logical_not(safe))
    def shifted_by_maximum():
        def row_step(step, _):
            h, i = step // tiles, step % tiles
            at = i * (i + 1) // 2

            def advance(j, state):
                top, exp_sum = state
                value = tile_logits(key_op, row_op, h, i, j, allowed)
                logits_ref[h, at + j] = value
                new = jnp.maximum(top, jnp.max(value, axis=0, keepdims=True))
                return new, exp_sum * jnp.exp2(top - new) + total(jnp.exp2(value - new))

            start = (jnp.full((1, rows), NEGATIVE, f32), jnp.zeros((1, rows), f32))
            top, exp_sum = lax.fori_loop(0, i + 1, advance, start)
            lse_ref[h, i] = top + jnp.log2(exp_sum)
            return 0

        lax.fori_loop(0, heads * tiles, row_step, 0)


def teacher_kernel(first, heads, tiles, n_in, me_ref, counts_ref, place_ref, *refs):
    sources = arrived(refs[:n_in])
    student_logits, student_lse, student_col, student_pad, *rest = refs[n_in:]
    kl_before, key_before = None, None
    if first:
        kl_before, key_before, *rest = rest
    row_grad, key_grad, kl_out, pack, key_op, row_op, prob, weights_ref, kl_sum = rest
    f32, bf16 = jnp.float32, jnp.bfloat16
    rows = row_op.shape[3]
    live = tiles * rows
    lay_out(sources, me_ref[0], counts_ref, place_ref, pack)
    norms = []
    operands(pack, key_op, row_op, heads, TEACHER_DIM, TEACHER_SCALE, norms)
    safe = is_safe(norms)
    allowed = diagonal_mask(rows)
    key_grad[...] = key_before[...] if first else jnp.zeros(key_grad.shape, f32)

    def weights(h, i, j, inverse):
        student = student_logits[first + h, i * (i + 1) // 2 + j] - student_lse[first + h, i]
        return (jnp.exp2(student) - prob[i % 2, j] * inverse).astype(bf16)

    @pl.when(safe)
    def shifted_by_own_logit():
        def head_step(h, kl_total):
            inverse = None
            for i in range(tiles + 1):
                if i < tiles:
                    exp_sum = cross = jnp.zeros((8, rows), f32)
                    for j, value in enumerate(row_logits(key_op, row_op, h, i, allowed)):
                        exp = jnp.exp2(value)
                        prob[i % 2, j] = exp
                        exp_sum = exp_sum + fold(exp)
                        student = student_logits[first + h, i * (i + 1) // 2 + j]
                        cross = cross + fold(exp * (value - student))
                if i:
                    upto = i * rows
                    for j in range(i):
                        weights_ref[j * rows : (j + 1) * rows, upto - rows : upto] = weights(
                            h, i - 1, j, inverse
                        )
                    row_grad[h, :, upto - rows : upto] = jnp.dot(
                        student_col[first + h, :, :upto],
                        weights_ref[:upto, upto - rows : upto],
                        preferred_element_type=f32,
                    )
                if i < tiles:
                    exp_sum = total(exp_sum)
                    inverse = 1.0 / exp_sum
                    kl_total = kl_total + (
                        total(cross) * inverse - jnp.log2(exp_sum) + student_lse[first + h, i]
                    )
            for j in range(tiles):
                here = slice(j * rows, (j + 1) * rows)
                key_grad[here, :] = key_grad[here, :] + jnp.dot(
                    weights_ref[here, j * rows :],
                    student_pad[first + h, j * rows :, :],
                    preferred_element_type=f32,
                )
            return kl_total

        kl_sum[...] = lax.fori_loop(0, heads, head_step, jnp.zeros((1, rows), f32))

    @pl.when(jnp.logical_not(safe))
    def shifted_by_maximum():
        kl_sum[...] = jnp.zeros((1, rows), f32)

        def row_step(step, _):
            h, i = step // tiles, step % tiles
            here = pl.ds(pl.multiple_of(i * rows, rows), rows)

            def advance(j, top):
                value = tile_logits(key_op, row_op, h, i, j, allowed)
                prob[i % 2, j] = value
                return jnp.maximum(top, jnp.max(value, axis=0, keepdims=True))

            top = lax.fori_loop(0, i + 1, advance, jnp.full((1, rows), NEGATIVE, f32))

            def exponentials(j, state):
                value = prob[i % 2, j]
                exp = jnp.exp2(value - top)
                prob[i % 2, j] = exp
                student = student_logits[first + h, i * (i + 1) // 2 + j]
                return state[0] + total(exp), state[1] + total(exp * (value - student))

            zeros = jnp.zeros((1, rows), f32)
            exp_sum, cross = lax.fori_loop(0, i + 1, exponentials, (zeros, zeros))
            inverse = 1.0 / exp_sum
            kl_sum[...] = kl_sum[...] + (
                cross * inverse - top - jnp.log2(exp_sum) + student_lse[first + h, i]
            )

            def spread(j, row_total):
                value = weights(h, i, j, inverse)
                keys = pl.ds(pl.multiple_of(j * rows, rows), rows)
                key_grad[keys, :] = key_grad[keys, :] + jnp.dot(
                    value, student_pad[first + h, here, :], preferred_element_type=f32
                )
                return row_total + jnp.dot(
                    student_col[first + h, :, keys], value, preferred_element_type=f32
                )

            row_grad[h, :, here] = lax.fori_loop(
                0, i + 1, spread, jnp.zeros((STUDENT_DIM, rows), f32)
            )
            return 0

        lax.fori_loop(0, heads * tiles, row_step, 0)

    tokens = sum(counts_ref[b] for b in range(len(sources)))
    share = jnp.full((1, rows), math.log(2.0), f32) / (H_REL * tokens).astype(f32)
    kl_total = jnp.sum(kl_sum[...] * share, axis=1, keepdims=True)
    kl_out[...] = jnp.broadcast_to(kl_total, kl_out.shape) + (kl_before[...] if first else 0.0)


def turn_kernel(tiles, *refs):
    row_parts, (key_grad, out_ref) = refs[:-2], refs[-2:]
    live = row_parts[0].shape[2]
    rows = live // tiles
    for i in range(tiles):
        here = slice(i * rows, (i + 1) * rows)
        columns = jnp.concatenate(
            [part[h, :, here] for part in row_parts for h in range(part.shape[0])], axis=0
        )
        value = (columns.T + key_grad[here, :]) * (STUDENT_DIM**-0.5)
        out_ref[here, :] = value
    out_ref[live:, :] = jnp.zeros((out_ref.shape[0] - live, out_ref.shape[1]), jnp.float32)


def finish_kernel(groups, me_ref, counts_ref, place_t_ref, grad_rows, *refs):
    kls, (kept_ref, swapped_ref) = refs[:groups], refs[groups:]
    blocks, rows, window = place_t_ref.shape
    width = grad_rows.shape[1]
    tail = tail_rows(pair_sum([kl[:, :width] for kl in kls]), width)
    for k in range(blocks):
        base, _, _ = packed_start(me_ref[0], counts_ref, blocks, k)
        block = grad_rows[pl.ds(base, window), :].astype(jnp.bfloat16)
        out = swapped_ref if k % 2 else kept_ref
        value = jnp.dot(place_t_ref[k], block, preferred_element_type=jnp.float32)
        out[k // 2, :rows, :] = value.astype(jnp.bfloat16)
        out[k // 2, rows:, :] = tail


def local(teacher_queries, student_queries, token_counts):
    f32, bf16 = jnp.float32, jnp.bfloat16
    blocks = lax.axis_size("seq")
    chips = blocks // 2
    groups = lax.axis_size("head")
    rows = teacher_queries.shape[0]
    heads = teacher_queries.shape[1] // TEACHER_DIM // blocks
    tiles = blocks * 3 // 4
    live = tiles * rows
    window = rows + PAD
    wide = heads * STUDENT_DIM == LANES
    chunks = 2 if wide else 1
    chunk_heads = heads // chunks
    student_width = heads * STUDENT_DIM
    teacher_width = chunk_heads * TEACHER_DIM
    triangle = tiles * (tiles + 1) // 2
    vmem = pl.BlockSpec(memory_space=pltpu.VMEM)
    smem = pl.BlockSpec(memory_space=pltpu.SMEM)
    mib = 1024 * 1024
    me = lax.axis_index("seq").reshape(1)

    def shape(*dims, dtype=f32):
        return jax.ShapeDtypeStruct(dims, dtype)

    def call(kernel, name, out_shape, *inputs, n_smem=0, vmem_mib=8, **kwargs):
        in_specs = [smem] * n_smem + [vmem] * (len(inputs) - n_smem)
        kwargs = {"in_specs": in_specs, **kwargs}
        return pl.pallas_call(
            kernel,
            out_specs=[vmem] * len(out_shape),
            out_shape=out_shape,
            compiler_params=pltpu.CompilerParams(vmem_limit_bytes=vmem_mib * mib),
            name=name,
            **kwargs,
        )(*inputs)

    def cost(n_heads, flops):
        pairs = n_heads * triangle * rows * rows
        return pl.CostEstimate(
            flops=flops * pairs * LANES, bytes_accessed=4 * pairs, transcendentals=pairs
        )

    def exchange(kept, swapped):
        swapped = lax.ppermute(swapped, "seq", [(i, i ^ 1) for i in range(blocks)])
        sends = call(
            merge_kernel,
            "merge",
            [shape(2, *kept.shape[1:], dtype=bf16)] * (chips - 1),
            kept,
            swapped,
        )
        return [kept, swapped] + [
            lax.ppermute(send, "seq", [(i, i ^ (2 * k)) for i in range(blocks)])
            for k, send in enumerate(sends, 1)
        ]

    widths = [student_width] + [teacher_width] * chunks
    packed = [shape(chips, rows, width, dtype=bf16) for width in widths for _ in range(2)]
    if wide:
        hbm = pl.BlockSpec(memory_space=pltpu.HBM)
        sends = call(
            functools.partial(pack_kernel, blocks, chunks),
            "pack",
            packed,
            me,
            teacher_queries,
            student_queries,
            vmem_mib=52,
            in_specs=[smem, hbm, hbm],
            scratch_shapes=[pltpu.SemaphoreType.DMA(((chunks + 1) * blocks,))],
        )
    else:
        sends = call(
            functools.partial(pack_narrow_kernel, blocks),
            "pack",
            packed,
            me,
            teacher_queries,
            student_queries,
            n_smem=1,
        )
    incoming = [exchange(*sends[2 * c : 2 * c + 2]) for c in range(chunks + 1)]
    place, place_t = call(
        place_kernel,
        "place",
        [shape(blocks, window, rows, dtype=bf16), shape(blocks, rows, window, dtype=bf16)],
        me,
        token_counts,
        n_smem=2,
    )
    n_in = chips + 1
    student = call(
        functools.partial(student_kernel, heads, tiles, n_in),
        "student",
        [
            shape(heads, triangle, rows, rows),
            shape(heads, tiles, 1, rows),
            shape(heads, STUDENT_DIM, live, dtype=bf16),
            shape(heads, live, student_width, dtype=bf16),
        ],
        me,
        token_counts,
        place,
        *incoming[0],
        n_smem=2,
        vmem_mib=10 if wide else 24,
        scratch_shapes=[
            pltpu.VMEM((live + window, student_width), f32),
            pltpu.VMEM((heads, live, LANES), bf16),
            pltpu.VMEM((heads, tiles, LANES, rows), bf16),
        ],
        cost_estimate=cost(heads, 2),
    )
    row_parts, before = [], []
    for c in range(chunks):
        row_grad, key_grad, kl = call(
            functools.partial(teacher_kernel, c * chunk_heads, chunk_heads, tiles, n_in),
            "teacher",
            [
                shape(chunk_heads, STUDENT_DIM, live),
                shape(live, student_width),
                shape(1, LANES),
            ],
            me,
            token_counts,
            place,
            *incoming[1 + c],
            *student,
            *before,
            n_smem=2,
            vmem_mib=16 if wide else 44,
            scratch_shapes=[
                pltpu.VMEM((live + window, teacher_width), f32),
                pltpu.VMEM((chunk_heads, live, 2 * LANES), bf16),
                pltpu.VMEM((chunk_heads, tiles, 2 * LANES, rows), bf16),
                pltpu.VMEM((2, tiles, rows, rows), f32),
                pltpu.VMEM((live, live), bf16),
                pltpu.VMEM((1, rows), f32),
            ],
            cost_estimate=cost(chunk_heads, 6),
        )
        row_parts.append(row_grad)
        before = [kl, key_grad]
    kls = [kl] + [
        lax.ppermute(kl, "head", [(i, i ^ k) for i in range(groups)]) for k in range(1, groups)
    ]
    (grad_rows,) = call(
        functools.partial(turn_kernel, tiles),
        "turn",
        [shape(live + window, student_width)],
        *row_parts,
        key_grad,
        cost_estimate=cost(heads, 1),
    )
    kept, swapped = call(
        functools.partial(finish_kernel, groups),
        "finish",
        [shape(chips, rows + TAIL, student_width, dtype=bf16)] * 2,
        me,
        token_counts,
        place_t,
        grad_rows,
        *kls,
        n_smem=2,
    )
    returned = exchange(kept, swapped)
    grad, loss = call(
        unpack_kernel,
        "unpack",
        [shape(rows, student_queries.shape[1]), shape(1, student_width)],
        me,
        *returned,
        n_smem=1,
    )
    return (grad, loss[0, 0])


def solution(mesh):
    return jax.shard_map(
        local,
        mesh=mesh,
        in_specs=(P("seq", "head"), P("seq", "head"), P()),
        out_specs=(P("seq", "head"), P()),
        check_vma=False,
    )
```

```python
import functools
import math

import jax
import jax.numpy as jnp
from jax import lax
from jax.experimental import pallas as pl
from jax.experimental.pallas import tpu as pltpu
from jax.sharding import PartitionSpec as P

DT = 8192
DS = 4096
H_REL = 128
TEACHER_DIM = DT // H_REL
STUDENT_DIM = DS // H_REL

NEGATIVE = -1e30
LOG2E = math.log2(math.e)
TEACHER_SCALE = LOG2E * TEACHER_DIM**-0.5
STUDENT_SCALE = LOG2E * STUDENT_DIM**-0.5
PAD = 8
LANES = 128
DEPTH = 256
SAFE_NORM = 320.0


def split_high_low(values):
    high = values.astype(jnp.bfloat16)
    low = (values - high.astype(jnp.float32)).astype(jnp.bfloat16)
    return high, low


def split_three(values):
    high = values.astype(jnp.bfloat16)
    rest = values - high.astype(jnp.float32)
    return (high,) + split_high_low(rest)


def at_columns(index, count, width, act):
    if width % LANES == 0:
        act(pl.ds(pl.multiple_of(index * width, LANES), width))
    else:
        for part in range(count):
            pl.when(index == part)(functools.partial(act, pl.ds(part * width, width)))


def pack_folded_kernel(blocks, chunks, me_ref, teacher_ref, student_ref, *refs):
    sends, student, sems = refs[: 2 * chunks], refs[2 * chunks], refs[2 * chunks + 1]
    rows = teacher_ref.shape[0]
    half = rows // 2
    copies = [pltpu.make_async_copy(student_ref, student, sems.at[2 * chunks * blocks // 2])]
    for chunk in range(chunks):
        for core in range(2):
            for k in range(blocks // 2):
                to = jnp.bitwise_xor(me_ref[0], 2 * k + core)
                at = pl.multiple_of((to * chunks + chunk) * LANES, LANES)
                copies.append(
                    pltpu.make_async_copy(
                        teacher_ref.at[:, pl.ds(at, LANES)],
                        sends[2 * chunk + core].at[k, pl.ds(0, rows)],
                        sems.at[(2 * chunk + core) * (blocks // 2) + k],
                    )
                )
    for copy in copies:
        copy.start()
    copies[0].wait()
    for core in range(2):
        for k in range(blocks // 2):
            to = jnp.bitwise_xor(me_ref[0], 2 * k + core)
            lanes = pl.ds(pl.multiple_of(to * LANES, LANES), LANES)
            top, bottom = student[:half, lanes], student[half:, lanes]
            for chunk in range(chunks):
                part = slice(chunk * (LANES // 2), (chunk + 1) * (LANES // 2))
                sends[2 * chunk + core][k, rows:, :] = jnp.concatenate(
                    [top[:, part], bottom[:, part]], axis=1
                )
    for copy in copies[1:]:
        copy.wait()


def pack_plain_kernel(blocks, me_ref, teacher_ref, student_ref, *sends):
    teacher_width = teacher_ref.shape[1] // blocks
    student_width = student_ref.shape[1] // blocks
    for core in range(2):
        for k in range(blocks // 2):
            to = jnp.bitwise_xor(me_ref[0], 2 * k + core)

            def put_teacher(columns, send=sends[core], k=k):
                send[k, :, :teacher_width] = teacher_ref[:, columns]

            def put_student(columns, send=sends[core], k=k):
                send[k, :, teacher_width:] = student_ref[:, columns]

            at_columns(to, blocks, teacher_width, put_teacher)
            at_columns(to, blocks, student_width, put_student)


def pair_sum(parts):
    while len(parts) > 1:
        parts = [a + b for a, b in zip(parts[::2], parts[1::2])]
    return parts[0]


def merge_kernel(kept_ref, swapped_ref, *sends):
    for k, send in enumerate(sends, 1):
        send[0] = kept_ref[k]
        send[1] = swapped_ref[k]


def arrived(refs):
    return [refs[0].at[0], refs[1].at[0]] + [ref.at[core] for ref in refs[2:] for core in range(2)]


def unpack_kernel(me_ref, *refs):
    grad_ref = refs[-1]
    blocks = arrived(refs[:-1])
    for k, block in enumerate(blocks):

        def put(columns, block=block):
            grad_ref[:, columns] = block[: grad_ref.shape[0], :].astype(jnp.float32)

        at_columns(jnp.bitwise_xor(me_ref[0], k), len(blocks), block.shape[1], put)


def packed_start(me, counts_ref, blocks, k):
    owner = jnp.bitwise_xor(me, k)
    start = sum(jnp.where(b < owner, counts_ref[b], 0) for b in range(blocks))
    base = pl.multiple_of(start // PAD * PAD, PAD)
    return base, start - base, counts_ref[owner]


def place_kernel(me_ref, counts_ref, place_ref, place_t_ref):
    blocks, window, rows = place_ref.shape
    position = lax.broadcasted_iota(jnp.int32, (window, rows), 0)
    token = lax.broadcasted_iota(jnp.int32, (window, rows), 1)
    position_t = lax.broadcasted_iota(jnp.int32, (rows, window), 1)
    token_t = lax.broadcasted_iota(jnp.int32, (rows, window), 0)
    for k in range(blocks):
        _, shift, count = packed_start(me_ref[0], counts_ref, blocks, k)
        place = (position == token + shift) & (token < count)
        place_ref[k] = place.astype(jnp.bfloat16)
        place = (position_t == token_t + shift) & (token_t < count)
        place_t_ref[k] = place.astype(jnp.bfloat16)


def fold(values):
    rows, columns = values.shape
    return jnp.sum(values.reshape(rows // 8, 8, columns), axis=0)


def relation_kernel(folded, heads, tiles, n_in, n_done, last, me_ref, counts_ref, place_ref, *refs):
    if last:
        place_t_ref, *refs = refs
    sources = arrived(refs[:n_in])
    done = refs[n_in : n_in + 3 * n_done]
    rest = list(refs[n_in + 3 * n_done :])
    out, rest = rest[:3], rest[3:]
    pack, key_op, row_op, student_col, student_pad, teacher_prob, student_prob, weights_ref = rest[:8]
    if last:
        row_grad, key_grad, kl_sum, grad_rows = rest[8:]
    else:
        row_grad, key_grad, kl_sum = out
    f32, bf16 = jnp.float32, jnp.bfloat16
    blocks = len(sources)
    rows = teacher_prob.shape[2]
    half = rows // 2
    live = tiles * rows
    window = rows + PAD
    student_at = heads * TEACHER_DIM
    student_width = heads * STUDENT_DIM
    filled = 2 * TEACHER_DIM + 2 * STUDENT_DIM

    pack[...] = jnp.zeros(pack.shape, f32)
    for k, source in enumerate(sources):
        base, _, _ = packed_start(me_ref[0], counts_ref, blocks, k)
        here = pl.ds(base, window)
        place = place_ref[k]
        if folded:
            moved = jnp.dot(place, source[:rows, :], preferred_element_type=f32)
            pack[here, :student_at] = pack[here, :student_at] + moved
            student = source[rows:, :]
            moved = jnp.dot(
                place[:, :half], student[:, :student_width], preferred_element_type=f32
            ) + jnp.dot(place[:, half:], student[:, student_width:], preferred_element_type=f32)
            pack[here, student_at:] = pack[here, student_at:] + moved
        else:
            moved = jnp.dot(place, source[...], preferred_element_type=f32)
            pack[here, :] = pack[here, :] + moved

    ones = jnp.ones((rows, DEPTH - filled), bf16)
    spare = lax.broadcasted_iota(jnp.int32, (DEPTH - filled, rows), 0)
    teacher_gap = jnp.zeros((2 * STUDENT_DIM, rows), bf16)
    student_gap = jnp.zeros((2 * TEACHER_DIM, rows), bf16)
    lane_head = lax.broadcasted_iota(jnp.int32, (rows, student_width), 1) // STUDENT_DIM
    norms = []

    def shift_rows(norm):
        parts = [part.astype(f32) for part in split_three(-norm)]
        out = jnp.where(spare == 0, parts[0], 0.0)
        out = jnp.where(spare == 1, parts[1], out)
        return jnp.where(spare == 2, parts[2], out).astype(bf16)

    for i in range(tiles):
        here = pl.ds(i * rows, rows)
        tile = pack[here, :]
        tile_t = tile.T
        tile_b = tile.astype(bf16)
        tile_s = tile[:, student_at:]
        for h in range(heads):
            tb = tile_b[:, h * TEACHER_DIM : (h + 1) * TEACHER_DIM]
            at = student_at + h * STUDENT_DIM
            sb = tile_b[:, at : at + STUDENT_DIM]
            key_op[h, here, :] = jnp.concatenate([tb, tb, sb, sb, ones], axis=1)
            teacher_t = tile_t[h * TEACHER_DIM : (h + 1) * TEACHER_DIM, :]
            student_t = tile_t[at : at + STUDENT_DIM, :]
            student_col[h, :, here] = student_t.astype(bf16)
            student_pad[h, here, :] = jnp.where(lane_head == h, tile_s, 0.0).astype(bf16)
            teacher_norm = TEACHER_SCALE * jnp.sum(teacher_t * teacher_t, axis=0, keepdims=True)
            student_norm = STUDENT_SCALE * jnp.sum(student_t * student_t, axis=0, keepdims=True)
            norms += [teacher_norm, student_norm]
            high, low = split_high_low(teacher_t * TEACHER_SCALE)
            teacher_op = [high, low, teacher_gap, shift_rows(teacher_norm)]
            row_op[h, i, :, :rows] = jnp.concatenate(teacher_op, axis=0)
            high, low = split_high_low(student_t * STUDENT_SCALE)
            student_op = [student_gap, high, low, shift_rows(student_norm)]
            row_op[h, i, :, rows:] = jnp.concatenate(student_op, axis=0)

    safe = jnp.max(functools.reduce(jnp.maximum, norms)) <= SAFE_NORM
    key_pos = lax.broadcasted_iota(jnp.int32, (rows, rows), 0)
    row_pos = lax.broadcasted_iota(jnp.int32, (rows, rows), 1)

    def logits(h, i, j):
        keys = pl.ds(pl.multiple_of(j * rows, rows), rows)
        both = jnp.dot(key_op[h, keys, :], row_op[h, i], preferred_element_type=f32)
        return both[:, :rows], both[:, rows:]

    @pl.when(safe)
    def shifted_by_own_logit():
        key_grad[...] = jnp.zeros(key_grad.shape, f32)

        def exponentials(h, i, model, prob):
            upto = (i + 1) * rows
            op = row_op[h, i, :, model * rows : (model + 1) * rows]
            values = jnp.dot(key_op[h, :upto, :], op, preferred_element_type=f32)
            diagonal = jnp.where(key_pos <= row_pos, values[i * rows :], NEGATIVE)
            total = cross = jnp.zeros((8, rows), f32)
            for j in range(i + 1):
                value = diagonal if j == i else values[j * rows : (j + 1) * rows]
                exp = jnp.exp2(value)
                prob[i % 2, j] = exp
                total = total + fold(exp)
                weight = teacher_prob[i % 2, j] if model else exp
                cross = cross + fold(weight * value)
            return [jnp.sum(part, axis=0, keepdims=True) for part in (total, cross)]

        def weights(i, j, teacher_inv, student_inv):
            value = student_prob[i % 2, j] * student_inv - teacher_prob[i % 2, j] * teacher_inv
            weights_ref[j * rows : (j + 1) * rows, i * rows : (i + 1) * rows] = value.astype(bf16)

        def head_step(h, kl_total):
            inverse = None
            for i in range(tiles + 1):
                if i < tiles:
                    teacher_sum, teacher_cross = exponentials(h, i, 0, teacher_prob)
                    student_sum, student_cross = exponentials(h, i, 1, student_prob)
                if i:
                    upto = i * rows
                    for j in range(i):
                        weights(i - 1, j, *inverse)
                    row_grad[h, :, upto - rows : upto] = jnp.dot(
                        student_col[h, :, :upto],
                        weights_ref[:upto, upto - rows : upto],
                        preferred_element_type=f32,
                    )
                if i < tiles:
                    inverse = (1.0 / teacher_sum, 1.0 / student_sum)
                    kl_total = kl_total + (
                        (teacher_cross - student_cross) * inverse[0]
                        - jnp.log2(teacher_sum)
                        + jnp.log2(student_sum)
                    )
            for j in range(tiles):
                here = slice(j * rows, (j + 1) * rows)
                key_grad[here, :] = key_grad[here, :] + jnp.dot(
                    weights_ref[here, j * rows :],
                    student_pad[h, j * rows :, :],
                    preferred_element_type=f32,
                )
            return kl_total

        kl_sum[...] = lax.fori_loop(0, heads, head_step, jnp.zeros((1, rows), f32))

    @pl.when(jnp.logical_not(safe))
    def shifted_by_maximum():
        kl_sum[...] = jnp.zeros((1, rows), f32)
        key_grad[...] = jnp.zeros(key_grad.shape, f32)

        def masked(h, i, j):
            allowed = key_pos + j * rows <= row_pos + i * rows
            teacher, student = logits(h, i, j)
            return jnp.where(allowed, teacher, NEGATIVE), jnp.where(allowed, student, NEGATIVE)

        def row_step(step, _):
            h, i = step // tiles, step % tiles
            here = pl.ds(pl.multiple_of(i * rows, rows), rows)

            def advance(j, state):
                teacher_max, teacher_sum, cross_sum, student_max, student_sum = state
                teacher, student = masked(h, i, j)
                teacher_top = jnp.maximum(teacher_max, jnp.max(teacher, axis=0, keepdims=True))
                student_top = jnp.maximum(student_max, jnp.max(student, axis=0, keepdims=True))
                teacher_exp = jnp.exp2(teacher - teacher_top)
                student_exp = jnp.exp2(student - student_top)
                shrink = jnp.exp2(teacher_max - teacher_top)
                cross = jnp.sum(teacher_exp * (teacher - student), axis=0, keepdims=True)
                return (
                    teacher_top,
                    teacher_sum * shrink + jnp.sum(teacher_exp, axis=0, keepdims=True),
                    cross_sum * shrink + cross,
                    student_top,
                    student_sum * jnp.exp2(student_max - student_top)
                    + jnp.sum(student_exp, axis=0, keepdims=True),
                )

            lowest = jnp.full((1, rows), NEGATIVE, f32)
            zeros = jnp.zeros((1, rows), f32)
            teacher_max, teacher_sum, cross_sum, student_max, student_sum = lax.fori_loop(
                0, i + 1, advance, (lowest, zeros, zeros, lowest, zeros)
            )
            teacher_lse = teacher_max + jnp.log2(teacher_sum)
            student_lse = student_max + jnp.log2(student_sum)
            kl_sum[...] = kl_sum[...] + (cross_sum / teacher_sum - teacher_lse + student_lse)

            def spread(j, total):
                teacher, student = masked(h, i, j)
                value = jnp.exp2(student - student_lse) - jnp.exp2(teacher - teacher_lse)
                value = value.astype(bf16)
                keys = pl.ds(pl.multiple_of(j * rows, rows), rows)
                key_grad[keys, :] = key_grad[keys, :] + jnp.dot(
                    value, student_pad[h, here, :], preferred_element_type=f32
                )
                return total + jnp.dot(
                    student_col[h, :, keys], value, preferred_element_type=f32
                )

            row_grad[h, :, here] = lax.fori_loop(
                0, i + 1, spread, jnp.zeros((STUDENT_DIM, rows), f32)
            )
            return 0

        lax.fori_loop(0, heads * tiles, row_step, 0)

    if not last:
        return

    row_parts = [*done[::3], row_grad]
    key_parts = [*done[1::3], key_grad]
    total_width = len(row_parts) * student_width
    for i in range(tiles):
        here = slice(i * rows, (i + 1) * rows)
        columns = jnp.concatenate(
            [part[h, :, here] for part in row_parts for h in range(heads)], axis=0
        )
        lanes = jnp.concatenate([part[here, :] for part in key_parts], axis=1)
        grad_rows[here, :] = (columns.T + lanes) * (STUDENT_DIM**-0.5)
    grad_rows[pl.ds(live, window), :] = jnp.zeros((window, total_width), f32)
    kl_total = sum([ref[...] for ref in done[2::3]] + [kl_sum[...]])
    tokens = sum(counts_ref[b] for b in range(blocks))
    share = jnp.full((1, rows), math.log(2.0), f32) / (H_REL * tokens).astype(f32)
    kl_total = jnp.sum(kl_total * share, axis=1, keepdims=True)
    out[2][...] = jnp.broadcast_to(kl_total, out[2].shape)
    for k in range(blocks):
        base, _, _ = packed_start(me_ref[0], counts_ref, blocks, k)
        block = grad_rows[pl.ds(base, window), :].astype(bf16)
        out[k % 2][k // 2] = jnp.dot(
            place_t_ref[k], block, preferred_element_type=f32
        ).astype(bf16)


def local(teacher_queries, student_queries, token_counts):
    f32, bf16 = jnp.float32, jnp.bfloat16
    blocks = lax.axis_size("seq")
    chips = blocks // 2
    groups = lax.axis_size("head")
    rows = teacher_queries.shape[0]
    heads = teacher_queries.shape[1] // TEACHER_DIM // blocks
    tiles = blocks * 3 // 4
    live = tiles * rows
    folded = heads * STUDENT_DIM == LANES
    chunks = 2 if folded else 1
    chunk_heads = heads // chunks
    teacher_width = chunk_heads * TEACHER_DIM
    student_width = chunk_heads * STUDENT_DIM
    if folded:
        send_shape = (chips, rows + rows // 2, LANES)
    else:
        send_shape = (chips, rows, teacher_width + student_width)
    vmem = pl.BlockSpec(memory_space=pltpu.VMEM)
    smem = pl.BlockSpec(memory_space=pltpu.SMEM)
    params = pltpu.CompilerParams(vmem_limit_bytes=40 * 1024 * 1024)
    me = lax.axis_index("seq").reshape(1)

    def exchange(kept, swapped):
        swapped = lax.ppermute(swapped, "seq", [(i, i ^ 1) for i in range(blocks)])
        sends = pl.pallas_call(
            merge_kernel,
            in_specs=[vmem] * 2,
            out_specs=[vmem] * (chips - 1),
            out_shape=[jax.ShapeDtypeStruct((2,) + kept.shape[1:], bf16)] * (chips - 1),
            compiler_params=params,
            name="merge",
        )(kept, swapped)
        return [kept, swapped] + [
            lax.ppermute(send, "seq", [(i, i ^ (2 * k)) for i in range(blocks)])
            for k, send in enumerate(sends, 1)
        ]

    packed = jax.ShapeDtypeStruct(send_shape, bf16)
    if folded:
        anywhere = pl.BlockSpec(memory_space=pltpu.HBM)
        sends = pl.pallas_call(
            functools.partial(pack_folded_kernel, blocks, chunks),
            in_specs=[smem, anywhere, anywhere],
            out_specs=[vmem] * (2 * chunks),
            out_shape=[packed] * (2 * chunks),
            scratch_shapes=[
                pltpu.VMEM(student_queries.shape, bf16),
                pltpu.SemaphoreType.DMA((chunks * blocks + 1,)),
            ],
            compiler_params=pltpu.CompilerParams(vmem_limit_bytes=52 * 1024 * 1024),
            name="pack",
        )(me, teacher_queries, student_queries)
    else:
        sends = pl.pallas_call(
            functools.partial(pack_plain_kernel, blocks),
            in_specs=[smem, vmem, vmem],
            out_specs=[vmem] * 2,
            out_shape=[packed] * 2,
            compiler_params=params,
            name="pack",
        )(me, teacher_queries, student_queries)
    incoming = [exchange(*sends[2 * c : 2 * c + 2]) for c in range(chunks)]

    window = rows + PAD
    place, place_t = pl.pallas_call(
        place_kernel,
        in_specs=[smem] * 2,
        out_specs=[vmem] * 2,
        out_shape=[
            jax.ShapeDtypeStruct((blocks, window, rows), bf16),
            jax.ShapeDtypeStruct((blocks, rows, window), bf16),
        ],
        compiler_params=params,
        name="place",
    )(me, token_counts)
    result = [
        jax.ShapeDtypeStruct((chunk_heads, STUDENT_DIM, live), f32),
        jax.ShapeDtypeStruct((live, student_width), f32),
        jax.ShapeDtypeStruct((1, rows), f32),
    ]
    message = jax.ShapeDtypeStruct((chips, rows, heads * STUDENT_DIM), bf16)
    divergence = jax.ShapeDtypeStruct((8, LANES), f32)
    pairs = chunk_heads * tiles * (tiles + 1) // 2 * rows * rows
    done = []
    for c in range(chunks):
        last = c == chunks - 1
        scratch = [
            pltpu.VMEM((live + rows + PAD, teacher_width + student_width), f32),
            pltpu.VMEM((chunk_heads, live, DEPTH), bf16),
            pltpu.VMEM((chunk_heads, tiles, DEPTH, 2 * rows), bf16),
            pltpu.VMEM((chunk_heads, STUDENT_DIM, live), bf16),
            pltpu.VMEM((chunk_heads, live, student_width), bf16),
            pltpu.VMEM((2, tiles, rows, rows), f32),
            pltpu.VMEM((2, tiles, rows, rows), f32),
            pltpu.VMEM((live, live), bf16),
        ]
        if last:
            scratch += [pltpu.VMEM(part.shape, f32) for part in result]
            scratch.append(pltpu.VMEM((live + rows + PAD, heads * STUDENT_DIM), f32))
        inputs = [me, token_counts, place, *([place_t] if last else []), *incoming[c], *done]
        done += pl.pallas_call(
            functools.partial(
                relation_kernel, folded, chunk_heads, tiles, len(incoming[c]), c, last
            ),
            in_specs=[smem, smem] + [vmem] * (len(inputs) - 2),
            out_specs=[vmem] * 3,
            out_shape=[message, message, divergence] if last else result,
            scratch_shapes=scratch,
            compiler_params=params,
            cost_estimate=pl.CostEstimate(
                flops=4 * pairs * DEPTH, bytes_accessed=8 * pairs, transcendentals=2 * pairs
            ),
            name="relation",
        )(*inputs)
    kept, swapped, kl = done[-3:]
    loss = jnp.sum(lax.all_gather(kl, ("seq", "head")), axis=0)
    returned = exchange(kept, swapped)
    grad = pl.pallas_call(
        unpack_kernel,
        in_specs=[smem] + [vmem] * len(returned),
        out_specs=vmem,
        out_shape=jax.ShapeDtypeStruct((rows, student_queries.shape[1]), f32),
        compiler_params=params,
        name="unpack",
    )(me, *returned)
    return (grad, loss[0, 0])


def solution(mesh):
    return jax.shard_map(
        local,
        mesh=mesh,
        in_specs=(P("seq", "head"), P("seq", "head"), P()),
        out_specs=(P("seq", "head"), P()),
        check_vma=False,
    )
```

```python
import functools
import math

import jax
import jax.numpy as jnp
from jax import lax
from jax.experimental import pallas as pl
from jax.experimental.pallas import tpu as pltpu
from jax.sharding import PartitionSpec as P

DT = 8192
DS = 4096
H_REL = 128
TEACHER_DIM = DT // H_REL
STUDENT_DIM = DS // H_REL

NEGATIVE = -1e30
LOG2E = math.log2(math.e)
TEACHER_SCALE = LOG2E * TEACHER_DIM**-0.5
STUDENT_SCALE = LOG2E * STUDENT_DIM**-0.5
PAD = 8
LANES = 128
TAIL = 16
DEPTH = 256
SAFE_NORM = 320.0


def split_high_low(values):
    high = values.astype(jnp.bfloat16)
    low = (values - high.astype(jnp.float32)).astype(jnp.bfloat16)
    return high, low


def split_three(values):
    high = values.astype(jnp.bfloat16)
    rest = values - high.astype(jnp.float32)
    return (high,) + split_high_low(rest)


def at_columns(index, count, width, act):
    if width % LANES == 0:
        act(pl.ds(pl.multiple_of(index * width, LANES), width))
    else:
        for part in range(count):
            pl.when(index == part)(functools.partial(act, pl.ds(part * width, width)))


def pack_folded_kernel(blocks, chunks, me_ref, teacher_ref, student_ref, *refs):
    sends, student, sems = refs[:-2], refs[-2], refs[-1]
    rows = teacher_ref.shape[0]
    half = rows // 2

    def block(chunk, k):
        if chunk == 0:
            return sends[k]
        return sends[blocks + 2 * (chunk - 1) + k % 2].at[k // 2]

    copies = [pltpu.make_async_copy(student_ref, student, sems.at[chunks * blocks])]
    for chunk in range(chunks):
        for k in range(blocks):
            to = jnp.bitwise_xor(me_ref[0], k)
            at = pl.multiple_of((to * chunks + chunk) * LANES, LANES)
            copies.append(
                pltpu.make_async_copy(
                    teacher_ref.at[:, pl.ds(at, LANES)],
                    block(chunk, k).at[pl.ds(0, rows)],
                    sems.at[chunk * blocks + k],
                )
            )
    for copy in copies:
        copy.start()
    copies[0].wait()
    for k in range(blocks):
        to = jnp.bitwise_xor(me_ref[0], k)
        lanes = pl.ds(pl.multiple_of(to * LANES, LANES), LANES)
        top, bottom = student[:half, lanes], student[half:, lanes]
        for chunk in range(chunks):
            part = slice(chunk * (LANES // 2), (chunk + 1) * (LANES // 2))
            block(chunk, k)[rows:, :] = jnp.concatenate([top[:, part], bottom[:, part]], axis=1)
    for copy in copies[1:]:
        copy.wait()


def pack_plain_kernel(blocks, me_ref, teacher_ref, student_ref, *sends):
    teacher_width = teacher_ref.shape[1] // blocks
    student_width = student_ref.shape[1] // blocks
    for core in range(2):
        for k in range(blocks // 2):
            to = jnp.bitwise_xor(me_ref[0], 2 * k + core)

            def put_teacher(columns, send=sends[core], k=k):
                send[k, :, :teacher_width] = teacher_ref[:, columns]

            def put_student(columns, send=sends[core], k=k):
                send[k, :, teacher_width:] = student_ref[:, columns]

            at_columns(to, blocks, teacher_width, put_teacher)
            at_columns(to, blocks, student_width, put_student)


def pair_sum(parts):
    while len(parts) > 1:
        parts = [a + b for a, b in zip(parts[::2], parts[1::2])]
    return parts[0]


def tail_rows(value, width):
    thirds = [part.astype(jnp.float32) for part in split_three(value)]
    line = lax.broadcasted_iota(jnp.int32, (TAIL, width), 0)
    tail = jnp.where(line == 0, thirds[0], 0.0)
    tail = jnp.where(line == 1, thirds[1], tail)
    return jnp.where(line == 2, thirds[2], tail).astype(jnp.bfloat16)


def merge_kernel(chips, kept_ref, swapped_ref, *refs):
    kls, sends = refs[: 1 - chips], refs[1 - chips :]
    rows = kept_ref.shape[1]
    tail = tail_rows(pair_sum([kl[...] for kl in kls]), kept_ref.shape[2]) if kls else None
    for k, send in enumerate(sends):
        send[0, :rows, :] = kept_ref[k + 1]
        send[1, :rows, :] = swapped_ref[k + 1]
        if kls:
            send[0, rows:, :] = tail
            send[1, rows:, :] = tail


def arrived(refs):
    return [refs[0].at[0], refs[1].at[0]] + [ref.at[core] for ref in refs[2:] for core in range(2)]


def sum_kernel(groups, counts_ref, *refs):
    out_ref = refs[-1]
    own = pair_sum([ref[...] for ref in refs[:groups]])
    tails = [ref[0, ref.shape[1] - TAIL :, :].astype(jnp.float32) for ref in refs[groups:-1]]
    total = pair_sum(
        [jnp.broadcast_to(own, out_ref.shape)] + [jnp.sum(t, axis=0, keepdims=True) for t in tails]
    )
    tokens = sum(counts_ref[b] for b in range(counts_ref.shape[0]))
    out_ref[...] = total / (H_REL * tokens).astype(jnp.float32)


def unpack_kernel(me_ref, *refs):
    grad_ref = refs[-1]
    blocks = arrived(refs[:-1])
    for k, block in enumerate(blocks):

        def put(columns, block=block):
            grad_ref[:, columns] = block[: grad_ref.shape[0], :].astype(jnp.float32)

        at_columns(jnp.bitwise_xor(me_ref[0], k), len(blocks), block.shape[1], put)


def fold(values):
    rows, columns = values.shape
    return jnp.sum(values.reshape(rows // 8, 8, columns), axis=0)


def relation_kernel(folded, heads, tiles, order, n_in, n_done, last, me_ref, counts_ref, *refs):
    if order:
        sources = [refs[order.index(k)] for k in range(n_in)]
    else:
        sources = arrived(refs[:n_in])
    done = refs[n_in : n_in + 3 * n_done]
    rest = list(refs[n_in + 3 * n_done :])
    out, rest = rest[:3], rest[3:]
    pack, key_op, row_op, student_col, student_pad, teacher_prob, student_prob, weights_ref = rest[:8]
    if last:
        row_grad, key_grad, kl_sum, grad_rows = rest[8:]
    else:
        row_grad, key_grad, kl_sum = out
    f32, bf16 = jnp.float32, jnp.bfloat16
    blocks = len(sources)
    rows = teacher_prob.shape[2]
    half = rows // 2
    live = tiles * rows
    window = rows + PAD
    student_at = heads * TEACHER_DIM
    student_width = heads * STUDENT_DIM
    filled = 2 * TEACHER_DIM + 2 * STUDENT_DIM

    position = lax.broadcasted_iota(jnp.int32, (window, rows), 0)
    token = lax.broadcasted_iota(jnp.int32, (window, rows), 1)
    pack[...] = jnp.zeros(pack.shape, f32)
    places = []
    for k in range(blocks):
        owner = jnp.bitwise_xor(me_ref[0], k)
        start = sum(jnp.where(b < owner, counts_ref[b], 0) for b in range(blocks))
        base = pl.multiple_of(start // PAD * PAD, PAD)
        places.append((base, start - base, counts_ref[owner]))
    for source, (base, shift, count) in zip(sources, places):
        place = ((position == token + shift) & (token < count)).astype(bf16)
        here = pl.ds(base, window)
        if folded:
            moved = jnp.dot(place, source[:rows, :], preferred_element_type=f32)
            pack[here, :student_at] = pack[here, :student_at] + moved
            student = source[rows:, :]
            moved = jnp.dot(
                place[:, :half], student[:, :student_width], preferred_element_type=f32
            ) + jnp.dot(place[:, half:], student[:, student_width:], preferred_element_type=f32)
            pack[here, student_at:] = pack[here, student_at:] + moved
        else:
            moved = jnp.dot(place, source[...], preferred_element_type=f32)
            pack[here, :] = pack[here, :] + moved

    ones = jnp.ones((rows, DEPTH - filled), bf16)
    spare = lax.broadcasted_iota(jnp.int32, (DEPTH - filled, rows), 0)
    teacher_gap = jnp.zeros((2 * STUDENT_DIM, rows), bf16)
    student_gap = jnp.zeros((2 * TEACHER_DIM, rows), bf16)
    lane_head = lax.broadcasted_iota(jnp.int32, (rows, student_width), 1) // STUDENT_DIM
    norms = []

    def shift_rows(norm):
        parts = [part.astype(f32) for part in split_three(-norm)]
        out = jnp.where(spare == 0, parts[0], 0.0)
        out = jnp.where(spare == 1, parts[1], out)
        return jnp.where(spare == 2, parts[2], out).astype(bf16)

    for i in range(tiles):
        here = pl.ds(i * rows, rows)
        tile = pack[here, :]
        tile_t = tile.T
        tile_b = tile.astype(bf16)
        tile_s = tile[:, student_at:]
        for h in range(heads):
            tb = tile_b[:, h * TEACHER_DIM : (h + 1) * TEACHER_DIM]
            at = student_at + h * STUDENT_DIM
            sb = tile_b[:, at : at + STUDENT_DIM]
            key_op[h, here, :] = jnp.concatenate([tb, tb, sb, sb, ones], axis=1)
            teacher_t = tile_t[h * TEACHER_DIM : (h + 1) * TEACHER_DIM, :]
            student_t = tile_t[at : at + STUDENT_DIM, :]
            student_col[h, :, here] = student_t.astype(bf16)
            student_pad[h, here, :] = jnp.where(lane_head == h, tile_s, 0.0).astype(bf16)
            teacher_norm = TEACHER_SCALE * jnp.sum(teacher_t * teacher_t, axis=0, keepdims=True)
            student_norm = STUDENT_SCALE * jnp.sum(student_t * student_t, axis=0, keepdims=True)
            norms += [teacher_norm, student_norm]
            high, low = split_high_low(teacher_t * TEACHER_SCALE)
            teacher_op = [high, low, teacher_gap, shift_rows(teacher_norm)]
            row_op[h, i, :, :rows] = jnp.concatenate(teacher_op, axis=0)
            high, low = split_high_low(student_t * STUDENT_SCALE)
            student_op = [student_gap, high, low, shift_rows(student_norm)]
            row_op[h, i, :, rows:] = jnp.concatenate(student_op, axis=0)

    safe = jnp.max(functools.reduce(jnp.maximum, norms)) <= SAFE_NORM
    key_pos = lax.broadcasted_iota(jnp.int32, (rows, rows), 0)
    row_pos = lax.broadcasted_iota(jnp.int32, (rows, rows), 1)

    def logits(h, i, j):
        keys = pl.ds(pl.multiple_of(j * rows, rows), rows)
        both = jnp.dot(key_op[h, keys, :], row_op[h, i], preferred_element_type=f32)
        return both[:, :rows], both[:, rows:]

    @pl.when(safe)
    def shifted_by_own_logit():
        key_grad[...] = jnp.zeros(key_grad.shape, f32)

        def exponentials(h, i, model, prob):
            upto = (i + 1) * rows
            op = row_op[h, i, :, model * rows : (model + 1) * rows]
            values = jnp.dot(key_op[h, :upto, :], op, preferred_element_type=f32)
            diagonal = jnp.where(key_pos <= row_pos, values[i * rows :], NEGATIVE)
            total = cross = jnp.zeros((8, rows), f32)
            for j in range(i + 1):
                value = diagonal if j == i else values[j * rows : (j + 1) * rows]
                exp = jnp.exp2(value)
                prob[i % 2, j] = exp
                total = total + fold(exp)
                weight = teacher_prob[i % 2, j] if model else exp
                cross = cross + fold(weight * value)
            return [jnp.sum(part, axis=0, keepdims=True) for part in (total, cross)]

        def weights(i, j, teacher_inv, student_inv):
            value = student_prob[i % 2, j] * student_inv - teacher_prob[i % 2, j] * teacher_inv
            weights_ref[j * rows : (j + 1) * rows, i * rows : (i + 1) * rows] = value.astype(bf16)

        def head_step(h, kl_total):
            inverse = None
            for i in range(tiles + 1):
                if i < tiles:
                    teacher_sum, teacher_cross = exponentials(h, i, 0, teacher_prob)
                    student_sum, student_cross = exponentials(h, i, 1, student_prob)
                if i:
                    upto = i * rows
                    for j in range(i):
                        weights(i - 1, j, *inverse)
                    row_grad[h, :, upto - rows : upto] = jnp.dot(
                        student_col[h, :, :upto],
                        weights_ref[:upto, upto - rows : upto],
                        preferred_element_type=f32,
                    )
                if i < tiles:
                    inverse = (1.0 / teacher_sum, 1.0 / student_sum)
                    kl_total = kl_total + (
                        (teacher_cross - student_cross) * inverse[0]
                        - jnp.log2(teacher_sum)
                        + jnp.log2(student_sum)
                    )
            for j in range(tiles):
                here = slice(j * rows, (j + 1) * rows)
                key_grad[here, :] = key_grad[here, :] + jnp.dot(
                    weights_ref[here, j * rows :],
                    student_pad[h, j * rows :, :],
                    preferred_element_type=f32,
                )
            return kl_total

        kl_sum[...] = lax.fori_loop(0, heads, head_step, jnp.zeros((1, rows), f32))

    @pl.when(jnp.logical_not(safe))
    def shifted_by_maximum():
        kl_sum[...] = jnp.zeros((1, rows), f32)
        key_grad[...] = jnp.zeros(key_grad.shape, f32)

        def masked(h, i, j):
            allowed = key_pos + j * rows <= row_pos + i * rows
            teacher, student = logits(h, i, j)
            return jnp.where(allowed, teacher, NEGATIVE), jnp.where(allowed, student, NEGATIVE)

        def row_step(step, _):
            h, i = step // tiles, step % tiles
            here = pl.ds(pl.multiple_of(i * rows, rows), rows)

            def advance(j, state):
                teacher_max, teacher_sum, cross_sum, student_max, student_sum = state
                teacher, student = masked(h, i, j)
                teacher_top = jnp.maximum(teacher_max, jnp.max(teacher, axis=0, keepdims=True))
                student_top = jnp.maximum(student_max, jnp.max(student, axis=0, keepdims=True))
                teacher_exp = jnp.exp2(teacher - teacher_top)
                student_exp = jnp.exp2(student - student_top)
                shrink = jnp.exp2(teacher_max - teacher_top)
                cross = jnp.sum(teacher_exp * (teacher - student), axis=0, keepdims=True)
                return (
                    teacher_top,
                    teacher_sum * shrink + jnp.sum(teacher_exp, axis=0, keepdims=True),
                    cross_sum * shrink + cross,
                    student_top,
                    student_sum * jnp.exp2(student_max - student_top)
                    + jnp.sum(student_exp, axis=0, keepdims=True),
                )

            lowest = jnp.full((1, rows), NEGATIVE, f32)
            zeros = jnp.zeros((1, rows), f32)
            teacher_max, teacher_sum, cross_sum, student_max, student_sum = lax.fori_loop(
                0, i + 1, advance, (lowest, zeros, zeros, lowest, zeros)
            )
            teacher_lse = teacher_max + jnp.log2(teacher_sum)
            student_lse = student_max + jnp.log2(student_sum)
            kl_sum[...] = kl_sum[...] + (cross_sum / teacher_sum - teacher_lse + student_lse)

            def spread(j, total):
                teacher, student = masked(h, i, j)
                value = jnp.exp2(student - student_lse) - jnp.exp2(teacher - teacher_lse)
                value = value.astype(bf16)
                keys = pl.ds(pl.multiple_of(j * rows, rows), rows)
                key_grad[keys, :] = key_grad[keys, :] + jnp.dot(
                    value, student_pad[h, here, :], preferred_element_type=f32
                )
                return total + jnp.dot(
                    student_col[h, :, keys], value, preferred_element_type=f32
                )

            row_grad[h, :, here] = lax.fori_loop(
                0, i + 1, spread, jnp.zeros((STUDENT_DIM, rows), f32)
            )
            return 0

        lax.fori_loop(0, heads * tiles, row_step, 0)

    if not last:
        return

    row_parts = [*done[::3], row_grad]
    key_parts = [*done[1::3], key_grad]
    total_width = len(row_parts) * student_width
    for i in range(tiles):
        here = slice(i * rows, (i + 1) * rows)
        columns = jnp.concatenate(
            [part[h, :, here] for part in row_parts for h in range(heads)], axis=0
        )
        lanes = jnp.concatenate([part[here, :] for part in key_parts], axis=1)
        grad_rows[here, :] = (columns.T + lanes) * (STUDENT_DIM**-0.5)
    grad_rows[pl.ds(live, window), :] = jnp.zeros((window, total_width), f32)
    kl_total = sum([ref[...] for ref in done[2::3]] + [kl_sum[...]])
    out[2][...] = jnp.broadcast_to(
        jnp.sum(kl_total, axis=1, keepdims=True) * math.log(2.0), out[2].shape
    )
    position = lax.broadcasted_iota(jnp.int32, (rows, window), 1)
    token = lax.broadcasted_iota(jnp.int32, (rows, window), 0)
    for k, (base, shift, count) in enumerate(places):
        place = ((position == token + shift) & (token < count)).astype(bf16)
        block = grad_rows[pl.ds(base, window), :].astype(bf16)
        out[k % 2][k // 2] = jnp.dot(place, block, preferred_element_type=f32).astype(bf16)


def local(teacher_queries, student_queries, token_counts):
    f32, bf16 = jnp.float32, jnp.bfloat16
    blocks = lax.axis_size("seq")
    chips = blocks // 2
    groups = lax.axis_size("head")
    rows = teacher_queries.shape[0]
    heads = teacher_queries.shape[1] // TEACHER_DIM // blocks
    tiles = blocks * 3 // 4
    live = tiles * rows
    folded = heads * STUDENT_DIM == LANES
    chunks = 2 if folded else 1
    chunk_heads = heads // chunks
    teacher_width = chunk_heads * TEACHER_DIM
    student_width = chunk_heads * STUDENT_DIM
    if folded:
        send_shape = (chips, rows + rows // 2, LANES)
    else:
        send_shape = (chips, rows, teacher_width + student_width)
    vmem = pl.BlockSpec(memory_space=pltpu.VMEM)
    smem = pl.BlockSpec(memory_space=pltpu.SMEM)
    params = pltpu.CompilerParams(vmem_limit_bytes=40 * 1024 * 1024)
    me = lax.axis_index("seq").reshape(1)
    far_first = sorted(range(1, chips), key=lambda k: -k.bit_count())

    def exchange(kept, swapped, kls=()):
        swapped = lax.ppermute(swapped, "seq", [(i, i ^ 1) for i in range(blocks)])
        shape = (2, kept.shape[1] + (TAIL if kls else 0), kept.shape[2])
        sends = pl.pallas_call(
            functools.partial(merge_kernel, chips),
            in_specs=[vmem] * (2 + len(kls)),
            out_specs=[vmem] * (chips - 1),
            out_shape=[jax.ShapeDtypeStruct(shape, bf16)] * (chips - 1),
            compiler_params=params,
            name="merge",
        )(kept, swapped, *kls)
        out = [None] * (chips - 1)
        for k in far_first:
            pairs = [(i, i ^ (2 * k)) for i in range(blocks)]
            out[k - 1] = lax.ppermute(sends[k - 1], "seq", pairs)
        return [kept, swapped] + out

    packed = jax.ShapeDtypeStruct(send_shape, bf16)
    first = jax.ShapeDtypeStruct(send_shape[1:], bf16)
    order = [0, 1, *range(2, blocks, 2), *range(3, blocks, 2)] if folded else None
    if folded:
        anywhere = pl.BlockSpec(memory_space=pltpu.HBM)
        sends = pl.pallas_call(
            functools.partial(pack_folded_kernel, blocks, chunks),
            in_specs=[smem, anywhere, anywhere],
            out_specs=[vmem] * (blocks + 2 * chunks - 2),
            out_shape=[first] * blocks + [packed] * (2 * chunks - 2),
            scratch_shapes=[
                pltpu.VMEM(student_queries.shape, bf16),
                pltpu.SemaphoreType.DMA((chunks * blocks + 1,)),
            ],
            compiler_params=pltpu.CompilerParams(vmem_limit_bytes=52 * 1024 * 1024),
            name="pack",
        )(me, teacher_queries, student_queries)
    else:
        sends = pl.pallas_call(
            functools.partial(pack_plain_kernel, blocks),
            in_specs=[smem, vmem, vmem],
            out_specs=[vmem] * 2,
            out_shape=[packed] * 2,
            compiler_params=params,
            name="pack",
        )(me, teacher_queries, student_queries)
    incoming = []
    if folded:
        incoming.append(
            [sends[0]]
            + [
                lax.ppermute(sends[k], "seq", [(i, i ^ k) for i in range(blocks)])
                for k in order[1:]
            ]
        )
        sends = sends[blocks:]
    incoming += [exchange(*pair) for pair in zip(sends[::2], sends[1::2])]

    result = [
        jax.ShapeDtypeStruct((chunk_heads, STUDENT_DIM, live), f32),
        jax.ShapeDtypeStruct((live, student_width), f32),
        jax.ShapeDtypeStruct((1, rows), f32),
    ]
    message = jax.ShapeDtypeStruct((chips, rows, heads * STUDENT_DIM), bf16)
    divergence = jax.ShapeDtypeStruct((1, heads * STUDENT_DIM), f32)
    pairs = chunk_heads * tiles * (tiles + 1) // 2 * rows * rows
    done = []
    for c in range(chunks):
        last = c == chunks - 1
        scratch = [
            pltpu.VMEM((live + rows + PAD, teacher_width + student_width), f32),
            pltpu.VMEM((chunk_heads, live, DEPTH), bf16),
            pltpu.VMEM((chunk_heads, tiles, DEPTH, 2 * rows), bf16),
            pltpu.VMEM((chunk_heads, STUDENT_DIM, live), bf16),
            pltpu.VMEM((chunk_heads, live, student_width), bf16),
            pltpu.VMEM((2, tiles, rows, rows), f32),
            pltpu.VMEM((2, tiles, rows, rows), f32),
            pltpu.VMEM((live, live), bf16),
        ]
        if last:
            scratch += [pltpu.VMEM(part.shape, f32) for part in result]
            scratch.append(pltpu.VMEM((live + rows + PAD, heads * STUDENT_DIM), f32))
        inputs = [me, token_counts, *incoming[c], *done]
        done += pl.pallas_call(
            functools.partial(
                relation_kernel,
                folded,
                chunk_heads,
                tiles,
                order if c == 0 else None,
                len(incoming[c]),
                c,
                last,
            ),
            in_specs=[smem, smem] + [vmem] * (len(inputs) - 2),
            out_specs=[vmem] * 3,
            out_shape=[message, message, divergence] if last else result,
            scratch_shapes=scratch,
            compiler_params=params,
            cost_estimate=pl.CostEstimate(
                flops=4 * pairs * DEPTH, bytes_accessed=8 * pairs, transcendentals=2 * pairs
            ),
            name="relation",
        )(*inputs)
    kept, swapped, kl = done[-3:]
    kls = [kl]
    for bit in range(groups.bit_length() - 1):
        own = pair_sum(kls)
        pairs = [(i, i ^ (1 << bit)) for i in range(groups)]
        kls = [own, lax.ppermute(own, "head", pairs)]
    returned = exchange(kept, swapped, kls)
    half_loss = pl.pallas_call(
        functools.partial(sum_kernel, len(kls)),
        in_specs=[smem] + [vmem] * (len(kls) + chips - 1),
        out_specs=vmem,
        out_shape=divergence,
        compiler_params=params,
        name="sum_kl",
    )(token_counts, *kls, *returned[2:])
    loss = half_loss + lax.ppermute(half_loss, "seq", [(i, i ^ 1) for i in range(blocks)])
    grad = pl.pallas_call(
        unpack_kernel,
        in_specs=[smem] + [vmem] * len(returned),
        out_specs=vmem,
        out_shape=jax.ShapeDtypeStruct((rows, student_queries.shape[1]), f32),
        compiler_params=params,
        name="unpack",
    )(me, *returned)
    return (grad, loss[0, 0])


def solution(mesh):
    return jax.shard_map(
        local,
        mesh=mesh,
        in_specs=(P("seq", "head"), P("seq", "head"), P()),
        out_specs=(P("seq", "head"), P()),
        check_vma=False,
    )
```

```python
import functools
import math

import jax
import jax.numpy as jnp
from jax import lax
from jax.experimental import pallas as pl
from jax.experimental.pallas import tpu as pltpu
from jax.sharding import PartitionSpec as P

DT = 8192
DS = 4096
H_REL = 128
TEACHER_DIM = DT // H_REL
STUDENT_DIM = DS // H_REL

NEGATIVE = -1e30
LOG2E = math.log2(math.e)
TEACHER_SCALE = LOG2E * TEACHER_DIM**-0.5
STUDENT_SCALE = LOG2E * STUDENT_DIM**-0.5
PAD = 8
LANES = 128
TAIL = 16
DEPTH = 256
SAFE_NORM = 320.0


def split_high_low(values):
    high = values.astype(jnp.bfloat16)
    low = (values - high.astype(jnp.float32)).astype(jnp.bfloat16)
    return high, low


def split_three(values):
    high = values.astype(jnp.bfloat16)
    rest = values - high.astype(jnp.float32)
    return (high,) + split_high_low(rest)


def at_columns(index, count, width, act):
    if width % LANES == 0:
        act(pl.ds(pl.multiple_of(index * width, LANES), width))
    else:
        for part in range(count):
            pl.when(index == part)(functools.partial(act, pl.ds(part * width, width)))


def late_block(refs, k):
    return refs[k] if k < 2 else refs[k // 2 + 1].at[k % 2]


def pack_folded_kernel(blocks, chunks, me_ref, teacher_ref, student_ref, *refs):
    sends, student, sems = refs[:-2], refs[-2], refs[-1]
    late = blocks // 2 + 1
    rows = teacher_ref.shape[0]
    half = rows // 2

    def block(chunk, k):
        if chunk == 0:
            return late_block(sends, k)
        return sends[late + 2 * (chunk - 1) + k % 2].at[k // 2]

    copies = [pltpu.make_async_copy(student_ref, student, sems.at[chunks * blocks])]
    for chunk in range(chunks):
        for k in range(blocks):
            to = jnp.bitwise_xor(me_ref[0], k)
            at = pl.multiple_of((to * chunks + chunk) * LANES, LANES)
            copies.append(
                pltpu.make_async_copy(
                    teacher_ref.at[:, pl.ds(at, LANES)],
                    block(chunk, k).at[pl.ds(0, rows)],
                    sems.at[chunk * blocks + k],
                )
            )
    for copy in copies:
        copy.start()
    copies[0].wait()
    for k in range(blocks):
        to = jnp.bitwise_xor(me_ref[0], k)
        lanes = pl.ds(pl.multiple_of(to * LANES, LANES), LANES)
        top, bottom = student[:half, lanes], student[half:, lanes]
        for chunk in range(chunks):
            part = slice(chunk * (LANES // 2), (chunk + 1) * (LANES // 2))
            block(chunk, k)[rows:, :] = jnp.concatenate([top[:, part], bottom[:, part]], axis=1)
    for copy in copies[1:]:
        copy.wait()


def pack_plain_kernel(blocks, me_ref, teacher_ref, student_ref, *sends):
    teacher_width = teacher_ref.shape[1] // blocks
    student_width = student_ref.shape[1] // blocks
    for k in range(blocks):
        to = jnp.bitwise_xor(me_ref[0], k)

        def put_teacher(columns, send=late_block(sends, k)):
            send[:, :teacher_width] = teacher_ref[:, columns]

        def put_student(columns, send=late_block(sends, k)):
            send[:, teacher_width:] = student_ref[:, columns]

        at_columns(to, blocks, teacher_width, put_teacher)
        at_columns(to, blocks, student_width, put_student)


def tail_rows(value, width):
    thirds = [part.astype(jnp.float32) for part in split_three(value)]
    line = lax.broadcasted_iota(jnp.int32, (TAIL, width), 0)
    tail = jnp.where(line == 0, thirds[0], 0.0)
    tail = jnp.where(line == 1, thirds[1], tail)
    return jnp.where(line == 2, thirds[2], tail).astype(jnp.bfloat16)


def pair_sum(parts):
    while len(parts) > 1:
        parts = [a + b for a, b in zip(parts[::2], parts[1::2])]
    return parts[0]


def merge_kernel(kept_ref, swapped_ref, *sends):
    for k, send in enumerate(sends, 1):
        send[0] = kept_ref[k]
        send[1] = swapped_ref[k]


def forward_kernel(chips, own_ref, other_ref, *refs):
    messages, forward_ref = refs[: chips - 1], refs[chips - 1]
    rows = forward_ref.shape[1]
    forward_ref[0] = other_ref[:rows, :]
    for k, message in enumerate(messages, 1):
        forward_ref[k] = message[1, :rows, :]
    if len(refs) > chips:
        tails = [own_ref[rows:, :]] + [message[0, rows:, :] for message in messages]
        sums = [jnp.sum(tail.astype(jnp.float32), axis=0, keepdims=True) for tail in tails]
        refs[chips][...] = pair_sum(sums)


def arrived(refs, late):
    if late:
        blocks = [refs[0], refs[1].at[0]]
        for chip, ref in enumerate(refs[2:], 1):
            blocks += [ref.at[0], refs[1].at[chip]]
        return blocks
    return [refs[0].at[0], refs[1].at[0]] + [ref.at[core] for ref in refs[2:] for core in range(2)]


def unpack_kernel(me_ref, *refs):
    grad_ref = refs[-1]
    blocks = arrived(refs[:-1], True)
    for k, block in enumerate(blocks):

        def put(columns, block=block):
            grad_ref[:, columns] = block[: grad_ref.shape[0], :].astype(jnp.float32)

        at_columns(jnp.bitwise_xor(me_ref[0], k), len(blocks), block.shape[1], put)


def fold(values):
    rows, columns = values.shape
    return jnp.sum(values.reshape(rows // 8, 8, columns), axis=0)


def relation_kernel(folded, heads, tiles, late, n_in, n_done, last, me_ref, counts_ref, *refs):
    sources = arrived(refs[:n_in], late)
    done = refs[n_in : n_in + 3 * n_done]
    rest = list(refs[n_in + 3 * n_done :])
    n_out = len(sources) // 2 + 1 if last else 3
    out, rest = rest[:n_out], rest[n_out:]
    pack, key_op, row_op, student_col, student_pad, teacher_prob, student_prob, weights_ref = rest[:8]
    if last:
        row_grad, key_grad, kl_sum, grad_rows = rest[8:]
    else:
        row_grad, key_grad, kl_sum = out
    f32, bf16 = jnp.float32, jnp.bfloat16
    blocks = len(sources)
    rows = teacher_prob.shape[2]
    half = rows // 2
    live = tiles * rows
    window = rows + PAD
    student_at = heads * TEACHER_DIM
    student_width = heads * STUDENT_DIM
    filled = 2 * TEACHER_DIM + 2 * STUDENT_DIM

    position = lax.broadcasted_iota(jnp.int32, (window, rows), 0)
    token = lax.broadcasted_iota(jnp.int32, (window, rows), 1)
    pack[...] = jnp.zeros(pack.shape, f32)
    places = []
    for k in range(blocks):
        owner = jnp.bitwise_xor(me_ref[0], k)
        start = sum(jnp.where(b < owner, counts_ref[b], 0) for b in range(blocks))
        base = pl.multiple_of(start // PAD * PAD, PAD)
        places.append((base, start - base, counts_ref[owner]))
    for source, (base, shift, count) in zip(sources, places):
        place = ((position == token + shift) & (token < count)).astype(bf16)
        here = pl.ds(base, window)
        if folded:
            moved = jnp.dot(place, source[:rows, :], preferred_element_type=f32)
            pack[here, :student_at] = pack[here, :student_at] + moved
            student = source[rows:, :]
            moved = jnp.dot(
                place[:, :half], student[:, :student_width], preferred_element_type=f32
            ) + jnp.dot(place[:, half:], student[:, student_width:], preferred_element_type=f32)
            pack[here, student_at:] = pack[here, student_at:] + moved
        else:
            moved = jnp.dot(place, source[...], preferred_element_type=f32)
            pack[here, :] = pack[here, :] + moved

    ones = jnp.ones((rows, DEPTH - filled), bf16)
    spare = lax.broadcasted_iota(jnp.int32, (DEPTH - filled, rows), 0)
    teacher_gap = jnp.zeros((2 * STUDENT_DIM, rows), bf16)
    student_gap = jnp.zeros((2 * TEACHER_DIM, rows), bf16)
    lane_head = lax.broadcasted_iota(jnp.int32, (rows, student_width), 1) // STUDENT_DIM
    norms = []

    def shift_rows(norm):
        parts = [part.astype(f32) for part in split_three(-norm)]
        out = jnp.where(spare == 0, parts[0], 0.0)
        out = jnp.where(spare == 1, parts[1], out)
        return jnp.where(spare == 2, parts[2], out).astype(bf16)

    for i in range(tiles):
        here = pl.ds(i * rows, rows)
        tile = pack[here, :]
        tile_t = tile.T
        tile_b = tile.astype(bf16)
        tile_s = tile[:, student_at:]
        for h in range(heads):
            tb = tile_b[:, h * TEACHER_DIM : (h + 1) * TEACHER_DIM]
            at = student_at + h * STUDENT_DIM
            sb = tile_b[:, at : at + STUDENT_DIM]
            key_op[h, here, :] = jnp.concatenate([tb, tb, sb, sb, ones], axis=1)
            teacher_t = tile_t[h * TEACHER_DIM : (h + 1) * TEACHER_DIM, :]
            student_t = tile_t[at : at + STUDENT_DIM, :]
            student_col[h, :, here] = student_t.astype(bf16)
            student_pad[h, here, :] = jnp.where(lane_head == h, tile_s, 0.0).astype(bf16)
            teacher_norm = TEACHER_SCALE * jnp.sum(teacher_t * teacher_t, axis=0, keepdims=True)
            student_norm = STUDENT_SCALE * jnp.sum(student_t * student_t, axis=0, keepdims=True)
            norms += [teacher_norm, student_norm]
            high, low = split_high_low(teacher_t * TEACHER_SCALE)
            teacher_op = [high, low, teacher_gap, shift_rows(teacher_norm)]
            row_op[h, i, :, :rows] = jnp.concatenate(teacher_op, axis=0)
            high, low = split_high_low(student_t * STUDENT_SCALE)
            student_op = [student_gap, high, low, shift_rows(student_norm)]
            row_op[h, i, :, rows:] = jnp.concatenate(student_op, axis=0)

    safe = jnp.max(functools.reduce(jnp.maximum, norms)) <= SAFE_NORM
    key_pos = lax.broadcasted_iota(jnp.int32, (rows, rows), 0)
    row_pos = lax.broadcasted_iota(jnp.int32, (rows, rows), 1)

    def logits(h, i, j):
        keys = pl.ds(pl.multiple_of(j * rows, rows), rows)
        both = jnp.dot(key_op[h, keys, :], row_op[h, i], preferred_element_type=f32)
        return both[:, :rows], both[:, rows:]

    @pl.when(safe)
    def shifted_by_own_logit():
        key_grad[...] = jnp.zeros(key_grad.shape, f32)

        def exponentials(h, i, model, prob):
            upto = (i + 1) * rows
            op = row_op[h, i, :, model * rows : (model + 1) * rows]
            values = jnp.dot(key_op[h, :upto, :], op, preferred_element_type=f32)
            diagonal = jnp.where(key_pos <= row_pos, values[i * rows :], NEGATIVE)
            total = cross = jnp.zeros((8, rows), f32)
            for j in range(i + 1):
                value = diagonal if j == i else values[j * rows : (j + 1) * rows]
                exp = jnp.exp2(value)
                prob[i % 2, j] = exp
                total = total + fold(exp)
                weight = teacher_prob[i % 2, j] if model else exp
                cross = cross + fold(weight * value)
            return [jnp.sum(part, axis=0, keepdims=True) for part in (total, cross)]

        def weights(i, j, teacher_inv, student_inv):
            value = student_prob[i % 2, j] * student_inv - teacher_prob[i % 2, j] * teacher_inv
            weights_ref[j * rows : (j + 1) * rows, i * rows : (i + 1) * rows] = value.astype(bf16)

        def head_step(h, kl_total):
            inverse = None
            for i in range(tiles + 1):
                if i < tiles:
                    teacher_sum, teacher_cross = exponentials(h, i, 0, teacher_prob)
                    student_sum, student_cross = exponentials(h, i, 1, student_prob)
                if i:
                    upto = i * rows
                    for j in range(i):
                        weights(i - 1, j, *inverse)
                    row_grad[h, :, upto - rows : upto] = jnp.dot(
                        student_col[h, :, :upto],
                        weights_ref[:upto, upto - rows : upto],
                        preferred_element_type=f32,
                    )
                if i < tiles:
                    inverse = (1.0 / teacher_sum, 1.0 / student_sum)
                    kl_total = kl_total + (
                        (teacher_cross - student_cross) * inverse[0]
                        - jnp.log2(teacher_sum)
                        + jnp.log2(student_sum)
                    )
            for j in range(tiles):
                here = slice(j * rows, (j + 1) * rows)
                key_grad[here, :] = key_grad[here, :] + jnp.dot(
                    weights_ref[here, j * rows :],
                    student_pad[h, j * rows :, :],
                    preferred_element_type=f32,
                )
            return kl_total

        kl_sum[...] = lax.fori_loop(0, heads, head_step, jnp.zeros((1, rows), f32))

    @pl.when(jnp.logical_not(safe))
    def shifted_by_maximum():
        kl_sum[...] = jnp.zeros((1, rows), f32)
        key_grad[...] = jnp.zeros(key_grad.shape, f32)

        def masked(h, i, j):
            allowed = key_pos + j * rows <= row_pos + i * rows
            teacher, student = logits(h, i, j)
            return jnp.where(allowed, teacher, NEGATIVE), jnp.where(allowed, student, NEGATIVE)

        def row_step(step, _):
            h, i = step // tiles, step % tiles
            here = pl.ds(pl.multiple_of(i * rows, rows), rows)

            def advance(j, state):
                teacher_max, teacher_sum, cross_sum, student_max, student_sum = state
                teacher, student = masked(h, i, j)
                teacher_top = jnp.maximum(teacher_max, jnp.max(teacher, axis=0, keepdims=True))
                student_top = jnp.maximum(student_max, jnp.max(student, axis=0, keepdims=True))
                teacher_exp = jnp.exp2(teacher - teacher_top)
                student_exp = jnp.exp2(student - student_top)
                shrink = jnp.exp2(teacher_max - teacher_top)
                cross = jnp.sum(teacher_exp * (teacher - student), axis=0, keepdims=True)
                return (
                    teacher_top,
                    teacher_sum * shrink + jnp.sum(teacher_exp, axis=0, keepdims=True),
                    cross_sum * shrink + cross,
                    student_top,
                    student_sum * jnp.exp2(student_max - student_top)
                    + jnp.sum(student_exp, axis=0, keepdims=True),
                )

            lowest = jnp.full((1, rows), NEGATIVE, f32)
            zeros = jnp.zeros((1, rows), f32)
            teacher_max, teacher_sum, cross_sum, student_max, student_sum = lax.fori_loop(
                0, i + 1, advance, (lowest, zeros, zeros, lowest, zeros)
            )
            teacher_lse = teacher_max + jnp.log2(teacher_sum)
            student_lse = student_max + jnp.log2(student_sum)
            kl_sum[...] = kl_sum[...] + (cross_sum / teacher_sum - teacher_lse + student_lse)

            def spread(j, total):
                teacher, student = masked(h, i, j)
                value = jnp.exp2(student - student_lse) - jnp.exp2(teacher - teacher_lse)
                value = value.astype(bf16)
                keys = pl.ds(pl.multiple_of(j * rows, rows), rows)
                key_grad[keys, :] = key_grad[keys, :] + jnp.dot(
                    value, student_pad[h, here, :], preferred_element_type=f32
                )
                return total + jnp.dot(
                    student_col[h, :, keys], value, preferred_element_type=f32
                )

            row_grad[h, :, here] = lax.fori_loop(
                0, i + 1, spread, jnp.zeros((STUDENT_DIM, rows), f32)
            )
            return 0

        lax.fori_loop(0, heads * tiles, row_step, 0)

    if not last:
        return

    row_parts = [*done[::3], row_grad]
    key_parts = [*done[1::3], key_grad]
    total_width = len(row_parts) * student_width
    for i in range(tiles):
        here = slice(i * rows, (i + 1) * rows)
        columns = jnp.concatenate(
            [part[h, :, here] for part in row_parts for h in range(heads)], axis=0
        )
        lanes = jnp.concatenate([part[here, :] for part in key_parts], axis=1)
        grad_rows[here, :] = (columns.T + lanes) * (STUDENT_DIM**-0.5)
    grad_rows[pl.ds(live, window), :] = jnp.zeros((window, total_width), f32)
    kl_total = sum([ref[...] for ref in done[2::3]] + [kl_sum[...]])
    tokens = sum(counts_ref[b] for b in range(blocks))
    share = jnp.full((1, rows), math.log(2.0), f32) / (H_REL * tokens).astype(f32)
    tail = tail_rows(jnp.sum(kl_total * share, axis=1, keepdims=True), total_width)
    position = lax.broadcasted_iota(jnp.int32, (rows, window), 1)
    token = lax.broadcasted_iota(jnp.int32, (rows, window), 0)
    for k, (base, shift, count) in enumerate(places):
        place = ((position == token + shift) & (token < count)).astype(bf16)
        block = grad_rows[pl.ds(base, window), :].astype(bf16)
        send = late_block(out, k)
        moved = jnp.dot(place, block, preferred_element_type=f32)
        send[:rows, :] = moved.astype(bf16)
        send[rows:, :] = tail


def local(teacher_queries, student_queries, token_counts):
    f32, bf16 = jnp.float32, jnp.bfloat16
    blocks = lax.axis_size("seq")
    chips = blocks // 2
    groups = lax.axis_size("head")
    rows = teacher_queries.shape[0]
    heads = teacher_queries.shape[1] // TEACHER_DIM // blocks
    tiles = blocks * 3 // 4
    live = tiles * rows
    folded = heads * STUDENT_DIM == LANES
    chunks = 2 if folded else 1
    chunk_heads = heads // chunks
    teacher_width = chunk_heads * TEACHER_DIM
    student_width = chunk_heads * STUDENT_DIM
    if folded:
        send_shape = (chips, rows + rows // 2, LANES)
    else:
        send_shape = (chips, rows, teacher_width + student_width)
    vmem = pl.BlockSpec(memory_space=pltpu.VMEM)
    smem = pl.BlockSpec(memory_space=pltpu.SMEM)
    params = pltpu.CompilerParams(vmem_limit_bytes=40 * 1024 * 1024)
    me = lax.axis_index("seq").reshape(1)
    far_first = sorted(range(1, chips), key=lambda k: -k.bit_count())

    def call(kernel, name, out_shape, *inputs):
        return pl.pallas_call(
            kernel,
            in_specs=[vmem] * len(inputs),
            out_specs=[vmem] * len(out_shape),
            out_shape=out_shape,
            compiler_params=params,
            name=name,
        )(*inputs)

    def to_chips(sends):
        return [
            lax.ppermute(send, "seq", [(i, i ^ (2 * k)) for i in range(blocks)])
            for k, send in enumerate(sends, 1)
        ]

    def to_other_core(send):
        return lax.ppermute(send, "seq", [(i, i ^ 1) for i in range(blocks)])

    def exchange(kept, swapped):
        swapped = to_other_core(swapped)
        message = jax.ShapeDtypeStruct((2,) + kept.shape[1:], bf16)
        sends = call(merge_kernel, "merge", [message] * (chips - 1), kept, swapped)
        return [kept, swapped, *to_chips(sends)]

    def exchange_late(own, other, sends, tail=0):
        messages = to_chips(sends)
        forward = jax.ShapeDtypeStruct((chips, own.shape[0] - tail, own.shape[1]), bf16)
        kl = [jax.ShapeDtypeStruct((1, own.shape[1]), f32)] if tail else []
        forward, *kl = call(
            functools.partial(forward_kernel, chips),
            "forward",
            [forward, *kl],
            own,
            other,
            *messages,
        )
        return [own, to_other_core(forward), *messages], kl

    packed = jax.ShapeDtypeStruct(send_shape, bf16)
    first = [jax.ShapeDtypeStruct(send_shape[1:], bf16)] * 2
    first += [jax.ShapeDtypeStruct((2,) + send_shape[1:], bf16)] * (chips - 1)
    if folded:
        anywhere = pl.BlockSpec(memory_space=pltpu.HBM)
        sends = pl.pallas_call(
            functools.partial(pack_folded_kernel, blocks, chunks),
            in_specs=[smem, anywhere, anywhere],
            out_specs=[vmem] * (len(first) + 2 * chunks - 2),
            out_shape=first + [packed] * (2 * chunks - 2),
            scratch_shapes=[
                pltpu.VMEM(student_queries.shape, bf16),
                pltpu.SemaphoreType.DMA((chunks * blocks + 1,)),
            ],
            compiler_params=pltpu.CompilerParams(vmem_limit_bytes=52 * 1024 * 1024),
            name="pack",
        )(me, teacher_queries, student_queries)
    else:
        sends = pl.pallas_call(
            functools.partial(pack_plain_kernel, blocks),
            in_specs=[smem, vmem, vmem],
            out_specs=[vmem] * len(first),
            out_shape=first,
            compiler_params=params,
            name="pack",
        )(me, teacher_queries, student_queries)
    own, other, *sends = sends
    incoming = [exchange_late(own, other, sends[: chips - 1])[0]]
    sends = sends[chips - 1 :]
    incoming += [exchange(*pair) for pair in zip(sends[::2], sends[1::2])]

    result = [
        jax.ShapeDtypeStruct((chunk_heads, STUDENT_DIM, live), f32),
        jax.ShapeDtypeStruct((live, student_width), f32),
        jax.ShapeDtypeStruct((1, rows), f32),
    ]
    block = jax.ShapeDtypeStruct((rows + TAIL, heads * STUDENT_DIM), bf16)
    messages = [block] * 2 + [jax.ShapeDtypeStruct((2,) + block.shape, bf16)] * (chips - 1)
    pairs = chunk_heads * tiles * (tiles + 1) // 2 * rows * rows
    done = []
    for c in range(chunks):
        last = c == chunks - 1
        scratch = [
            pltpu.VMEM((live + rows + PAD, teacher_width + student_width), f32),
            pltpu.VMEM((chunk_heads, live, DEPTH), bf16),
            pltpu.VMEM((chunk_heads, tiles, DEPTH, 2 * rows), bf16),
            pltpu.VMEM((chunk_heads, STUDENT_DIM, live), bf16),
            pltpu.VMEM((chunk_heads, live, student_width), bf16),
            pltpu.VMEM((2, tiles, rows, rows), f32),
            pltpu.VMEM((2, tiles, rows, rows), f32),
            pltpu.VMEM((live, live), bf16),
        ]
        if last:
            scratch += [pltpu.VMEM(part.shape, f32) for part in result]
            scratch.append(pltpu.VMEM((live + rows + PAD, heads * STUDENT_DIM), f32))
        inputs = [me, token_counts, *incoming[c], *done]
        done += pl.pallas_call(
            functools.partial(
                relation_kernel,
                folded,
                chunk_heads,
                tiles,
                c == 0,
                len(incoming[c]),
                c,
                last,
            ),
            in_specs=[smem, smem] + [vmem] * (len(inputs) - 2),
            out_specs=[vmem] * len(messages if last else result),
            out_shape=messages if last else result,
            scratch_shapes=scratch,
            compiler_params=params,
            cost_estimate=pl.CostEstimate(
                flops=4 * pairs * DEPTH, bytes_accessed=8 * pairs, transcendentals=2 * pairs
            ),
            name="relation",
        )(*inputs)
    own, other, *sends = done[-len(messages) :]
    returned, (kl,) = exchange_late(own, other, sends, TAIL)
    kl = pair_sum(
        [kl]
        + [
            lax.ppermute(kl, "head", [(i, i ^ k) for i in range(groups)])
            for k in range(1, groups)
        ]
    )
    kl_other = to_other_core(kl)
    grad = pl.pallas_call(
        unpack_kernel,
        in_specs=[smem] + [vmem] * len(returned),
        out_specs=vmem,
        out_shape=jax.ShapeDtypeStruct((rows, student_queries.shape[1]), f32),
        compiler_params=params,
        name="unpack",
    )(me, *returned)
    grad, kl, kl_other = lax.optimization_barrier((grad, kl, kl_other))
    return (grad, (kl + kl_other)[0, 0])


def solution(mesh):
    return jax.shard_map(
        local,
        mesh=mesh,
        in_specs=(P("seq", "head"), P("seq", "head"), P()),
        out_specs=(P("seq", "head"), P()),
        check_vma=False,
    )
```

```python
import functools
import math

import jax
import jax.numpy as jnp
from jax import lax
from jax.experimental import pallas as pl
from jax.experimental.pallas import tpu as pltpu
from jax.sharding import PartitionSpec as P

DT = 8192
DS = 4096
H_REL = 128
TEACHER_DIM = DT // H_REL
STUDENT_DIM = DS // H_REL

NEGATIVE = -1e30
LOG2E = math.log2(math.e)
TEACHER_SCALE = LOG2E * TEACHER_DIM**-0.5
STUDENT_SCALE = LOG2E * STUDENT_DIM**-0.5
PAD = 8
LANES = 128
TAIL = 16
DEPTH = 256
SAFE_NORM = 320.0


def split_high_low(values):
    high = values.astype(jnp.bfloat16)
    low = (values - high.astype(jnp.float32)).astype(jnp.bfloat16)
    return high, low


def split_three(values):
    high = values.astype(jnp.bfloat16)
    rest = values - high.astype(jnp.float32)
    return (high,) + split_high_low(rest)


def at_columns(index, count, width, act):
    if width % LANES == 0:
        act(pl.ds(pl.multiple_of(index * width, LANES), width))
    else:
        for part in range(count):
            pl.when(index == part)(functools.partial(act, pl.ds(part * width, width)))


def late_block(refs, k):
    return refs[k] if k < 2 else refs[k // 2 + 1].at[k % 2]


def pack_folded_kernel(blocks, chunks, me_ref, teacher_ref, student_ref, *refs):
    sends, student, sems = refs[:-2], refs[-2], refs[-1]
    rows = teacher_ref.shape[0]
    half = rows // 2

    def block(chunk, k):
        if chunk == 0:
            return sends[k]
        return sends[blocks + 2 * (chunk - 1) + k % 2].at[k // 2]

    copies = [pltpu.make_async_copy(student_ref, student, sems.at[chunks * blocks])]
    for chunk in range(chunks):
        for k in range(blocks):
            to = jnp.bitwise_xor(me_ref[0], k)
            at = pl.multiple_of((to * chunks + chunk) * LANES, LANES)
            copies.append(
                pltpu.make_async_copy(
                    teacher_ref.at[:, pl.ds(at, LANES)],
                    block(chunk, k).at[pl.ds(0, rows)],
                    sems.at[chunk * blocks + k],
                )
            )
    for copy in copies:
        copy.start()
    copies[0].wait()
    for k in range(blocks):
        to = jnp.bitwise_xor(me_ref[0], k)
        lanes = pl.ds(pl.multiple_of(to * LANES, LANES), LANES)
        top, bottom = student[:half, lanes], student[half:, lanes]
        for chunk in range(chunks):
            part = slice(chunk * (LANES // 2), (chunk + 1) * (LANES // 2))
            block(chunk, k)[rows:, :] = jnp.concatenate([top[:, part], bottom[:, part]], axis=1)
    for copy in copies[1:]:
        copy.wait()


def pack_plain_kernel(blocks, me_ref, teacher_ref, student_ref, *sends):
    teacher_width = teacher_ref.shape[1] // blocks
    student_width = student_ref.shape[1] // blocks
    for k in range(blocks):
        to = jnp.bitwise_xor(me_ref[0], k)

        def put_teacher(columns, send=sends[k % 2], k=k):
            send[k // 2, :, :teacher_width] = teacher_ref[:, columns]

        def put_student(columns, send=sends[k % 2], k=k):
            send[k // 2, :, teacher_width:] = student_ref[:, columns]

        at_columns(to, blocks, teacher_width, put_teacher)
        at_columns(to, blocks, student_width, put_student)


def tail_rows(value, width):
    thirds = [part.astype(jnp.float32) for part in split_three(value)]
    line = lax.broadcasted_iota(jnp.int32, (TAIL, width), 0)
    tail = jnp.where(line == 0, thirds[0], 0.0)
    tail = jnp.where(line == 1, thirds[1], tail)
    return jnp.where(line == 2, thirds[2], tail).astype(jnp.bfloat16)


def pair_sum(parts):
    while len(parts) > 1:
        parts = [a + b for a, b in zip(parts[::2], parts[1::2])]
    return parts[0]


def merge_kernel(kept_ref, swapped_ref, *sends):
    for k, send in enumerate(sends, 1):
        send[0] = kept_ref[k]
        send[1] = swapped_ref[k]


def forward_kernel(other_ref, *refs):
    messages, forward_ref = refs[:-1], refs[-1]
    forward_ref[0] = other_ref[...]
    for k, message in enumerate(messages, 1):
        forward_ref[k] = message[1]


def arrived(refs, late):
    if late:
        blocks = [refs[0], refs[1].at[0]]
        for chip, ref in enumerate(refs[2:], 1):
            blocks += [ref.at[0], refs[1].at[chip]]
        return blocks
    return [refs[0].at[0], refs[1].at[0]] + [ref.at[core] for ref in refs[2:] for core in range(2)]


def unpack_kernel(me_ref, *refs):
    grad_ref, loss_ref = refs[-2:]
    rows = grad_ref.shape[0]
    blocks = arrived(refs[:-2], True)
    for k, block in enumerate(blocks):

        def put(columns, block=block):
            grad_ref[:, columns] = block[:rows, :].astype(jnp.float32)

        at_columns(jnp.bitwise_xor(me_ref[0], k), len(blocks), block.shape[1], put)
    total = pair_sum([block[rows:, :].astype(jnp.float32) for block in blocks])
    loss_ref[...] = jnp.sum(total, axis=0, keepdims=True)


def fold(values):
    rows, columns = values.shape
    return jnp.sum(values.reshape(rows // 8, 8, columns), axis=0)


def relation_kernel(folded, heads, tiles, order, n_in, me_ref, counts_ref, *refs):
    if order:
        sources = [refs[order.index(k)] for k in range(n_in)]
    else:
        sources = arrived(refs[:n_in], False)
    row_grad, key_grad, kl_out = refs[n_in : n_in + 3]
    pack, key_op, row_op, student_col, student_pad, teacher_prob, student_prob, weights_ref, kl_sum = (
        refs[n_in + 3 :]
    )
    f32, bf16 = jnp.float32, jnp.bfloat16
    blocks = len(sources)
    rows = teacher_prob.shape[2]
    half = rows // 2
    live = tiles * rows
    window = rows + PAD
    student_at = heads * TEACHER_DIM
    student_width = heads * STUDENT_DIM
    filled = 2 * TEACHER_DIM + 2 * STUDENT_DIM

    position = lax.broadcasted_iota(jnp.int32, (window, rows), 0)
    token = lax.broadcasted_iota(jnp.int32, (window, rows), 1)
    pack[...] = jnp.zeros(pack.shape, f32)
    places = []
    for k in range(blocks):
        owner = jnp.bitwise_xor(me_ref[0], k)
        start = sum(jnp.where(b < owner, counts_ref[b], 0) for b in range(blocks))
        base = pl.multiple_of(start // PAD * PAD, PAD)
        places.append((base, start - base, counts_ref[owner]))
    for source, (base, shift, count) in zip(sources, places):
        place = ((position == token + shift) & (token < count)).astype(bf16)
        here = pl.ds(base, window)
        if folded:
            moved = jnp.dot(place, source[:rows, :], preferred_element_type=f32)
            pack[here, :student_at] = pack[here, :student_at] + moved
            student = source[rows:, :]
            moved = jnp.dot(
                place[:, :half], student[:, :student_width], preferred_element_type=f32
            ) + jnp.dot(place[:, half:], student[:, student_width:], preferred_element_type=f32)
            pack[here, student_at:] = pack[here, student_at:] + moved
        else:
            moved = jnp.dot(place, source[...], preferred_element_type=f32)
            pack[here, :] = pack[here, :] + moved

    ones = jnp.ones((rows, DEPTH - filled), bf16)
    spare = lax.broadcasted_iota(jnp.int32, (DEPTH - filled, rows), 0)
    teacher_gap = jnp.zeros((2 * STUDENT_DIM, rows), bf16)
    student_gap = jnp.zeros((2 * TEACHER_DIM, rows), bf16)
    lane_head = lax.broadcasted_iota(jnp.int32, (rows, student_width), 1) // STUDENT_DIM
    norms = []

    def shift_rows(norm):
        parts = [part.astype(f32) for part in split_three(-norm)]
        out = jnp.where(spare == 0, parts[0], 0.0)
        out = jnp.where(spare == 1, parts[1], out)
        return jnp.where(spare == 2, parts[2], out).astype(bf16)

    for i in range(tiles):
        here = pl.ds(i * rows, rows)
        tile = pack[here, :]
        tile_t = tile.T
        tile_b = tile.astype(bf16)
        tile_s = tile[:, student_at:]
        for h in range(heads):
            tb = tile_b[:, h * TEACHER_DIM : (h + 1) * TEACHER_DIM]
            at = student_at + h * STUDENT_DIM
            sb = tile_b[:, at : at + STUDENT_DIM]
            key_op[h, here, :] = jnp.concatenate([tb, tb, sb, sb, ones], axis=1)
            teacher_t = tile_t[h * TEACHER_DIM : (h + 1) * TEACHER_DIM, :]
            student_t = tile_t[at : at + STUDENT_DIM, :]
            student_col[h, :, here] = student_t.astype(bf16)
            student_pad[h, here, :] = jnp.where(lane_head == h, tile_s, 0.0).astype(bf16)
            teacher_norm = TEACHER_SCALE * jnp.sum(teacher_t * teacher_t, axis=0, keepdims=True)
            student_norm = STUDENT_SCALE * jnp.sum(student_t * student_t, axis=0, keepdims=True)
            norms += [teacher_norm, student_norm]
            high, low = split_high_low(teacher_t * TEACHER_SCALE)
            teacher_op = [high, low, teacher_gap, shift_rows(teacher_norm)]
            row_op[h, i, :, :rows] = jnp.concatenate(teacher_op, axis=0)
            high, low = split_high_low(student_t * STUDENT_SCALE)
            student_op = [student_gap, high, low, shift_rows(student_norm)]
            row_op[h, i, :, rows:] = jnp.concatenate(student_op, axis=0)

    safe = jnp.max(functools.reduce(jnp.maximum, norms)) <= SAFE_NORM
    key_pos = lax.broadcasted_iota(jnp.int32, (rows, rows), 0)
    row_pos = lax.broadcasted_iota(jnp.int32, (rows, rows), 1)

    def logits(h, i, j):
        keys = pl.ds(pl.multiple_of(j * rows, rows), rows)
        both = jnp.dot(key_op[h, keys, :], row_op[h, i], preferred_element_type=f32)
        return both[:, :rows], both[:, rows:]

    @pl.when(safe)
    def shifted_by_own_logit():
        key_grad[...] = jnp.zeros(key_grad.shape, f32)

        def exponentials(h, i, model, prob):
            upto = (i + 1) * rows
            op = row_op[h, i, :, model * rows : (model + 1) * rows]
            values = jnp.dot(key_op[h, :upto, :], op, preferred_element_type=f32)
            diagonal = jnp.where(key_pos <= row_pos, values[i * rows :], NEGATIVE)
            total = cross = jnp.zeros((8, rows), f32)
            for j in range(i + 1):
                value = diagonal if j == i else values[j * rows : (j + 1) * rows]
                exp = jnp.exp2(value)
                prob[i % 2, j] = exp
                total = total + fold(exp)
                weight = teacher_prob[i % 2, j] if model else exp
                cross = cross + fold(weight * value)
            return [jnp.sum(part, axis=0, keepdims=True) for part in (total, cross)]

        def weights(i, j, teacher_inv, student_inv):
            value = student_prob[i % 2, j] * student_inv - teacher_prob[i % 2, j] * teacher_inv
            weights_ref[j * rows : (j + 1) * rows, i * rows : (i + 1) * rows] = value.astype(bf16)

        def head_step(h, kl_total):
            inverse = None
            for i in range(tiles + 1):
                if i < tiles:
                    teacher_sum, teacher_cross = exponentials(h, i, 0, teacher_prob)
                    student_sum, student_cross = exponentials(h, i, 1, student_prob)
                if i:
                    upto = i * rows
                    for j in range(i):
                        weights(i - 1, j, *inverse)
                    row_grad[h, :, upto - rows : upto] = jnp.dot(
                        student_col[h, :, :upto],
                        weights_ref[:upto, upto - rows : upto],
                        preferred_element_type=f32,
                    )
                if i < tiles:
                    inverse = (1.0 / teacher_sum, 1.0 / student_sum)
                    kl_total = kl_total + (
                        (teacher_cross - student_cross) * inverse[0]
                        - jnp.log2(teacher_sum)
                        + jnp.log2(student_sum)
                    )
            for j in range(tiles):
                here = slice(j * rows, (j + 1) * rows)
                key_grad[here, :] = key_grad[here, :] + jnp.dot(
                    weights_ref[here, j * rows :],
                    student_pad[h, j * rows :, :],
                    preferred_element_type=f32,
                )
            return kl_total

        kl_sum[...] = lax.fori_loop(0, heads, head_step, jnp.zeros((1, rows), f32))

    @pl.when(jnp.logical_not(safe))
    def shifted_by_maximum():
        kl_sum[...] = jnp.zeros((1, rows), f32)
        key_grad[...] = jnp.zeros(key_grad.shape, f32)

        def masked(h, i, j):
            allowed = key_pos + j * rows <= row_pos + i * rows
            teacher, student = logits(h, i, j)
            return jnp.where(allowed, teacher, NEGATIVE), jnp.where(allowed, student, NEGATIVE)

        def row_step(step, _):
            h, i = step // tiles, step % tiles
            here = pl.ds(pl.multiple_of(i * rows, rows), rows)

            def advance(j, state):
                teacher_max, teacher_sum, cross_sum, student_max, student_sum = state
                teacher, student = masked(h, i, j)
                teacher_top = jnp.maximum(teacher_max, jnp.max(teacher, axis=0, keepdims=True))
                student_top = jnp.maximum(student_max, jnp.max(student, axis=0, keepdims=True))
                teacher_exp = jnp.exp2(teacher - teacher_top)
                student_exp = jnp.exp2(student - student_top)
                shrink = jnp.exp2(teacher_max - teacher_top)
                cross = jnp.sum(teacher_exp * (teacher - student), axis=0, keepdims=True)
                return (
                    teacher_top,
                    teacher_sum * shrink + jnp.sum(teacher_exp, axis=0, keepdims=True),
                    cross_sum * shrink + cross,
                    student_top,
                    student_sum * jnp.exp2(student_max - student_top)
                    + jnp.sum(student_exp, axis=0, keepdims=True),
                )

            lowest = jnp.full((1, rows), NEGATIVE, f32)
            zeros = jnp.zeros((1, rows), f32)
            teacher_max, teacher_sum, cross_sum, student_max, student_sum = lax.fori_loop(
                0, i + 1, advance, (lowest, zeros, zeros, lowest, zeros)
            )
            teacher_lse = teacher_max + jnp.log2(teacher_sum)
            student_lse = student_max + jnp.log2(student_sum)
            kl_sum[...] = kl_sum[...] + (cross_sum / teacher_sum - teacher_lse + student_lse)

            def spread(j, total):
                teacher, student = masked(h, i, j)
                value = jnp.exp2(student - student_lse) - jnp.exp2(teacher - teacher_lse)
                value = value.astype(bf16)
                keys = pl.ds(pl.multiple_of(j * rows, rows), rows)
                key_grad[keys, :] = key_grad[keys, :] + jnp.dot(
                    value, student_pad[h, here, :], preferred_element_type=f32
                )
                return total + jnp.dot(
                    student_col[h, :, keys], value, preferred_element_type=f32
                )

            row_grad[h, :, here] = lax.fori_loop(
                0, i + 1, spread, jnp.zeros((STUDENT_DIM, rows), f32)
            )
            return 0

        lax.fori_loop(0, heads * tiles, row_step, 0)

    tokens = sum(counts_ref[b] for b in range(blocks))
    share = jnp.full((1, rows), math.log(2.0), f32) / (H_REL * tokens).astype(f32)
    kl_total = jnp.sum(kl_sum[...] * share, axis=1, keepdims=True)
    kl_out[...] = jnp.broadcast_to(kl_total, kl_out.shape)


def packed_start(me, counts_ref, blocks, k):
    owner = jnp.bitwise_xor(me, k)
    start = sum(jnp.where(b < owner, counts_ref[b], 0) for b in range(blocks))
    base = pl.multiple_of(start // PAD * PAD, PAD)
    return base, start - base, counts_ref[owner]


def turn_kernel(tiles, chunks, me_ref, counts_ref, *refs):
    row_parts, key_parts = refs[:chunks], refs[chunks : 2 * chunks]
    grad_rows, place_ref = refs[2 * chunks :]
    blocks, rows, window = place_ref.shape
    live = tiles * rows
    for i in range(tiles):
        here = slice(i * rows, (i + 1) * rows)
        columns = jnp.concatenate(
            [part[h, :, here] for part in row_parts for h in range(part.shape[0])], axis=0
        )
        lanes = jnp.concatenate([part[here, :] for part in key_parts], axis=1)
        grad_rows[here, :] = (columns.T + lanes) * (STUDENT_DIM**-0.5)
    grad_rows[live:, :] = jnp.zeros((window, grad_rows.shape[1]), jnp.float32)
    position = lax.broadcasted_iota(jnp.int32, (rows, window), 1)
    token = lax.broadcasted_iota(jnp.int32, (rows, window), 0)
    for k in range(blocks):
        _, shift, count = packed_start(me_ref[0], counts_ref, blocks, k)
        place = (position == token + shift) & (token < count)
        place_ref[k] = place.astype(jnp.bfloat16)


def finish_kernel(groups, me_ref, counts_ref, grad_rows, place_ref, *refs):
    kls, sends = refs[:groups], refs[groups:]
    blocks, rows, window = place_ref.shape
    width = grad_rows.shape[1]
    tail = tail_rows(pair_sum([kl[:, :width] for kl in kls]), width)
    for k in range(blocks):
        base, _, _ = packed_start(me_ref[0], counts_ref, blocks, k)
        block = grad_rows[pl.ds(base, window), :].astype(jnp.bfloat16)
        send = late_block(sends, k)
        moved = jnp.dot(place_ref[k], block, preferred_element_type=jnp.float32)
        send[:rows, :] = moved.astype(jnp.bfloat16)
        send[rows:, :] = tail


def local(teacher_queries, student_queries, token_counts):
    f32, bf16 = jnp.float32, jnp.bfloat16
    blocks = lax.axis_size("seq")
    chips = blocks // 2
    groups = lax.axis_size("head")
    rows = teacher_queries.shape[0]
    heads = teacher_queries.shape[1] // TEACHER_DIM // blocks
    tiles = blocks * 3 // 4
    live = tiles * rows
    folded = heads * STUDENT_DIM == LANES
    chunks = 2 if folded else 1
    chunk_heads = heads // chunks
    teacher_width = chunk_heads * TEACHER_DIM
    student_width = chunk_heads * STUDENT_DIM
    if folded:
        send_shape = (chips, rows + rows // 2, LANES)
    else:
        send_shape = (chips, rows, teacher_width + student_width)
    vmem = pl.BlockSpec(memory_space=pltpu.VMEM)
    smem = pl.BlockSpec(memory_space=pltpu.SMEM)
    params = pltpu.CompilerParams(vmem_limit_bytes=40 * 1024 * 1024)
    me = lax.axis_index("seq").reshape(1)
    far_first = sorted(range(1, chips), key=lambda k: -k.bit_count())

    def call(kernel, name, out_shape, *inputs, n_smem=0, **kwargs):
        return pl.pallas_call(
            kernel,
            in_specs=[smem] * n_smem + [vmem] * (len(inputs) - n_smem),
            out_specs=[vmem] * len(out_shape),
            out_shape=out_shape,
            compiler_params=params,
            name=name,
            **kwargs,
        )(*inputs)

    def to_chips(sends):
        return [
            lax.ppermute(send, "seq", [(i, i ^ (2 * k)) for i in range(blocks)])
            for k, send in enumerate(sends, 1)
        ]

    def to_other_core(send):
        return lax.ppermute(send, "seq", [(i, i ^ 1) for i in range(blocks)])

    def exchange(kept, swapped):
        swapped = to_other_core(swapped)
        message = jax.ShapeDtypeStruct((2,) + kept.shape[1:], bf16)
        sends = call(merge_kernel, "merge", [message] * (chips - 1), kept, swapped)
        return [kept, swapped, *to_chips(sends)]

    def exchange_late(own, other, *sends):
        messages = to_chips(sends)
        forward = jax.ShapeDtypeStruct((chips, *own.shape), bf16)
        (forward,) = call(forward_kernel, "forward", [forward], other, *messages)
        return [own, to_other_core(forward), *messages]

    packed = jax.ShapeDtypeStruct(send_shape, bf16)
    first = jax.ShapeDtypeStruct(send_shape[1:], bf16)
    order = [0, 1, *range(2, blocks, 2), *range(3, blocks, 2)] if folded else None
    if folded:
        anywhere = pl.BlockSpec(memory_space=pltpu.HBM)
        sends = pl.pallas_call(
            functools.partial(pack_folded_kernel, blocks, chunks),
            in_specs=[smem, anywhere, anywhere],
            out_specs=[vmem] * (blocks + 2 * chunks - 2),
            out_shape=[first] * blocks + [packed] * (2 * chunks - 2),
            scratch_shapes=[
                pltpu.VMEM(student_queries.shape, bf16),
                pltpu.SemaphoreType.DMA((chunks * blocks + 1,)),
            ],
            compiler_params=pltpu.CompilerParams(vmem_limit_bytes=52 * 1024 * 1024),
            name="pack",
        )(me, teacher_queries, student_queries)
    else:
        sends = pl.pallas_call(
            functools.partial(pack_plain_kernel, blocks),
            in_specs=[smem, vmem, vmem],
            out_specs=[vmem] * 2,
            out_shape=[packed] * 2,
            compiler_params=params,
            name="pack",
        )(me, teacher_queries, student_queries)
    incoming = []
    if folded:
        incoming.append(
            [sends[0]]
            + [
                lax.ppermute(sends[k], "seq", [(i, i ^ k) for i in range(blocks)])
                for k in order[1:]
            ]
        )
        sends = sends[blocks:]
    incoming += [exchange(*pair) for pair in zip(sends[::2], sends[1::2])]

    window = rows + PAD
    result = [
        jax.ShapeDtypeStruct((chunk_heads, STUDENT_DIM, live), f32),
        jax.ShapeDtypeStruct((live, student_width), f32),
        jax.ShapeDtypeStruct((1, LANES), f32),
    ]
    pairs = chunk_heads * tiles * (tiles + 1) // 2 * rows * rows
    row_parts, key_parts, kls = zip(
        *[
            call(
                functools.partial(
                    relation_kernel,
                    folded,
                    chunk_heads,
                    tiles,
                    order if c == 0 else None,
                    len(incoming[c]),
                ),
                "relation",
                result,
                me,
                token_counts,
                *incoming[c],
                n_smem=2,
                scratch_shapes=[
                    pltpu.VMEM((live + window, teacher_width + student_width), f32),
                    pltpu.VMEM((chunk_heads, live, DEPTH), bf16),
                    pltpu.VMEM((chunk_heads, tiles, DEPTH, 2 * rows), bf16),
                    pltpu.VMEM((chunk_heads, STUDENT_DIM, live), bf16),
                    pltpu.VMEM((chunk_heads, live, student_width), bf16),
                    pltpu.VMEM((2, tiles, rows, rows), f32),
                    pltpu.VMEM((2, tiles, rows, rows), f32),
                    pltpu.VMEM((live, live), bf16),
                    pltpu.VMEM((1, rows), f32),
                ],
                cost_estimate=pl.CostEstimate(
                    flops=4 * pairs * DEPTH, bytes_accessed=8 * pairs, transcendentals=2 * pairs
                ),
            )
            for c in range(chunks)
        ]
    )
    kl = functools.reduce(jnp.add, kls)
    kls = [kl] + [
        lax.ppermute(kl, "head", [(i, i ^ k) for i in range(groups)]) for k in range(1, groups)
    ]
    width = heads * STUDENT_DIM
    grad_rows, place = call(
        functools.partial(turn_kernel, tiles, chunks),
        "turn",
        [
            jax.ShapeDtypeStruct((live + window, width), f32),
            jax.ShapeDtypeStruct((blocks, rows, window), bf16),
        ],
        me,
        token_counts,
        *row_parts,
        *key_parts,
        n_smem=2,
        cost_estimate=pl.CostEstimate(flops=pairs, bytes_accessed=8 * pairs, transcendentals=0),
    )
    block = jax.ShapeDtypeStruct((rows + TAIL, width), bf16)
    sends = call(
        functools.partial(finish_kernel, groups),
        "finish",
        [block] * 2 + [jax.ShapeDtypeStruct((2, *block.shape), bf16)] * (chips - 1),
        me,
        token_counts,
        grad_rows,
        place,
        *kls,
        n_smem=2,
    )
    grad, loss = call(
        unpack_kernel,
        "unpack",
        [
            jax.ShapeDtypeStruct((rows, student_queries.shape[1]), f32),
            jax.ShapeDtypeStruct((1, width), f32),
        ],
        me,
        *exchange_late(*sends),
        n_smem=1,
    )
    return (grad, loss[0, 0])


def solution(mesh):
    return jax.shard_map(
        local,
        mesh=mesh,
        in_specs=(P("seq", "head"), P("seq", "head"), P()),
        out_specs=(P("seq", "head"), P()),
        check_vma=False,
    )
```

```python
import functools
import math

import jax
import jax.numpy as jnp
from jax import lax
from jax.experimental import pallas as pl
from jax.experimental.pallas import tpu as pltpu
from jax.sharding import PartitionSpec as P

DT = 8192
DS = 4096
H_REL = 128
TEACHER_DIM = DT // H_REL
STUDENT_DIM = DS // H_REL

NEGATIVE = -1e30
LOG2E = math.log2(math.e)
TEACHER_SCALE = LOG2E * TEACHER_DIM**-0.5
STUDENT_SCALE = LOG2E * STUDENT_DIM**-0.5
PAD = 8
LANES = 128
TAIL = 16
DEPTH = 256
SAFE_NORM = 320.0


def split_high_low(values):
    high = values.astype(jnp.bfloat16)
    low = (values - high.astype(jnp.float32)).astype(jnp.bfloat16)
    return high, low


def split_three(values):
    high = values.astype(jnp.bfloat16)
    rest = values - high.astype(jnp.float32)
    return (high,) + split_high_low(rest)


def at_columns(index, count, width, act):
    if width % LANES == 0:
        act(pl.ds(pl.multiple_of(index * width, LANES), width))
    else:
        for part in range(count):
            pl.when(index == part)(functools.partial(act, pl.ds(part * width, width)))


def late_block(refs, k):
    return refs[k] if k < 2 else refs[k // 2 + 1].at[k % 2]


def pack_folded_kernel(blocks, chunks, me_ref, teacher_ref, student_ref, *refs):
    sends, student, sems = refs[:-2], refs[-2], refs[-1]
    rows = teacher_ref.shape[0]
    half = rows // 2

    def block(chunk, k):
        if chunk == 0:
            return sends[k]
        return sends[blocks + 2 * (chunk - 1) + k % 2].at[k // 2]

    copies = [pltpu.make_async_copy(student_ref, student, sems.at[chunks * blocks])]
    for chunk in range(chunks):
        for k in range(blocks):
            to = jnp.bitwise_xor(me_ref[0], k)
            at = pl.multiple_of((to * chunks + chunk) * LANES, LANES)
            copies.append(
                pltpu.make_async_copy(
                    teacher_ref.at[:, pl.ds(at, LANES)],
                    block(chunk, k).at[pl.ds(0, rows)],
                    sems.at[chunk * blocks + k],
                )
            )
    for copy in copies:
        copy.start()
    copies[0].wait()
    for k in range(blocks):
        to = jnp.bitwise_xor(me_ref[0], k)
        lanes = pl.ds(pl.multiple_of(to * LANES, LANES), LANES)
        top, bottom = student[:half, lanes], student[half:, lanes]
        for chunk in range(chunks):
            part = slice(chunk * (LANES // 2), (chunk + 1) * (LANES // 2))
            block(chunk, k)[rows:, :] = jnp.concatenate([top[:, part], bottom[:, part]], axis=1)
    for copy in copies[1:]:
        copy.wait()


def pack_plain_kernel(blocks, me_ref, teacher_ref, student_ref, *sends):
    teacher_width = teacher_ref.shape[1] // blocks
    student_width = student_ref.shape[1] // blocks
    for k in range(blocks):
        to = jnp.bitwise_xor(me_ref[0], k)

        def put_teacher(columns, send=sends[k % 2], k=k):
            send[k // 2, :, :teacher_width] = teacher_ref[:, columns]

        def put_student(columns, send=sends[k % 2], k=k):
            send[k // 2, :, teacher_width:] = student_ref[:, columns]

        at_columns(to, blocks, teacher_width, put_teacher)
        at_columns(to, blocks, student_width, put_student)


def tail_rows(value, width):
    thirds = [part.astype(jnp.float32) for part in split_three(value)]
    line = lax.broadcasted_iota(jnp.int32, (TAIL, width), 0)
    tail = jnp.where(line == 0, thirds[0], 0.0)
    tail = jnp.where(line == 1, thirds[1], tail)
    return jnp.where(line == 2, thirds[2], tail).astype(jnp.bfloat16)


def pair_sum(parts):
    while len(parts) > 1:
        parts = [a + b for a, b in zip(parts[::2], parts[1::2])]
    return parts[0]


def merge_kernel(kept_ref, swapped_ref, *sends):
    for k, send in enumerate(sends, 1):
        send[0] = kept_ref[k]
        send[1] = swapped_ref[k]


def forward_kernel(own_ref, other_ref, *refs):
    messages, (forward_ref, kl_ref) = refs[:-2], refs[-2:]
    rows = forward_ref.shape[1]
    forward_ref[0] = other_ref[:rows, :]
    for k, message in enumerate(messages, 1):
        forward_ref[k] = message[1, :rows, :]
    tails = [own_ref[rows:, :]] + [message[0, rows:, :] for message in messages]
    sums = [jnp.sum(tail.astype(jnp.float32), axis=0, keepdims=True) for tail in tails]
    kl_ref[...] = pair_sum(sums)


def arrived(refs, late):
    if late:
        blocks = [refs[0], refs[1].at[0]]
        for chip, ref in enumerate(refs[2:], 1):
            blocks += [ref.at[0], refs[1].at[chip]]
        return blocks
    return [refs[0].at[0], refs[1].at[0]] + [ref.at[core] for ref in refs[2:] for core in range(2)]


def unpack_kernel(me_ref, *refs):
    grad_ref = refs[-1]
    blocks = arrived(refs[:-1], True)
    for k, block in enumerate(blocks):

        def put(columns, block=block):
            grad_ref[:, columns] = block[: grad_ref.shape[0], :].astype(jnp.float32)

        at_columns(jnp.bitwise_xor(me_ref[0], k), len(blocks), block.shape[1], put)


def fold(values):
    rows, columns = values.shape
    return jnp.sum(values.reshape(rows // 8, 8, columns), axis=0)


def relation_kernel(folded, heads, tiles, order, n_in, n_done, last, me_ref, counts_ref, *refs):
    if order:
        sources = [refs[order.index(k)] for k in range(n_in)]
    else:
        sources = arrived(refs[:n_in], False)
    done = refs[n_in : n_in + 3 * n_done]
    rest = list(refs[n_in + 3 * n_done :])
    n_out = len(sources) // 2 + 1 if last else 3
    out, rest = rest[:n_out], rest[n_out:]
    pack, key_op, row_op, student_col, student_pad, teacher_prob, student_prob, weights_ref = rest[:8]
    if last:
        row_grad, key_grad, kl_sum, grad_rows = rest[8:]
    else:
        row_grad, key_grad, kl_sum = out
    f32, bf16 = jnp.float32, jnp.bfloat16
    blocks = len(sources)
    rows = teacher_prob.shape[2]
    half = rows // 2
    live = tiles * rows
    window = rows + PAD
    student_at = heads * TEACHER_DIM
    student_width = heads * STUDENT_DIM
    filled = 2 * TEACHER_DIM + 2 * STUDENT_DIM

    position = lax.broadcasted_iota(jnp.int32, (window, rows), 0)
    token = lax.broadcasted_iota(jnp.int32, (window, rows), 1)
    pack[...] = jnp.zeros(pack.shape, f32)
    places = []
    for k in range(blocks):
        owner = jnp.bitwise_xor(me_ref[0], k)
        start = sum(jnp.where(b < owner, counts_ref[b], 0) for b in range(blocks))
        base = pl.multiple_of(start // PAD * PAD, PAD)
        places.append((base, start - base, counts_ref[owner]))
    for source, (base, shift, count) in zip(sources, places):
        place = ((position == token + shift) & (token < count)).astype(bf16)
        here = pl.ds(base, window)
        if folded:
            moved = jnp.dot(place, source[:rows, :], preferred_element_type=f32)
            pack[here, :student_at] = pack[here, :student_at] + moved
            student = source[rows:, :]
            moved = jnp.dot(
                place[:, :half], student[:, :student_width], preferred_element_type=f32
            ) + jnp.dot(place[:, half:], student[:, student_width:], preferred_element_type=f32)
            pack[here, student_at:] = pack[here, student_at:] + moved
        else:
            moved = jnp.dot(place, source[...], preferred_element_type=f32)
            pack[here, :] = pack[here, :] + moved

    ones = jnp.ones((rows, DEPTH - filled), bf16)
    spare = lax.broadcasted_iota(jnp.int32, (DEPTH - filled, rows), 0)
    teacher_gap = jnp.zeros((2 * STUDENT_DIM, rows), bf16)
    student_gap = jnp.zeros((2 * TEACHER_DIM, rows), bf16)
    lane_head = lax.broadcasted_iota(jnp.int32, (rows, student_width), 1) // STUDENT_DIM
    norms = []

    def shift_rows(norm):
        parts = [part.astype(f32) for part in split_three(-norm)]
        out = jnp.where(spare == 0, parts[0], 0.0)
        out = jnp.where(spare == 1, parts[1], out)
        return jnp.where(spare == 2, parts[2], out).astype(bf16)

    for i in range(tiles):
        here = pl.ds(i * rows, rows)
        tile = pack[here, :]
        tile_t = tile.T
        tile_b = tile.astype(bf16)
        tile_s = tile[:, student_at:]
        for h in range(heads):
            tb = tile_b[:, h * TEACHER_DIM : (h + 1) * TEACHER_DIM]
            at = student_at + h * STUDENT_DIM
            sb = tile_b[:, at : at + STUDENT_DIM]
            key_op[h, here, :] = jnp.concatenate([tb, tb, sb, sb, ones], axis=1)
            teacher_t = tile_t[h * TEACHER_DIM : (h + 1) * TEACHER_DIM, :]
            student_t = tile_t[at : at + STUDENT_DIM, :]
            student_col[h, :, here] = student_t.astype(bf16)
            student_pad[h, here, :] = jnp.where(lane_head == h, tile_s, 0.0).astype(bf16)
            teacher_norm = TEACHER_SCALE * jnp.sum(teacher_t * teacher_t, axis=0, keepdims=True)
            student_norm = STUDENT_SCALE * jnp.sum(student_t * student_t, axis=0, keepdims=True)
            norms += [teacher_norm, student_norm]
            high, low = split_high_low(teacher_t * TEACHER_SCALE)
            teacher_op = [high, low, teacher_gap, shift_rows(teacher_norm)]
            row_op[h, i, :, :rows] = jnp.concatenate(teacher_op, axis=0)
            high, low = split_high_low(student_t * STUDENT_SCALE)
            student_op = [student_gap, high, low, shift_rows(student_norm)]
            row_op[h, i, :, rows:] = jnp.concatenate(student_op, axis=0)

    safe = jnp.max(functools.reduce(jnp.maximum, norms)) <= SAFE_NORM
    key_pos = lax.broadcasted_iota(jnp.int32, (rows, rows), 0)
    row_pos = lax.broadcasted_iota(jnp.int32, (rows, rows), 1)

    def logits(h, i, j):
        keys = pl.ds(pl.multiple_of(j * rows, rows), rows)
        both = jnp.dot(key_op[h, keys, :], row_op[h, i], preferred_element_type=f32)
        return both[:, :rows], both[:, rows:]

    @pl.when(safe)
    def shifted_by_own_logit():
        key_grad[...] = jnp.zeros(key_grad.shape, f32)

        def exponentials(h, i, model, prob):
            upto = (i + 1) * rows
            op = row_op[h, i, :, model * rows : (model + 1) * rows]
            values = jnp.dot(key_op[h, :upto, :], op, preferred_element_type=f32)
            diagonal = jnp.where(key_pos <= row_pos, values[i * rows :], NEGATIVE)
            total = cross = jnp.zeros((8, rows), f32)
            for j in range(i + 1):
                value = diagonal if j == i else values[j * rows : (j + 1) * rows]
                exp = jnp.exp2(value)
                prob[i % 2, j] = exp
                total = total + fold(exp)
                weight = teacher_prob[i % 2, j] if model else exp
                cross = cross + fold(weight * value)
            return [jnp.sum(part, axis=0, keepdims=True) for part in (total, cross)]

        def weights(i, j, teacher_inv, student_inv):
            value = student_prob[i % 2, j] * student_inv - teacher_prob[i % 2, j] * teacher_inv
            weights_ref[j * rows : (j + 1) * rows, i * rows : (i + 1) * rows] = value.astype(bf16)

        def head_step(h, kl_total):
            inverse = None
            for i in range(tiles + 1):
                if i < tiles:
                    teacher_sum, teacher_cross = exponentials(h, i, 0, teacher_prob)
                    student_sum, student_cross = exponentials(h, i, 1, student_prob)
                if i:
                    upto = i * rows
                    for j in range(i):
                        weights(i - 1, j, *inverse)
                    row_grad[h, :, upto - rows : upto] = jnp.dot(
                        student_col[h, :, :upto],
                        weights_ref[:upto, upto - rows : upto],
                        preferred_element_type=f32,
                    )
                if i < tiles:
                    inverse = (1.0 / teacher_sum, 1.0 / student_sum)
                    kl_total = kl_total + (
                        (teacher_cross - student_cross) * inverse[0]
                        - jnp.log2(teacher_sum)
                        + jnp.log2(student_sum)
                    )
            for j in range(tiles):
                here = slice(j * rows, (j + 1) * rows)
                key_grad[here, :] = key_grad[here, :] + jnp.dot(
                    weights_ref[here, j * rows :],
                    student_pad[h, j * rows :, :],
                    preferred_element_type=f32,
                )
            return kl_total

        kl_sum[...] = lax.fori_loop(0, heads, head_step, jnp.zeros((1, rows), f32))

    @pl.when(jnp.logical_not(safe))
    def shifted_by_maximum():
        kl_sum[...] = jnp.zeros((1, rows), f32)
        key_grad[...] = jnp.zeros(key_grad.shape, f32)

        def masked(h, i, j):
            allowed = key_pos + j * rows <= row_pos + i * rows
            teacher, student = logits(h, i, j)
            return jnp.where(allowed, teacher, NEGATIVE), jnp.where(allowed, student, NEGATIVE)

        def row_step(step, _):
            h, i = step // tiles, step % tiles
            here = pl.ds(pl.multiple_of(i * rows, rows), rows)

            def advance(j, state):
                teacher_max, teacher_sum, cross_sum, student_max, student_sum = state
                teacher, student = masked(h, i, j)
                teacher_top = jnp.maximum(teacher_max, jnp.max(teacher, axis=0, keepdims=True))
                student_top = jnp.maximum(student_max, jnp.max(student, axis=0, keepdims=True))
                teacher_exp = jnp.exp2(teacher - teacher_top)
                student_exp = jnp.exp2(student - student_top)
                shrink = jnp.exp2(teacher_max - teacher_top)
                cross = jnp.sum(teacher_exp * (teacher - student), axis=0, keepdims=True)
                return (
                    teacher_top,
                    teacher_sum * shrink + jnp.sum(teacher_exp, axis=0, keepdims=True),
                    cross_sum * shrink + cross,
                    student_top,
                    student_sum * jnp.exp2(student_max - student_top)
                    + jnp.sum(student_exp, axis=0, keepdims=True),
                )

            lowest = jnp.full((1, rows), NEGATIVE, f32)
            zeros = jnp.zeros((1, rows), f32)
            teacher_max, teacher_sum, cross_sum, student_max, student_sum = lax.fori_loop(
                0, i + 1, advance, (lowest, zeros, zeros, lowest, zeros)
            )
            teacher_lse = teacher_max + jnp.log2(teacher_sum)
            student_lse = student_max + jnp.log2(student_sum)
            kl_sum[...] = kl_sum[...] + (cross_sum / teacher_sum - teacher_lse + student_lse)

            def spread(j, total):
                teacher, student = masked(h, i, j)
                value = jnp.exp2(student - student_lse) - jnp.exp2(teacher - teacher_lse)
                value = value.astype(bf16)
                keys = pl.ds(pl.multiple_of(j * rows, rows), rows)
                key_grad[keys, :] = key_grad[keys, :] + jnp.dot(
                    value, student_pad[h, here, :], preferred_element_type=f32
                )
                return total + jnp.dot(
                    student_col[h, :, keys], value, preferred_element_type=f32
                )

            row_grad[h, :, here] = lax.fori_loop(
                0, i + 1, spread, jnp.zeros((STUDENT_DIM, rows), f32)
            )
            return 0

        lax.fori_loop(0, heads * tiles, row_step, 0)

    if not last:
        return

    row_parts = [*done[::3], row_grad]
    key_parts = [*done[1::3], key_grad]
    total_width = len(row_parts) * student_width
    for i in range(tiles):
        here = slice(i * rows, (i + 1) * rows)
        columns = jnp.concatenate(
            [part[h, :, here] for part in row_parts for h in range(heads)], axis=0
        )
        lanes = jnp.concatenate([part[here, :] for part in key_parts], axis=1)
        grad_rows[here, :] = (columns.T + lanes) * (STUDENT_DIM**-0.5)
    grad_rows[pl.ds(live, window), :] = jnp.zeros((window, total_width), f32)
    kl_total = sum([ref[...] for ref in done[2::3]] + [kl_sum[...]])
    tokens = sum(counts_ref[b] for b in range(blocks))
    share = jnp.full((1, rows), math.log(2.0), f32) / (H_REL * tokens).astype(f32)
    tail = tail_rows(jnp.sum(kl_total * share, axis=1, keepdims=True), total_width)
    position = lax.broadcasted_iota(jnp.int32, (rows, window), 1)
    token = lax.broadcasted_iota(jnp.int32, (rows, window), 0)
    for k, (base, shift, count) in enumerate(places):
        place = ((position == token + shift) & (token < count)).astype(bf16)
        block = grad_rows[pl.ds(base, window), :].astype(bf16)
        send = late_block(out, k)
        moved = jnp.dot(place, block, preferred_element_type=f32)
        send[:rows, :] = moved.astype(bf16)
        send[rows:, :] = tail


def local(teacher_queries, student_queries, token_counts):
    f32, bf16 = jnp.float32, jnp.bfloat16
    blocks = lax.axis_size("seq")
    chips = blocks // 2
    groups = lax.axis_size("head")
    rows = teacher_queries.shape[0]
    heads = teacher_queries.shape[1] // TEACHER_DIM // blocks
    tiles = blocks * 3 // 4
    live = tiles * rows
    folded = heads * STUDENT_DIM == LANES
    chunks = 2 if folded else 1
    chunk_heads = heads // chunks
    teacher_width = chunk_heads * TEACHER_DIM
    student_width = chunk_heads * STUDENT_DIM
    if folded:
        send_shape = (chips, rows + rows // 2, LANES)
    else:
        send_shape = (chips, rows, teacher_width + student_width)
    vmem = pl.BlockSpec(memory_space=pltpu.VMEM)
    smem = pl.BlockSpec(memory_space=pltpu.SMEM)
    params = pltpu.CompilerParams(vmem_limit_bytes=40 * 1024 * 1024)
    me = lax.axis_index("seq").reshape(1)
    far_first = sorted(range(1, chips), key=lambda k: -k.bit_count())

    def call(kernel, name, out_shape, *inputs):
        return pl.pallas_call(
            kernel,
            in_specs=[vmem] * len(inputs),
            out_specs=[vmem] * len(out_shape),
            out_shape=out_shape,
            compiler_params=params,
            name=name,
        )(*inputs)

    def to_chips(sends):
        return [
            lax.ppermute(send, "seq", [(i, i ^ (2 * k)) for i in range(blocks)])
            for k, send in enumerate(sends, 1)
        ]

    def to_other_core(send):
        return lax.ppermute(send, "seq", [(i, i ^ 1) for i in range(blocks)])

    def exchange(kept, swapped):
        swapped = to_other_core(swapped)
        message = jax.ShapeDtypeStruct((2,) + kept.shape[1:], bf16)
        sends = call(merge_kernel, "merge", [message] * (chips - 1), kept, swapped)
        return [kept, swapped, *to_chips(sends)]

    def exchange_late(own, other, *sends):
        messages = to_chips(sends)
        forward = jax.ShapeDtypeStruct((chips, own.shape[0] - TAIL, own.shape[1]), bf16)
        kl = jax.ShapeDtypeStruct((1, own.shape[1]), f32)
        forward, kl = call(forward_kernel, "forward", [forward, kl], own, other, *messages)
        return [own, to_other_core(forward), *messages], kl

    packed = jax.ShapeDtypeStruct(send_shape, bf16)
    first = jax.ShapeDtypeStruct(send_shape[1:], bf16)
    order = [0, 1, *range(2, blocks, 2), *range(3, blocks, 2)] if folded else None
    if folded:
        anywhere = pl.BlockSpec(memory_space=pltpu.HBM)
        sends = pl.pallas_call(
            functools.partial(pack_folded_kernel, blocks, chunks),
            in_specs=[smem, anywhere, anywhere],
            out_specs=[vmem] * (blocks + 2 * chunks - 2),
            out_shape=[first] * blocks + [packed] * (2 * chunks - 2),
            scratch_shapes=[
                pltpu.VMEM(student_queries.shape, bf16),
                pltpu.SemaphoreType.DMA((chunks * blocks + 1,)),
            ],
            compiler_params=pltpu.CompilerParams(vmem_limit_bytes=52 * 1024 * 1024),
            name="pack",
        )(me, teacher_queries, student_queries)
    else:
        sends = pl.pallas_call(
            functools.partial(pack_plain_kernel, blocks),
            in_specs=[smem, vmem, vmem],
            out_specs=[vmem] * 2,
            out_shape=[packed] * 2,
            compiler_params=params,
            name="pack",
        )(me, teacher_queries, student_queries)
    incoming = []
    if folded:
        incoming.append(
            [sends[0]]
            + [
                lax.ppermute(sends[k], "seq", [(i, i ^ k) for i in range(blocks)])
                for k in order[1:]
            ]
        )
        sends = sends[blocks:]
    incoming += [exchange(*pair) for pair in zip(sends[::2], sends[1::2])]

    result = [
        jax.ShapeDtypeStruct((chunk_heads, STUDENT_DIM, live), f32),
        jax.ShapeDtypeStruct((live, student_width), f32),
        jax.ShapeDtypeStruct((1, rows), f32),
    ]
    block = jax.ShapeDtypeStruct((rows + TAIL, heads * STUDENT_DIM), bf16)
    messages = [block] * 2 + [jax.ShapeDtypeStruct((2,) + block.shape, bf16)] * (chips - 1)
    pairs = chunk_heads * tiles * (tiles + 1) // 2 * rows * rows
    done = []
    for c in range(chunks):
        last = c == chunks - 1
        scratch = [
            pltpu.VMEM((live + rows + PAD, teacher_width + student_width), f32),
            pltpu.VMEM((chunk_heads, live, DEPTH), bf16),
            pltpu.VMEM((chunk_heads, tiles, DEPTH, 2 * rows), bf16),
            pltpu.VMEM((chunk_heads, STUDENT_DIM, live), bf16),
            pltpu.VMEM((chunk_heads, live, student_width), bf16),
            pltpu.VMEM((2, tiles, rows, rows), f32),
            pltpu.VMEM((2, tiles, rows, rows), f32),
            pltpu.VMEM((live, live), bf16),
        ]
        if last:
            scratch += [pltpu.VMEM(part.shape, f32) for part in result]
            scratch.append(pltpu.VMEM((live + rows + PAD, heads * STUDENT_DIM), f32))
        inputs = [me, token_counts, *incoming[c], *done]
        done += pl.pallas_call(
            functools.partial(
                relation_kernel,
                folded,
                chunk_heads,
                tiles,
                order if c == 0 else None,
                len(incoming[c]),
                c,
                last,
            ),
            in_specs=[smem, smem] + [vmem] * (len(inputs) - 2),
            out_specs=[vmem] * len(messages if last else result),
            out_shape=messages if last else result,
            scratch_shapes=scratch,
            compiler_params=params,
            cost_estimate=pl.CostEstimate(
                flops=4 * pairs * DEPTH, bytes_accessed=8 * pairs, transcendentals=2 * pairs
            ),
            name="relation",
        )(*inputs)
    returned, kl = exchange_late(*done[-len(messages) :])
    kl = kl + to_other_core(kl)
    kls = [kl] + [
        lax.ppermute(kl, "head", [(i, i ^ k) for i in range(groups)]) for k in range(1, groups)
    ]
    grad = pl.pallas_call(
        unpack_kernel,
        in_specs=[smem] + [vmem] * len(returned),
        out_specs=vmem,
        out_shape=jax.ShapeDtypeStruct((rows, student_queries.shape[1]), f32),
        compiler_params=params,
        name="unpack",
    )(me, *returned)
    grad, *kls = lax.optimization_barrier((grad, *kls))
    return (grad, pair_sum(kls)[0, 0])


def solution(mesh):
    return jax.shard_map(
        local,
        mesh=mesh,
        in_specs=(P("seq", "head"), P("seq", "head"), P()),
        out_specs=(P("seq", "head"), P()),
        check_vma=False,
    )
```

```python
import functools
import math

import jax
import jax.numpy as jnp
from jax import lax
from jax.experimental import pallas as pl
from jax.experimental.pallas import tpu as pltpu
from jax.sharding import PartitionSpec as P

DT = 8192
DS = 4096
H_REL = 128
TEACHER_DIM = DT // H_REL
STUDENT_DIM = DS // H_REL

NEGATIVE = -1e30
LOG2E = math.log2(math.e)
TEACHER_SCALE = LOG2E * TEACHER_DIM**-0.5
STUDENT_SCALE = LOG2E * STUDENT_DIM**-0.5
PAD = 8
LANES = 128
TAIL = 16
DEPTH = 256
SAFE_NORM = 320.0


def split_high_low(values):
    high = values.astype(jnp.bfloat16)
    low = (values - high.astype(jnp.float32)).astype(jnp.bfloat16)
    return high, low


def split_three(values):
    high = values.astype(jnp.bfloat16)
    rest = values - high.astype(jnp.float32)
    return (high,) + split_high_low(rest)


def at_columns(index, count, width, act):
    if width % LANES == 0:
        act(pl.ds(pl.multiple_of(index * width, LANES), width))
    else:
        for part in range(count):
            pl.when(index == part)(functools.partial(act, pl.ds(part * width, width)))


def pack_folded_kernel(blocks, chunks, me_ref, teacher_ref, student_ref, *refs):
    sends, student, sems = refs[:-2], refs[-2], refs[-1]
    rows = teacher_ref.shape[0]
    half = rows // 2

    def block(chunk, k):
        if chunk == 0:
            return sends[k]
        return sends[blocks + 2 * (chunk - 1) + k % 2].at[k // 2]

    copies = [pltpu.make_async_copy(student_ref, student, sems.at[chunks * blocks])]
    for chunk in range(chunks):
        for k in range(blocks):
            to = jnp.bitwise_xor(me_ref[0], k)
            at = pl.multiple_of((to * chunks + chunk) * LANES, LANES)
            copies.append(
                pltpu.make_async_copy(
                    teacher_ref.at[:, pl.ds(at, LANES)],
                    block(chunk, k).at[pl.ds(0, rows)],
                    sems.at[chunk * blocks + k],
                )
            )
    for copy in copies:
        copy.start()
    copies[0].wait()
    for k in range(blocks):
        to = jnp.bitwise_xor(me_ref[0], k)
        lanes = pl.ds(pl.multiple_of(to * LANES, LANES), LANES)
        top, bottom = student[:half, lanes], student[half:, lanes]
        for chunk in range(chunks):
            part = slice(chunk * (LANES // 2), (chunk + 1) * (LANES // 2))
            block(chunk, k)[rows:, :] = jnp.concatenate([top[:, part], bottom[:, part]], axis=1)
    for copy in copies[1:]:
        copy.wait()


def pack_plain_kernel(blocks, me_ref, teacher_ref, student_ref, *sends):
    teacher_width = teacher_ref.shape[1] // blocks
    student_width = student_ref.shape[1] // blocks
    for core in range(2):
        for k in range(blocks // 2):
            to = jnp.bitwise_xor(me_ref[0], 2 * k + core)

            def put_teacher(columns, send=sends[core], k=k):
                send[k, :, :teacher_width] = teacher_ref[:, columns]

            def put_student(columns, send=sends[core], k=k):
                send[k, :, teacher_width:] = student_ref[:, columns]

            at_columns(to, blocks, teacher_width, put_teacher)
            at_columns(to, blocks, student_width, put_student)


def pair_sum(parts):
    while len(parts) > 1:
        parts = [a + b for a, b in zip(parts[::2], parts[1::2])]
    return parts[0]


def tail_rows(value, width):
    thirds = [part.astype(jnp.float32) for part in split_three(value)]
    line = lax.broadcasted_iota(jnp.int32, (TAIL, width), 0)
    tail = jnp.where(line == 0, thirds[0], 0.0)
    tail = jnp.where(line == 1, thirds[1], tail)
    return jnp.where(line == 2, thirds[2], tail).astype(jnp.bfloat16)


def merge_kernel(chips, kept_ref, swapped_ref, *refs):
    kls, sends = refs[: 1 - chips], refs[1 - chips :]
    rows = kept_ref.shape[1]
    tail = tail_rows(pair_sum([kl[...] for kl in kls]), kept_ref.shape[2]) if kls else None
    for k, send in enumerate(sends):
        send[0, :rows, :] = kept_ref[k + 1]
        send[1, :rows, :] = swapped_ref[k + 1]
        if kls:
            send[0, rows:, :] = tail
            send[1, rows:, :] = tail


def arrived(refs):
    return [refs[0].at[0], refs[1].at[0]] + [ref.at[core] for ref in refs[2:] for core in range(2)]


def sum_kernel(groups, counts_ref, *refs):
    out_ref = refs[-1]
    own = pair_sum([ref[...] for ref in refs[:groups]])
    tails = [ref[0, ref.shape[1] - TAIL :, :].astype(jnp.float32) for ref in refs[groups:-1]]
    total = pair_sum(
        [jnp.broadcast_to(own, out_ref.shape)] + [jnp.sum(t, axis=0, keepdims=True) for t in tails]
    )
    tokens = sum(counts_ref[b] for b in range(counts_ref.shape[0]))
    out_ref[...] = total / (H_REL * tokens).astype(jnp.float32)


def unpack_kernel(me_ref, *refs):
    grad_ref = refs[-1]
    blocks = arrived(refs[:-1])
    for k, block in enumerate(blocks):

        def put(columns, block=block):
            grad_ref[:, columns] = block[: grad_ref.shape[0], :].astype(jnp.float32)

        at_columns(jnp.bitwise_xor(me_ref[0], k), len(blocks), block.shape[1], put)


def fold(values):
    rows, columns = values.shape
    return jnp.sum(values.reshape(rows // 8, 8, columns), axis=0)


def relation_kernel(folded, heads, tiles, order, n_in, n_done, last, me_ref, counts_ref, *refs):
    if order:
        sources = [refs[order.index(k)] for k in range(n_in)]
    else:
        sources = arrived(refs[:n_in])
    done = refs[n_in : n_in + 3 * n_done]
    rest = list(refs[n_in + 3 * n_done :])
    out, rest = rest[:3], rest[3:]
    pack, key_op, row_op, student_col, student_pad, teacher_prob, student_prob = rest[:7]
    if last:
        row_grad, key_grad, kl_sum, grad_rows = rest[7:]
    else:
        row_grad, key_grad, kl_sum = out
    f32, bf16 = jnp.float32, jnp.bfloat16
    blocks = len(sources)
    rows = teacher_prob.shape[2]
    half = rows // 2
    live = tiles * rows
    window = rows + PAD
    student_at = heads * TEACHER_DIM
    student_width = heads * STUDENT_DIM
    filled = 2 * TEACHER_DIM + 2 * STUDENT_DIM

    position = lax.broadcasted_iota(jnp.int32, (window, rows), 0)
    token = lax.broadcasted_iota(jnp.int32, (window, rows), 1)
    pack[...] = jnp.zeros(pack.shape, f32)
    places = []
    for k in range(blocks):
        owner = jnp.bitwise_xor(me_ref[0], k)
        start = sum(jnp.where(b < owner, counts_ref[b], 0) for b in range(blocks))
        base = pl.multiple_of(start // PAD * PAD, PAD)
        places.append((base, start - base, counts_ref[owner]))
    for source, (base, shift, count) in zip(sources, places):
        place = ((position == token + shift) & (token < count)).astype(bf16)
        here = pl.ds(base, window)
        if folded:
            moved = jnp.dot(place, source[:rows, :], preferred_element_type=f32)
            pack[here, :student_at] = pack[here, :student_at] + moved
            student = source[rows:, :]
            moved = jnp.dot(
                place[:, :half], student[:, :student_width], preferred_element_type=f32
            ) + jnp.dot(place[:, half:], student[:, student_width:], preferred_element_type=f32)
            pack[here, student_at:] = pack[here, student_at:] + moved
        else:
            moved = jnp.dot(place, source[...], preferred_element_type=f32)
            pack[here, :] = pack[here, :] + moved

    ones = jnp.ones((rows, DEPTH - filled), bf16)
    spare = lax.broadcasted_iota(jnp.int32, (DEPTH - filled, rows), 0)
    teacher_gap = jnp.zeros((2 * STUDENT_DIM, rows), bf16)
    student_gap = jnp.zeros((2 * TEACHER_DIM, rows), bf16)
    lane_head = lax.broadcasted_iota(jnp.int32, (rows, student_width), 1) // STUDENT_DIM
    norms = []

    def shift_rows(norm):
        parts = [part.astype(f32) for part in split_three(-norm)]
        out = jnp.where(spare == 0, parts[0], 0.0)
        out = jnp.where(spare == 1, parts[1], out)
        return jnp.where(spare == 2, parts[2], out).astype(bf16)

    for i in range(tiles):
        here = pl.ds(i * rows, rows)
        tile = pack[here, :]
        tile_t = tile.T
        tile_b = tile.astype(bf16)
        tile_s = tile[:, student_at:]
        for h in range(heads):
            tb = tile_b[:, h * TEACHER_DIM : (h + 1) * TEACHER_DIM]
            at = student_at + h * STUDENT_DIM
            sb = tile_b[:, at : at + STUDENT_DIM]
            key_op[h, here, :] = jnp.concatenate([tb, tb, sb, sb, ones], axis=1)
            teacher_t = tile_t[h * TEACHER_DIM : (h + 1) * TEACHER_DIM, :]
            student_t = tile_t[at : at + STUDENT_DIM, :]
            student_col[h, :, here] = student_t.astype(bf16)
            student_pad[h, here, :] = jnp.where(lane_head == h, tile_s, 0.0).astype(bf16)
            teacher_norm = TEACHER_SCALE * jnp.sum(teacher_t * teacher_t, axis=0, keepdims=True)
            student_norm = STUDENT_SCALE * jnp.sum(student_t * student_t, axis=0, keepdims=True)
            norms += [teacher_norm, student_norm]
            high, low = split_high_low(teacher_t * TEACHER_SCALE)
            teacher_op = [high, low, teacher_gap, shift_rows(teacher_norm)]
            row_op[h, i, :, :rows] = jnp.concatenate(teacher_op, axis=0)
            high, low = split_high_low(student_t * STUDENT_SCALE)
            student_op = [student_gap, high, low, shift_rows(student_norm)]
            row_op[h, i, :, rows:] = jnp.concatenate(student_op, axis=0)

    safe = jnp.max(functools.reduce(jnp.maximum, norms)) <= SAFE_NORM
    key_pos = lax.broadcasted_iota(jnp.int32, (rows, rows), 0)
    row_pos = lax.broadcasted_iota(jnp.int32, (rows, rows), 1)

    def logits(h, i, j):
        keys = pl.ds(pl.multiple_of(j * rows, rows), rows)
        both = jnp.dot(key_op[h, keys, :], row_op[h, i], preferred_element_type=f32)
        return both[:, :rows], both[:, rows:]

    @pl.when(safe)
    def shifted_by_own_logit():
        key_grad[...] = jnp.zeros(key_grad.shape, f32)

        def exponentials(h, i, j, sums):
            both = jnp.dot(
                key_op[h, j * rows : (j + 1) * rows, :], row_op[h, i], preferred_element_type=f32
            )
            teacher, student = both[:, :rows], both[:, rows:]
            if i == j:
                teacher = jnp.where(key_pos <= row_pos, teacher, NEGATIVE)
                student = jnp.where(key_pos <= row_pos, student, NEGATIVE)
            teacher_exp = jnp.exp2(teacher)
            student_exp = jnp.exp2(student)
            teacher_prob[i % 2, j] = teacher_exp
            student_prob[i % 2, j] = student_exp
            new = (fold(teacher_exp), fold(student_exp), fold(teacher_exp * (teacher - student)))
            return new if sums is None else tuple(a + b for a, b in zip(sums, new))

        def gradients(h, i, j, inverse, row_total):
            weights = (
                student_prob[i % 2, j] * inverse[1] - teacher_prob[i % 2, j] * inverse[0]
            ).astype(bf16)
            keys, here = slice(j * rows, (j + 1) * rows), slice(i * rows, (i + 1) * rows)
            key_grad[keys, :] = key_grad[keys, :] + jnp.dot(
                weights, student_pad[h, here, :], preferred_element_type=f32
            )
            return row_total + jnp.dot(
                student_col[h, :, keys], weights, preferred_element_type=f32
            )

        def head_step(h, kl_total):
            inverse = None
            for i in range(tiles + 1):
                sums = None
                row_total = jnp.zeros((STUDENT_DIM, rows), f32)
                for j in range(i + 1):
                    if i < tiles:
                        sums = exponentials(h, i, j, sums)
                    if j < i:
                        row_total = gradients(h, i - 1, j, inverse, row_total)
                if i:
                    row_grad[h, :, (i - 1) * rows : i * rows] = row_total
                if i < tiles:
                    teacher_sum, student_sum, cross_sum = [
                        jnp.sum(part, axis=0, keepdims=True) for part in sums
                    ]
                    inverse = (1.0 / teacher_sum, 1.0 / student_sum)
                    kl_total = kl_total + (
                        cross_sum * inverse[0] - jnp.log2(teacher_sum) + jnp.log2(student_sum)
                    )
            return kl_total

        kl_sum[...] = lax.fori_loop(0, heads, head_step, jnp.zeros((1, rows), f32))

    @pl.when(jnp.logical_not(safe))
    def shifted_by_maximum():
        kl_sum[...] = jnp.zeros((1, rows), f32)
        key_grad[...] = jnp.zeros(key_grad.shape, f32)

        def masked(h, i, j):
            allowed = key_pos + j * rows <= row_pos + i * rows
            teacher, student = logits(h, i, j)
            return jnp.where(allowed, teacher, NEGATIVE), jnp.where(allowed, student, NEGATIVE)

        def row_step(step, _):
            h, i = step // tiles, step % tiles
            here = pl.ds(pl.multiple_of(i * rows, rows), rows)

            def advance(j, state):
                teacher_max, teacher_sum, cross_sum, student_max, student_sum = state
                teacher, student = masked(h, i, j)
                teacher_top = jnp.maximum(teacher_max, jnp.max(teacher, axis=0, keepdims=True))
                student_top = jnp.maximum(student_max, jnp.max(student, axis=0, keepdims=True))
                teacher_exp = jnp.exp2(teacher - teacher_top)
                student_exp = jnp.exp2(student - student_top)
                shrink = jnp.exp2(teacher_max - teacher_top)
                cross = jnp.sum(teacher_exp * (teacher - student), axis=0, keepdims=True)
                return (
                    teacher_top,
                    teacher_sum * shrink + jnp.sum(teacher_exp, axis=0, keepdims=True),
                    cross_sum * shrink + cross,
                    student_top,
                    student_sum * jnp.exp2(student_max - student_top)
                    + jnp.sum(student_exp, axis=0, keepdims=True),
                )

            lowest = jnp.full((1, rows), NEGATIVE, f32)
            zeros = jnp.zeros((1, rows), f32)
            teacher_max, teacher_sum, cross_sum, student_max, student_sum = lax.fori_loop(
                0, i + 1, advance, (lowest, zeros, zeros, lowest, zeros)
            )
            teacher_lse = teacher_max + jnp.log2(teacher_sum)
            student_lse = student_max + jnp.log2(student_sum)
            kl_sum[...] = kl_sum[...] + (cross_sum / teacher_sum - teacher_lse + student_lse)

            def spread(j, total):
                teacher, student = masked(h, i, j)
                value = jnp.exp2(student - student_lse) - jnp.exp2(teacher - teacher_lse)
                value = value.astype(bf16)
                keys = pl.ds(pl.multiple_of(j * rows, rows), rows)
                key_grad[keys, :] = key_grad[keys, :] + jnp.dot(
                    value, student_pad[h, here, :], preferred_element_type=f32
                )
                return total + jnp.dot(
                    student_col[h, :, keys], value, preferred_element_type=f32
                )

            row_grad[h, :, here] = lax.fori_loop(
                0, i + 1, spread, jnp.zeros((STUDENT_DIM, rows), f32)
            )
            return 0

        lax.fori_loop(0, heads * tiles, row_step, 0)

    if not last:
        return

    row_parts = [*done[::3], row_grad]
    key_parts = [*done[1::3], key_grad]
    total_width = len(row_parts) * student_width
    for i in range(tiles):
        here = slice(i * rows, (i + 1) * rows)
        columns = jnp.concatenate(
            [part[h, :, here] for part in row_parts for h in range(heads)], axis=0
        )
        lanes = jnp.concatenate([part[here, :] for part in key_parts], axis=1)
        grad_rows[here, :] = (columns.T + lanes) * (STUDENT_DIM**-0.5)
    grad_rows[pl.ds(live, window), :] = jnp.zeros((window, total_width), f32)
    kl_total = sum([ref[...] for ref in done[2::3]] + [kl_sum[...]])
    out[2][...] = jnp.broadcast_to(
        jnp.sum(kl_total, axis=1, keepdims=True) * math.log(2.0), out[2].shape
    )
    position = lax.broadcasted_iota(jnp.int32, (rows, window), 1)
    token = lax.broadcasted_iota(jnp.int32, (rows, window), 0)
    for k, (base, shift, count) in enumerate(places):
        place = ((position == token + shift) & (token < count)).astype(bf16)
        block = grad_rows[pl.ds(base, window), :].astype(bf16)
        out[k % 2][k // 2] = jnp.dot(place, block, preferred_element_type=f32).astype(bf16)


def local(teacher_queries, student_queries, token_counts):
    f32, bf16 = jnp.float32, jnp.bfloat16
    blocks = lax.axis_size("seq")
    chips = blocks // 2
    groups = lax.axis_size("head")
    rows = teacher_queries.shape[0]
    heads = teacher_queries.shape[1] // TEACHER_DIM // blocks
    tiles = blocks * 3 // 4
    live = tiles * rows
    folded = heads * STUDENT_DIM == LANES
    chunks = 2 if folded else 1
    chunk_heads = heads // chunks
    teacher_width = chunk_heads * TEACHER_DIM
    student_width = chunk_heads * STUDENT_DIM
    if folded:
        send_shape = (chips, rows + rows // 2, LANES)
    else:
        send_shape = (chips, rows, teacher_width + student_width)
    vmem = pl.BlockSpec(memory_space=pltpu.VMEM)
    smem = pl.BlockSpec(memory_space=pltpu.SMEM)
    params = pltpu.CompilerParams(vmem_limit_bytes=40 * 1024 * 1024)
    me = lax.axis_index("seq").reshape(1)
    far_first = sorted(range(1, chips), key=lambda k: -k.bit_count())

    def exchange(kept, swapped, kls=()):
        swapped = lax.ppermute(swapped, "seq", [(i, i ^ 1) for i in range(blocks)])
        shape = (2, kept.shape[1] + (TAIL if kls else 0), kept.shape[2])
        sends = pl.pallas_call(
            functools.partial(merge_kernel, chips),
            in_specs=[vmem] * (2 + len(kls)),
            out_specs=[vmem] * (chips - 1),
            out_shape=[jax.ShapeDtypeStruct(shape, bf16)] * (chips - 1),
            compiler_params=params,
            name="merge",
        )(kept, swapped, *kls)
        out = [None] * (chips - 1)
        for k in far_first:
            pairs = [(i, i ^ (2 * k)) for i in range(blocks)]
            out[k - 1] = lax.ppermute(sends[k - 1], "seq", pairs)
        return [kept, swapped] + out

    packed = jax.ShapeDtypeStruct(send_shape, bf16)
    first = jax.ShapeDtypeStruct(send_shape[1:], bf16)
    order = [0, 1, *range(2, blocks, 2), *range(3, blocks, 2)] if folded else None
    if folded:
        anywhere = pl.BlockSpec(memory_space=pltpu.HBM)
        sends = pl.pallas_call(
            functools.partial(pack_folded_kernel, blocks, chunks),
            in_specs=[smem, anywhere, anywhere],
            out_specs=[vmem] * (blocks + 2 * chunks - 2),
            out_shape=[first] * blocks + [packed] * (2 * chunks - 2),
            scratch_shapes=[
                pltpu.VMEM(student_queries.shape, bf16),
                pltpu.SemaphoreType.DMA((chunks * blocks + 1,)),
            ],
            compiler_params=pltpu.CompilerParams(vmem_limit_bytes=52 * 1024 * 1024),
            name="pack",
        )(me, teacher_queries, student_queries)
    else:
        sends = pl.pallas_call(
            functools.partial(pack_plain_kernel, blocks),
            in_specs=[smem, vmem, vmem],
            out_specs=[vmem] * 2,
            out_shape=[packed] * 2,
            compiler_params=params,
            name="pack",
        )(me, teacher_queries, student_queries)
    incoming = []
    if folded:
        incoming.append(
            [sends[0]]
            + [
                lax.ppermute(sends[k], "seq", [(i, i ^ k) for i in range(blocks)])
                for k in order[1:]
            ]
        )
        sends = sends[blocks:]
    incoming += [exchange(*pair) for pair in zip(sends[::2], sends[1::2])]

    result = [
        jax.ShapeDtypeStruct((chunk_heads, STUDENT_DIM, live), f32),
        jax.ShapeDtypeStruct((live, student_width), f32),
        jax.ShapeDtypeStruct((1, rows), f32),
    ]
    message = jax.ShapeDtypeStruct((chips, rows, heads * STUDENT_DIM), bf16)
    divergence = jax.ShapeDtypeStruct((1, heads * STUDENT_DIM), f32)
    pairs = chunk_heads * tiles * (tiles + 1) // 2 * rows * rows
    done = []
    for c in range(chunks):
        last = c == chunks - 1
        scratch = [
            pltpu.VMEM((live + rows + PAD, teacher_width + student_width), f32),
            pltpu.VMEM((chunk_heads, live, DEPTH), bf16),
            pltpu.VMEM((chunk_heads, tiles, DEPTH, 2 * rows), bf16),
            pltpu.VMEM((chunk_heads, STUDENT_DIM, live), bf16),
            pltpu.VMEM((chunk_heads, live, student_width), bf16),
            pltpu.VMEM((2, tiles, rows, rows), f32),
            pltpu.VMEM((2, tiles, rows, rows), f32),
        ]
        if last:
            scratch += [pltpu.VMEM(part.shape, f32) for part in result]
            scratch.append(pltpu.VMEM((live + rows + PAD, heads * STUDENT_DIM), f32))
        inputs = [me, token_counts, *incoming[c], *done]
        done += pl.pallas_call(
            functools.partial(
                relation_kernel,
                folded,
                chunk_heads,
                tiles,
                order if c == 0 else None,
                len(incoming[c]),
                c,
                last,
            ),
            in_specs=[smem, smem] + [vmem] * (len(inputs) - 2),
            out_specs=[vmem] * 3,
            out_shape=[message, message, divergence] if last else result,
            scratch_shapes=scratch,
            compiler_params=params,
            cost_estimate=pl.CostEstimate(
                flops=4 * pairs * DEPTH, bytes_accessed=8 * pairs, transcendentals=2 * pairs
            ),
            name="relation",
        )(*inputs)
    kept, swapped, kl = done[-3:]
    kls = [kl]
    for bit in range(groups.bit_length() - 1):
        own = pair_sum(kls)
        pairs = [(i, i ^ (1 << bit)) for i in range(groups)]
        kls = [own, lax.ppermute(own, "head", pairs)]
    returned = exchange(kept, swapped, kls)
    half_loss = pl.pallas_call(
        functools.partial(sum_kernel, len(kls)),
        in_specs=[smem] + [vmem] * (len(kls) + chips - 1),
        out_specs=vmem,
        out_shape=divergence,
        compiler_params=params,
        name="sum_kl",
    )(token_counts, *kls, *returned[2:])
    loss = half_loss + lax.ppermute(half_loss, "seq", [(i, i ^ 1) for i in range(blocks)])
    grad = pl.pallas_call(
        unpack_kernel,
        in_specs=[smem] + [vmem] * len(returned),
        out_specs=vmem,
        out_shape=jax.ShapeDtypeStruct((rows, student_queries.shape[1]), f32),
        compiler_params=params,
        name="unpack",
    )(me, *returned)
    return (grad, loss[0, 0])


def solution(mesh):
    return jax.shard_map(
        local,
        mesh=mesh,
        in_specs=(P("seq", "head"), P("seq", "head"), P()),
        out_specs=(P("seq", "head"), P()),
        check_vma=False,
    )
```

```python
import functools
import math

import jax
import jax.numpy as jnp
from jax import lax
from jax.experimental import pallas as pl
from jax.experimental.pallas import tpu as pltpu
from jax.sharding import PartitionSpec as P

DT = 8192
DS = 4096
H_REL = 128
TEACHER_DIM = DT // H_REL
STUDENT_DIM = DS // H_REL

NEGATIVE = -1e30
LOG2E = math.log2(math.e)
TEACHER_SCALE = LOG2E * TEACHER_DIM**-0.5
STUDENT_SCALE = LOG2E * STUDENT_DIM**-0.5
PAD = 8
LANES = 128
TAIL = 16
DEPTH = 256
SAFE_NORM = 320.0


def split_high_low(values):
    high = values.astype(jnp.bfloat16)
    low = (values - high.astype(jnp.float32)).astype(jnp.bfloat16)
    return high, low


def split_three(values):
    high = values.astype(jnp.bfloat16)
    rest = values - high.astype(jnp.float32)
    return (high,) + split_high_low(rest)


def at_columns(index, count, width, act):
    if width % LANES == 0:
        act(pl.ds(pl.multiple_of(index * width, LANES), width))
    else:
        for part in range(count):
            pl.when(index == part)(functools.partial(act, pl.ds(part * width, width)))


def pack_folded_kernel(blocks, chunks, me_ref, teacher_ref, student_ref, *refs):
    sends, student, sems = refs[:-2], refs[-2], refs[-1]
    rows = teacher_ref.shape[0]
    half = rows // 2

    def block(chunk, k):
        if chunk == 0:
            return sends[k]
        return sends[blocks + 2 * (chunk - 1) + k % 2].at[k // 2]

    copies = [pltpu.make_async_copy(student_ref, student, sems.at[chunks * blocks])]
    for chunk in range(chunks):
        for k in range(blocks):
            to = jnp.bitwise_xor(me_ref[0], k)
            at = pl.multiple_of((to * chunks + chunk) * LANES, LANES)
            copies.append(
                pltpu.make_async_copy(
                    teacher_ref.at[:, pl.ds(at, LANES)],
                    block(chunk, k).at[pl.ds(0, rows)],
                    sems.at[chunk * blocks + k],
                )
            )
    for copy in copies:
        copy.start()
    copies[0].wait()
    for k in range(blocks):
        to = jnp.bitwise_xor(me_ref[0], k)
        lanes = pl.ds(pl.multiple_of(to * LANES, LANES), LANES)
        top, bottom = student[:half, lanes], student[half:, lanes]
        for chunk in range(chunks):
            part = slice(chunk * (LANES // 2), (chunk + 1) * (LANES // 2))
            block(chunk, k)[rows:, :] = jnp.concatenate([top[:, part], bottom[:, part]], axis=1)
    for copy in copies[1:]:
        copy.wait()


def pack_plain_kernel(blocks, me_ref, teacher_ref, student_ref, *sends):
    teacher_width = teacher_ref.shape[1] // blocks
    student_width = student_ref.shape[1] // blocks
    for core in range(2):
        for k in range(blocks // 2):
            to = jnp.bitwise_xor(me_ref[0], 2 * k + core)

            def put_teacher(columns, send=sends[core], k=k):
                send[k, :, :teacher_width] = teacher_ref[:, columns]

            def put_student(columns, send=sends[core], k=k):
                send[k, :, teacher_width:] = student_ref[:, columns]

            at_columns(to, blocks, teacher_width, put_teacher)
            at_columns(to, blocks, student_width, put_student)


def pair_sum(parts):
    while len(parts) > 1:
        parts = [a + b for a, b in zip(parts[::2], parts[1::2])]
    return parts[0]


def tail_rows(value, width):
    thirds = [part.astype(jnp.float32) for part in split_three(value)]
    line = lax.broadcasted_iota(jnp.int32, (TAIL, width), 0)
    tail = jnp.where(line == 0, thirds[0], 0.0)
    tail = jnp.where(line == 1, thirds[1], tail)
    return jnp.where(line == 2, thirds[2], tail).astype(jnp.bfloat16)


def merge_kernel(chips, kept_ref, swapped_ref, *refs):
    kls, sends = refs[: 1 - chips], refs[1 - chips :]
    rows = kept_ref.shape[1]
    tail = tail_rows(pair_sum([kl[...] for kl in kls]), kept_ref.shape[2]) if kls else None
    for k, send in enumerate(sends):
        send[0, :rows, :] = kept_ref[k + 1]
        send[1, :rows, :] = swapped_ref[k + 1]
        if kls:
            send[0, rows:, :] = tail
            send[1, rows:, :] = tail


def arrived(refs):
    return [refs[0].at[0], refs[1].at[0]] + [ref.at[core] for ref in refs[2:] for core in range(2)]


def unpack_kernel(n_kl, me_ref, *refs):
    kls, returned, (grad_ref, loss_ref) = refs[:n_kl], refs[n_kl:-2], refs[-2:]
    rows = grad_ref.shape[0]
    blocks = arrived(returned)
    for k, block in enumerate(blocks):

        def put(columns, block=block):
            grad_ref[:, columns] = block[:rows, :].astype(jnp.float32)

        at_columns(jnp.bitwise_xor(me_ref[0], k), len(blocks), block.shape[1], put)
    own = tail_rows(pair_sum([kl[...] for kl in kls]), kls[0].shape[1])
    tails = [own] + [ref[0, rows:, :] for ref in returned[2:]]
    loss_ref[...] = pair_sum(
        [jnp.sum(tail.astype(jnp.float32), axis=0, keepdims=True) for tail in tails]
    )


def fold(values):
    rows, columns = values.shape
    return jnp.sum(values.reshape(rows // 8, 8, columns), axis=0)


def relation_kernel(folded, heads, tiles, order, n_in, n_done, last, me_ref, counts_ref, *refs):
    if order:
        sources = [refs[order.index(k)] for k in range(n_in)]
    else:
        sources = arrived(refs[:n_in])
    done = refs[n_in : n_in + 3 * n_done]
    rest = list(refs[n_in + 3 * n_done :])
    out, rest = rest[:3], rest[3:]
    pack, key_op, row_op, student_col, student_pad, teacher_prob, student_prob, weights_ref = rest[:8]
    if last:
        row_grad, key_grad, kl_sum, grad_rows = rest[8:]
    else:
        row_grad, key_grad, kl_sum = out
    f32, bf16 = jnp.float32, jnp.bfloat16
    blocks = len(sources)
    rows = teacher_prob.shape[2]
    half = rows // 2
    live = tiles * rows
    window = rows + PAD
    student_at = heads * TEACHER_DIM
    student_width = heads * STUDENT_DIM
    filled = 2 * TEACHER_DIM + 2 * STUDENT_DIM

    position = lax.broadcasted_iota(jnp.int32, (window, rows), 0)
    token = lax.broadcasted_iota(jnp.int32, (window, rows), 1)
    pack[...] = jnp.zeros(pack.shape, f32)
    places = []
    for k in range(blocks):
        owner = jnp.bitwise_xor(me_ref[0], k)
        start = sum(jnp.where(b < owner, counts_ref[b], 0) for b in range(blocks))
        base = pl.multiple_of(start // PAD * PAD, PAD)
        places.append((base, start - base, counts_ref[owner]))
    for source, (base, shift, count) in zip(sources, places):
        place = ((position == token + shift) & (token < count)).astype(bf16)
        here = pl.ds(base, window)
        if folded:
            moved = jnp.dot(place, source[:rows, :], preferred_element_type=f32)
            pack[here, :student_at] = pack[here, :student_at] + moved
            student = source[rows:, :]
            moved = jnp.dot(
                place[:, :half], student[:, :student_width], preferred_element_type=f32
            ) + jnp.dot(place[:, half:], student[:, student_width:], preferred_element_type=f32)
            pack[here, student_at:] = pack[here, student_at:] + moved
        else:
            moved = jnp.dot(place, source[...], preferred_element_type=f32)
            pack[here, :] = pack[here, :] + moved

    ones = jnp.ones((rows, DEPTH - filled), bf16)
    spare = lax.broadcasted_iota(jnp.int32, (DEPTH - filled, rows), 0)
    teacher_gap = jnp.zeros((2 * STUDENT_DIM, rows), bf16)
    student_gap = jnp.zeros((2 * TEACHER_DIM, rows), bf16)
    lane_head = lax.broadcasted_iota(jnp.int32, (rows, student_width), 1) // STUDENT_DIM
    norms = []

    def shift_rows(norm):
        parts = [part.astype(f32) for part in split_three(-norm)]
        out = jnp.where(spare == 0, parts[0], 0.0)
        out = jnp.where(spare == 1, parts[1], out)
        return jnp.where(spare == 2, parts[2], out).astype(bf16)

    for i in range(tiles):
        here = pl.ds(i * rows, rows)
        tile = pack[here, :]
        tile_t = tile.T
        tile_b = tile.astype(bf16)
        tile_s = tile[:, student_at:]
        for h in range(heads):
            tb = tile_b[:, h * TEACHER_DIM : (h + 1) * TEACHER_DIM]
            at = student_at + h * STUDENT_DIM
            sb = tile_b[:, at : at + STUDENT_DIM]
            key_op[h, here, :] = jnp.concatenate([tb, tb, sb, sb, ones], axis=1)
            teacher_t = tile_t[h * TEACHER_DIM : (h + 1) * TEACHER_DIM, :]
            student_t = tile_t[at : at + STUDENT_DIM, :]
            student_col[h, :, here] = student_t.astype(bf16)
            student_pad[h, here, :] = jnp.where(lane_head == h, tile_s, 0.0).astype(bf16)
            teacher_norm = TEACHER_SCALE * jnp.sum(teacher_t * teacher_t, axis=0, keepdims=True)
            student_norm = STUDENT_SCALE * jnp.sum(student_t * student_t, axis=0, keepdims=True)
            norms += [teacher_norm, student_norm]
            high, low = split_high_low(teacher_t * TEACHER_SCALE)
            teacher_op = [high, low, teacher_gap, shift_rows(teacher_norm)]
            row_op[h, i, :, :rows] = jnp.concatenate(teacher_op, axis=0)
            high, low = split_high_low(student_t * STUDENT_SCALE)
            student_op = [student_gap, high, low, shift_rows(student_norm)]
            row_op[h, i, :, rows:] = jnp.concatenate(student_op, axis=0)

    safe = jnp.max(functools.reduce(jnp.maximum, norms)) <= SAFE_NORM
    key_pos = lax.broadcasted_iota(jnp.int32, (rows, rows), 0)
    row_pos = lax.broadcasted_iota(jnp.int32, (rows, rows), 1)

    def logits(h, i, j):
        keys = pl.ds(pl.multiple_of(j * rows, rows), rows)
        both = jnp.dot(key_op[h, keys, :], row_op[h, i], preferred_element_type=f32)
        return both[:, :rows], both[:, rows:]

    @pl.when(safe)
    def shifted_by_own_logit():
        key_grad[...] = jnp.zeros(key_grad.shape, f32)

        def exponentials(h, i, model, prob):
            upto = (i + 1) * rows
            op = row_op[h, i, :, model * rows : (model + 1) * rows]
            values = jnp.dot(key_op[h, :upto, :], op, preferred_element_type=f32)
            diagonal = jnp.where(key_pos <= row_pos, values[i * rows :], NEGATIVE)
            total = cross = jnp.zeros((8, rows), f32)
            for j in range(i + 1):
                value = diagonal if j == i else values[j * rows : (j + 1) * rows]
                exp = jnp.exp2(value)
                prob[i % 2, j] = exp
                total = total + fold(exp)
                weight = teacher_prob[i % 2, j] if model else exp
                cross = cross + fold(weight * value)
            return [jnp.sum(part, axis=0, keepdims=True) for part in (total, cross)]

        def weights(i, j, teacher_inv, student_inv):
            value = student_prob[i % 2, j] * student_inv - teacher_prob[i % 2, j] * teacher_inv
            weights_ref[j * rows : (j + 1) * rows, i * rows : (i + 1) * rows] = value.astype(bf16)

        def head_step(h, kl_total):
            inverse = None
            for i in range(tiles + 1):
                if i < tiles:
                    teacher_sum, teacher_cross = exponentials(h, i, 0, teacher_prob)
                    student_sum, student_cross = exponentials(h, i, 1, student_prob)
                if i:
                    upto = i * rows
                    for j in range(i):
                        weights(i - 1, j, *inverse)
                    row_grad[h, :, upto - rows : upto] = jnp.dot(
                        student_col[h, :, :upto],
                        weights_ref[:upto, upto - rows : upto],
                        preferred_element_type=f32,
                    )
                if i < tiles:
                    inverse = (1.0 / teacher_sum, 1.0 / student_sum)
                    kl_total = kl_total + (
                        (teacher_cross - student_cross) * inverse[0]
                        - jnp.log2(teacher_sum)
                        + jnp.log2(student_sum)
                    )
            for j in range(tiles):
                here = slice(j * rows, (j + 1) * rows)
                key_grad[here, :] = key_grad[here, :] + jnp.dot(
                    weights_ref[here, j * rows :],
                    student_pad[h, j * rows :, :],
                    preferred_element_type=f32,
                )
            return kl_total

        kl_sum[...] = lax.fori_loop(0, heads, head_step, jnp.zeros((1, rows), f32))

    @pl.when(jnp.logical_not(safe))
    def shifted_by_maximum():
        kl_sum[...] = jnp.zeros((1, rows), f32)
        key_grad[...] = jnp.zeros(key_grad.shape, f32)

        def masked(h, i, j):
            allowed = key_pos + j * rows <= row_pos + i * rows
            teacher, student = logits(h, i, j)
            return jnp.where(allowed, teacher, NEGATIVE), jnp.where(allowed, student, NEGATIVE)

        def row_step(step, _):
            h, i = step // tiles, step % tiles
            here = pl.ds(pl.multiple_of(i * rows, rows), rows)

            def advance(j, state):
                teacher_max, teacher_sum, cross_sum, student_max, student_sum = state
                teacher, student = masked(h, i, j)
                teacher_top = jnp.maximum(teacher_max, jnp.max(teacher, axis=0, keepdims=True))
                student_top = jnp.maximum(student_max, jnp.max(student, axis=0, keepdims=True))
                teacher_exp = jnp.exp2(teacher - teacher_top)
                student_exp = jnp.exp2(student - student_top)
                shrink = jnp.exp2(teacher_max - teacher_top)
                cross = jnp.sum(teacher_exp * (teacher - student), axis=0, keepdims=True)
                return (
                    teacher_top,
                    teacher_sum * shrink + jnp.sum(teacher_exp, axis=0, keepdims=True),
                    cross_sum * shrink + cross,
                    student_top,
                    student_sum * jnp.exp2(student_max - student_top)
                    + jnp.sum(student_exp, axis=0, keepdims=True),
                )

            lowest = jnp.full((1, rows), NEGATIVE, f32)
            zeros = jnp.zeros((1, rows), f32)
            teacher_max, teacher_sum, cross_sum, student_max, student_sum = lax.fori_loop(
                0, i + 1, advance, (lowest, zeros, zeros, lowest, zeros)
            )
            teacher_lse = teacher_max + jnp.log2(teacher_sum)
            student_lse = student_max + jnp.log2(student_sum)
            kl_sum[...] = kl_sum[...] + (cross_sum / teacher_sum - teacher_lse + student_lse)

            def spread(j, total):
                teacher, student = masked(h, i, j)
                value = jnp.exp2(student - student_lse) - jnp.exp2(teacher - teacher_lse)
                value = value.astype(bf16)
                keys = pl.ds(pl.multiple_of(j * rows, rows), rows)
                key_grad[keys, :] = key_grad[keys, :] + jnp.dot(
                    value, student_pad[h, here, :], preferred_element_type=f32
                )
                return total + jnp.dot(
                    student_col[h, :, keys], value, preferred_element_type=f32
                )

            row_grad[h, :, here] = lax.fori_loop(
                0, i + 1, spread, jnp.zeros((STUDENT_DIM, rows), f32)
            )
            return 0

        lax.fori_loop(0, heads * tiles, row_step, 0)

    if not last:
        return

    row_parts = [*done[::3], row_grad]
    key_parts = [*done[1::3], key_grad]
    total_width = len(row_parts) * student_width
    for i in range(tiles):
        here = slice(i * rows, (i + 1) * rows)
        columns = jnp.concatenate(
            [part[h, :, here] for part in row_parts for h in range(heads)], axis=0
        )
        lanes = jnp.concatenate([part[here, :] for part in key_parts], axis=1)
        grad_rows[here, :] = (columns.T + lanes) * (STUDENT_DIM**-0.5)
    grad_rows[pl.ds(live, window), :] = jnp.zeros((window, total_width), f32)
    kl_total = sum([ref[...] for ref in done[2::3]] + [kl_sum[...]])
    tokens = sum(counts_ref[b] for b in range(blocks))
    share = jnp.full((1, rows), math.log(2.0), f32) / (H_REL * tokens).astype(f32)
    kl_total = jnp.sum(kl_total * share, axis=1, keepdims=True)
    out[2][...] = jnp.broadcast_to(kl_total, out[2].shape)
    position = lax.broadcasted_iota(jnp.int32, (rows, window), 1)
    token = lax.broadcasted_iota(jnp.int32, (rows, window), 0)
    for k, (base, shift, count) in enumerate(places):
        place = ((position == token + shift) & (token < count)).astype(bf16)
        block = grad_rows[pl.ds(base, window), :].astype(bf16)
        out[k % 2][k // 2] = jnp.dot(place, block, preferred_element_type=f32).astype(bf16)


def local(teacher_queries, student_queries, token_counts):
    f32, bf16 = jnp.float32, jnp.bfloat16
    blocks = lax.axis_size("seq")
    chips = blocks // 2
    groups = lax.axis_size("head")
    rows = teacher_queries.shape[0]
    heads = teacher_queries.shape[1] // TEACHER_DIM // blocks
    tiles = blocks * 3 // 4
    live = tiles * rows
    folded = heads * STUDENT_DIM == LANES
    chunks = 2 if folded else 1
    chunk_heads = heads // chunks
    teacher_width = chunk_heads * TEACHER_DIM
    student_width = chunk_heads * STUDENT_DIM
    if folded:
        send_shape = (chips, rows + rows // 2, LANES)
    else:
        send_shape = (chips, rows, teacher_width + student_width)
    vmem = pl.BlockSpec(memory_space=pltpu.VMEM)
    smem = pl.BlockSpec(memory_space=pltpu.SMEM)
    params = pltpu.CompilerParams(vmem_limit_bytes=40 * 1024 * 1024)
    me = lax.axis_index("seq").reshape(1)
    far_first = sorted(range(1, chips), key=lambda k: -k.bit_count())

    def exchange(kept, swapped, kls=()):
        swapped = lax.ppermute(swapped, "seq", [(i, i ^ 1) for i in range(blocks)])
        shape = (2, kept.shape[1] + (TAIL if kls else 0), kept.shape[2])
        sends = pl.pallas_call(
            functools.partial(merge_kernel, chips),
            in_specs=[vmem] * (2 + len(kls)),
            out_specs=[vmem] * (chips - 1),
            out_shape=[jax.ShapeDtypeStruct(shape, bf16)] * (chips - 1),
            compiler_params=params,
            name="merge",
        )(kept, swapped, *kls)
        out = [None] * (chips - 1)
        for k in far_first:
            pairs = [(i, i ^ (2 * k)) for i in range(blocks)]
            out[k - 1] = lax.ppermute(sends[k - 1], "seq", pairs)
        return [kept, swapped] + out

    packed = jax.ShapeDtypeStruct(send_shape, bf16)
    first = jax.ShapeDtypeStruct(send_shape[1:], bf16)
    order = [0, 1, *range(2, blocks, 2), *range(3, blocks, 2)] if folded else None
    if folded:
        anywhere = pl.BlockSpec(memory_space=pltpu.HBM)
        sends = pl.pallas_call(
            functools.partial(pack_folded_kernel, blocks, chunks),
            in_specs=[smem, anywhere, anywhere],
            out_specs=[vmem] * (blocks + 2 * chunks - 2),
            out_shape=[first] * blocks + [packed] * (2 * chunks - 2),
            scratch_shapes=[
                pltpu.VMEM(student_queries.shape, bf16),
                pltpu.SemaphoreType.DMA((chunks * blocks + 1,)),
            ],
            compiler_params=pltpu.CompilerParams(vmem_limit_bytes=52 * 1024 * 1024),
            name="pack",
        )(me, teacher_queries, student_queries)
    else:
        sends = pl.pallas_call(
            functools.partial(pack_plain_kernel, blocks),
            in_specs=[smem, vmem, vmem],
            out_specs=[vmem] * 2,
            out_shape=[packed] * 2,
            compiler_params=params,
            name="pack",
        )(me, teacher_queries, student_queries)
    incoming = []
    if folded:
        incoming.append(
            [sends[0]]
            + [
                lax.ppermute(sends[k], "seq", [(i, i ^ k) for i in range(blocks)])
                for k in order[1:]
            ]
        )
        sends = sends[blocks:]
    incoming += [exchange(*pair) for pair in zip(sends[::2], sends[1::2])]

    result = [
        jax.ShapeDtypeStruct((chunk_heads, STUDENT_DIM, live), f32),
        jax.ShapeDtypeStruct((live, student_width), f32),
        jax.ShapeDtypeStruct((1, rows), f32),
    ]
    message = jax.ShapeDtypeStruct((chips, rows, heads * STUDENT_DIM), bf16)
    divergence = jax.ShapeDtypeStruct((1, heads * STUDENT_DIM), f32)
    pairs = chunk_heads * tiles * (tiles + 1) // 2 * rows * rows
    done = []
    for c in range(chunks):
        last = c == chunks - 1
        scratch = [
            pltpu.VMEM((live + rows + PAD, teacher_width + student_width), f32),
            pltpu.VMEM((chunk_heads, live, DEPTH), bf16),
            pltpu.VMEM((chunk_heads, tiles, DEPTH, 2 * rows), bf16),
            pltpu.VMEM((chunk_heads, STUDENT_DIM, live), bf16),
            pltpu.VMEM((chunk_heads, live, student_width), bf16),
            pltpu.VMEM((2, tiles, rows, rows), f32),
            pltpu.VMEM((2, tiles, rows, rows), f32),
            pltpu.VMEM((live, live), bf16),
        ]
        if last:
            scratch += [pltpu.VMEM(part.shape, f32) for part in result]
            scratch.append(pltpu.VMEM((live + rows + PAD, heads * STUDENT_DIM), f32))
        inputs = [me, token_counts, *incoming[c], *done]
        done += pl.pallas_call(
            functools.partial(
                relation_kernel,
                folded,
                chunk_heads,
                tiles,
                order if c == 0 else None,
                len(incoming[c]),
                c,
                last,
            ),
            in_specs=[smem, smem] + [vmem] * (len(inputs) - 2),
            out_specs=[vmem] * 3,
            out_shape=[message, message, divergence] if last else result,
            scratch_shapes=scratch,
            compiler_params=params,
            cost_estimate=pl.CostEstimate(
                flops=4 * pairs * DEPTH, bytes_accessed=8 * pairs, transcendentals=2 * pairs
            ),
            name="relation",
        )(*inputs)
    kept, swapped, kl = done[-3:]
    kl = kl + lax.ppermute(kl, "seq", [(i, i ^ 1) for i in range(blocks)])
    kls = [kl] + [
        lax.ppermute(kl, "head", [(i, i ^ k) for i in range(groups)]) for k in range(1, groups)
    ]
    returned = exchange(kept, swapped, kls)
    grad, loss = pl.pallas_call(
        functools.partial(unpack_kernel, groups),
        in_specs=[smem] + [vmem] * (groups + len(returned)),
        out_specs=[vmem] * 2,
        out_shape=[
            jax.ShapeDtypeStruct((rows, student_queries.shape[1]), f32),
            divergence,
        ],
        compiler_params=params,
        name="unpack",
    )(me, *kls, *returned)
    return (grad, loss[0, 0])


def solution(mesh):
    return jax.shard_map(
        local,
        mesh=mesh,
        in_specs=(P("seq", "head"), P("seq", "head"), P()),
        out_specs=(P("seq", "head"), P()),
        check_vma=False,
    )
```

```python
import functools
import math

import jax
import jax.numpy as jnp
from jax import lax
from jax.experimental import pallas as pl
from jax.experimental.pallas import tpu as pltpu
from jax.sharding import PartitionSpec as P

DT = 8192
DS = 4096
H_REL = 128
TEACHER_DIM = DT // H_REL
STUDENT_DIM = DS // H_REL

NEGATIVE = -1e30
LOG2E = math.log2(math.e)
TEACHER_SCALE = LOG2E * TEACHER_DIM**-0.5
STUDENT_SCALE = LOG2E * STUDENT_DIM**-0.5
PAD = 8
LANES = 128
TAIL = 16
DEPTH = 256
SAFE_NORM = 320.0


def split_high_low(values):
    high = values.astype(jnp.bfloat16)
    low = (values - high.astype(jnp.float32)).astype(jnp.bfloat16)
    return high, low


def split_three(values):
    high = values.astype(jnp.bfloat16)
    rest = values - high.astype(jnp.float32)
    return (high,) + split_high_low(rest)


def at_columns(index, count, width, act):
    if width % LANES == 0:
        act(pl.ds(pl.multiple_of(index * width, LANES), width))
    else:
        for part in range(count):
            pl.when(index == part)(functools.partial(act, pl.ds(part * width, width)))


def pack_folded_kernel(blocks, chunks, me_ref, teacher_ref, student_ref, *refs):
    sends, student, sems = refs[:-2], refs[-2], refs[-1]
    rows = teacher_ref.shape[0]
    half = rows // 2

    def block(chunk, k):
        if chunk == 0:
            return sends[k]
        return sends[blocks + 2 * (chunk - 1) + k % 2].at[k // 2]

    copies = [pltpu.make_async_copy(student_ref, student, sems.at[chunks * blocks])]
    for chunk in range(chunks):
        for k in range(blocks):
            to = jnp.bitwise_xor(me_ref[0], k)
            at = pl.multiple_of((to * chunks + chunk) * LANES, LANES)
            copies.append(
                pltpu.make_async_copy(
                    teacher_ref.at[:, pl.ds(at, LANES)],
                    block(chunk, k).at[pl.ds(0, rows)],
                    sems.at[chunk * blocks + k],
                )
            )
    for copy in copies:
        copy.start()
    copies[0].wait()
    for k in range(blocks):
        to = jnp.bitwise_xor(me_ref[0], k)
        lanes = pl.ds(pl.multiple_of(to * LANES, LANES), LANES)
        top, bottom = student[:half, lanes], student[half:, lanes]
        for chunk in range(chunks):
            part = slice(chunk * (LANES // 2), (chunk + 1) * (LANES // 2))
            block(chunk, k)[rows:, :] = jnp.concatenate([top[:, part], bottom[:, part]], axis=1)
    for copy in copies[1:]:
        copy.wait()


def pack_plain_kernel(blocks, me_ref, teacher_ref, student_ref, *sends):
    teacher_width = teacher_ref.shape[1] // blocks
    student_width = student_ref.shape[1] // blocks
    for core in range(2):
        for k in range(blocks // 2):
            to = jnp.bitwise_xor(me_ref[0], 2 * k + core)

            def put_teacher(columns, send=sends[core], k=k):
                send[k, :, :teacher_width] = teacher_ref[:, columns]

            def put_student(columns, send=sends[core], k=k):
                send[k, :, teacher_width:] = student_ref[:, columns]

            at_columns(to, blocks, teacher_width, put_teacher)
            at_columns(to, blocks, student_width, put_student)


def pair_sum(parts):
    while len(parts) > 1:
        parts = [a + b for a, b in zip(parts[::2], parts[1::2])]
    return parts[0]


def tail_rows(value, width):
    thirds = [part.astype(jnp.float32) for part in split_three(value)]
    line = lax.broadcasted_iota(jnp.int32, (TAIL, width), 0)
    tail = jnp.where(line == 0, thirds[0], 0.0)
    tail = jnp.where(line == 1, thirds[1], tail)
    return jnp.where(line == 2, thirds[2], tail).astype(jnp.bfloat16)


def merge_kernel(chips, kept_ref, swapped_ref, *refs):
    kls, sends = refs[: 1 - chips], refs[1 - chips :]
    rows = kept_ref.shape[1]
    tail = tail_rows(pair_sum([kl[...] for kl in kls]), kept_ref.shape[2]) if kls else None
    for k, send in enumerate(sends):
        send[0, :rows, :] = kept_ref[k + 1]
        send[1, :rows, :] = swapped_ref[k + 1]
        if kls:
            send[0, rows:, :] = tail
            send[1, rows:, :] = tail


def arrived(refs):
    return [refs[0].at[0], refs[1].at[0]] + [ref.at[core] for ref in refs[2:] for core in range(2)]


def unpack_kernel(n_kl, me_ref, *refs):
    kls, returned, (grad_ref, loss_ref) = refs[:n_kl], refs[n_kl:-2], refs[-2:]
    rows = grad_ref.shape[0]
    blocks = arrived(returned)
    for k, block in enumerate(blocks):

        def put(columns, block=block):
            grad_ref[:, columns] = block[:rows, :].astype(jnp.float32)

        at_columns(jnp.bitwise_xor(me_ref[0], k), len(blocks), block.shape[1], put)
    own = tail_rows(pair_sum([kl[...] for kl in kls]), kls[0].shape[1])
    tails = [own] + [ref[0, rows:, :] for ref in returned[2:]]
    loss_ref[...] = pair_sum(
        [jnp.sum(tail.astype(jnp.float32), axis=0, keepdims=True) for tail in tails]
    )


def fold(values):
    rows, columns = values.shape
    return jnp.sum(values.reshape(rows // 8, 8, columns), axis=0)


def relation_kernel(folded, heads, tiles, order, n_in, n_done, last, me_ref, counts_ref, *refs):
    if order:
        sources = [refs[order.index(k)] for k in range(n_in)]
    else:
        sources = arrived(refs[:n_in])
    done = refs[n_in : n_in + 3 * n_done]
    rest = list(refs[n_in + 3 * n_done :])
    out, rest = rest[:3], rest[3:]
    pack, key_op, row_op, student_col, student_pad, teacher_prob, student_prob, weights_ref = rest[:8]
    if last:
        row_grad, key_grad, kl_sum, grad_rows = rest[8:]
    else:
        row_grad, key_grad, kl_sum = out
    f32, bf16 = jnp.float32, jnp.bfloat16
    blocks = len(sources)
    rows = teacher_prob.shape[2]
    half = rows // 2
    live = tiles * rows
    window = rows + PAD
    student_at = heads * TEACHER_DIM
    student_width = heads * STUDENT_DIM
    filled = 2 * TEACHER_DIM + 2 * STUDENT_DIM

    position = lax.broadcasted_iota(jnp.int32, (window, rows), 0)
    token = lax.broadcasted_iota(jnp.int32, (window, rows), 1)
    pack[...] = jnp.zeros(pack.shape, f32)
    places = []
    for k in range(blocks):
        owner = jnp.bitwise_xor(me_ref[0], k)
        start = sum(jnp.where(b < owner, counts_ref[b], 0) for b in range(blocks))
        base = pl.multiple_of(start // PAD * PAD, PAD)
        places.append((base, start - base, counts_ref[owner]))
    for source, (base, shift, count) in zip(sources, places):
        place = ((position == token + shift) & (token < count)).astype(bf16)
        here = pl.ds(base, window)
        if folded:
            moved = jnp.dot(place, source[:rows, :], preferred_element_type=f32)
            pack[here, :student_at] = pack[here, :student_at] + moved
            student = source[rows:, :]
            moved = jnp.dot(
                place[:, :half], student[:, :student_width], preferred_element_type=f32
            ) + jnp.dot(place[:, half:], student[:, student_width:], preferred_element_type=f32)
            pack[here, student_at:] = pack[here, student_at:] + moved
        else:
            moved = jnp.dot(place, source[...], preferred_element_type=f32)
            pack[here, :] = pack[here, :] + moved

    ones = jnp.ones((rows, DEPTH - filled), bf16)
    spare = lax.broadcasted_iota(jnp.int32, (DEPTH - filled, rows), 0)
    teacher_gap = jnp.zeros((2 * STUDENT_DIM, rows), bf16)
    student_gap = jnp.zeros((2 * TEACHER_DIM, rows), bf16)
    lane_head = lax.broadcasted_iota(jnp.int32, (rows, student_width), 1) // STUDENT_DIM
    norms = []

    def shift_rows(norm):
        parts = [part.astype(f32) for part in split_three(-norm)]
        out = jnp.where(spare == 0, parts[0], 0.0)
        out = jnp.where(spare == 1, parts[1], out)
        return jnp.where(spare == 2, parts[2], out).astype(bf16)

    for i in range(tiles):
        here = pl.ds(i * rows, rows)
        tile = pack[here, :]
        tile_t = tile.T
        tile_b = tile.astype(bf16)
        tile_s = tile[:, student_at:]
        for h in range(heads):
            tb = tile_b[:, h * TEACHER_DIM : (h + 1) * TEACHER_DIM]
            at = student_at + h * STUDENT_DIM
            sb = tile_b[:, at : at + STUDENT_DIM]
            key_op[h, here, :] = jnp.concatenate([tb, tb, sb, sb, ones], axis=1)
            teacher_t = tile_t[h * TEACHER_DIM : (h + 1) * TEACHER_DIM, :]
            student_t = tile_t[at : at + STUDENT_DIM, :]
            student_col[h, :, here] = student_t.astype(bf16)
            student_pad[h, here, :] = jnp.where(lane_head == h, tile_s, 0.0).astype(bf16)
            teacher_norm = TEACHER_SCALE * jnp.sum(teacher_t * teacher_t, axis=0, keepdims=True)
            student_norm = STUDENT_SCALE * jnp.sum(student_t * student_t, axis=0, keepdims=True)
            norms += [teacher_norm, student_norm]
            high, low = split_high_low(teacher_t * TEACHER_SCALE)
            teacher_op = [high, low, teacher_gap, shift_rows(teacher_norm)]
            row_op[h, i, :, :rows] = jnp.concatenate(teacher_op, axis=0)
            high, low = split_high_low(student_t * STUDENT_SCALE)
            student_op = [student_gap, high, low, shift_rows(student_norm)]
            row_op[h, i, :, rows:] = jnp.concatenate(student_op, axis=0)

    safe = jnp.max(functools.reduce(jnp.maximum, norms)) <= SAFE_NORM
    key_pos = lax.broadcasted_iota(jnp.int32, (rows, rows), 0)
    row_pos = lax.broadcasted_iota(jnp.int32, (rows, rows), 1)

    def logits(h, i, j):
        keys = pl.ds(pl.multiple_of(j * rows, rows), rows)
        both = jnp.dot(key_op[h, keys, :], row_op[h, i], preferred_element_type=f32)
        return both[:, :rows], both[:, rows:]

    @pl.when(safe)
    def shifted_by_own_logit():
        key_grad[...] = jnp.zeros(key_grad.shape, f32)

        def exponentials(h, i, model, prob):
            upto = (i + 1) * rows
            op = row_op[h, i, :, model * rows : (model + 1) * rows]
            values = jnp.dot(key_op[h, :upto, :], op, preferred_element_type=f32)
            diagonal = jnp.where(key_pos <= row_pos, values[i * rows :], NEGATIVE)
            total = cross = jnp.zeros((8, rows), f32)
            for j in range(i + 1):
                value = diagonal if j == i else values[j * rows : (j + 1) * rows]
                exp = jnp.exp2(value)
                prob[i % 2, j] = exp
                total = total + fold(exp)
                weight = teacher_prob[i % 2, j] if model else exp
                cross = cross + fold(weight * value)
            return [jnp.sum(part, axis=0, keepdims=True) for part in (total, cross)]

        def weights(i, j, teacher_inv, student_inv):
            value = student_prob[i % 2, j] * student_inv - teacher_prob[i % 2, j] * teacher_inv
            weights_ref[j * rows : (j + 1) * rows, i * rows : (i + 1) * rows] = value.astype(bf16)

        def head_step(h, kl_total):
            inverse = None
            for i in range(tiles + 1):
                if i < tiles:
                    teacher_sum, teacher_cross = exponentials(h, i, 0, teacher_prob)
                    student_sum, student_cross = exponentials(h, i, 1, student_prob)
                if i:
                    upto = i * rows
                    for j in range(i):
                        weights(i - 1, j, *inverse)
                    row_grad[h, :, upto - rows : upto] = jnp.dot(
                        student_col[h, :, :upto],
                        weights_ref[:upto, upto - rows : upto],
                        preferred_element_type=f32,
                    )
                if i < tiles:
                    inverse = (1.0 / teacher_sum, 1.0 / student_sum)
                    kl_total = kl_total + (
                        (teacher_cross - student_cross) * inverse[0]
                        - jnp.log2(teacher_sum)
                        + jnp.log2(student_sum)
                    )
            for j in range(tiles):
                here = slice(j * rows, (j + 1) * rows)
                key_grad[here, :] = key_grad[here, :] + jnp.dot(
                    weights_ref[here, j * rows :],
                    student_pad[h, j * rows :, :],
                    preferred_element_type=f32,
                )
            return kl_total

        kl_sum[...] = lax.fori_loop(0, heads, head_step, jnp.zeros((1, rows), f32))

    @pl.when(jnp.logical_not(safe))
    def shifted_by_maximum():
        kl_sum[...] = jnp.zeros((1, rows), f32)
        key_grad[...] = jnp.zeros(key_grad.shape, f32)

        def masked(h, i, j):
            allowed = key_pos + j * rows <= row_pos + i * rows
            teacher, student = logits(h, i, j)
            return jnp.where(allowed, teacher, NEGATIVE), jnp.where(allowed, student, NEGATIVE)

        def row_step(step, _):
            h, i = step // tiles, step % tiles
            here = pl.ds(pl.multiple_of(i * rows, rows), rows)

            def advance(j, state):
                teacher_max, teacher_sum, cross_sum, student_max, student_sum = state
                teacher, student = masked(h, i, j)
                teacher_top = jnp.maximum(teacher_max, jnp.max(teacher, axis=0, keepdims=True))
                student_top = jnp.maximum(student_max, jnp.max(student, axis=0, keepdims=True))
                teacher_exp = jnp.exp2(teacher - teacher_top)
                student_exp = jnp.exp2(student - student_top)
                shrink = jnp.exp2(teacher_max - teacher_top)
                cross = jnp.sum(teacher_exp * (teacher - student), axis=0, keepdims=True)
                return (
                    teacher_top,
                    teacher_sum * shrink + jnp.sum(teacher_exp, axis=0, keepdims=True),
                    cross_sum * shrink + cross,
                    student_top,
                    student_sum * jnp.exp2(student_max - student_top)
                    + jnp.sum(student_exp, axis=0, keepdims=True),
                )

            lowest = jnp.full((1, rows), NEGATIVE, f32)
            zeros = jnp.zeros((1, rows), f32)
            teacher_max, teacher_sum, cross_sum, student_max, student_sum = lax.fori_loop(
                0, i + 1, advance, (lowest, zeros, zeros, lowest, zeros)
            )
            teacher_lse = teacher_max + jnp.log2(teacher_sum)
            student_lse = student_max + jnp.log2(student_sum)
            kl_sum[...] = kl_sum[...] + (cross_sum / teacher_sum - teacher_lse + student_lse)

            def spread(j, total):
                teacher, student = masked(h, i, j)
                value = jnp.exp2(student - student_lse) - jnp.exp2(teacher - teacher_lse)
                value = value.astype(bf16)
                keys = pl.ds(pl.multiple_of(j * rows, rows), rows)
                key_grad[keys, :] = key_grad[keys, :] + jnp.dot(
                    value, student_pad[h, here, :], preferred_element_type=f32
                )
                return total + jnp.dot(
                    student_col[h, :, keys], value, preferred_element_type=f32
                )

            row_grad[h, :, here] = lax.fori_loop(
                0, i + 1, spread, jnp.zeros((STUDENT_DIM, rows), f32)
            )
            return 0

        lax.fori_loop(0, heads * tiles, row_step, 0)

    if not last:
        return

    row_parts = [*done[::3], row_grad]
    key_parts = [*done[1::3], key_grad]
    total_width = len(row_parts) * student_width
    for i in range(tiles):
        here = slice(i * rows, (i + 1) * rows)
        columns = jnp.concatenate(
            [part[h, :, here] for part in row_parts for h in range(heads)], axis=0
        )
        lanes = jnp.concatenate([part[here, :] for part in key_parts], axis=1)
        grad_rows[here, :] = (columns.T + lanes) * (STUDENT_DIM**-0.5)
    grad_rows[pl.ds(live, window), :] = jnp.zeros((window, total_width), f32)
    kl_total = sum([ref[...] for ref in done[2::3]] + [kl_sum[...]])
    tokens = sum(counts_ref[b] for b in range(blocks))
    share = jnp.full((1, rows), math.log(2.0), f32) / (H_REL * tokens).astype(f32)
    kl_total = jnp.sum(kl_total * share, axis=1, keepdims=True)
    out[2][...] = jnp.broadcast_to(kl_total, out[2].shape)
    position = lax.broadcasted_iota(jnp.int32, (rows, window), 1)
    token = lax.broadcasted_iota(jnp.int32, (rows, window), 0)
    for k, (base, shift, count) in enumerate(places):
        place = ((position == token + shift) & (token < count)).astype(bf16)
        block = grad_rows[pl.ds(base, window), :].astype(bf16)
        out[k % 2][k // 2] = jnp.dot(place, block, preferred_element_type=f32).astype(bf16)


def local(teacher_queries, student_queries, token_counts):
    f32, bf16 = jnp.float32, jnp.bfloat16
    blocks = lax.axis_size("seq")
    chips = blocks // 2
    groups = lax.axis_size("head")
    rows = teacher_queries.shape[0]
    heads = teacher_queries.shape[1] // TEACHER_DIM // blocks
    tiles = blocks * 3 // 4
    live = tiles * rows
    folded = heads * STUDENT_DIM == LANES
    chunks = 2 if folded else 1
    chunk_heads = heads // chunks
    teacher_width = chunk_heads * TEACHER_DIM
    student_width = chunk_heads * STUDENT_DIM
    if folded:
        send_shape = (chips, rows + rows // 2, LANES)
    else:
        send_shape = (chips, rows, teacher_width + student_width)
    vmem = pl.BlockSpec(memory_space=pltpu.VMEM)
    smem = pl.BlockSpec(memory_space=pltpu.SMEM)
    params = pltpu.CompilerParams(vmem_limit_bytes=40 * 1024 * 1024)
    me = lax.axis_index("seq").reshape(1)
    far_first = sorted(range(1, chips), key=lambda k: -k.bit_count())

    def exchange(kept, swapped, kls=()):
        swapped = lax.ppermute(swapped, "seq", [(i, i ^ 1) for i in range(blocks)])
        shape = (2, kept.shape[1] + (TAIL if kls else 0), kept.shape[2])
        sends = pl.pallas_call(
            functools.partial(merge_kernel, chips),
            in_specs=[vmem] * (2 + len(kls)),
            out_specs=[vmem] * (chips - 1),
            out_shape=[jax.ShapeDtypeStruct(shape, bf16)] * (chips - 1),
            compiler_params=params,
            name="merge",
        )(kept, swapped, *kls)
        out = [None] * (chips - 1)
        for k in far_first:
            pairs = [(i, i ^ (2 * k)) for i in range(blocks)]
            out[k - 1] = lax.ppermute(sends[k - 1], "seq", pairs)
        return [kept, swapped] + out

    packed = jax.ShapeDtypeStruct(send_shape, bf16)
    first = jax.ShapeDtypeStruct(send_shape[1:], bf16)
    order = [0, 1, *range(2, blocks, 2), *range(3, blocks, 2)] if folded else None
    if folded:
        anywhere = pl.BlockSpec(memory_space=pltpu.HBM)
        sends = pl.pallas_call(
            functools.partial(pack_folded_kernel, blocks, chunks),
            in_specs=[smem, anywhere, anywhere],
            out_specs=[vmem] * (blocks + 2 * chunks - 2),
            out_shape=[first] * blocks + [packed] * (2 * chunks - 2),
            scratch_shapes=[
                pltpu.VMEM(student_queries.shape, bf16),
                pltpu.SemaphoreType.DMA((chunks * blocks + 1,)),
            ],
            compiler_params=pltpu.CompilerParams(vmem_limit_bytes=52 * 1024 * 1024),
            name="pack",
        )(me, teacher_queries, student_queries)
    else:
        sends = pl.pallas_call(
            functools.partial(pack_plain_kernel, blocks),
            in_specs=[smem, vmem, vmem],
            out_specs=[vmem] * 2,
            out_shape=[packed] * 2,
            compiler_params=params,
            name="pack",
        )(me, teacher_queries, student_queries)
    incoming = []
    if folded:
        incoming.append(
            [sends[0]]
            + [
                lax.ppermute(sends[k], "seq", [(i, i ^ k) for i in range(blocks)])
                for k in order[1:]
            ]
        )
        sends = sends[blocks:]
    incoming += [exchange(*pair) for pair in zip(sends[::2], sends[1::2])]

    result = [
        jax.ShapeDtypeStruct((chunk_heads, STUDENT_DIM, live), f32),
        jax.ShapeDtypeStruct((live, student_width), f32),
        jax.ShapeDtypeStruct((1, rows), f32),
    ]
    message = jax.ShapeDtypeStruct((chips, rows, heads * STUDENT_DIM), bf16)
    divergence = jax.ShapeDtypeStruct((1, heads * STUDENT_DIM), f32)
    pairs = chunk_heads * tiles * (tiles + 1) // 2 * rows * rows
    done = []
    for c in range(chunks):
        last = c == chunks - 1
        scratch = [
            pltpu.VMEM((live + rows + PAD, teacher_width + student_width), f32),
            pltpu.VMEM((chunk_heads, live, DEPTH), bf16),
            pltpu.VMEM((chunk_heads, tiles, DEPTH, 2 * rows), bf16),
            pltpu.VMEM((chunk_heads, STUDENT_DIM, live), bf16),
            pltpu.VMEM((chunk_heads, live, student_width), bf16),
            pltpu.VMEM((2, tiles, rows, rows), f32),
            pltpu.VMEM((2, tiles, rows, rows), f32),
            pltpu.VMEM((live, live), bf16),
        ]
        if last:
            scratch += [pltpu.VMEM(part.shape, f32) for part in result]
            scratch.append(pltpu.VMEM((live + rows + PAD, heads * STUDENT_DIM), f32))
        inputs = [me, token_counts, *incoming[c], *done]
        done += pl.pallas_call(
            functools.partial(
                relation_kernel,
                folded,
                chunk_heads,
                tiles,
                order if c == 0 else None,
                len(incoming[c]),
                c,
                last,
            ),
            in_specs=[smem, smem] + [vmem] * (len(inputs) - 2),
            out_specs=[vmem] * 3,
            out_shape=[message, message, divergence] if last else result,
            scratch_shapes=scratch,
            compiler_params=params,
            cost_estimate=pl.CostEstimate(
                flops=4 * pairs * DEPTH, bytes_accessed=8 * pairs, transcendentals=2 * pairs
            ),
            name="relation",
        )(*inputs)
    kept, swapped, kl = done[-3:]
    kl = kl + lax.ppermute(kl, "seq", [(i, i ^ 1) for i in range(blocks)])
    kls = [kl]
    for bit in range(groups.bit_length() - 1):
        own = pair_sum(kls)
        pairs = [(i, i ^ (1 << bit)) for i in range(groups)]
        kls = [own, lax.ppermute(own, "head", pairs)]
    returned = exchange(kept, swapped, kls)
    grad, loss = pl.pallas_call(
        functools.partial(unpack_kernel, len(kls)),
        in_specs=[smem] + [vmem] * (len(kls) + len(returned)),
        out_specs=[vmem] * 2,
        out_shape=[
            jax.ShapeDtypeStruct((rows, student_queries.shape[1]), f32),
            divergence,
        ],
        compiler_params=params,
        name="unpack",
    )(me, *kls, *returned)
    return (grad, loss[0, 0])


def solution(mesh):
    return jax.shard_map(
        local,
        mesh=mesh,
        in_specs=(P("seq", "head"), P("seq", "head"), P()),
        out_specs=(P("seq", "head"), P()),
        check_vma=False,
    )
```

```python
import functools
import math

import jax
import jax.numpy as jnp
from jax import lax
from jax.experimental import pallas as pl
from jax.experimental.pallas import tpu as pltpu
from jax.sharding import PartitionSpec as P

DT = 8192
DS = 4096
H_REL = 128
TEACHER_DIM = DT // H_REL
STUDENT_DIM = DS // H_REL

NEGATIVE = -1e30
LOG2E = math.log2(math.e)
TEACHER_SCALE = LOG2E * TEACHER_DIM**-0.5
STUDENT_SCALE = LOG2E * STUDENT_DIM**-0.5
PAD = 8
LANES = 128
TAIL = 16
DEPTH = 256
SAFE_NORM = 320.0


def split_high_low(values):
    high = values.astype(jnp.bfloat16)
    low = (values - high.astype(jnp.float32)).astype(jnp.bfloat16)
    return high, low


def split_three(values):
    high = values.astype(jnp.bfloat16)
    rest = values - high.astype(jnp.float32)
    return (high,) + split_high_low(rest)


def at_columns(index, count, width, act):
    if width % LANES == 0:
        act(pl.ds(pl.multiple_of(index * width, LANES), width))
    else:
        for part in range(count):
            pl.when(index == part)(functools.partial(act, pl.ds(part * width, width)))


def pack_folded_kernel(blocks, chunks, me_ref, teacher_ref, student_ref, *refs):
    sends, student, sems = refs[:-2], refs[-2], refs[-1]
    rows = teacher_ref.shape[0]
    half = rows // 2

    def block(chunk, k):
        if chunk == 0:
            return sends[k]
        return sends[blocks + 2 * (chunk - 1) + k % 2].at[k // 2]

    copies = [pltpu.make_async_copy(student_ref, student, sems.at[chunks * blocks])]
    for chunk in range(chunks):
        for k in range(blocks):
            to = jnp.bitwise_xor(me_ref[0], k)
            at = pl.multiple_of((to * chunks + chunk) * LANES, LANES)
            copies.append(
                pltpu.make_async_copy(
                    teacher_ref.at[:, pl.ds(at, LANES)],
                    block(chunk, k).at[pl.ds(0, rows)],
                    sems.at[chunk * blocks + k],
                )
            )
    for copy in copies:
        copy.start()
    copies[0].wait()
    for k in range(blocks):
        to = jnp.bitwise_xor(me_ref[0], k)
        lanes = pl.ds(pl.multiple_of(to * LANES, LANES), LANES)
        top, bottom = student[:half, lanes], student[half:, lanes]
        for chunk in range(chunks):
            part = slice(chunk * (LANES // 2), (chunk + 1) * (LANES // 2))
            block(chunk, k)[rows:, :] = jnp.concatenate([top[:, part], bottom[:, part]], axis=1)
    for copy in copies[1:]:
        copy.wait()


def pack_plain_kernel(blocks, me_ref, teacher_ref, student_ref, *sends):
    teacher_width = teacher_ref.shape[1] // blocks
    student_width = student_ref.shape[1] // blocks
    for core in range(2):
        for k in range(blocks // 2):
            to = jnp.bitwise_xor(me_ref[0], 2 * k + core)

            def put_teacher(columns, send=sends[core], k=k):
                send[k, :, :teacher_width] = teacher_ref[:, columns]

            def put_student(columns, send=sends[core], k=k):
                send[k, :, teacher_width:] = student_ref[:, columns]

            at_columns(to, blocks, teacher_width, put_teacher)
            at_columns(to, blocks, student_width, put_student)


def pair_sum(parts):
    while len(parts) > 1:
        parts = [a + b for a, b in zip(parts[::2], parts[1::2])]
    return parts[0]


def tail_rows(value, width):
    thirds = [part.astype(jnp.float32) for part in split_three(value)]
    line = lax.broadcasted_iota(jnp.int32, (TAIL, width), 0)
    tail = jnp.where(line == 0, thirds[0], 0.0)
    tail = jnp.where(line == 1, thirds[1], tail)
    return jnp.where(line == 2, thirds[2], tail).astype(jnp.bfloat16)


def merge_kernel(chips, kept_ref, swapped_ref, *refs):
    kls, sends = refs[: 1 - chips], refs[1 - chips :]
    rows = kept_ref.shape[1]
    tail = tail_rows(pair_sum([kl[...] for kl in kls]), kept_ref.shape[2]) if kls else None
    for k, send in enumerate(sends):
        send[0, :rows, :] = kept_ref[k + 1]
        send[1, :rows, :] = swapped_ref[k + 1]
        if kls:
            send[0, rows:, :] = tail
            send[1, rows:, :] = tail


def arrived(refs):
    return [refs[0].at[0], refs[1].at[0]] + [ref.at[core] for ref in refs[2:] for core in range(2)]


def unpack_kernel(n_kl, me_ref, *refs):
    kls, returned, (grad_ref, loss_ref) = refs[:n_kl], refs[n_kl:-2], refs[-2:]
    rows = grad_ref.shape[0]
    blocks = arrived(returned)
    for k, block in enumerate(blocks):

        def put(columns, block=block):
            grad_ref[:, columns] = block[:rows, :].astype(jnp.float32)

        at_columns(jnp.bitwise_xor(me_ref[0], k), len(blocks), block.shape[1], put)
    own = tail_rows(pair_sum([kl[...] for kl in kls]), kls[0].shape[1])
    tails = [own] + [ref[0, rows:, :] for ref in returned[2:]]
    loss_ref[...] = pair_sum(
        [jnp.sum(tail.astype(jnp.float32), axis=0, keepdims=True) for tail in tails]
    )


def fold(values):
    rows, columns = values.shape
    return jnp.sum(values.reshape(rows // 8, 8, columns), axis=0)


def relation_kernel(folded, heads, tiles, order, n_in, n_done, last, me_ref, counts_ref, *refs):
    if order:
        sources = [refs[order.index(k)] for k in range(n_in)]
    else:
        sources = arrived(refs[:n_in])
    done = refs[n_in : n_in + 3 * n_done]
    rest = list(refs[n_in + 3 * n_done :])
    out, rest = rest[:3], rest[3:]
    pack, key_op, row_op, student_col, student_pad, teacher_prob, student_prob, weights_ref = rest[:8]
    if last:
        row_grad, key_grad, kl_sum, grad_rows = rest[8:]
    else:
        row_grad, key_grad, kl_sum = out
    f32, bf16 = jnp.float32, jnp.bfloat16
    blocks = len(sources)
    rows = teacher_prob.shape[2]
    half = rows // 2
    live = tiles * rows
    window = rows + PAD
    student_at = heads * TEACHER_DIM
    student_width = heads * STUDENT_DIM
    filled = 2 * TEACHER_DIM + 2 * STUDENT_DIM

    position = lax.broadcasted_iota(jnp.int32, (window, rows), 0)
    token = lax.broadcasted_iota(jnp.int32, (window, rows), 1)
    pack[...] = jnp.zeros(pack.shape, f32)
    places = []
    for k in range(blocks):
        owner = jnp.bitwise_xor(me_ref[0], k)
        start = sum(jnp.where(b < owner, counts_ref[b], 0) for b in range(blocks))
        base = pl.multiple_of(start // PAD * PAD, PAD)
        places.append((base, start - base, counts_ref[owner]))
    for source, (base, shift, count) in zip(sources, places):
        place = ((position == token + shift) & (token < count)).astype(bf16)
        here = pl.ds(base, window)
        if folded:
            moved = jnp.dot(place, source[:rows, :], preferred_element_type=f32)
            pack[here, :student_at] = pack[here, :student_at] + moved
            student = source[rows:, :]
            moved = jnp.dot(
                place[:, :half], student[:, :student_width], preferred_element_type=f32
            ) + jnp.dot(place[:, half:], student[:, student_width:], preferred_element_type=f32)
            pack[here, student_at:] = pack[here, student_at:] + moved
        else:
            moved = jnp.dot(place, source[...], preferred_element_type=f32)
            pack[here, :] = pack[here, :] + moved

    ones = jnp.ones((rows, DEPTH - filled), bf16)
    spare = lax.broadcasted_iota(jnp.int32, (DEPTH - filled, rows), 0)
    teacher_gap = jnp.zeros((2 * STUDENT_DIM, rows), bf16)
    student_gap = jnp.zeros((2 * TEACHER_DIM, rows), bf16)
    lane_head = lax.broadcasted_iota(jnp.int32, (rows, student_width), 1) // STUDENT_DIM
    norms = []

    def shift_rows(norm):
        parts = [part.astype(f32) for part in split_three(-norm)]
        out = jnp.where(spare == 0, parts[0], 0.0)
        out = jnp.where(spare == 1, parts[1], out)
        return jnp.where(spare == 2, parts[2], out).astype(bf16)

    for i in range(tiles):
        here = pl.ds(i * rows, rows)
        tile = pack[here, :]
        tile_t = tile.T
        tile_b = tile.astype(bf16)
        tile_s = tile[:, student_at:]
        for h in range(heads):
            tb = tile_b[:, h * TEACHER_DIM : (h + 1) * TEACHER_DIM]
            at = student_at + h * STUDENT_DIM
            sb = tile_b[:, at : at + STUDENT_DIM]
            key_op[h, here, :] = jnp.concatenate([tb, tb, sb, sb, ones], axis=1)
            teacher_t = tile_t[h * TEACHER_DIM : (h + 1) * TEACHER_DIM, :]
            student_t = tile_t[at : at + STUDENT_DIM, :]
            student_col[h, :, here] = student_t.astype(bf16)
            student_pad[h, here, :] = jnp.where(lane_head == h, tile_s, 0.0).astype(bf16)
            teacher_norm = TEACHER_SCALE * jnp.sum(teacher_t * teacher_t, axis=0, keepdims=True)
            student_norm = STUDENT_SCALE * jnp.sum(student_t * student_t, axis=0, keepdims=True)
            norms += [teacher_norm, student_norm]
            high, low = split_high_low(teacher_t * TEACHER_SCALE)
            teacher_op = [high, low, teacher_gap, shift_rows(teacher_norm)]
            row_op[h, i, :, :rows] = jnp.concatenate(teacher_op, axis=0)
            high, low = split_high_low(student_t * STUDENT_SCALE)
            student_op = [student_gap, high, low, shift_rows(student_norm)]
            row_op[h, i, :, rows:] = jnp.concatenate(student_op, axis=0)

    safe = jnp.max(functools.reduce(jnp.maximum, norms)) <= SAFE_NORM
    key_pos = lax.broadcasted_iota(jnp.int32, (rows, rows), 0)
    row_pos = lax.broadcasted_iota(jnp.int32, (rows, rows), 1)

    def logits(h, i, j):
        keys = pl.ds(pl.multiple_of(j * rows, rows), rows)
        both = jnp.dot(key_op[h, keys, :], row_op[h, i], preferred_element_type=f32)
        return both[:, :rows], both[:, rows:]

    @pl.when(safe)
    def shifted_by_own_logit():
        key_grad[...] = jnp.zeros(key_grad.shape, f32)

        def exponentials(h, i, model, prob):
            upto = (i + 1) * rows
            depth = slice(2 * TEACHER_DIM if model else 0, DEPTH)
            op = row_op[h, i, depth, model * rows : (model + 1) * rows]
            values = jnp.dot(key_op[h, :upto, depth], op, preferred_element_type=f32)
            diagonal = jnp.where(key_pos <= row_pos, values[i * rows :], NEGATIVE)
            total = cross = jnp.zeros((8, rows), f32)
            for j in range(i + 1):
                value = diagonal if j == i else values[j * rows : (j + 1) * rows]
                exp = jnp.exp2(value)
                prob[i % 2, j] = exp
                total = total + fold(exp)
                weight = teacher_prob[i % 2, j] if model else exp
                cross = cross + fold(weight * value)
            return [jnp.sum(part, axis=0, keepdims=True) for part in (total, cross)]

        def weights(i, j, teacher_inv, student_inv):
            value = student_prob[i % 2, j] * student_inv - teacher_prob[i % 2, j] * teacher_inv
            weights_ref[j * rows : (j + 1) * rows, i * rows : (i + 1) * rows] = value.astype(bf16)

        def head_step(h, kl_total):
            inverse = None
            for i in range(tiles + 1):
                if i < tiles:
                    teacher_sum, teacher_cross = exponentials(h, i, 0, teacher_prob)
                    student_sum, student_cross = exponentials(h, i, 1, student_prob)
                if i:
                    upto = i * rows
                    for j in range(i):
                        weights(i - 1, j, *inverse)
                    row_grad[h, :, upto - rows : upto] = jnp.dot(
                        student_col[h, :, :upto],
                        weights_ref[:upto, upto - rows : upto],
                        preferred_element_type=f32,
                    )
                if i < tiles:
                    inverse = (1.0 / teacher_sum, 1.0 / student_sum)
                    kl_total = kl_total + (
                        (teacher_cross - student_cross) * inverse[0]
                        - jnp.log2(teacher_sum)
                        + jnp.log2(student_sum)
                    )
            for j in range(tiles):
                here = slice(j * rows, (j + 1) * rows)
                key_grad[here, :] = key_grad[here, :] + jnp.dot(
                    weights_ref[here, j * rows :],
                    student_pad[h, j * rows :, :],
                    preferred_element_type=f32,
                )
            return kl_total

        kl_sum[...] = lax.fori_loop(0, heads, head_step, jnp.zeros((1, rows), f32))

    @pl.when(jnp.logical_not(safe))
    def shifted_by_maximum():
        kl_sum[...] = jnp.zeros((1, rows), f32)
        key_grad[...] = jnp.zeros(key_grad.shape, f32)

        def masked(h, i, j):
            allowed = key_pos + j * rows <= row_pos + i * rows
            teacher, student = logits(h, i, j)
            return jnp.where(allowed, teacher, NEGATIVE), jnp.where(allowed, student, NEGATIVE)

        def row_step(step, _):
            h, i = step // tiles, step % tiles
            here = pl.ds(pl.multiple_of(i * rows, rows), rows)

            def advance(j, state):
                teacher_max, teacher_sum, cross_sum, student_max, student_sum = state
                teacher, student = masked(h, i, j)
                teacher_top = jnp.maximum(teacher_max, jnp.max(teacher, axis=0, keepdims=True))
                student_top = jnp.maximum(student_max, jnp.max(student, axis=0, keepdims=True))
                teacher_exp = jnp.exp2(teacher - teacher_top)
                student_exp = jnp.exp2(student - student_top)
                shrink = jnp.exp2(teacher_max - teacher_top)
                cross = jnp.sum(teacher_exp * (teacher - student), axis=0, keepdims=True)
                return (
                    teacher_top,
                    teacher_sum * shrink + jnp.sum(teacher_exp, axis=0, keepdims=True),
                    cross_sum * shrink + cross,
                    student_top,
                    student_sum * jnp.exp2(student_max - student_top)
                    + jnp.sum(student_exp, axis=0, keepdims=True),
                )

            lowest = jnp.full((1, rows), NEGATIVE, f32)
            zeros = jnp.zeros((1, rows), f32)
            teacher_max, teacher_sum, cross_sum, student_max, student_sum = lax.fori_loop(
                0, i + 1, advance, (lowest, zeros, zeros, lowest, zeros)
            )
            teacher_lse = teacher_max + jnp.log2(teacher_sum)
            student_lse = student_max + jnp.log2(student_sum)
            kl_sum[...] = kl_sum[...] + (cross_sum / teacher_sum - teacher_lse + student_lse)

            def spread(j, total):
                teacher, student = masked(h, i, j)
                value = jnp.exp2(student - student_lse) - jnp.exp2(teacher - teacher_lse)
                value = value.astype(bf16)
                keys = pl.ds(pl.multiple_of(j * rows, rows), rows)
                key_grad[keys, :] = key_grad[keys, :] + jnp.dot(
                    value, student_pad[h, here, :], preferred_element_type=f32
                )
                return total + jnp.dot(
                    student_col[h, :, keys], value, preferred_element_type=f32
                )

            row_grad[h, :, here] = lax.fori_loop(
                0, i + 1, spread, jnp.zeros((STUDENT_DIM, rows), f32)
            )
            return 0

        lax.fori_loop(0, heads * tiles, row_step, 0)

    if not last:
        return

    row_parts = [*done[::3], row_grad]
    key_parts = [*done[1::3], key_grad]
    total_width = len(row_parts) * student_width
    for i in range(tiles):
        here = slice(i * rows, (i + 1) * rows)
        columns = jnp.concatenate(
            [part[h, :, here] for part in row_parts for h in range(heads)], axis=0
        )
        lanes = jnp.concatenate([part[here, :] for part in key_parts], axis=1)
        grad_rows[here, :] = (columns.T + lanes) * (STUDENT_DIM**-0.5)
    grad_rows[pl.ds(live, window), :] = jnp.zeros((window, total_width), f32)
    kl_total = sum([ref[...] for ref in done[2::3]] + [kl_sum[...]])
    tokens = sum(counts_ref[b] for b in range(blocks))
    share = jnp.full((1, rows), math.log(2.0), f32) / (H_REL * tokens).astype(f32)
    kl_total = jnp.sum(kl_total * share, axis=1, keepdims=True)
    out[2][...] = jnp.broadcast_to(kl_total, out[2].shape)
    position = lax.broadcasted_iota(jnp.int32, (rows, window), 1)
    token = lax.broadcasted_iota(jnp.int32, (rows, window), 0)
    for k, (base, shift, count) in enumerate(places):
        place = ((position == token + shift) & (token < count)).astype(bf16)
        block = grad_rows[pl.ds(base, window), :].astype(bf16)
        out[k % 2][k // 2] = jnp.dot(place, block, preferred_element_type=f32).astype(bf16)


def local(teacher_queries, student_queries, token_counts):
    f32, bf16 = jnp.float32, jnp.bfloat16
    blocks = lax.axis_size("seq")
    chips = blocks // 2
    groups = lax.axis_size("head")
    rows = teacher_queries.shape[0]
    heads = teacher_queries.shape[1] // TEACHER_DIM // blocks
    tiles = blocks * 3 // 4
    live = tiles * rows
    folded = heads * STUDENT_DIM == LANES
    chunks = 2 if folded else 1
    chunk_heads = heads // chunks
    teacher_width = chunk_heads * TEACHER_DIM
    student_width = chunk_heads * STUDENT_DIM
    if folded:
        send_shape = (chips, rows + rows // 2, LANES)
    else:
        send_shape = (chips, rows, teacher_width + student_width)
    vmem = pl.BlockSpec(memory_space=pltpu.VMEM)
    smem = pl.BlockSpec(memory_space=pltpu.SMEM)
    params = pltpu.CompilerParams(vmem_limit_bytes=40 * 1024 * 1024)
    me = lax.axis_index("seq").reshape(1)
    far_first = sorted(range(1, chips), key=lambda k: -k.bit_count())

    def exchange(kept, swapped, kls=()):
        swapped = lax.ppermute(swapped, "seq", [(i, i ^ 1) for i in range(blocks)])
        shape = (2, kept.shape[1] + (TAIL if kls else 0), kept.shape[2])
        sends = pl.pallas_call(
            functools.partial(merge_kernel, chips),
            in_specs=[vmem] * (2 + len(kls)),
            out_specs=[vmem] * (chips - 1),
            out_shape=[jax.ShapeDtypeStruct(shape, bf16)] * (chips - 1),
            compiler_params=params,
            name="merge",
        )(kept, swapped, *kls)
        out = [None] * (chips - 1)
        for k in far_first:
            pairs = [(i, i ^ (2 * k)) for i in range(blocks)]
            out[k - 1] = lax.ppermute(sends[k - 1], "seq", pairs)
        return [kept, swapped] + out

    packed = jax.ShapeDtypeStruct(send_shape, bf16)
    first = jax.ShapeDtypeStruct(send_shape[1:], bf16)
    order = [0, 1, *range(2, blocks, 2), *range(3, blocks, 2)] if folded else None
    if folded:
        anywhere = pl.BlockSpec(memory_space=pltpu.HBM)
        sends = pl.pallas_call(
            functools.partial(pack_folded_kernel, blocks, chunks),
            in_specs=[smem, anywhere, anywhere],
            out_specs=[vmem] * (blocks + 2 * chunks - 2),
            out_shape=[first] * blocks + [packed] * (2 * chunks - 2),
            scratch_shapes=[
                pltpu.VMEM(student_queries.shape, bf16),
                pltpu.SemaphoreType.DMA((chunks * blocks + 1,)),
            ],
            compiler_params=pltpu.CompilerParams(vmem_limit_bytes=52 * 1024 * 1024),
            name="pack",
        )(me, teacher_queries, student_queries)
    else:
        sends = pl.pallas_call(
            functools.partial(pack_plain_kernel, blocks),
            in_specs=[smem, vmem, vmem],
            out_specs=[vmem] * 2,
            out_shape=[packed] * 2,
            compiler_params=params,
            name="pack",
        )(me, teacher_queries, student_queries)
    incoming = []
    if folded:
        incoming.append(
            [sends[0]]
            + [
                lax.ppermute(sends[k], "seq", [(i, i ^ k) for i in range(blocks)])
                for k in order[1:]
            ]
        )
        sends = sends[blocks:]
    incoming += [exchange(*pair) for pair in zip(sends[::2], sends[1::2])]

    result = [
        jax.ShapeDtypeStruct((chunk_heads, STUDENT_DIM, live), f32),
        jax.ShapeDtypeStruct((live, student_width), f32),
        jax.ShapeDtypeStruct((1, rows), f32),
    ]
    message = jax.ShapeDtypeStruct((chips, rows, heads * STUDENT_DIM), bf16)
    divergence = jax.ShapeDtypeStruct((1, heads * STUDENT_DIM), f32)
    pairs = chunk_heads * tiles * (tiles + 1) // 2 * rows * rows
    done = []
    for c in range(chunks):
        last = c == chunks - 1
        scratch = [
            pltpu.VMEM((live + rows + PAD, teacher_width + student_width), f32),
            pltpu.VMEM((chunk_heads, live, DEPTH), bf16),
            pltpu.VMEM((chunk_heads, tiles, DEPTH, 2 * rows), bf16),
            pltpu.VMEM((chunk_heads, STUDENT_DIM, live), bf16),
            pltpu.VMEM((chunk_heads, live, student_width), bf16),
            pltpu.VMEM((2, tiles, rows, rows), f32),
            pltpu.VMEM((2, tiles, rows, rows), f32),
            pltpu.VMEM((live, live), bf16),
        ]
        if last:
            scratch += [pltpu.VMEM(part.shape, f32) for part in result]
            scratch.append(pltpu.VMEM((live + rows + PAD, heads * STUDENT_DIM), f32))
        inputs = [me, token_counts, *incoming[c], *done]
        done += pl.pallas_call(
            functools.partial(
                relation_kernel,
                folded,
                chunk_heads,
                tiles,
                order if c == 0 else None,
                len(incoming[c]),
                c,
                last,
            ),
            in_specs=[smem, smem] + [vmem] * (len(inputs) - 2),
            out_specs=[vmem] * 3,
            out_shape=[message, message, divergence] if last else result,
            scratch_shapes=scratch,
            compiler_params=params,
            cost_estimate=pl.CostEstimate(
                flops=4 * pairs * DEPTH, bytes_accessed=8 * pairs, transcendentals=2 * pairs
            ),
            name="relation",
        )(*inputs)
    kept, swapped, kl = done[-3:]
    kl = kl + lax.ppermute(kl, "seq", [(i, i ^ 1) for i in range(blocks)])
    kls = [kl]
    for bit in range(groups.bit_length() - 1):
        own = pair_sum(kls)
        pairs = [(i, i ^ (1 << bit)) for i in range(groups)]
        kls = [own, lax.ppermute(own, "head", pairs)]
    returned = exchange(kept, swapped, kls)
    grad, loss = pl.pallas_call(
        functools.partial(unpack_kernel, len(kls)),
        in_specs=[smem] + [vmem] * (len(kls) + len(returned)),
        out_specs=[vmem] * 2,
        out_shape=[
            jax.ShapeDtypeStruct((rows, student_queries.shape[1]), f32),
            divergence,
        ],
        compiler_params=params,
        name="unpack",
    )(me, *kls, *returned)
    return (grad, loss[0, 0])


def solution(mesh):
    return jax.shard_map(
        local,
        mesh=mesh,
        in_specs=(P("seq", "head"), P("seq", "head"), P()),
        out_specs=(P("seq", "head"), P()),
        check_vma=False,
    )
```

```python
import functools
import math

import jax
import jax.numpy as jnp
from jax import lax
from jax.experimental import pallas as pl
from jax.experimental.pallas import tpu as pltpu
from jax.sharding import PartitionSpec as P

DT = 8192
DS = 4096
H_REL = 128
TEACHER_DIM = DT // H_REL
STUDENT_DIM = DS // H_REL

NEGATIVE = -1e30
LOG2E = math.log2(math.e)
TEACHER_SCALE = LOG2E * TEACHER_DIM**-0.5
STUDENT_SCALE = LOG2E * STUDENT_DIM**-0.5
PAD = 8
LANES = 128
TAIL = 16
DEPTH = 256
SAFE_NORM = 320.0


def split_high_low(values):
    high = values.astype(jnp.bfloat16)
    low = (values - high.astype(jnp.float32)).astype(jnp.bfloat16)
    return high, low


def split_three(values):
    high = values.astype(jnp.bfloat16)
    rest = values - high.astype(jnp.float32)
    return (high,) + split_high_low(rest)


def at_columns(index, count, width, act):
    if width % LANES == 0:
        act(pl.ds(pl.multiple_of(index * width, LANES), width))
    else:
        for part in range(count):
            pl.when(index == part)(functools.partial(act, pl.ds(part * width, width)))


def pack_folded_kernel(blocks, chunks, me_ref, teacher_ref, student_ref, *refs):
    sends, student, sems = refs[:-2], refs[-2], refs[-1]
    rows = teacher_ref.shape[0]
    half = rows // 2

    def block(chunk, k):
        if chunk == 0:
            return sends[k]
        return sends[blocks + 2 * (chunk - 1) + k % 2].at[k // 2]

    copies = [pltpu.make_async_copy(student_ref, student, sems.at[chunks * blocks])]
    for chunk in range(chunks):
        for k in range(blocks):
            to = jnp.bitwise_xor(me_ref[0], k)
            at = pl.multiple_of((to * chunks + chunk) * LANES, LANES)
            copies.append(
                pltpu.make_async_copy(
                    teacher_ref.at[:, pl.ds(at, LANES)],
                    block(chunk, k).at[pl.ds(0, rows)],
                    sems.at[chunk * blocks + k],
                )
            )
    for copy in copies:
        copy.start()
    copies[0].wait()
    for k in range(blocks):
        to = jnp.bitwise_xor(me_ref[0], k)
        lanes = pl.ds(pl.multiple_of(to * LANES, LANES), LANES)
        top, bottom = student[:half, lanes], student[half:, lanes]
        for chunk in range(chunks):
            part = slice(chunk * (LANES // 2), (chunk + 1) * (LANES // 2))
            block(chunk, k)[rows:, :] = jnp.concatenate([top[:, part], bottom[:, part]], axis=1)
    for copy in copies[1:]:
        copy.wait()


def pack_plain_kernel(blocks, me_ref, teacher_ref, student_ref, *sends):
    teacher_width = teacher_ref.shape[1] // blocks
    student_width = student_ref.shape[1] // blocks
    for core in range(2):
        for k in range(blocks // 2):
            to = jnp.bitwise_xor(me_ref[0], 2 * k + core)

            def put_teacher(columns, send=sends[core], k=k):
                send[k, :, :teacher_width] = teacher_ref[:, columns]

            def put_student(columns, send=sends[core], k=k):
                send[k, :, teacher_width:] = student_ref[:, columns]

            at_columns(to, blocks, teacher_width, put_teacher)
            at_columns(to, blocks, student_width, put_student)


def pair_sum(parts):
    while len(parts) > 1:
        parts = [a + b for a, b in zip(parts[::2], parts[1::2])]
    return parts[0]


def tail_rows(value, width):
    thirds = [part.astype(jnp.float32) for part in split_three(value)]
    line = lax.broadcasted_iota(jnp.int32, (TAIL, width), 0)
    tail = jnp.where(line == 0, thirds[0], 0.0)
    tail = jnp.where(line == 1, thirds[1], tail)
    return jnp.where(line == 2, thirds[2], tail).astype(jnp.bfloat16)


def merge_kernel(chips, kept_ref, swapped_ref, *refs):
    kls, sends = refs[: 1 - chips], refs[1 - chips :]
    rows = kept_ref.shape[1]
    tail = tail_rows(pair_sum([kl[...] for kl in kls]), kept_ref.shape[2]) if kls else None
    for k, send in enumerate(sends):
        send[0, :rows, :] = kept_ref[k + 1]
        send[1, :rows, :] = swapped_ref[k + 1]
        if kls:
            send[0, rows:, :] = tail
            send[1, rows:, :] = tail


def arrived(refs):
    return [refs[0].at[0], refs[1].at[0]] + [ref.at[core] for ref in refs[2:] for core in range(2)]


def unpack_kernel(n_kl, me_ref, *refs):
    kls, returned, (grad_ref, loss_ref) = refs[:n_kl], refs[n_kl:-2], refs[-2:]
    rows = grad_ref.shape[0]
    blocks = arrived(returned)
    for k, block in enumerate(blocks):

        def put(columns, block=block):
            grad_ref[:, columns] = block[:rows, :].astype(jnp.float32)

        at_columns(jnp.bitwise_xor(me_ref[0], k), len(blocks), block.shape[1], put)
    own = tail_rows(pair_sum([kl[...] for kl in kls]), kls[0].shape[1])
    tails = [own] + [ref[0, rows:, :] for ref in returned[2:]]
    loss_ref[...] = pair_sum(
        [jnp.sum(tail.astype(jnp.float32), axis=0, keepdims=True) for tail in tails]
    )


def fold(values):
    rows, columns = values.shape
    return jnp.sum(values.reshape(rows // 8, 8, columns), axis=0)


def relation_kernel(folded, heads, tiles, order, n_in, n_done, last, me_ref, counts_ref, *refs):
    if order:
        sources = [refs[order.index(k)] for k in range(n_in)]
    else:
        sources = arrived(refs[:n_in])
    done = refs[n_in : n_in + 3 * n_done]
    rest = list(refs[n_in + 3 * n_done :])
    out, rest = rest[:3], rest[3:]
    pack, key_op, row_op, student_col, student_pad, teacher_prob, student_prob, weights_ref = rest[:8]
    if last:
        row_grad, key_grad, kl_sum, grad_rows = rest[8:]
    else:
        row_grad, key_grad, kl_sum = out
    f32, bf16 = jnp.float32, jnp.bfloat16
    blocks = len(sources)
    rows = teacher_prob.shape[2]
    half = rows // 2
    live = tiles * rows
    window = rows + PAD
    student_at = heads * TEACHER_DIM
    student_width = heads * STUDENT_DIM
    filled = 2 * TEACHER_DIM + 2 * STUDENT_DIM

    position = lax.broadcasted_iota(jnp.int32, (window, rows), 0)
    token = lax.broadcasted_iota(jnp.int32, (window, rows), 1)
    pack[...] = jnp.zeros(pack.shape, f32)
    places = []
    for k in range(blocks):
        owner = jnp.bitwise_xor(me_ref[0], k)
        start = sum(jnp.where(b < owner, counts_ref[b], 0) for b in range(blocks))
        base = pl.multiple_of(start // PAD * PAD, PAD)
        places.append((base, start - base, counts_ref[owner]))
    for source, (base, shift, count) in zip(sources, places):
        place = ((position == token + shift) & (token < count)).astype(bf16)
        here = pl.ds(base, window)
        if folded:
            moved = jnp.dot(place, source[:rows, :], preferred_element_type=f32)
            pack[here, :student_at] = pack[here, :student_at] + moved
            student = source[rows:, :]
            moved = jnp.dot(
                place[:, :half], student[:, :student_width], preferred_element_type=f32
            ) + jnp.dot(place[:, half:], student[:, student_width:], preferred_element_type=f32)
            pack[here, student_at:] = pack[here, student_at:] + moved
        else:
            moved = jnp.dot(place, source[...], preferred_element_type=f32)
            pack[here, :] = pack[here, :] + moved

    ones = jnp.ones((rows, DEPTH - filled), bf16)
    spare = lax.broadcasted_iota(jnp.int32, (DEPTH - filled, rows), 0)
    teacher_gap = jnp.zeros((2 * STUDENT_DIM, rows), bf16)
    student_gap = jnp.zeros((2 * TEACHER_DIM, rows), bf16)
    lane_head = lax.broadcasted_iota(jnp.int32, (rows, student_width), 1) // STUDENT_DIM
    norms = []

    def shift_rows(norm):
        parts = [part.astype(f32) for part in split_three(-norm)]
        out = jnp.where(spare == 0, parts[0], 0.0)
        out = jnp.where(spare == 1, parts[1], out)
        return jnp.where(spare == 2, parts[2], out).astype(bf16)

    for i in range(tiles):
        here = pl.ds(i * rows, rows)
        tile = pack[here, :]
        tile_t = tile.T
        tile_b = tile.astype(bf16)
        tile_s = tile[:, student_at:]
        for h in range(heads):
            tb = tile_b[:, h * TEACHER_DIM : (h + 1) * TEACHER_DIM]
            at = student_at + h * STUDENT_DIM
            sb = tile_b[:, at : at + STUDENT_DIM]
            key_op[h, here, :] = jnp.concatenate([tb, tb, sb, sb, ones], axis=1)
            teacher_t = tile_t[h * TEACHER_DIM : (h + 1) * TEACHER_DIM, :]
            student_t = tile_t[at : at + STUDENT_DIM, :]
            student_col[h, :, here] = student_t.astype(bf16)
            student_pad[h, here, :] = jnp.where(lane_head == h, tile_s, 0.0).astype(bf16)
            teacher_norm = TEACHER_SCALE * jnp.sum(teacher_t * teacher_t, axis=0, keepdims=True)
            student_norm = STUDENT_SCALE * jnp.sum(student_t * student_t, axis=0, keepdims=True)
            norms += [teacher_norm, student_norm]
            high, low = split_high_low(teacher_t * TEACHER_SCALE)
            teacher_op = [high, low, teacher_gap, shift_rows(teacher_norm)]
            row_op[h, i, :, :rows] = jnp.concatenate(teacher_op, axis=0)
            high, low = split_high_low(student_t * STUDENT_SCALE)
            student_op = [student_gap, high, low, shift_rows(student_norm)]
            row_op[h, i, :, rows:] = jnp.concatenate(student_op, axis=0)

    safe = jnp.max(functools.reduce(jnp.maximum, norms)) <= SAFE_NORM
    key_pos = lax.broadcasted_iota(jnp.int32, (rows, rows), 0)
    row_pos = lax.broadcasted_iota(jnp.int32, (rows, rows), 1)

    def logits(h, i, j):
        keys = pl.ds(pl.multiple_of(j * rows, rows), rows)
        both = jnp.dot(key_op[h, keys, :], row_op[h, i], preferred_element_type=f32)
        return both[:, :rows], both[:, rows:]

    @pl.when(safe)
    def shifted_by_own_logit():
        key_grad[...] = jnp.zeros(key_grad.shape, f32)

        def exponentials(h, i, model, prob):
            upto = (i + 1) * rows
            depth = slice(2 * TEACHER_DIM if model else 0, DEPTH)
            op = row_op[h, i, depth, model * rows : (model + 1) * rows]
            values = jnp.dot(key_op[h, :upto, depth], op, preferred_element_type=f32)
            total = cross = jnp.zeros((8, rows), f32)
            for j in range(i):
                value = values[j * rows : (j + 1) * rows]
                exp = jnp.exp2(value)
                prob[i % 2, j] = exp
                total = total + fold(exp)
                weight = teacher_prob[i % 2, j] if model else exp
                cross = cross + fold(weight * value)
            diagonal = jnp.where(key_pos <= row_pos, values[i * rows :], NEGATIVE)
            half = rows // 2
            prob[i % 2, i, half:, :half] = jnp.zeros((half, half), f32)
            gap = jnp.zeros((8, half), f32)
            for keys, here in ((slice(0, half), slice(0, rows)), (slice(half, rows),) * 2):
                value = diagonal[keys, here]
                exp = jnp.exp2(value)
                prob[i % 2, i, keys, here] = exp
                weight = teacher_prob[i % 2, i, keys, here] if model else exp
                sums = [fold(exp), fold(weight * value)]
                if keys.start:
                    sums = [jnp.concatenate([gap, part], axis=1) for part in sums]
                total, cross = total + sums[0], cross + sums[1]
            return [jnp.sum(part, axis=0, keepdims=True) for part in (total, cross)]

        def weights(i, j, teacher_inv, student_inv):
            value = student_prob[i % 2, j] * student_inv - teacher_prob[i % 2, j] * teacher_inv
            weights_ref[j * rows : (j + 1) * rows, i * rows : (i + 1) * rows] = value.astype(bf16)

        def head_step(h, kl_total):
            inverse = None
            for i in range(tiles + 1):
                if i < tiles:
                    teacher_sum, teacher_cross = exponentials(h, i, 0, teacher_prob)
                    student_sum, student_cross = exponentials(h, i, 1, student_prob)
                if i:
                    upto = i * rows
                    for j in range(i):
                        weights(i - 1, j, *inverse)
                    row_grad[h, :, upto - rows : upto] = jnp.dot(
                        student_col[h, :, :upto],
                        weights_ref[:upto, upto - rows : upto],
                        preferred_element_type=f32,
                    )
                if i < tiles:
                    inverse = (1.0 / teacher_sum, 1.0 / student_sum)
                    kl_total = kl_total + (
                        (teacher_cross - student_cross) * inverse[0]
                        - jnp.log2(teacher_sum)
                        + jnp.log2(student_sum)
                    )
            for j in range(tiles):
                here = slice(j * rows, (j + 1) * rows)
                key_grad[here, :] = key_grad[here, :] + jnp.dot(
                    weights_ref[here, j * rows :],
                    student_pad[h, j * rows :, :],
                    preferred_element_type=f32,
                )
            return kl_total

        kl_sum[...] = lax.fori_loop(0, heads, head_step, jnp.zeros((1, rows), f32))

    @pl.when(jnp.logical_not(safe))
    def shifted_by_maximum():
        kl_sum[...] = jnp.zeros((1, rows), f32)
        key_grad[...] = jnp.zeros(key_grad.shape, f32)

        def masked(h, i, j):
            allowed = key_pos + j * rows <= row_pos + i * rows
            teacher, student = logits(h, i, j)
            return jnp.where(allowed, teacher, NEGATIVE), jnp.where(allowed, student, NEGATIVE)

        def row_step(step, _):
            h, i = step // tiles, step % tiles
            here = pl.ds(pl.multiple_of(i * rows, rows), rows)

            def advance(j, state):
                teacher_max, teacher_sum, cross_sum, student_max, student_sum = state
                teacher, student = masked(h, i, j)
                teacher_top = jnp.maximum(teacher_max, jnp.max(teacher, axis=0, keepdims=True))
                student_top = jnp.maximum(student_max, jnp.max(student, axis=0, keepdims=True))
                teacher_exp = jnp.exp2(teacher - teacher_top)
                student_exp = jnp.exp2(student - student_top)
                shrink = jnp.exp2(teacher_max - teacher_top)
                cross = jnp.sum(teacher_exp * (teacher - student), axis=0, keepdims=True)
                return (
                    teacher_top,
                    teacher_sum * shrink + jnp.sum(teacher_exp, axis=0, keepdims=True),
                    cross_sum * shrink + cross,
                    student_top,
                    student_sum * jnp.exp2(student_max - student_top)
                    + jnp.sum(student_exp, axis=0, keepdims=True),
                )

            lowest = jnp.full((1, rows), NEGATIVE, f32)
            zeros = jnp.zeros((1, rows), f32)
            teacher_max, teacher_sum, cross_sum, student_max, student_sum = lax.fori_loop(
                0, i + 1, advance, (lowest, zeros, zeros, lowest, zeros)
            )
            teacher_lse = teacher_max + jnp.log2(teacher_sum)
            student_lse = student_max + jnp.log2(student_sum)
            kl_sum[...] = kl_sum[...] + (cross_sum / teacher_sum - teacher_lse + student_lse)

            def spread(j, total):
                teacher, student = masked(h, i, j)
                value = jnp.exp2(student - student_lse) - jnp.exp2(teacher - teacher_lse)
                value = value.astype(bf16)
                keys = pl.ds(pl.multiple_of(j * rows, rows), rows)
                key_grad[keys, :] = key_grad[keys, :] + jnp.dot(
                    value, student_pad[h, here, :], preferred_element_type=f32
                )
                return total + jnp.dot(
                    student_col[h, :, keys], value, preferred_element_type=f32
                )

            row_grad[h, :, here] = lax.fori_loop(
                0, i + 1, spread, jnp.zeros((STUDENT_DIM, rows), f32)
            )
            return 0

        lax.fori_loop(0, heads * tiles, row_step, 0)

    if not last:
        return

    row_parts = [*done[::3], row_grad]
    key_parts = [*done[1::3], key_grad]
    total_width = len(row_parts) * student_width
    for i in range(tiles):
        here = slice(i * rows, (i + 1) * rows)
        columns = jnp.concatenate(
            [part[h, :, here] for part in row_parts for h in range(heads)], axis=0
        )
        lanes = jnp.concatenate([part[here, :] for part in key_parts], axis=1)
        grad_rows[here, :] = (columns.T + lanes) * (STUDENT_DIM**-0.5)
    grad_rows[pl.ds(live, window), :] = jnp.zeros((window, total_width), f32)
    kl_total = sum([ref[...] for ref in done[2::3]] + [kl_sum[...]])
    tokens = sum(counts_ref[b] for b in range(blocks))
    share = jnp.full((1, rows), math.log(2.0), f32) / (H_REL * tokens).astype(f32)
    kl_total = jnp.sum(kl_total * share, axis=1, keepdims=True)
    out[2][...] = jnp.broadcast_to(kl_total, out[2].shape)
    position = lax.broadcasted_iota(jnp.int32, (rows, window), 1)
    token = lax.broadcasted_iota(jnp.int32, (rows, window), 0)
    for k, (base, shift, count) in enumerate(places):
        place = ((position == token + shift) & (token < count)).astype(bf16)
        block = grad_rows[pl.ds(base, window), :].astype(bf16)
        out[k % 2][k // 2] = jnp.dot(place, block, preferred_element_type=f32).astype(bf16)


def local(teacher_queries, student_queries, token_counts):
    f32, bf16 = jnp.float32, jnp.bfloat16
    blocks = lax.axis_size("seq")
    chips = blocks // 2
    groups = lax.axis_size("head")
    rows = teacher_queries.shape[0]
    heads = teacher_queries.shape[1] // TEACHER_DIM // blocks
    tiles = blocks * 3 // 4
    live = tiles * rows
    folded = heads * STUDENT_DIM == LANES
    chunks = 2 if folded else 1
    chunk_heads = heads // chunks
    teacher_width = chunk_heads * TEACHER_DIM
    student_width = chunk_heads * STUDENT_DIM
    if folded:
        send_shape = (chips, rows + rows // 2, LANES)
    else:
        send_shape = (chips, rows, teacher_width + student_width)
    vmem = pl.BlockSpec(memory_space=pltpu.VMEM)
    smem = pl.BlockSpec(memory_space=pltpu.SMEM)
    params = pltpu.CompilerParams(vmem_limit_bytes=40 * 1024 * 1024)
    me = lax.axis_index("seq").reshape(1)
    far_first = sorted(range(1, chips), key=lambda k: -k.bit_count())

    def exchange(kept, swapped, kls=()):
        swapped = lax.ppermute(swapped, "seq", [(i, i ^ 1) for i in range(blocks)])
        shape = (2, kept.shape[1] + (TAIL if kls else 0), kept.shape[2])
        sends = pl.pallas_call(
            functools.partial(merge_kernel, chips),
            in_specs=[vmem] * (2 + len(kls)),
            out_specs=[vmem] * (chips - 1),
            out_shape=[jax.ShapeDtypeStruct(shape, bf16)] * (chips - 1),
            compiler_params=params,
            name="merge",
        )(kept, swapped, *kls)
        out = [None] * (chips - 1)
        for k in far_first:
            pairs = [(i, i ^ (2 * k)) for i in range(blocks)]
            out[k - 1] = lax.ppermute(sends[k - 1], "seq", pairs)
        return [kept, swapped] + out

    packed = jax.ShapeDtypeStruct(send_shape, bf16)
    first = jax.ShapeDtypeStruct(send_shape[1:], bf16)
    order = [0, 1, *range(2, blocks, 2), *range(3, blocks, 2)] if folded else None
    if folded:
        anywhere = pl.BlockSpec(memory_space=pltpu.HBM)
        sends = pl.pallas_call(
            functools.partial(pack_folded_kernel, blocks, chunks),
            in_specs=[smem, anywhere, anywhere],
            out_specs=[vmem] * (blocks + 2 * chunks - 2),
            out_shape=[first] * blocks + [packed] * (2 * chunks - 2),
            scratch_shapes=[
                pltpu.VMEM(student_queries.shape, bf16),
                pltpu.SemaphoreType.DMA((chunks * blocks + 1,)),
            ],
            compiler_params=pltpu.CompilerParams(vmem_limit_bytes=52 * 1024 * 1024),
            name="pack",
        )(me, teacher_queries, student_queries)
    else:
        sends = pl.pallas_call(
            functools.partial(pack_plain_kernel, blocks),
            in_specs=[smem, vmem, vmem],
            out_specs=[vmem] * 2,
            out_shape=[packed] * 2,
            compiler_params=params,
            name="pack",
        )(me, teacher_queries, student_queries)
    incoming = []
    if folded:
        incoming.append(
            [sends[0]]
            + [
                lax.ppermute(sends[k], "seq", [(i, i ^ k) for i in range(blocks)])
                for k in order[1:]
            ]
        )
        sends = sends[blocks:]
    incoming += [exchange(*pair) for pair in zip(sends[::2], sends[1::2])]

    result = [
        jax.ShapeDtypeStruct((chunk_heads, STUDENT_DIM, live), f32),
        jax.ShapeDtypeStruct((live, student_width), f32),
        jax.ShapeDtypeStruct((1, rows), f32),
    ]
    message = jax.ShapeDtypeStruct((chips, rows, heads * STUDENT_DIM), bf16)
    divergence = jax.ShapeDtypeStruct((1, heads * STUDENT_DIM), f32)
    pairs = chunk_heads * tiles * (tiles + 1) // 2 * rows * rows
    done = []
    for c in range(chunks):
        last = c == chunks - 1
        scratch = [
            pltpu.VMEM((live + rows + PAD, teacher_width + student_width), f32),
            pltpu.VMEM((chunk_heads, live, DEPTH), bf16),
            pltpu.VMEM((chunk_heads, tiles, DEPTH, 2 * rows), bf16),
            pltpu.VMEM((chunk_heads, STUDENT_DIM, live), bf16),
            pltpu.VMEM((chunk_heads, live, student_width), bf16),
            pltpu.VMEM((2, tiles, rows, rows), f32),
            pltpu.VMEM((2, tiles, rows, rows), f32),
            pltpu.VMEM((live, live), bf16),
        ]
        if last:
            scratch += [pltpu.VMEM(part.shape, f32) for part in result]
            scratch.append(pltpu.VMEM((live + rows + PAD, heads * STUDENT_DIM), f32))
        inputs = [me, token_counts, *incoming[c], *done]
        done += pl.pallas_call(
            functools.partial(
                relation_kernel,
                folded,
                chunk_heads,
                tiles,
                order if c == 0 else None,
                len(incoming[c]),
                c,
                last,
            ),
            in_specs=[smem, smem] + [vmem] * (len(inputs) - 2),
            out_specs=[vmem] * 3,
            out_shape=[message, message, divergence] if last else result,
            scratch_shapes=scratch,
            compiler_params=params,
            cost_estimate=pl.CostEstimate(
                flops=4 * pairs * DEPTH, bytes_accessed=8 * pairs, transcendentals=2 * pairs
            ),
            name="relation",
        )(*inputs)
    kept, swapped, kl = done[-3:]
    kl = kl + lax.ppermute(kl, "seq", [(i, i ^ 1) for i in range(blocks)])
    kls = [kl]
    for bit in range(groups.bit_length() - 1):
        own = pair_sum(kls)
        pairs = [(i, i ^ (1 << bit)) for i in range(groups)]
        kls = [own, lax.ppermute(own, "head", pairs)]
    returned = exchange(kept, swapped, kls)
    grad, loss = pl.pallas_call(
        functools.partial(unpack_kernel, len(kls)),
        in_specs=[smem] + [vmem] * (len(kls) + len(returned)),
        out_specs=[vmem] * 2,
        out_shape=[
            jax.ShapeDtypeStruct((rows, student_queries.shape[1]), f32),
            divergence,
        ],
        compiler_params=params,
        name="unpack",
    )(me, *kls, *returned)
    return (grad, loss[0, 0])


def solution(mesh):
    return jax.shard_map(
        local,
        mesh=mesh,
        in_specs=(P("seq", "head"), P("seq", "head"), P()),
        out_specs=(P("seq", "head"), P()),
        check_vma=False,
    )
```
